32 devices in a mesh: dp: 8 (over z, x), seq: 4 (over y, core).
Axes of the slice: x: 2, y: 2, z: 4, core: 2. Of those that a mesh axis runs over, the one named last changes fastest.
Arguments:
- tokens: bfloat16 [16384, 768], P(('dp', 'seq')), may hold values from -6 to 6
- filled_blocks: int32 [8], P('dp'), may hold values from 25 to 32, as said below
- random_blocks: int32 [8, 32, 12, 3], P('dp', None, 'seq'), may hold values from 1 to 30, as said below
- query_weight: bfloat16 [768, 768], replicated, may hold values from -0.3125 to 0.3125
- query_bias: float32 [768], replicated, may hold values from -1.75 to 1.75
- key_weight: bfloat16 [768, 768], replicated, may hold values from -0.21875 to 0.21875
- value_weight: bfloat16 [768, 768], replicated, may hold values from -0.21875 to 0.21875
- value_bias: float32 [768], replicated, may hold values from -1.75 to 1.75
- out_weight: bfloat16 [768, 768], replicated, may hold values from -1.75 to 1.75
- out_bias: float32 [768], replicated, may hold values from -1.75 to 1.75
- attn_gain: float32 [768], replicated, may hold values from 0.1 to 1.9
- attn_shift: float32 [768], replicated, may hold values from -1.75 to 1.75
- up_weight: bfloat16 [768, 3072], replicated, may hold values from -0.21875 to 0.21875
- up_bias: float32 [3072], replicated, may hold values from -1.75 to 1.75
- down_weight: bfloat16 [3072, 768], replicated, may hold values from -0.109375 to 0.109375
- down_bias: float32 [768], replicated, may hold values from -1.75 to 1.75
- ffn_gain: float32 [768], replicated, may hold values from 0.1 to 1.9
- ffn_shift: float32 [768], replicated, may hold values from -1.75 to 1.75
- cotangent: bfloat16 [16384, 768], P(('dp', 'seq')), may hold values from -6 to 6
Outputs:
- layer_out: bfloat16 [16384, 768], P(('dp', 'seq'))
- grad_tokens: float32 [16384, 768], P(('dp', 'seq'))
- grad_query_weight: float32 [768, 768], P(('dp', 'seq'))
- grad_query_bias: float32 [768], P(('dp', 'seq'))
- grad_key_weight: float32 [768, 768], P(('dp', 'seq'))
- grad_value_weight: float32 [768, 768], P(('dp', 'seq'))
- grad_value_bias: float32 [768], P(('dp', 'seq'))
- grad_out_weight: float32 [768, 768], P(('dp', 'seq'))
- grad_out_bias: float32 [768], P(('dp', 'seq'))
- grad_attn_gain: float32 [768], P(('dp', 'seq'))
- grad_attn_shift: float32 [768], P(('dp', 'seq'))
- grad_up_weight: float32 [768, 3072], P(('dp', 'seq'))
- grad_up_bias: float32 [3072], P(('dp', 'seq'))
- grad_down_weight: float32 [3072, 768], P(('dp', 'seq'))
- grad_down_bias: float32 [768], P(('dp', 'seq'))
- grad_ffn_gain: float32 [768], P(('dp', 'seq'))
- grad_ffn_shift: float32 [768], P(('dp', 'seq'))
The draws below stay inside these ranges and needn't reach their ends.
Inputs may be any that keep to these rules, and one draw needn't show every extreme that they name: Slot s holds 64 * filled_blocks[s] tokens of one document, the rest padding; in every draw some slot is full and some other slot has the fewest. `random_blocks`: the three entries of a slot, query block and head differ from each other, lie below the slot's filled_blocks, and are none of block 0, the slot's last filled block, the query block and its two neighbours.
All inputs are finite; a program needn't handle non-finite values.
Results may differ from the reference program's by a relative error of at most 0.015.
The reference program's roundings to bfloat16 on the way count: a program that leaves them out, or rounds other values in their place, can miss the bound.
Values may be sent and summed in bfloat16 or wider, within the bound.
A program may use at most 192 MiB of HBM per device.

```python
import jax
import jax.numpy as jnp
from jax import lax

D = 768
HEADS = 12
HEAD_DIM = 64
FF = 3072
BLK = 64
SLOT = 2048
NBLK = 32
NB_MIN = 25
SLOTS = 8
TOKENS = 16384


def slot_counts(key):
    first, second, third = jax.random.split(key, 3)
    counts = jax.random.randint(first, (SLOTS,), NB_MIN, NBLK + 1)
    fullest = jax.random.randint(second, (), 0, SLOTS)
    fewest = (fullest + 1 + jax.random.randint(third, (), 0, SLOTS - 1)) % SLOTS
    slots_at = jnp.arange(SLOTS)
    counts = jnp.where(slots_at == fewest, NB_MIN, counts)
    counts = jnp.where(slots_at == fullest, NBLK, counts)
    return counts.astype(jnp.int32)


def draw_filled_blocks(key, part):
    return slot_counts(key)


def draw_random_blocks(key, part):
    counts = slot_counts(key)
    key = jax.random.fold_in(key, 7)
    raw = jax.random.randint(key, (SLOTS, NBLK, HEADS, NBLK), 0, 1 << 20)
    candidate = jnp.arange(NBLK, dtype=jnp.int32)[None, None, None, :]
    query_at = jnp.arange(NBLK, dtype=jnp.int32)[None, :, None, None]
    filled = counts[:, None, None, None]
    allowed = (candidate < filled) & (candidate != 0) & (candidate != filled - 1) & (jnp.abs(candidate - query_at) > 1)
    score = jnp.where(allowed, raw * NBLK + candidate + NBLK, candidate)
    picked = lax.top_k(score, 3)[0]
    return (picked % NBLK).astype(jnp.int32)


def shard_levels(key, dims, shards, least, largest):
    def one(position, blocks):
        draws = jax.random.uniform(jax.random.fold_in(jax.random.fold_in(key, 6), position), (blocks,), jnp.float32, least / len(shards), largest / len(shards))
        return jnp.repeat(jnp.exp(draws), dims[position] // blocks).reshape((-1,) + (1,) * (len(dims) - position - 1))

    level = one(*shards[0])
    for cut in shards[1:]:
        level = level * one(*cut)
    return level


def noise(rng, dims, spread, most, pieces=(), kind=jnp.bfloat16):
    drawn = jax.random.normal(rng, dims, jnp.float32) * spread
    if len(pieces) > 0:
        drawn = shard_levels(rng, dims, pieces, -0.22, 0.18) * drawn
    return jnp.clip(drawn, min=-most, max=most).astype(kind)


def setup_inputs(seed: int = 0) -> dict:
    splits = jax.random.split(jax.random.key(seed), 20)
    return {
        "tokens": noise(splits[0], (TOKENS, D), 1.0, 6.0, ((0, 32),)),
        "filled_blocks": draw_filled_blocks(jax.random.fold_in(splits[19], 71), 0),
        "random_blocks": draw_random_blocks(jax.random.fold_in(splits[19], 71), 0),
        "query_weight": noise(splits[3], (D, D), (D // 2) ** -0.5, 0.3125),
        "query_bias": noise(splits[4], (D,), 0.3, 1.75, (), jnp.float32),
        "key_weight": noise(splits[5], (D, D), D ** -0.5, 0.21875),
        "value_weight": noise(splits[6], (D, D), D ** -0.5, 0.21875),
        "value_bias": noise(splits[7], (D,), 0.3, 1.75, (), jnp.float32),
        "out_weight": noise(splits[8], (D, D), (D // 64) ** -0.5, 1.75),
        "out_bias": noise(splits[9], (D,), 0.3, 1.75, (), jnp.float32),
        "attn_gain": jnp.clip(1.0 + 0.18 * jax.random.normal(splits[10], (D,), jnp.float32), 0.1, 1.9),
        "attn_shift": noise(splits[11], (D,), 0.3, 1.75, (), jnp.float32),
        "up_weight": noise(splits[12], (D, FF), D ** -0.5, 0.21875),
        "up_bias": noise(splits[13], (FF,), 0.3, 1.75, (), jnp.float32),
        "down_weight": noise(splits[14], (FF, D), FF ** -0.5, 0.109375),
        "down_bias": noise(splits[15], (D,), 0.3, 1.75, (), jnp.float32),
        "ffn_gain": jnp.clip(1.0 + 0.18 * jax.random.normal(splits[16], (D,), jnp.float32), 0.1, 1.9),
        "ffn_shift": noise(splits[17], (D,), 0.3, 1.75, (), jnp.float32),
        "cotangent": noise(splits[18], (TOKENS, D), 1.0, 6.0, ((0, 32),)),
    }


NORM_EPS = 1e-05
MASKED = -1e+30

@jax.custom_vjp
def low(v):
    return lax.optimization_barrier(v.astype(jnp.bfloat16)).astype(jnp.float32)

@jax.custom_vjp
def low_back(v):
    return v

def low_keep(v):
    return (low(v), None)

def low_pass(kept, grad):
    return (grad,)

def back_keep(v):
    return (v, None)

def back_low(kept, grad):
    return (low(grad),)
low.defvjp(low_keep, low_pass)
low_back.defvjp(back_keep, back_low)

def key_table(filled, chosen, block_count):
    rows_at = jnp.arange(block_count, dtype=jnp.int32)[:, None]
    window = rows_at + jnp.array([-1, 0, 1], dtype=jnp.int32)[None, :]
    window_ok = (window >= 0) & (window < filled)
    window = jnp.clip(window, 0, block_count - 1)
    head_count = chosen.shape[1]
    last_block = jnp.zeros_like(rows_at) + (filled - 1)
    global_index = jnp.concatenate([jnp.zeros_like(rows_at), last_block], axis=1)
    global_ok = jnp.concatenate([rows_at >= 2, jnp.abs(rows_at - (filled - 1)) > 1], axis=1)
    index = jnp.concatenate([jnp.broadcast_to(window[:, None, :], (block_count, head_count, 3)), chosen.astype(jnp.int32), jnp.broadcast_to(global_index[:, None, :], (block_count, head_count, 2))], axis=2)
    allowed = jnp.concatenate([jnp.broadcast_to(window_ok[:, None, :], (block_count, head_count, 3)), jnp.ones((block_count, head_count, 3), dtype=jnp.bool_), jnp.broadcast_to(global_ok[:, None, :], (block_count, head_count, 2))], axis=2)
    return (index, allowed)

def attend_head(query, keys, values, index, allowed):
    group_len, block_len, head_len = query.shape
    picked_keys = keys[index].reshape(group_len, -1, head_len)
    picked_values = values[index].reshape(group_len, -1, head_len)
    scores = jnp.einsum('pqd,pkd->pqk', query, picked_keys, precision=lax.Precision.HIGHEST) * HEAD_DIM ** (-0.5)
    scores = low_back(scores)
    mask = jnp.repeat(allowed, block_len, axis=1)[:, None, :]
    scores = jnp.where(mask, scores, MASKED)
    highest = lax.optimization_barrier(jnp.max(scores, axis=-1, keepdims=True))
    weights = jnp.exp(scores - highest)
    share = weights / lax.optimization_barrier(jnp.sum(weights, axis=-1, keepdims=True))
    return jnp.einsum('pqk,pkd->pqd', low(share), picked_values, precision=lax.Precision.HIGHEST)

def attend_slot(query, keys, values, index, allowed):
    per_group = min(NBLK, 512 // BLK)
    groups = NBLK // per_group
    query_groups = query.reshape(HEADS, groups, per_group, BLK, HEAD_DIM).transpose(1, 0, 2, 3, 4)
    index_groups = index.reshape(groups, per_group, HEADS, 8).transpose(0, 2, 1, 3)
    allowed_groups = allowed.reshape(groups, per_group, HEADS, 8).transpose(0, 2, 1, 3)

    def one_group(inputs):
        return jax.vmap(attend_head)(inputs[0], keys, values, inputs[1], inputs[2])
    outputs = lax.map(jax.checkpoint(one_group), (query_groups, index_groups, allowed_groups))
    return outputs.transpose(1, 0, 2, 3, 4).reshape(HEADS, NBLK, BLK, HEAD_DIM)

def layer_norm(values, gain, shift):
    center = lax.optimization_barrier(jnp.mean(values, axis=-1, keepdims=True))
    centered = values - center
    variance = lax.optimization_barrier(jnp.mean(centered * centered, axis=-1, keepdims=True))
    return centered * lax.rsqrt(variance + NORM_EPS) * gain + shift

def product(left, right):
    return jnp.dot(left, right, precision=lax.Precision.HIGHEST)

def split_heads(tensor):
    return tensor.reshape(NBLK, BLK, HEADS, HEAD_DIM).transpose(2, 0, 1, 3)

def layer(inputs, params, filled, chosen):
    query_weight, query_bias, key_weight, value_weight, value_bias, out_weight, out_bias, attn_gain, attn_shift, up_weight, up_bias, down_weight, down_bias, ffn_gain, ffn_shift = params
    query = low_back(low(product(inputs, query_weight) + query_bias))
    keys = low_back(low(product(inputs, key_weight)))
    values = low_back(low(product(inputs, value_weight) + value_bias))
    index, allowed = key_table(filled, chosen, NBLK)
    heads_out = attend_slot(split_heads(query), split_heads(keys), split_heads(values), index, allowed)
    live_blocks = (jnp.arange(NBLK, dtype=jnp.int32) < filled).astype(jnp.float32)
    heads_out = heads_out * live_blocks[None, :, None, None]
    merged = heads_out.transpose(1, 2, 0, 3).reshape(SLOT, D)
    merged = low_back(low(merged))
    attn = low_back(product(merged, out_weight) + out_bias)
    first = layer_norm(inputs + attn, attn_gain, attn_shift)
    hidden = low_back(product(low(first), up_weight) + up_bias)
    act = low(jax.nn.gelu(hidden))
    ffn = low_back(product(act, down_weight) + down_bias)
    return layer_norm(first + ffn, ffn_gain, ffn_shift)

def reference(tokens, filled_blocks, random_blocks, query_weight, query_bias, key_weight, value_weight, value_bias, out_weight, out_bias, attn_gain, attn_shift, up_weight, up_bias, down_weight, down_bias, ffn_gain, ffn_shift, cotangent):
    params = tuple((param.astype(jnp.float32) for param in (query_weight, query_bias, key_weight, value_weight, value_bias, out_weight, out_bias, attn_gain, attn_shift, up_weight, up_bias, down_weight, down_bias, ffn_gain, ffn_shift)))
    slot_inputs = tokens.astype(jnp.float32).reshape(SLOTS, SLOT, D)
    slot_cots = cotangent.astype(jnp.float32).reshape(SLOTS, SLOT, D)

    def one_slot(totals, inputs):
        slot_tokens, slot_cot, filled, chosen = inputs

        def forward(layer_in, weights):
            return layer(layer_in, weights, filled, chosen)
        output, pull = jax.vjp(forward, slot_tokens, params)
        live = (jnp.arange(SLOT, dtype=jnp.int32) < filled * BLK).astype(jnp.float32)
        grad_in, grad_weights = pull(slot_cot * live[:, None])
        totals = tuple((running + added for running, added in zip(totals, grad_weights)))
        return (totals, (output.astype(jnp.bfloat16), grad_in))
    zeros = tuple((jnp.zeros_like(param) for param in params))
    totals, (outputs, grad_inputs) = lax.scan(one_slot, zeros, (slot_inputs, slot_cots, filled_blocks, random_blocks))
    return (outputs.reshape(TOKENS, D), grad_inputs.reshape(TOKENS, D), totals[0], totals[1], totals[2], totals[3], totals[4], totals[5], totals[6], totals[7], totals[8], totals[9], totals[10], totals[11], totals[12], totals[13], totals[14])
```

```python
import functools

import jax
import jax.numpy as jnp
from jax import lax
from jax.experimental import pallas as pl
from jax.experimental.pallas import tpu as pltpu
from jax.sharding import PartitionSpec as P

HEAD_DIM = 64
BLK = 64
PAIR = 2 * HEAD_DIM
TABLE = 8
NORM_EPS = 1e-05
MASKED = -1e30
SCALE = HEAD_DIM ** (-0.5)
MESH = pl.DeviceIdType.MESH
BF16 = jnp.bfloat16
F32 = jnp.float32
VMEM = pltpu.VMEM
LIMIT = 60 << 20


def whole_vmem():
    return pl.BlockSpec(memory_space=pltpu.VMEM)


def dot(left, right):
    return jnp.dot(left, right, preferred_element_type=F32)


def dot_nt(left, right):
    return lax.dot_general(left, right, (((1,), (1,)), ((), ())), preferred_element_type=F32)


def dot_tn(left, right):
    return lax.dot_general(left, right, (((0,), (0,)), ((), ())), preferred_element_type=F32)


def gather_kernel(
    rows, width, x_ref, tab_ref, wq_ref, qb_ref, wk_ref, wv_ref, vb_ref,
    q_ref, k_ref, v_ref, far_ref, tab_out, land, tab_land, sends, recvs, tab_sends, tab_recvs,
):
    parts = 4
    part = rows // parts
    dp, me = lax.axis_index("dp"), lax.axis_index("seq")
    mate, across, diagonal = (lax.bitwise_xor(me, bit) for bit in (1, 2, 3))
    barrier = pltpu.get_barrier_semaphore()
    for other in (mate, across, diagonal):
        pl.semaphore_signal(barrier, inc=1, device_id=(dp, other), device_id_type=MESH)
    pl.semaphore_wait(barrier, 3)

    def send(src, dst, slot, target):
        copy = pltpu.make_async_remote_copy(
            src_ref=src, dst_ref=dst, send_sem=sends.at[slot], recv_sem=recvs.at[slot],
            device_id=(dp, target), device_id_type=MESH,
        )
        copy.start()
        return copy

    far = [
        send(x_ref.at[pl.ds(r * part, part)], land.at[0, pl.ds(r * part, part)], r, across)
        for r in range(parts)
    ]
    near = send(x_ref, land.at[1], parts, mate)
    tables = []
    own_blocks = tab_ref.shape[0] // 4
    for slot, other in enumerate((mate, across, diagonal)):
        copy = pltpu.make_async_remote_copy(
            src_ref=tab_ref.at[pl.ds(pl.multiple_of(other * own_blocks, 8), own_blocks)],
            dst_ref=tab_land.at[slot], send_sem=tab_sends.at[slot], recv_sem=tab_recvs.at[slot],
            device_id=(dp, other), device_id_type=MESH,
        )
        copy.start()
        tables.append(copy)

    def keys_values(x, at):
        k_ref[pl.ds(at, width), :] = dot(x, wk_ref[...]).astype(BF16)
        v_ref[pl.ds(at, width), :] = (dot(x, wv_ref[...]) + vb_ref[...]).astype(BF16)

    def own(r, _):
        at = pl.multiple_of(r * width, width)
        x = x_ref[pl.ds(at, width), :]
        q_ref[pl.ds(at, width), :] = (
            (dot(x, wq_ref[...]) + qb_ref[...]).astype(BF16) * jnp.asarray(SCALE, BF16)
        )
        keys_values(x, pl.multiple_of(me * rows + at, width))
        return 0

    lax.fori_loop(0, rows // width, own, 0)

    def block(slot, owner, start, count):
        def step(r, _):
            at = pl.multiple_of(start + r * width, width)
            keys_values(land[slot, pl.ds(at, width), :], pl.multiple_of(owner * rows + at, width))
            return 0

        lax.fori_loop(0, count // width, step, 0)

    near.wait()
    block(1, mate, 0, rows)
    relayed = []
    for r in range(parts):
        far[r].wait()
        piece = pl.ds(r * part, part)
        relayed.append(send(land.at[0, piece], land.at[2, piece], parts + 1 + r, mate))
        block(0, across, r * part, part)
        if r:
            relayed[r - 1].wait()
            block(2, diagonal, (r - 1) * part, part)
    far_ref[...] = land[0]
    for copy in tables:
        copy.wait()
    relayed[-1].wait()
    block(2, diagonal, (parts - 1) * part, part)
    tab_out[pl.ds(me, 1)] = tab_ref[pl.ds(pl.multiple_of(me * own_blocks, 8), own_blocks)][None]
    for slot, other in enumerate((mate, across, diagonal)):
        tab_out[pl.ds(other, 1)] = tab_land[slot][None]


def gather_project(tokens, table, query_weight, query_bias, key_weight, value_weight, value_bias):
    rows, features = tokens.shape
    own_blocks = rows // BLK
    copies = 4 + 1 + 4
    return pl.pallas_call(
        functools.partial(gather_kernel, rows, 128),
        out_shape=(
            jax.ShapeDtypeStruct((rows, features), BF16),
            jax.ShapeDtypeStruct((4 * rows, features), BF16),
            jax.ShapeDtypeStruct((4 * rows, features), BF16),
            jax.ShapeDtypeStruct((rows, features), BF16),
            jax.ShapeDtypeStruct((4, own_blocks, 128), jnp.int32),
        ),
        in_specs=[whole_vmem()] * 7,
        out_specs=(whole_vmem(),) * 5,
        scratch_shapes=[
            VMEM((3, rows, features), BF16),
            VMEM((3, own_blocks, 128), jnp.int32),
            pltpu.SemaphoreType.DMA((copies,)),
            pltpu.SemaphoreType.DMA((copies,)),
            pltpu.SemaphoreType.DMA((3,)),
            pltpu.SemaphoreType.DMA((3,)),
        ],
        compiler_params=pltpu.CompilerParams(
            collective_id=0, has_side_effects=True, vmem_limit_bytes=LIMIT
        ),
        name="gather_project",
    )(tokens, table, query_weight, query_bias[None], key_weight, value_weight, value_bias[None])


def picks(tab_ref, filled, pair, i, at, own_blocks, last_row):
    def chosen(head, t):
        group, inner = head // 3, head % 3
        return tab_ref[(group * own_blocks + i) * 128 + inner * 3 + t]

    head = 2 * pair
    both = [(chosen(head, t), chosen(head + 1, t)) for t in range(3)]
    shared = [
        (jnp.maximum(at - 1, 0), (at >= 1) & (at - 1 < filled)),
        (at, at < filled),
        (jnp.minimum(at + 1, last_row), at + 1 < filled),
        (jnp.int32(0), at >= 2),
        (filled - 1, jnp.abs(at - (filled - 1)) > 1),
    ]
    return shared, both


def rows_of(block):
    return pl.ds(pl.multiple_of(block * BLK, BLK), BLK)


def lanes_low(rows):
    return lax.broadcasted_iota(jnp.int32, (rows, PAIR), 1) < HEAD_DIM


def split_pair(x, low):
    zero = jnp.zeros_like(x)
    return jnp.concatenate([jnp.where(low, x, zero), jnp.where(low, zero, x)], axis=0)


def gathered(ref, shared, both, low):
    tiles = [ref[rows_of(b), :] for b, _ in shared]
    for first, second in both:
        tiles.append(jnp.where(low, ref[rows_of(first), :], ref[rows_of(second), :]))
    return jnp.concatenate(tiles, axis=0)


def bias_scores(scores, shared):
    parts = []
    for slot, (_, ok) in enumerate(shared):
        parts.append(scores[slot * BLK:(slot + 1) * BLK] + jnp.where(ok, 0.0, MASKED).astype(F32))
    parts.append(scores[len(shared) * BLK:])
    return jnp.concatenate(parts, axis=0)


def forward_kernel(own_blocks, tab_ref, filled_ref, q_ref, k_ref, v_ref, out_ref, lse_ref):
    pair = pl.program_id(0)
    filled = filled_ref[0]
    first_block = lax.axis_index("seq") * own_blocks
    last_row = k_ref.shape[0] // BLK - 1
    low = lanes_low(BLK)

    def step(i, _):
        at = first_block + i
        shared, both = picks(tab_ref, filled, pair, i, at, own_blocks, last_row)
        keys = gathered(k_ref, shared, both, low)
        values = gathered(v_ref, shared, both, low)
        query = split_pair(q_ref[rows_of(i), :], low)
        scores = bias_scores(dot_nt(keys, query), shared)
        highest = jnp.max(scores, axis=0, keepdims=True)
        weights = jnp.exp(scores - highest)
        total = jnp.sum(weights, axis=0, keepdims=True)
        share = (weights * (1.0 / total)).astype(BF16)
        output = dot_tn(share, values)
        merged = jnp.where(low, output[:BLK], output[BLK:])
        merged = jnp.where(at < filled, merged, 0.0)
        out_ref[rows_of(i), :] = merged.astype(BF16)
        lse_ref[0, pl.ds(i, 1), :] = highest + jnp.log(total)
        return 0

    lax.fori_loop(0, own_blocks, step, 0, unroll=2)


def attention_forward(table, filled, query, keys, values):
    rows, features = query.shape
    own_blocks = rows // BLK
    pairs = features // PAIR
    column = lambda n: pl.BlockSpec((n, PAIR), lambda p, *_: (0, p))
    return pl.pallas_call(
        functools.partial(forward_kernel, own_blocks),
        out_shape=(
            jax.ShapeDtypeStruct((rows, features), BF16),
            jax.ShapeDtypeStruct((pairs, own_blocks, PAIR), F32),
        ),
        grid_spec=pltpu.PrefetchScalarGridSpec(
            num_scalar_prefetch=2,
            grid=(pairs,),
            in_specs=[column(rows), column(keys.shape[0]), column(keys.shape[0])],
            out_specs=(column(rows), pl.BlockSpec((1, own_blocks, PAIR), lambda p, *_: (p, 0, 0))),
        ),
        compiler_params=pltpu.CompilerParams(vmem_limit_bytes=LIMIT),
        name="attention_forward",
    )(table, filled, query, keys, values)


def backward_kernel(
    own_blocks, tab_ref, filled_ref, q_ref, k_ref, v_ref, g_ref, lse_ref,
    dq_ref, dk_ref, dv_ref, dk_sum, dv_sum,
):
    pair = pl.program_id(0)
    filled = filled_ref[0]
    first_block = lax.axis_index("seq") * own_blocks
    last_row = k_ref.shape[0] // BLK - 1
    low = lanes_low(BLK)
    dk_sum[...] = jnp.zeros_like(dk_sum)
    dv_sum[...] = jnp.zeros_like(dv_sum)

    def step(i, _):
        at = first_block + i
        shared, both = picks(tab_ref, filled, pair, i, at, own_blocks, last_row)
        keys = gathered(k_ref, shared, both, low)
        values = gathered(v_ref, shared, both, low)
        query = split_pair(q_ref[rows_of(i), :], low)
        grad = split_pair(jnp.where(at < filled, g_ref[rows_of(i), :], jnp.zeros((), BF16)), low)
        scores = bias_scores(dot_nt(keys, query), shared)
        share = jnp.exp(scores - lse_ref[0, pl.ds(i, 1), :])
        d_share = dot_nt(values, grad)
        centre = jnp.sum(share * d_share, axis=0, keepdims=True)
        d_scores = (share * (d_share - centre)).astype(BF16)
        d_query = dot_tn(d_scores, keys) * SCALE
        dq_ref[rows_of(i), :] = jnp.where(low, d_query[:BLK], d_query[BLK:]).astype(BF16)
        for total, part in ((dk_sum, dot(d_scores, query)), (dv_sum, dot(share.astype(BF16), grad))):
            for slot, (block, _) in enumerate(shared):
                total[rows_of(block), :] += part[slot * BLK:(slot + 1) * BLK]
            for t, (one, two) in enumerate(both):
                tile = part[(5 + t) * BLK:(6 + t) * BLK]
                total[rows_of(one), :] += jnp.where(low, tile, 0.0)
                total[rows_of(two), :] += jnp.where(low, 0.0, tile)
        return 0

    lax.fori_loop(0, own_blocks, step, 0)
    dk_ref[...] = dk_sum[...].astype(BF16)
    dv_ref[...] = dv_sum[...].astype(BF16)


def attention_backward(table, filled, query, keys, values, grad, lse):
    rows, features = query.shape
    slot_rows = keys.shape[0]
    own_blocks = rows // BLK
    pairs = features // PAIR
    column = lambda n: pl.BlockSpec((n, PAIR), lambda p, *_: (0, p))
    return pl.pallas_call(
        functools.partial(backward_kernel, own_blocks),
        out_shape=(
            jax.ShapeDtypeStruct((rows, features), BF16),
            jax.ShapeDtypeStruct((slot_rows, features), BF16),
            jax.ShapeDtypeStruct((slot_rows, features), BF16),
        ),
        grid_spec=pltpu.PrefetchScalarGridSpec(
            num_scalar_prefetch=2,
            grid=(pairs,),
            in_specs=[
                column(rows), column(slot_rows), column(slot_rows), column(rows),
                pl.BlockSpec((1, own_blocks, PAIR), lambda p, *_: (p, 0, 0)),
            ],
            out_specs=(column(rows), column(slot_rows), column(slot_rows)),
            scratch_shapes=[VMEM((slot_rows, PAIR), F32), VMEM((slot_rows, PAIR), F32)],
        ),
        compiler_params=pltpu.CompilerParams(vmem_limit_bytes=LIMIT),
        name="attention_backward",
    )(table, filled, query, keys, values, grad, lse)


def exchange_kernel(
    rows, width, dk_ref, dv_ref, dq_ref, base_ref, wq_ref, wk_ref, wv_ref,
    dx_ref, dko_ref, dvo_ref, dkr_ref, dvr_ref,
    land, out_far, in_far, sends, recvs,
):
    dp, me = lax.axis_index("dp"), lax.axis_index("seq")
    mate, across, diagonal = (lax.bitwise_xor(me, bit) for bit in (1, 2, 3))
    barrier = pltpu.get_barrier_semaphore()
    for other in (mate, across):
        pl.semaphore_signal(barrier, inc=1, device_id=(dp, other), device_id_type=MESH)
    pl.semaphore_wait(barrier, 2)

    def send(src, dst, slot, target):
        copy = pltpu.make_async_remote_copy(
            src_ref=src, dst_ref=dst, send_sem=sends.at[slot], recv_sem=recvs.at[slot],
            device_id=(dp, target), device_id_type=MESH,
        )
        copy.start()
        return copy

    def owned(index):
        return pl.ds(pl.multiple_of(index * rows, rows), rows)

    copies = [
        send(ref.at[owned(owner)], land.at[slot], slot, mate)
        for slot, (ref, owner) in enumerate(
            ((dk_ref, diagonal), (dv_ref, diagonal), (dk_ref, mate), (dv_ref, mate))
        )
    ]

    def summed(ref, owner, slot, to_ref):
        to_ref[...] = (ref[owned(owner), :].astype(F32) + land[slot].astype(F32)).astype(BF16)

    copies[0].wait()
    summed(dk_ref, across, 0, dkr_ref)
    copies[1].wait()
    summed(dv_ref, across, 1, dvr_ref)

    steps = rows // width
    for r in range(steps):
        at = pl.ds(r * width, width)
        out_far[at, :] = (
            dot_nt(dkr_ref[at, :], wk_ref[...]) + dot_nt(dvr_ref[at, :], wv_ref[...])
        ).astype(BF16)
    far = send(out_far, in_far, 4, across)
    copies[2].wait()
    summed(dk_ref, me, 2, dko_ref)
    copies[3].wait()
    summed(dv_ref, me, 3, dvo_ref)

    def one(r, _):
        at = pl.ds(pl.multiple_of(r * width, width), width)
        dx_ref[at, :] = (
            base_ref[at, :]
            + dot_nt(dq_ref[at, :], wq_ref[...])
            + dot_nt(dko_ref[at, :], wk_ref[...])
            + dot_nt(dvo_ref[at, :], wv_ref[...])
        )
        return 0

    lax.fori_loop(0, steps, one, 0)
    far.wait()
    dx_ref[...] += in_far[...].astype(F32)


def exchange(d_keys, d_values, d_query, base, query_weight, key_weight, value_weight):
    rows, features = d_query.shape
    small = jax.ShapeDtypeStruct((rows, features), BF16)
    return pl.pallas_call(
        functools.partial(exchange_kernel, rows, 128),
        out_shape=(jax.ShapeDtypeStruct((rows, features), F32), small, small, small, small),
        in_specs=[whole_vmem()] * 7,
        out_specs=(whole_vmem(),) * 5,
        scratch_shapes=[
            VMEM((4, rows, features), BF16),
            VMEM((rows, features), BF16),
            VMEM((rows, features), BF16),
            pltpu.SemaphoreType.DMA((5,)),
            pltpu.SemaphoreType.DMA((5,)),
        ],
        compiler_params=pltpu.CompilerParams(
            collective_id=1, has_side_effects=True, vmem_limit_bytes=LIMIT
        ),
        name="exchange",
    )(d_keys, d_values, d_query, base, query_weight, key_weight, value_weight)


def reduce_kernel(
    chunks, groups, g_ref, s_ref, out_ref, small_out, work, small, land_c, land_1, land_2, land_z,
    small_c, small_1, small_2, small_z, sends, recvs, z_sends, z_recvs, load_sem,
):
    dp, seq = lax.axis_index("dp"), lax.axis_index("seq")
    x, z = lax.rem(dp, 2), dp // 2
    core, y = lax.rem(seq, 2), seq // 2
    barrier = pltpu.get_barrier_semaphore()
    partners = {
        "core": (dp, lax.bitwise_xor(seq, 1)),
        "y": (dp, lax.bitwise_xor(seq, 2)),
        "x": (lax.bitwise_xor(dp, 1), seq),
    }
    columns = [(lax.rem(z + step, groups) * 2 + x, seq) for step in range(1, groups)]
    for target in list(partners.values()) + columns:
        pl.semaphore_signal(barrier, inc=1, device_id=target, device_id_type=MESH)
    pl.semaphore_wait(barrier, 3 + groups - 1)

    def send(src, dst, one, two, target):
        copy = pltpu.make_async_remote_copy(
            src_ref=src, dst_ref=dst, send_sem=one, recv_sem=two, device_id=target,
            device_id_type=MESH,
        )
        copy.start()
        return copy

    small[...] = s_ref[...]

    def item(k):
        if k == chunks:
            return small, small_c, small_1, small_2, small_z
        return work.at[k], land_c.at[k], land_1.at[k], land_2.at[k], land_z.at[k]

    def axes(k):
        return (("y", y), ("x", x)) if k % 2 == 0 else (("x", x), ("y", y))

    def add(total, part):
        total[...] = (total[...].astype(F32) + part[...].astype(F32)).astype(total.dtype)

    def loop_add(total, part):
        def body(r, _):
            add(total.at[r], part.at[r])
            return 0

        lax.fori_loop(0, total.shape[0], body, 0)

    loads = []
    for k in range(chunks):
        copy = pltpu.make_async_copy(g_ref.at[k], work.at[k], load_sem.at[k])
        copy.start()
        loads.append(copy)

    live = {}

    def start_core(k):
        total, land, _, _, _ = item(k)
        if k < chunks:
            loads[k].wait()
        live[k] = send(total.at[1 - core], land, sends.at[0, k], recvs.at[0, k], partners["core"])

    def end_core(k):
        total, land, land_a, _, _ = item(k)
        live[k].wait()
        (name, at), _ = axes(k)
        mine = total.at[core]
        for half in range(2):
            for other in range(2):
                loop_add(mine.at[half, other], land.at[half, other])
        live[k] = send(mine.at[1 - at], land_a, sends.at[1, k], recvs.at[1, k], partners[name])

    def end_first(k):
        total, _, land_a, land_b, _ = item(k)
        (_, at), (name, then) = axes(k)
        live[k].wait()
        mine = total.at[core, at]
        for half in range(2):
            loop_add(mine.at[half], land_a.at[half])
        live[k] = send(mine.at[1 - then], land_b, sends.at[2, k], recvs.at[2, k], partners[name])

    def end_second(k):
        total, _, _, land_b, land = item(k)
        (_, at), (_, then) = axes(k)
        live[k].wait()
        mine = total.at[core, at, then]
        loop_add(mine, land_b)
        live[k] = [
            send(mine.at[lax.rem(z + step, groups)], land.at[step - 1], z_sends.at[k, step - 1],
                 z_recvs.at[k, step - 1], columns[step - 1])
            for step in range(1, groups)
        ]

    def finish(k):
        total, _, _, _, land = item(k)
        (_, at), (_, then) = axes(k)
        result = total[core, at, then, z].astype(F32)
        for step in range(1, groups):
            live[k][step - 1].wait()
            result = result + land[step - 1].astype(F32)
        if k == chunks:
            small_out[...] = result
        else:
            out_ref[k] = result

    order = [chunks] + list(range(chunks))
    for n, k in enumerate(order[:3]):
        start_core(k)
    for n, k in enumerate(order):
        end_core(k)
        if n + 3 < len(order):
            start_core(order[n + 3])
    for n in range(len(order) + 2):
        if n < len(order):
            end_first(order[n])
        if 0 <= n - 1 < len(order):
            end_second(order[n - 1])
        if 0 <= n - 2 < len(order):
            finish(order[n - 2])


def reduce_scatter(grads, small):
    chunks, rows, features = grads.shape[0], grads.shape[-2], grads.shape[-1]
    groups = grads.shape[4]
    little = small.shape[-2:]
    return pl.pallas_call(
        functools.partial(reduce_kernel, chunks, groups),
        out_shape=(
            jax.ShapeDtypeStruct((chunks, rows, features), F32),
            jax.ShapeDtypeStruct(little, F32),
        ),
        in_specs=[pl.BlockSpec(memory_space=pl.ANY), whole_vmem()],
        out_specs=(whole_vmem(), whole_vmem()),
        scratch_shapes=[
            VMEM(grads.shape, BF16),
            VMEM(small.shape, F32),
            VMEM((chunks,) + grads.shape[2:], BF16),
            VMEM((chunks,) + grads.shape[3:], BF16),
            VMEM((chunks,) + grads.shape[4:], BF16),
            VMEM((chunks, groups - 1, rows, features), BF16),
            VMEM(small.shape[1:], F32),
            VMEM(small.shape[2:], F32),
            VMEM(small.shape[3:], F32),
            VMEM((groups - 1,) + little, F32),
            pltpu.SemaphoreType.DMA((3, chunks + 1)),
            pltpu.SemaphoreType.DMA((3, chunks + 1)),
            pltpu.SemaphoreType.DMA((chunks + 1, groups - 1)),
            pltpu.SemaphoreType.DMA((chunks + 1, groups - 1)),
            pltpu.SemaphoreType.DMA((chunks,)),
        ],
        compiler_params=pltpu.CompilerParams(
            collective_id=2, has_side_effects=True, vmem_limit_bytes=LIMIT
        ),
        name="reduce_scatter",
    )(grads, small)


def summed_on_box(square, up, down, vectors, up_bias, groups):
    features = up.shape[0]
    devices = 8 * groups
    share = features // devices
    wide = up.shape[1] // features
    low = [g.astype(BF16).reshape(devices, share, features) for g in square]
    ups = up.astype(BF16).reshape(devices, share, wide, features)
    downs = down.astype(BF16).reshape(devices, wide * share, features)
    pieces = [
        jnp.concatenate(low[:2], axis=1),
        jnp.concatenate(low[2:], axis=1),
    ]
    for j in range(0, wide, 2):
        pieces.append(jnp.concatenate([ups[:, :, j], ups[:, :, j + 1]], axis=1))
    for j in range(0, wide, 2):
        pieces.append(downs[:, j * share:(j + 2) * share])
    placed = []
    for k, piece in enumerate(pieces):
        piece = piece.reshape(groups, 2, 2, 2, 2 * share, features)
        order = (3, 2, 1, 0, 4, 5) if k % 2 == 0 else (3, 1, 2, 0, 4, 5)
        placed.append(piece.transpose(order))
    grads = jnp.stack(placed)
    count = len(vectors)
    flat = jnp.concatenate(
        [jnp.stack(vectors).reshape(count, devices, share).transpose(1, 0, 2),
         up_bias.reshape(devices, wide, share)], axis=1)
    flat = jnp.pad(flat, ((0, 0), (0, 16 - count - wide), (0, 128 - share)))
    flat = flat.reshape(groups, 2, 2, 2, 16, 128).transpose(3, 2, 1, 0, 4, 5)
    big, little = reduce_scatter(grads, flat)
    out_square = [big[0, :share], big[0, share:], big[1, :share], big[1, share:]]
    out_up = jnp.concatenate(
        [big[2 + j // 2, (j % 2) * share:(j % 2 + 1) * share] for j in range(wide)], axis=1)
    out_down = jnp.concatenate([big[2 + wide // 2 + j] for j in range(wide // 2)], axis=0)
    out_vectors = [little[n, :share] for n in range(count)]
    out_up_bias = little[count:count + wide, :share].reshape(-1)
    return out_square, out_up, out_down, out_vectors, out_up_bias


def summed_anywhere(square, up, down, vectors, up_bias):
    def one(g):
        return lax.psum_scatter(g, ("dp", "seq"), scatter_dimension=0, tiled=True)

    return [one(g) for g in square], one(up), one(down), [one(v) for v in vectors], one(up_bias)


def layer_norm(values, gain, shift):
    center = jnp.mean(values, axis=-1, keepdims=True)
    centered = values - center
    variance = jnp.mean(centered * centered, axis=-1, keepdims=True)
    inv_root = lax.rsqrt(variance + NORM_EPS)
    normed = centered * inv_root
    return (normed * gain + shift, normed, inv_root)


def norm_back(grad_out, normed, inv_root, gain):
    d_normed = grad_out * gain
    grad_in = inv_root * (
        d_normed
        - jnp.mean(d_normed, axis=-1, keepdims=True)
        - normed * jnp.mean(d_normed * normed, axis=-1, keepdims=True)
    )
    return (grad_in, jnp.sum(grad_out * normed, axis=0), jnp.sum(grad_out, axis=0))


def on_device(
    groups,
    tokens, filled_blocks, random_blocks, query_weight, query_bias, key_weight, value_weight,
    value_bias, out_weight, out_bias, attn_gain, attn_shift, up_weight, up_bias, down_weight,
    down_bias, ffn_gain, ffn_shift, cotangent,
):
    row_count, feature_count = tokens.shape
    filled = filled_blocks[0]
    place = lax.axis_index("seq") * row_count + jnp.arange(row_count, dtype=jnp.int32)
    live_tokens = (place < filled * BLK).astype(F32)[:, None]

    table = random_blocks[0].reshape(random_blocks.shape[1], -1)
    table = jnp.pad(table, ((0, 0), (0, 128 - table.shape[1])))
    query, keys, values, far_tokens, table = gather_project(
        tokens, table, query_weight, query_bias, key_weight, value_weight, value_bias
    )
    table = table.reshape(-1)
    merged, lse = attention_forward(table, filled_blocks, query, keys, values)

    attn = dot(merged, out_weight) + out_bias
    first, normed_one, root_one = layer_norm(tokens.astype(F32) + attn, attn_gain, attn_shift)
    first_low = first.astype(BF16)
    hidden = dot(first_low, up_weight) + up_bias
    act, gelu_pull = jax.vjp(jax.nn.gelu, hidden)
    act_low = act.astype(BF16)
    ffn = dot(act_low, down_weight) + down_bias
    result, normed_two, root_two = layer_norm(first + ffn, ffn_gain, ffn_shift)
    grad_result = cotangent.astype(F32) * live_tokens
    d_sum_two, grad_ffn_gain, grad_ffn_shift = norm_back(
        grad_result, normed_two, root_two, ffn_gain
    )
    d_ffn = d_sum_two.astype(BF16)
    grad_down_bias = jnp.sum(d_ffn, axis=0, dtype=F32)
    grad_down_weight = dot_tn(act_low, d_ffn)
    d_act = dot_nt(d_ffn, down_weight)
    d_hidden = gelu_pull(d_act)[0].astype(BF16)
    grad_up_bias = jnp.sum(d_hidden, axis=0, dtype=F32)
    grad_up_weight = dot_tn(first_low, d_hidden)
    d_first = d_sum_two + dot_nt(d_hidden, up_weight)
    d_sum_one, grad_attn_gain, grad_attn_shift = norm_back(d_first, normed_one, root_one, attn_gain)
    d_attn = d_sum_one.astype(BF16)
    grad_out_bias = jnp.sum(d_attn, axis=0, dtype=F32)
    grad_out_weight = dot_tn(merged, d_attn)
    d_merged = dot_nt(d_attn, out_weight).astype(BF16)

    d_query, d_keys, d_values = attention_backward(
        table, filled_blocks, query, keys, values, d_merged, lse
    )
    grad_tokens, dk_own, dv_own, dk_far, dv_far = exchange(
        d_keys, d_values, d_query, d_sum_one, query_weight, key_weight, value_weight
    )
    grad_query_weight = dot_tn(tokens, d_query)
    grad_query_bias = jnp.sum(d_query, axis=0, dtype=F32)
    grad_key_weight = dot_tn(tokens, dk_own) + dot_tn(far_tokens, dk_far)
    grad_value_weight = dot_tn(tokens, dv_own) + dot_tn(far_tokens, dv_far)
    grad_value_bias = jnp.sum(dv_own, axis=0, dtype=F32) + jnp.sum(dv_far, axis=0, dtype=F32)

    square = (grad_query_weight, grad_key_weight, grad_value_weight, grad_out_weight)
    vectors = (
        grad_query_bias, grad_value_bias, grad_out_bias, grad_attn_gain, grad_attn_shift,
        grad_down_bias, grad_ffn_gain, grad_ffn_shift,
    )
    if groups:
        square, up, down, vectors, up_sum = summed_on_box(
            square, grad_up_weight, grad_down_weight, vectors, grad_up_bias, groups)
    else:
        square, up, down, vectors, up_sum = summed_anywhere(
            square, grad_up_weight, grad_down_weight, vectors, grad_up_bias)
    return (
        result.astype(BF16), grad_tokens, square[0], vectors[0], square[1], square[2], vectors[1],
        square[3], vectors[2], vectors[3], vectors[4], up, up_sum, down, vectors[5], vectors[6],
        vectors[7],
    )


def solution(mesh):
    both = P(("dp", "seq"), None)
    line = P(("dp", "seq"))
    placed = (both, P("dp"), P("dp", None, "seq", None)) + (P(),) * 15 + (both,)
    groups = 4 if mesh.shape["dp"] == 8 and mesh.shape["seq"] == 4 else 0
    return jax.shard_map(
        functools.partial(on_device, groups),
        mesh=mesh,
        in_specs=placed,
        out_specs=(
            both, both, both, line, both, both, line, both, line, line, line, both, line, both,
            line, line, line,
        ),
        check_vma=False,
    )
```

```python
import functools

import jax
import jax.numpy as jnp
from jax import lax
from jax.experimental import pallas as pl
from jax.experimental.pallas import tpu as pltpu
from jax.sharding import PartitionSpec as P

HEAD_DIM = 64
BLK = 64
PAIR = 2 * HEAD_DIM
TABLE = 8
NORM_EPS = 1e-05
MASKED = -1e30
SCALE = HEAD_DIM ** (-0.5)
MESH = pl.DeviceIdType.MESH
BF16 = jnp.bfloat16
F32 = jnp.float32
VMEM = pltpu.VMEM
LIMIT = 60 << 20


def whole_vmem():
    return pl.BlockSpec(memory_space=pltpu.VMEM)


def dot(left, right):
    return jnp.dot(left, right, preferred_element_type=F32)


def dot_nt(left, right):
    return lax.dot_general(left, right, (((1,), (1,)), ((), ())), preferred_element_type=F32)


def dot_tn(left, right):
    return lax.dot_general(left, right, (((0,), (0,)), ((), ())), preferred_element_type=F32)


def gather_kernel(
    rows, width, x_ref, tab_ref, wq_ref, qb_ref, wk_ref, wv_ref, vb_ref,
    q_ref, k_ref, v_ref, far_ref, tab_out, land, tab_land, sends, recvs, tab_sends, tab_recvs,
):
    parts = 4
    part = rows // parts
    dp, me = lax.axis_index("dp"), lax.axis_index("seq")
    mate, across, diagonal = (lax.bitwise_xor(me, bit) for bit in (1, 2, 3))
    barrier = pltpu.get_barrier_semaphore()
    for other in (mate, across, diagonal):
        pl.semaphore_signal(barrier, inc=1, device_id=(dp, other), device_id_type=MESH)
    pl.semaphore_wait(barrier, 3)

    def send(src, dst, slot, target):
        copy = pltpu.make_async_remote_copy(
            src_ref=src, dst_ref=dst, send_sem=sends.at[slot], recv_sem=recvs.at[slot],
            device_id=(dp, target), device_id_type=MESH,
        )
        copy.start()
        return copy

    far = [
        send(x_ref.at[pl.ds(r * part, part)], land.at[0, pl.ds(r * part, part)], r, across)
        for r in range(parts)
    ]
    near = send(x_ref, land.at[1], parts, mate)
    tables = []
    own_blocks = tab_ref.shape[0] // 4
    for slot, other in enumerate((mate, across, diagonal)):
        copy = pltpu.make_async_remote_copy(
            src_ref=tab_ref.at[pl.ds(pl.multiple_of(other * own_blocks, 8), own_blocks)],
            dst_ref=tab_land.at[slot], send_sem=tab_sends.at[slot], recv_sem=tab_recvs.at[slot],
            device_id=(dp, other), device_id_type=MESH,
        )
        copy.start()
        tables.append(copy)

    def keys_values(x, at):
        k_ref[pl.ds(at, width), :] = dot(x, wk_ref[...]).astype(BF16)
        v_ref[pl.ds(at, width), :] = (dot(x, wv_ref[...]) + vb_ref[...]).astype(BF16)

    def own(r, _):
        at = pl.multiple_of(r * width, width)
        x = x_ref[pl.ds(at, width), :]
        q_ref[pl.ds(at, width), :] = (
            (dot(x, wq_ref[...]) + qb_ref[...]).astype(BF16) * jnp.asarray(SCALE, BF16)
        )
        keys_values(x, pl.multiple_of(me * rows + at, width))
        return 0

    lax.fori_loop(0, rows // width, own, 0)

    def block(slot, owner, start, count):
        def step(r, _):
            at = pl.multiple_of(start + r * width, width)
            keys_values(land[slot, pl.ds(at, width), :], pl.multiple_of(owner * rows + at, width))
            return 0

        lax.fori_loop(0, count // width, step, 0)

    near.wait()
    block(1, mate, 0, rows)
    relayed = []
    for r in range(parts):
        far[r].wait()
        piece = pl.ds(r * part, part)
        relayed.append(send(land.at[0, piece], land.at[2, piece], parts + 1 + r, mate))
        block(0, across, r * part, part)
        if r:
            relayed[r - 1].wait()
            block(2, diagonal, (r - 1) * part, part)
    far_ref[...] = land[0]
    for copy in tables:
        copy.wait()
    relayed[-1].wait()
    block(2, diagonal, (parts - 1) * part, part)
    tab_out[pl.ds(me, 1)] = tab_ref[pl.ds(pl.multiple_of(me * own_blocks, 8), own_blocks)][None]
    for slot, other in enumerate((mate, across, diagonal)):
        tab_out[pl.ds(other, 1)] = tab_land[slot][None]


def gather_project(tokens, table, query_weight, query_bias, key_weight, value_weight, value_bias):
    rows, features = tokens.shape
    own_blocks = rows // BLK
    copies = 4 + 1 + 4
    return pl.pallas_call(
        functools.partial(gather_kernel, rows, 128),
        out_shape=(
            jax.ShapeDtypeStruct((rows, features), BF16),
            jax.ShapeDtypeStruct((4 * rows, features), BF16),
            jax.ShapeDtypeStruct((4 * rows, features), BF16),
            jax.ShapeDtypeStruct((rows, features), BF16),
            jax.ShapeDtypeStruct((4, own_blocks, 128), jnp.int32),
        ),
        in_specs=[whole_vmem()] * 7,
        out_specs=(whole_vmem(),) * 5,
        scratch_shapes=[
            VMEM((3, rows, features), BF16),
            VMEM((3, own_blocks, 128), jnp.int32),
            pltpu.SemaphoreType.DMA((copies,)),
            pltpu.SemaphoreType.DMA((copies,)),
            pltpu.SemaphoreType.DMA((3,)),
            pltpu.SemaphoreType.DMA((3,)),
        ],
        compiler_params=pltpu.CompilerParams(
            collective_id=0, has_side_effects=True, vmem_limit_bytes=LIMIT
        ),
        name="gather_project",
    )(tokens, table, query_weight, query_bias[None], key_weight, value_weight, value_bias[None])


def key_blocks(tab_ref, end, pair, i, at, own_blocks, last_row):
    def chosen(head, t):
        group, inner = lax.div(head, 3), lax.rem(head, 3)
        return tab_ref[(group * own_blocks + i) * 128 + inner * 3 + t]

    head = 2 * pair
    both = [(chosen(head, t), chosen(head + 1, t)) for t in range(3)]
    shared = [
        jnp.maximum(at - 1, 0), at, jnp.minimum(at + 1, last_row), jnp.int32(0), end,
    ]
    return shared, both


def rows_of(block):
    return pl.ds(pl.multiple_of(block * BLK, BLK), BLK)


def lanes_low(rows):
    return lax.broadcasted_iota(jnp.int32, (rows, PAIR), 1) < HEAD_DIM


def split_pair(x, low):
    zero = jnp.zeros_like(x)
    return jnp.concatenate([jnp.where(low, x, zero), jnp.where(low, zero, x)], axis=0)


def gathered(ref, shared, both, low, lanes=slice(None)):
    tiles = [ref[b, :, lanes] for b in shared]
    for first, second in both:
        tiles.append(jnp.where(low, ref[first, :, lanes], ref[second, :, lanes]))
    return jnp.concatenate(tiles, axis=0)


def masked_scores(scores, mask_ref, i):
    parts = [scores[n * BLK:(n + 1) * BLK] + mask_ref[i * 8 + n] for n in range(5)]
    return jnp.concatenate(parts + [scores[5 * BLK:]], axis=0)


def forward_kernel(own_blocks, tab_ref, filled_ref, mask_ref, q_ref, k_ref, v_ref, out_ref, lse_ref):
    pair = pl.program_id(0)
    filled = filled_ref[0]
    first_block = lax.axis_index("seq") * own_blocks
    last_row = k_ref.shape[0] - 1
    low = lanes_low(BLK)

    def step(i, _):
        at = first_block + i
        shared, both = key_blocks(tab_ref, filled - 1, pair, i, at, own_blocks, last_row)
        keys = gathered(k_ref, shared, both, low)
        values = gathered(v_ref, shared, both, low)
        query = split_pair(q_ref[rows_of(i), :], low)
        scores = masked_scores(dot_nt(keys, query), mask_ref, i)
        highest = jnp.max(scores, axis=0, keepdims=True)
        weights = jnp.exp(scores - highest)
        total = jnp.sum(weights, axis=0, keepdims=True)
        share = (weights * (1.0 / total)).astype(BF16)
        output = dot_tn(share, values)
        merged = jnp.where(low, output[:BLK], output[BLK:])
        merged = jnp.where(at < filled, merged, 0.0)
        out_ref[rows_of(i), :] = merged.astype(BF16)
        lse_ref[0, pl.ds(i, 1), :] = highest + jnp.log(total)
        return 0

    lax.fori_loop(0, own_blocks, step, 0, unroll=own_blocks)


def attention_forward(table, filled, mask, query, keys, values):
    rows, features = query.shape
    own_blocks = rows // BLK
    slot_blocks = keys.shape[0]
    pairs = features // PAIR
    column = lambda n: pl.BlockSpec((n, PAIR), lambda p, *_: (0, p))
    blocks = lambda n: pl.BlockSpec((n, BLK, PAIR), lambda p, *_: (0, 0, p))
    return pl.pallas_call(
        functools.partial(forward_kernel, own_blocks),
        out_shape=(
            jax.ShapeDtypeStruct((rows, features), BF16),
            jax.ShapeDtypeStruct((pairs, own_blocks, PAIR), F32),
        ),
        grid_spec=pltpu.PrefetchScalarGridSpec(
            num_scalar_prefetch=3,
            grid=(pairs,),
            in_specs=[column(rows), blocks(slot_blocks), blocks(slot_blocks)],
            out_specs=(column(rows), pl.BlockSpec((1, own_blocks, PAIR), lambda p, *_: (p, 0, 0))),
        ),
        compiler_params=pltpu.CompilerParams(vmem_limit_bytes=LIMIT),
        name="attention_forward",
    )(table, filled, mask, query, keys, values)


def backward_kernel(
    own_blocks, tab_ref, filled_ref, mask_ref, q_ref, k_ref, v_ref, g_ref, lse_ref,
    dq_ref, dk_ref, dv_ref, dk_sum, dv_sum,
):
    pair = pl.program_id(0)
    filled = filled_ref[0]
    first_block = lax.axis_index("seq") * own_blocks
    last_row = k_ref.shape[0] - 1
    low = lanes_low(BLK)
    dk_sum[...] = jnp.zeros_like(dk_sum)
    dv_sum[...] = jnp.zeros_like(dv_sum)

    def step(i, _):
        at = first_block + i
        shared, both = key_blocks(tab_ref, filled - 1, pair, i, at, own_blocks, last_row)
        keys = gathered(k_ref, shared, both, low)
        values = gathered(v_ref, shared, both, low)
        query = split_pair(q_ref[rows_of(i), :], low)
        grad = split_pair(jnp.where(at < filled, g_ref[rows_of(i), :], jnp.zeros((), BF16)), low)
        scores = masked_scores(dot_nt(keys, query), mask_ref, i)
        share = jnp.exp(scores - lse_ref[0, pl.ds(i, 1), :])
        d_share = dot_nt(values, grad)
        centre = jnp.sum(share * d_share, axis=0, keepdims=True)
        d_scores = (share * (d_share - centre)).astype(BF16)
        d_query = dot_tn(d_scores, keys) * SCALE
        dq_ref[rows_of(i), :] = jnp.where(low, d_query[:BLK], d_query[BLK:]).astype(BF16)
        for total, part in ((dk_sum, dot(d_scores, query)), (dv_sum, dot(share.astype(BF16), grad))):
            for slot, block in enumerate(shared):
                total[rows_of(block), :] += part[slot * BLK:(slot + 1) * BLK]
            for t, (one, two) in enumerate(both):
                tile = part[(5 + t) * BLK:(6 + t) * BLK]
                total[rows_of(one), :] += jnp.where(low, tile, 0.0)
                total[rows_of(two), :] += jnp.where(low, 0.0, tile)
        return 0

    lax.fori_loop(0, own_blocks, step, 0, unroll=own_blocks)
    dk_ref[...] = dk_sum[...].astype(BF16)
    dv_ref[...] = dv_sum[...].astype(BF16)


def attention_backward(table, filled, mask, query, keys, values, grad, lse):
    rows, features = query.shape
    slot_blocks = keys.shape[0]
    slot_rows = slot_blocks * BLK
    own_blocks = rows // BLK
    pairs = features // PAIR
    blocks = lambda n: pl.BlockSpec((n, BLK, PAIR), lambda p, *_: (0, 0, p))
    column = lambda n: pl.BlockSpec((n, PAIR), lambda p, *_: (0, p))
    return pl.pallas_call(
        functools.partial(backward_kernel, own_blocks),
        out_shape=(
            jax.ShapeDtypeStruct((rows, features), BF16),
            jax.ShapeDtypeStruct((slot_rows, features), BF16),
            jax.ShapeDtypeStruct((slot_rows, features), BF16),
        ),
        grid_spec=pltpu.PrefetchScalarGridSpec(
            num_scalar_prefetch=3,
            grid=(pairs,),
            in_specs=[
                column(rows), blocks(slot_blocks), blocks(slot_blocks), column(rows),
                pl.BlockSpec((1, own_blocks, PAIR), lambda p, *_: (p, 0, 0)),
            ],
            out_specs=(column(rows), column(slot_rows), column(slot_rows)),
            scratch_shapes=[VMEM((slot_rows, PAIR), F32), VMEM((slot_rows, PAIR), F32)],
        ),
        compiler_params=pltpu.CompilerParams(vmem_limit_bytes=LIMIT),
        name="attention_backward",
    )(table, filled, mask, query, keys, values, grad, lse)


def exchange_kernel(
    rows, width, dk_ref, dv_ref, dq_ref, base_ref, wq_ref, wk_ref, wv_ref,
    dx_ref, dko_ref, dvo_ref, dkr_ref, dvr_ref,
    land, out_far, in_far, sends, recvs,
):
    dp, me = lax.axis_index("dp"), lax.axis_index("seq")
    mate, across, diagonal = (lax.bitwise_xor(me, bit) for bit in (1, 2, 3))
    barrier = pltpu.get_barrier_semaphore()
    for other in (mate, across):
        pl.semaphore_signal(barrier, inc=1, device_id=(dp, other), device_id_type=MESH)
    pl.semaphore_wait(barrier, 2)

    def send(src, dst, slot, target):
        copy = pltpu.make_async_remote_copy(
            src_ref=src, dst_ref=dst, send_sem=sends.at[slot], recv_sem=recvs.at[slot],
            device_id=(dp, target), device_id_type=MESH,
        )
        copy.start()
        return copy

    def owned(index):
        return pl.ds(pl.multiple_of(index * rows, rows), rows)

    copies = [
        send(ref.at[owned(owner)], land.at[slot], slot, mate)
        for slot, (ref, owner) in enumerate(
            ((dk_ref, diagonal), (dv_ref, diagonal), (dk_ref, mate), (dv_ref, mate))
        )
    ]

    def summed(ref, owner, slot, to_ref):
        to_ref[...] = (ref[owned(owner), :].astype(F32) + land[slot].astype(F32)).astype(BF16)

    copies[0].wait()
    summed(dk_ref, across, 0, dkr_ref)
    copies[1].wait()
    summed(dv_ref, across, 1, dvr_ref)

    steps = rows // width
    for r in range(steps):
        at = pl.ds(r * width, width)
        out_far[at, :] = (
            dot_nt(dkr_ref[at, :], wk_ref[...]) + dot_nt(dvr_ref[at, :], wv_ref[...])
        ).astype(BF16)
    far = send(out_far, in_far, 4, across)
    copies[2].wait()
    summed(dk_ref, me, 2, dko_ref)
    copies[3].wait()
    summed(dv_ref, me, 3, dvo_ref)

    def one(r, _):
        at = pl.ds(pl.multiple_of(r * width, width), width)
        dx_ref[at, :] = (
            base_ref[at, :]
            + dot_nt(dq_ref[at, :], wq_ref[...])
            + dot_nt(dko_ref[at, :], wk_ref[...])
            + dot_nt(dvo_ref[at, :], wv_ref[...])
        )
        return 0

    lax.fori_loop(0, steps, one, 0)
    far.wait()
    dx_ref[...] += in_far[...].astype(F32)


def exchange(d_keys, d_values, d_query, base, query_weight, key_weight, value_weight):
    rows, features = d_query.shape
    small = jax.ShapeDtypeStruct((rows, features), BF16)
    return pl.pallas_call(
        functools.partial(exchange_kernel, rows, 128),
        out_shape=(jax.ShapeDtypeStruct((rows, features), F32), small, small, small, small),
        in_specs=[whole_vmem()] * 7,
        out_specs=(whole_vmem(),) * 5,
        scratch_shapes=[
            VMEM((4, rows, features), BF16),
            VMEM((rows, features), BF16),
            VMEM((rows, features), BF16),
            pltpu.SemaphoreType.DMA((5,)),
            pltpu.SemaphoreType.DMA((5,)),
        ],
        compiler_params=pltpu.CompilerParams(
            collective_id=1, has_side_effects=True, vmem_limit_bytes=LIMIT
        ),
        name="exchange",
    )(d_keys, d_values, d_query, base, query_weight, key_weight, value_weight)


def summed_anywhere(square, up, down, vectors, up_bias):
    def one(g):
        return lax.psum_scatter(g, ("dp", "seq"), scatter_dimension=0, tiled=True)

    return [one(g) for g in square], one(up), one(down), [one(v) for v in vectors], one(up_bias)


GELU_A = 0.044715
GELU_C = 0.7978845608028654


def normed_rows(values):
    center = jnp.mean(values, axis=-1, keepdims=True)
    centered = values - center
    variance = jnp.mean(centered * centered, axis=-1, keepdims=True)
    inv_root = lax.rsqrt(variance + NORM_EPS)
    return centered * inv_root, inv_root


def norm_pull(grad_out, normed, inv_root, gain):
    d_normed = grad_out * gain
    return inv_root * (
        d_normed
        - jnp.mean(d_normed, axis=-1, keepdims=True)
        - normed * jnp.mean(d_normed * normed, axis=-1, keepdims=True)
    )


def column_sum(values):
    return jnp.sum(values, axis=0, keepdims=True)


def dense_kernel(
    rows, tile, filled_ref, x_ref, merged_ref, cot_ref, bo_ref, g1_ref, s1_ref, bu_ref, bd_ref,
    g2_ref, s2_ref, wo_any, wu_any, wd_any,
    result_ref, base_ref, d_attn_ref, d_merged_ref, vec_ref, up_vec_ref, sum_ref,
    wo, wu, wd, normed_one, root_one, first, first_low, act, slope, ffn, d_ffn, tmp,
    down, up, down_in, up_in, loads, sends, recvs,
):
    features = x_ref.shape[1]
    wide = wu.shape[1] // features
    share = 24 * wide
    dp, seq = lax.axis_index("dp"), lax.axis_index("seq")
    core = lax.rem(seq, 2)
    mate = lax.bitwise_xor(seq, 1)
    copies = []
    for n, (src, dst) in enumerate(((wo_any, wo), (wu_any, wu), (wd_any, wd))):
        copy = pltpu.make_async_copy(src, dst, loads.at[n])
        copy.start()
        copies.append(copy)
    barrier = pltpu.get_barrier_semaphore()
    pl.semaphore_signal(barrier, inc=1, device_id=(dp, mate), device_id_type=MESH)
    pl.semaphore_wait(barrier, 1)

    def send(src, dst, slot):
        copy = pltpu.make_async_remote_copy(
            src_ref=src, dst_ref=dst, send_sem=sends.at[slot], recv_sem=recvs.at[slot],
            device_id=(dp, mate), device_id_type=MESH,
        )
        copy.start()
        return copy

    def tiles(body):
        def step(r, _):
            body(pl.ds(pl.multiple_of(r * tile, tile), tile), r)
            return 0

        lax.fori_loop(0, rows // tile, step, 0)

    def columns(j):
        return pl.ds(pl.multiple_of(j * features, features), features)

    copies[0].wait()
    ffn[...] = dot(merged_ref[...], wo[...])

    def norm_one(at, r):
        normed, inv_root = normed_rows(x_ref[at, :].astype(F32) + (ffn[at, :] + bo_ref[...]))
        normed_one[at, :] = normed
        root_one[at, :] = inv_root
        value = normed * g1_ref[...] + s1_ref[...]
        first[at, :] = value
        first_low[at, :] = value.astype(BF16)

    tiles(norm_one)

    copies[1].wait()
    copies[2].wait()
    ffn[...] = jnp.zeros_like(ffn)

    def forward(j, _):
        at = columns(j)
        u = dot(first_low[...], wu[:, at]) + bu_ref[:, at]
        square = u * u
        t = jnp.tanh(GELU_C * (u + GELU_A * (square * u)))
        half = 0.5 * (1.0 + t)
        act[j] = (u * half).astype(BF16)
        slope[j] = half + (0.5 * GELU_C) * u * (1.0 - t * t) * (1.0 + (3.0 * GELU_A) * square)
        ffn[...] += dot(act[j], wd[columns(j), :])
        return 0

    lax.fori_loop(0, wide, forward, 0)

    vec_ref[...] = jnp.zeros_like(vec_ref)
    limit = filled_ref[0] * BLK - seq * rows

    def norm_two(at, r):
        normed, inv_root = normed_rows(first[at, :] + (ffn[at, :] + bd_ref[...]))
        result_ref[at, :] = (normed * g2_ref[...] + s2_ref[...]).astype(BF16)
        place = lax.broadcasted_iota(jnp.int32, (tile, 1), 0) + r * tile
        grad = cot_ref[at, :].astype(F32) * (place < limit).astype(F32)
        pulled = norm_pull(grad, normed, inv_root, g2_ref[...])
        low = pulled.astype(BF16)
        ffn[at, :] = pulled
        d_ffn[at, :] = low
        vec_ref[0:1, :] += column_sum(grad * normed)
        vec_ref[1:2, :] += column_sum(grad)
        vec_ref[2:3, :] += column_sum(low.astype(F32))

    tiles(norm_two)

    moving = []
    for j in range(wide):
        grad = dot_tn(act[j], d_ffn[...]).astype(BF16)
        for n in range(8):
            down[n % 2, j, n // 4, (n // 2) % 2] = grad[n * share:(n + 1) * share]
        moving.append(send(down.at[1 - core, j], down_in.at[j], j))

    def backward(j, _):
        d_hidden = (dot_nt(d_ffn[...], wd[columns(j), :]) * slope[j]).astype(BF16)
        act[j] = d_hidden
        up_vec_ref[:, columns(j)] = column_sum(d_hidden.astype(F32))
        return 0

    lax.fori_loop(0, wide, backward, 0)

    for half in range(wide // 2):
        for part in range(2):
            tmp[part] = dot_tn(first_low[...], act[2 * half + part])

        def regroup(s, _):
            for n in range(2):
                at = pl.ds(pl.multiple_of((2 * s + n) * 24, 8), 24)
                up[n, half, s] = jnp.concatenate([tmp[0, at, :], tmp[1, at, :]], axis=0).astype(BF16)
            return 0

        lax.fori_loop(0, up.shape[2], regroup, 0)
        moving.append(send(up.at[1 - core, half], up_in.at[half], wide + half))

    for j in range(wide):
        ffn[...] += dot_nt(act[j], wu[:, j * features:(j + 1) * features])

    def pull_one(at, r):
        grad = ffn[at, :]
        normed = normed_one[at, :]
        pulled = norm_pull(grad, normed, root_one[at, :], g1_ref[...])
        low = pulled.astype(BF16)
        base_ref[at, :] = pulled
        d_attn_ref[at, :] = low
        vec_ref[3:4, :] += column_sum(grad * normed)
        vec_ref[4:5, :] += column_sum(grad)
        vec_ref[5:6, :] += column_sum(low.astype(F32))

    tiles(pull_one)
    live = lax.broadcasted_iota(jnp.int32, (rows, 1), 0) < limit
    d_merged_ref[...] = jnp.where(live, dot_nt(d_attn_ref[...], wo[...]), 0.0).astype(BF16)

    def added(mine, other):
        return (mine.astype(F32) + other.astype(F32)).astype(BF16)

    def put(k, x, y, z, value):
        if KINDS[k] == "A":
            sum_ref[k, y, x, z] = value
        else:
            sum_ref[k, x, y, z] = value

    for j in range(wide):
        moving[j].wait()

    def sum_down(s, _):
        z, x, y = s // 4, lax.rem(s // 2, 2), lax.rem(s, 2)
        total = added(down[core, z, x, y], down_in[z, x, y])
        put(0, x, y, z, total[:share // 2])
        put(1, x, y, z, total[share // 2:])
        return 0

    lax.fori_loop(0, up.shape[2], sum_down, 0)
    for copy in moving[wide:]:
        copy.wait()

    def sum_up(s, _):
        z, x, y = s // 4, lax.rem(s // 2, 2), lax.rem(s, 2)
        put(2, x, y, z, added(up[core, 0, s], up_in[0, s]))
        put(3, x, y, z, added(up[core, 1, s], up_in[1, s]))
        return 0

    lax.fori_loop(0, up.shape[2], sum_up, 0)


def dense(
    filled, tokens, merged, cotangent, out_weight, out_bias, attn_gain, attn_shift, up_weight,
    up_bias, down_weight, down_bias, ffn_gain, ffn_shift,
):
    rows, features = tokens.shape
    hidden = up_weight.shape[1]
    wide = hidden // features
    low = jax.ShapeDtypeStruct((rows, features), BF16)
    shards = 16
    piece = (2 * 24, features)
    any_space = pl.BlockSpec(memory_space=pl.ANY)
    return pl.pallas_call(
        functools.partial(dense_kernel, rows, 128),
        out_shape=(
            low, jax.ShapeDtypeStruct((rows, features), F32), low, low,
            jax.ShapeDtypeStruct((8, features), F32), jax.ShapeDtypeStruct((1, hidden), F32),
            jax.ShapeDtypeStruct((4, 2, 2, 4) + piece, BF16),
        ),
        in_specs=[pl.BlockSpec(memory_space=pltpu.SMEM)] + [whole_vmem()] * 10 + [any_space] * 3,
        out_specs=(whole_vmem(),) * 7,
        scratch_shapes=[
            VMEM((features, features), BF16),
            VMEM((features, hidden), BF16),
            VMEM((hidden, features), BF16),
            VMEM((rows, features), F32),
            VMEM((rows, 1), F32),
            VMEM((rows, features), F32),
            VMEM((rows, features), BF16),
            VMEM((wide, rows, features), BF16),
            VMEM((wide, rows, features), F32),
            VMEM((rows, features), F32),
            VMEM((rows, features), BF16),
            VMEM((2, features, features), F32),
            VMEM((2, 4, 2, 2, 24 * wide, features), BF16),
            VMEM((2, wide // 2, shards) + piece, BF16),
            VMEM((4, 2, 2, 24 * wide, features), BF16),
            VMEM((wide // 2, shards) + piece, BF16),
            pltpu.SemaphoreType.DMA((3,)),
            pltpu.SemaphoreType.DMA((wide + wide // 2,)),
            pltpu.SemaphoreType.DMA((wide + wide // 2,)),
        ],
        compiler_params=pltpu.CompilerParams(
            collective_id=3, has_side_effects=True, vmem_limit_bytes=LIMIT
        ),
        name="dense",
    )(
        filled, tokens, merged, cotangent, out_bias[None], attn_gain[None], attn_shift[None],
        up_bias[None], down_bias[None], ffn_gain[None], ffn_shift[None], out_weight, up_weight,
        down_weight,
    )


KINDS = "ABBBBA"


def masks(filled, seq, own_blocks):
    at = seq * own_blocks + jnp.arange(own_blocks, dtype=jnp.int32)[:, None]
    kind = jnp.arange(8, dtype=jnp.int32)[None, :]
    window = at + kind - 1
    ok = jnp.where(
        kind < 3, (window >= 0) & (window < filled),
        jnp.where(kind == 3, at >= 2, jnp.abs(at - (filled - 1)) > 1))
    last = jnp.arange(4 * own_blocks, dtype=jnp.int32) == filled - 1
    return jnp.concatenate([jnp.where(ok, 0.0, MASKED).astype(F32).reshape(-1), last.astype(F32)])


def links(table, filled, own_blocks):
    mine = table.reshape(4, own_blocks, 128)[:, :, :9].reshape(4, own_blocks, 3, 3)
    blocks = mine.transpose(0, 2, 1, 3).reshape(12, own_blocks * 3)
    count = blocks.shape[1]
    at = jnp.arange(count, dtype=jnp.int32)
    same = (blocks[:, :, None] == blocks[:, None, :]) & (at[None, None, :] < at[None, :, None])
    before = jnp.max(jnp.where(same, at[None, None, :], -1), axis=2)
    where = jnp.arange(32, dtype=jnp.int32)[None, :, None] == blocks[:, None, :]
    tail = jnp.max(jnp.where(where, at[None, None, :], -1), axis=2)
    both = jnp.concatenate([before.reshape(-1), tail.reshape(-1)])
    return jnp.concatenate([jnp.where(both < 0, count, both), (filled - 1)[None]])


def final_kernel(
    rows, own_blocks, groups, tab_ref, link_ref, mask_ref, vec_in, up_vec, lse_ref,
    sum_any, q_any, k_any, v_any, g_any, wk_any, wv_any, wq_any, x_any, far_any, merged_any,
    d_attn_any, base_any,
    dx_ref, gq_ref, gk_ref, gv_ref, go_ref, up_ref, down_ref, vec_ref,
    work_f, work_q, land_c, land_1, land_2, land_z, small, small_in, small_z,
    q_ref, g_ref, dq_ref, wq, wk, wv, x_ref, far_ref, merged_ref, d_attn_ref,
    acc, last, picked, buf, land, dko, dvo, dkr, dvr, out_far, in_far,
    loads, sends, recvs, z_sends, z_recvs, s_sends, s_recvs, d_sends, d_recvs, far_sems,
):
    features = q_ref.shape[1]
    pairs = features // PAIR
    picks_count = own_blocks * 3
    dp, seq = lax.axis_index("dp"), lax.axis_index("seq")
    x, z = lax.rem(dp, 2), dp // 2
    core, y = lax.rem(seq, 2), seq // 2
    mate, across, diagonal = (lax.bitwise_xor(seq, bit) for bit in (1, 2, 3))
    end = link_ref[2 * pairs * (picks_count + 4 * own_blocks)]
    first_block = seq * own_blocks
    low = lanes_low(BLK)
    to_mate, to_y, to_x = (dp, mate), (dp, across), (lax.bitwise_xor(dp, 1), seq)
    to_z = [(lax.rem(z + step, groups) * 2 + x, seq) for step in range(1, groups)]

    loading = {}

    def load(name, src, dst):
        copy = pltpu.make_async_copy(src, dst, loads.at[len(loading)])
        copy.start()
        loading[name] = copy

    load("sum", sum_any, work_f)
    load("q", q_any, q_ref)
    load("g", g_any, g_ref)

    barrier = pltpu.get_barrier_semaphore()
    for target in [to_mate, to_y, to_x] + to_z:
        pl.semaphore_signal(barrier, inc=1, device_id=target, device_id_type=MESH)
    pl.semaphore_wait(barrier, 3 + groups - 1)

    def remote(src, dst, one, two, target):
        return pltpu.make_async_remote_copy(
            src_ref=src, dst_ref=dst, send_sem=one, recv_sem=two, device_id=target,
            device_id_type=MESH,
        )

    ffn_chunks = work_f.shape[0]

    def own_half(k):
        return work_f.at[k] if k < ffn_chunks else work_q.at[k - ffn_chunks, core]

    def way(k):
        return ((y, to_y), (x, to_x)) if KINDS[k] == "A" else ((x, to_x), (y, to_y))

    def copy_core(k):
        return remote(work_q.at[k - ffn_chunks, 1 - core], land_c.at[k - ffn_chunks],
                      sends.at[0, k], recvs.at[0, k], to_mate)

    def copy_one(k):
        (at, target), _ = way(k)
        return remote(own_half(k).at[1 - at], land_1.at[k], sends.at[1, k], recvs.at[1, k], target)

    def copy_two(k):
        (at, _), (then, target) = way(k)
        return remote(own_half(k).at[at, 1 - then], land_2.at[k], sends.at[2, k], recvs.at[2, k],
                      target)

    def copy_z(k, step):
        (at, _), (then, _) = way(k)
        return remote(own_half(k).at[at, then, lax.rem(z + step, groups)], land_z.at[k, step - 1],
                      z_sends.at[k, step - 1], z_recvs.at[k, step - 1], to_z[step - 1])

    def add(total, part):
        total[...] = (total[...].astype(F32) + part[...].astype(F32)).astype(total.dtype)

    def end_core(k):
        copy_core(k).wait()
        mine, other = own_half(k), land_c.at[k - ffn_chunks]

        def body(n, _):
            for one in range(2):
                for two in range(2):
                    add(mine.at[one, two, n], other.at[one, two, n])
            return 0

        lax.fori_loop(0, groups, body, 0)
        copy_one(k).start()

    def end_one(k):
        (at, _), _ = way(k)
        copy_one(k).wait()
        mine, other = own_half(k).at[at], land_1.at[k]

        def body(n, _):
            for one in range(2):
                add(mine.at[one, n], other.at[one, n])
            return 0

        lax.fori_loop(0, groups, body, 0)
        copy_two(k).start()

    def end_two(k):
        (at, _), (then, _) = way(k)
        copy_two(k).wait()
        mine, other = own_half(k).at[at, then], land_2.at[k]

        def body(n, _):
            add(mine.at[n], other.at[n])
            return 0

        lax.fori_loop(0, groups, body, 0)
        for step in range(1, groups):
            copy_z(k, step).start()

    def finish(k):
        (at, _), (then, _) = way(k)
        total = own_half(k)[at, then, z].astype(F32)
        for step in range(1, groups):
            copy_z(k, step).wait()
            total = total + land_z[k, step - 1].astype(F32)
        half = total.shape[0] // 2
        if k < 2:
            down_ref[2 * half * k:2 * half * (k + 1), :] = total
        elif k < 4:
            up_ref[:, (2 * k - 4) * features:(2 * k - 3) * features] = total[:half]
            up_ref[:, (2 * k - 3) * features:(2 * k - 2) * features] = total[half:]
        else:
            one, two = (gq_ref, gk_ref) if k == 4 else (gv_ref, go_ref)
            one[...] = total[:half]
            two[...] = total[half:]

    loading["sum"].wait()
    copy_one(0).start()
    copy_one(1).start()
    for name, src, dst in (
        ("wk", wk_any, wk), ("wv", wv_any, wv), ("wq", wq_any, wq), ("x", x_any, x_ref),
        ("far", far_any, far_ref), ("merged", merged_any, merged_ref),
        ("d_attn", d_attn_any, d_attn_ref), ("base", base_any, dx_ref),
    ):
        load(name, src, dst)

    def copy_pair(p, slot, owner):
        return remote(buf.at[p, owner], land.at[p, slot], d_sends.at[p, slot], d_recvs.at[p, slot],
                      to_mate)

    def lanes_of(p):
        return pl.ds(pl.multiple_of(p * PAIR, PAIR), PAIR)

    def sum_pair(p):
        lanes = lanes_of(p)
        for slot, owner, keys_to, values_to in ((0, across, dkr, dvr), (1, seq, dko, dvo)):
            copy_pair(p, slot, diagonal if slot == 0 else mate).wait()
            for n, to in ((0, keys_to), (1, values_to)):
                to[:, lanes] = (
                    buf[p, owner, n].astype(F32) + land[p, slot, n].astype(F32)
                ).astype(BF16)

    for n in range(2):
        picked[n, picks_count] = jnp.zeros((BLK, PAIR), F32)

    def attention(k_ref, v_ref, kv_sems):
        fetch = [
            pltpu.make_async_copy(k_any, k_ref, kv_sems.at[0]),
            pltpu.make_async_copy(v_any, v_ref, kv_sems.at[1]),
        ]
        for copy in fetch:
            copy.start()
        loading["q"].wait()
        loading["g"].wait()
        for copy in fetch:
            copy.wait()
        last_row = k_ref.shape[0] - 1

        def one_pair(p, _):
            lanes = lanes_of(p)
            acc[...] = jnp.zeros_like(acc)
            last[...] = jnp.zeros_like(last)

            def step(i, _):
                at = first_block + i
                shared, both = key_blocks(tab_ref, end, p, i, at, own_blocks, last_row)
                keys = gathered(k_ref, shared, both, low, lanes)
                values = gathered(v_ref, shared, both, low, lanes)
                query = split_pair(q_ref[rows_of(i), lanes], low)
                grad = split_pair(g_ref[rows_of(i), lanes], low)
                scores = masked_scores(dot_nt(keys, query), mask_ref, i)
                share = jnp.exp(scores - lse_ref[p, pl.ds(i, 1), :])
                d_share = dot_nt(values, grad)
                centre = jnp.sum(share * d_share, axis=0, keepdims=True)
                d_scores = (share * (d_share - centre)).astype(BF16)
                d_query = dot_tn(d_scores, keys) * SCALE
                dq_ref[rows_of(i), lanes] = jnp.where(low, d_query[:BLK], d_query[BLK:]).astype(BF16)
                parts = (dot(d_scores, query), dot(share.astype(BF16), grad))
                for n, part in enumerate(parts):
                    for slot in range(3):
                        acc[n, rows_of(at + slot), :] += part[slot * BLK:(slot + 1) * BLK]
                    acc[n, BLK:2 * BLK, :] += part[3 * BLK:4 * BLK]
                    last[n] += part[4 * BLK:5 * BLK]
                for t in range(3):
                    one = link_ref[2 * p * picks_count + i * 3 + t]
                    two = link_ref[(2 * p + 1) * picks_count + i * 3 + t]
                    for n, part in enumerate(parts):
                        picked[n, i * 3 + t] = part[(5 + t) * BLK:(6 + t) * BLK] + jnp.where(
                            low, picked[n, one], picked[n, two])
                return 0

            lax.fori_loop(0, own_blocks, step, 0, unroll=own_blocks)
            tails = 2 * pairs * picks_count

            def gather(owner, _):
                for inner in range(own_blocks):
                    block = owner * own_blocks + inner
                    one = link_ref[tails + 2 * p * (last_row + 1) + block]
                    two = link_ref[tails + (2 * p + 1) * (last_row + 1) + block]
                    for n in range(2):
                        total = acc[n, rows_of(block + 1), :]
                        total = total + jnp.where(low, picked[n, one], picked[n, two])
                        total = total + last[n] * mask_ref[own_blocks * 8 + block]
                        buf[p, owner, n, inner * BLK:(inner + 1) * BLK] = total.astype(BF16)
                return 0

            lax.fori_loop(0, 4, gather, 0)
            copy_pair(p, 0, diagonal).start()
            copy_pair(p, 1, mate).start()

            @pl.when(p > 0)
            def _():
                sum_pair(p - 1)

            @pl.when(p == 2)
            def _():
                copy_one(2).start()

            @pl.when(p == 3)
            def _():
                end_one(0)
                end_one(1)

            return 0

        lax.fori_loop(0, pairs, one_pair, 0)

    slot = (4 * own_blocks, BLK, features)
    pl.run_scoped(
        attention, VMEM(slot, BF16), VMEM(slot, BF16),
        pltpu.SemaphoreType.DMA((2,)),
    )
    copy_one(3).start()
    sum_pair(pairs - 1)

    loading["wk"].wait()
    loading["wv"].wait()
    out_far[...] = (dot_nt(dkr[...], wk[...]) + dot_nt(dvr[...], wv[...])).astype(BF16)
    far = remote(out_far, in_far, far_sems.at[0], far_sems.at[1], to_y)
    far.start()
    end_two(1)
    for name in ("wq", "x", "far", "merged", "d_attn", "base"):
        loading[name].wait()

    def weights(tmp):
        def regroup(k):
            def body(s, _):
                third, rest = s // 4, lax.rem(s, 4)
                sx, sy = rest // 2, lax.rem(rest, 2)
                a, b = (sy, sx) if KINDS[k] == "A" else (sx, sy)
                for n in range(2):
                    at = pl.ds(pl.multiple_of((2 * s + n) * 24, 8), 24)
                    work_q[k - ffn_chunks, n, a, b, third] = jnp.concatenate(
                        [tmp[0, at, :], tmp[1, at, :]], axis=0).astype(BF16)
                return 0

            lax.fori_loop(0, 4 * groups, body, 0)
            copy_core(k).start()

        tmp[0] = dot_tn(x_ref[...], dq_ref[...])
        tmp[1] = dot_tn(x_ref[...], dko[...]) + dot_tn(far_ref[...], dkr[...])
        regroup(4)
        end_one(2)
        end_two(0)
        tmp[0] = dot_tn(x_ref[...], dvo[...]) + dot_tn(far_ref[...], dvr[...])
        tmp[1] = dot_tn(merged_ref[...], d_attn_ref[...])
        regroup(5)

    pl.run_scoped(weights, VMEM((2, features, features), F32))
    end_core(4)

    small[...] = jnp.zeros_like(small)
    small[0:6, :] = vec_in[0:6, :]
    small[6:7, :] = jnp.sum(dq_ref[...].astype(F32), axis=0, keepdims=True)
    small[7:8, :] = (
        jnp.sum(dvo[...].astype(F32), axis=0, keepdims=True)
        + jnp.sum(dvr[...].astype(F32), axis=0, keepdims=True)
    )
    for n in range(up_vec.shape[1] // features):
        small[8 + n:9 + n, :] = up_vec[:, n * features:(n + 1) * features]

    def copy_small(stage):
        target = (to_mate, to_y, to_x)[stage]
        return remote(small, small_in.at[stage], s_sends.at[stage], s_recvs.at[stage], target)

    def copy_small_z(step):
        return remote(small, small_z.at[step - 1], s_sends.at[2 + step], s_recvs.at[2 + step],
                      to_z[step - 1])

    copy_small(0).start()
    dx_ref[...] += (
        dot_nt(dq_ref[...], wq[...]) + dot_nt(dko[...], wk[...]) + dot_nt(dvo[...], wv[...])
    )
    end_core(5)
    copy_small(0).wait()
    small[...] += small_in[0]
    copy_small(1).start()
    end_one(3)
    end_two(2)
    finish(0)
    finish(1)
    copy_small(1).wait()
    small[...] += small_in[1]
    copy_small(2).start()
    far.wait()
    dx_ref[...] += in_far[...].astype(F32)
    end_one(4)
    copy_small(2).wait()
    small[...] += small_in[2]
    for step in range(1, groups):
        copy_small_z(step).start()
    end_two(3)
    finish(2)
    end_one(5)
    finish(3)
    end_two(4)
    total = small[...]
    for step in range(1, groups):
        copy_small_z(step).wait()
        total = total + small_z[step - 1]
    vec_ref[...] = total
    end_two(5)
    finish(4)
    finish(5)


def final(
    groups, table, link, mask, vectors, up_vector, lse, sums, query, keys, values, grad,
    key_weight, value_weight, query_weight, tokens, far_tokens, merged, d_attn, base,
):
    rows, features = tokens.shape
    own_blocks = rows // BLK
    pairs = features // PAIR
    piece = sums.shape[-2:]
    share = features // (8 * groups)
    wide = up_vector.shape[1] // features
    low = VMEM((rows, features), BF16)
    square = VMEM((features, features), BF16)
    line = jax.ShapeDtypeStruct((share, features), F32)
    any_space = pl.BlockSpec(memory_space=pl.ANY)
    in_smem = pl.BlockSpec(memory_space=pltpu.SMEM)
    dma = pltpu.SemaphoreType.DMA
    return pl.pallas_call(
        functools.partial(final_kernel, rows, own_blocks, groups),
        out_shape=(
            jax.ShapeDtypeStruct((rows, features), F32), line, line, line, line,
            jax.ShapeDtypeStruct((share, wide * features), F32),
            jax.ShapeDtypeStruct((wide * share, features), F32),
            jax.ShapeDtypeStruct((16, features), F32),
        ),
        in_specs=[in_smem] * 3 + [whole_vmem()] * 3 + [any_space] * 13,
        out_specs=(whole_vmem(),) * 8,
        scratch_shapes=[
            VMEM(sums.shape, BF16),
            VMEM((2, 2, 2, 2, groups) + piece, BF16),
            VMEM((2, 2, 2, groups) + piece, BF16),
            VMEM((6, 2, groups) + piece, BF16),
            VMEM((6, groups) + piece, BF16),
            VMEM((6, groups - 1) + piece, BF16),
            VMEM((16, features), F32),
            VMEM((3, 16, features), F32),
            VMEM((groups - 1, 16, features), F32),
            low, low, low, square, square, square, low, low, low, low,
            VMEM((2, (4 * own_blocks + 2) * BLK, PAIR), F32),
            VMEM((2, BLK, PAIR), F32),
            VMEM((2, own_blocks * 3 + 1, BLK, PAIR), F32),
            VMEM((pairs, 4, 2, rows, PAIR), BF16),
            VMEM((pairs, 2, 2, rows, PAIR), BF16),
            low, low, low, low, low, low,
            dma((11,)),
            dma((3, 6)), dma((3, 6)), dma((6, groups - 1)), dma((6, groups - 1)),
            dma((2 + groups,)), dma((2 + groups,)), dma((pairs, 2)), dma((pairs, 2)), dma((2,)),
        ],
        compiler_params=pltpu.CompilerParams(
            collective_id=4, has_side_effects=True, vmem_limit_bytes=LIMIT
        ),
        name="final",
    )(
        table, link, mask, vectors, up_vector, lse, sums, query, keys, values, grad, key_weight,
        value_weight, query_weight, tokens, far_tokens, merged, d_attn, base,
    )


def layer_norm(values, gain, shift):
    center = jnp.mean(values, axis=-1, keepdims=True)
    centered = values - center
    variance = jnp.mean(centered * centered, axis=-1, keepdims=True)
    inv_root = lax.rsqrt(variance + NORM_EPS)
    normed = centered * inv_root
    return (normed * gain + shift, normed, inv_root)


def norm_back(grad_out, normed, inv_root, gain):
    d_normed = grad_out * gain
    grad_in = inv_root * (
        d_normed
        - jnp.mean(d_normed, axis=-1, keepdims=True)
        - normed * jnp.mean(d_normed * normed, axis=-1, keepdims=True)
    )
    return (grad_in, jnp.sum(grad_out * normed, axis=0), jnp.sum(grad_out, axis=0))


def on_device(
    groups,
    tokens, filled_blocks, random_blocks, query_weight, query_bias, key_weight, value_weight,
    value_bias, out_weight, out_bias, attn_gain, attn_shift, up_weight, up_bias, down_weight,
    down_bias, ffn_gain, ffn_shift, cotangent,
):
    row_count, feature_count = tokens.shape
    filled = filled_blocks[0]
    place = lax.axis_index("seq") * row_count + jnp.arange(row_count, dtype=jnp.int32)
    live_tokens = (place < filled * BLK).astype(F32)[:, None]

    table = random_blocks[0].reshape(random_blocks.shape[1], -1)
    table = jnp.pad(table, ((0, 0), (0, 128 - table.shape[1])))
    query, keys, values, far_tokens, table = gather_project(
        tokens, table, query_weight, query_bias, key_weight, value_weight, value_bias
    )
    table = table.reshape(-1)
    mask = masks(filled, lax.axis_index("seq"), row_count // BLK)
    keys, values = (t.reshape(-1, BLK, feature_count) for t in (keys, values))
    merged, lse = attention_forward(table, filled_blocks, mask, query, keys, values)

    if groups:
        seq = lax.axis_index("seq")
        result, base, d_attn, d_merged, vectors, up_vector, sums = dense(
            filled_blocks, tokens, merged, cotangent, out_weight, out_bias, attn_gain, attn_shift,
            up_weight, up_bias, down_weight, down_bias, ffn_gain, ffn_shift)
        grad_tokens, gq, gk, gv, go, up, down, vectors = final(
            groups, table, links(table, filled, row_count // BLK),
            mask, vectors, up_vector,
            lse, sums, query, keys, values, d_merged, key_weight, value_weight, query_weight,
            tokens, far_tokens, merged, d_attn, base)
        shard = lax.axis_index("dp") * 4 + seq
        share = gq.shape[0]
        mine = lax.dynamic_slice(vectors, (0, shard * share), (8, share))
        wide = up.shape[1] // feature_count
        up_sum = lax.dynamic_slice(
            vectors[8:8 + wide].reshape(-1), (shard * wide * share,), (wide * share,))
        return (
            result, grad_tokens, gq, mine[6], gk, gv, mine[7], go, mine[5], mine[3], mine[4], up,
            up_sum, down, mine[2], mine[0], mine[1],
        )

    attn = dot(merged, out_weight) + out_bias
    first, normed_one, root_one = layer_norm(tokens.astype(F32) + attn, attn_gain, attn_shift)
    first_low = first.astype(BF16)
    hidden = dot(first_low, up_weight) + up_bias
    act, gelu_pull = jax.vjp(jax.nn.gelu, hidden)
    act_low = act.astype(BF16)
    ffn = dot(act_low, down_weight) + down_bias
    result, normed_two, root_two = layer_norm(first + ffn, ffn_gain, ffn_shift)
    grad_result = cotangent.astype(F32) * live_tokens
    d_sum_two, grad_ffn_gain, grad_ffn_shift = norm_back(
        grad_result, normed_two, root_two, ffn_gain
    )
    d_ffn = d_sum_two.astype(BF16)
    grad_down_bias = jnp.sum(d_ffn, axis=0, dtype=F32)
    grad_down_weight = dot_tn(act_low, d_ffn)
    d_act = dot_nt(d_ffn, down_weight)
    d_hidden = gelu_pull(d_act)[0].astype(BF16)
    grad_up_bias = jnp.sum(d_hidden, axis=0, dtype=F32)
    grad_up_weight = dot_tn(first_low, d_hidden)
    d_first = d_sum_two + dot_nt(d_hidden, up_weight)
    d_sum_one, grad_attn_gain, grad_attn_shift = norm_back(d_first, normed_one, root_one, attn_gain)
    d_attn = d_sum_one.astype(BF16)
    grad_out_bias = jnp.sum(d_attn, axis=0, dtype=F32)
    grad_out_weight = dot_tn(merged, d_attn)
    d_merged = dot_nt(d_attn, out_weight).astype(BF16)

    d_query, d_keys, d_values = attention_backward(
        table, filled_blocks, mask, query, keys, values, d_merged, lse
    )
    grad_tokens, dk_own, dv_own, dk_far, dv_far = exchange(
        d_keys, d_values, d_query, d_sum_one, query_weight, key_weight, value_weight
    )
    grad_query_weight = dot_tn(tokens, d_query)
    grad_query_bias = jnp.sum(d_query, axis=0, dtype=F32)
    grad_key_weight = dot_tn(tokens, dk_own) + dot_tn(far_tokens, dk_far)
    grad_value_weight = dot_tn(tokens, dv_own) + dot_tn(far_tokens, dv_far)
    grad_value_bias = jnp.sum(dv_own, axis=0, dtype=F32) + jnp.sum(dv_far, axis=0, dtype=F32)

    square = (grad_query_weight, grad_key_weight, grad_value_weight, grad_out_weight)
    vectors = (
        grad_query_bias, grad_value_bias, grad_out_bias, grad_attn_gain, grad_attn_shift,
        grad_down_bias, grad_ffn_gain, grad_ffn_shift,
    )
    square, up, down, vectors, up_sum = summed_anywhere(
        square, grad_up_weight, grad_down_weight, vectors, grad_up_bias)
    return (
        result.astype(BF16), grad_tokens, square[0], vectors[0], square[1], square[2], vectors[1],
        square[3], vectors[2], vectors[3], vectors[4], up, up_sum, down, vectors[5], vectors[6],
        vectors[7],
    )


def solution(mesh):
    both = P(("dp", "seq"), None)
    line = P(("dp", "seq"))
    placed = (both, P("dp"), P("dp", None, "seq", None)) + (P(),) * 15 + (both,)
    groups = 4 if mesh.shape["dp"] == 8 and mesh.shape["seq"] == 4 else 0
    return jax.shard_map(
        functools.partial(on_device, groups),
        mesh=mesh,
        in_specs=placed,
        out_specs=(
            both, both, both, line, both, both, line, both, line, line, line, both, line, both,
            line, line, line,
        ),
        check_vma=False,
    )
```

```python
import functools

import jax
import jax.numpy as jnp
from jax import lax
from jax.experimental import pallas as pl
from jax.experimental.pallas import tpu as pltpu
from jax.sharding import PartitionSpec as P

HEAD_DIM = 64
BLK = 64
PAIR = 2 * HEAD_DIM
TABLE = 8
NORM_EPS = 1e-05
MASKED = -1e30
SCALE = HEAD_DIM ** (-0.5)
MESH = pl.DeviceIdType.MESH
BF16 = jnp.bfloat16
F32 = jnp.float32
VMEM = pltpu.VMEM
LIMIT = 63 << 20


def whole_vmem():
    return pl.BlockSpec(memory_space=pltpu.VMEM)


def dot(left, right):
    return jnp.dot(left, right, preferred_element_type=F32)


def dot_nt(left, right):
    return lax.dot_general(left, right, (((1,), (1,)), ((), ())), preferred_element_type=F32)


def dot_tn(left, right):
    return lax.dot_general(left, right, (((0,), (0,)), ((), ())), preferred_element_type=F32)


def gather_kernel(
    rows, width, x_ref, tab_ref, wq_ref, wk_ref, wv_ref, bias_ref,
    q_ref, k_ref, v_ref, far_ref, tab_out, land, tab_land, sends, recvs, tab_sends, tab_recvs,
):
    parts = 4
    part = rows // parts
    dp, me = lax.axis_index("dp"), lax.axis_index("seq")
    mate, across, diagonal = (lax.bitwise_xor(me, bit) for bit in (1, 2, 3))
    barrier = pltpu.get_barrier_semaphore()
    for other in (mate, across, diagonal):
        pl.semaphore_signal(barrier, inc=1, device_id=(dp, other), device_id_type=MESH)
    pl.semaphore_wait(barrier, 3)

    def send(src, dst, slot, target):
        copy = pltpu.make_async_remote_copy(
            src_ref=src, dst_ref=dst, send_sem=sends.at[slot], recv_sem=recvs.at[slot],
            device_id=(dp, target), device_id_type=MESH,
        )
        copy.start()
        return copy

    far = [
        send(x_ref.at[pl.ds(r * part, part)], land.at[0, pl.ds(r * part, part)], r, across)
        for r in range(parts)
    ]
    near = send(x_ref, land.at[1], parts, mate)
    tables = []
    own_blocks = tab_ref.shape[0] // 4
    for slot, other in enumerate((mate, across, diagonal)):
        copy = pltpu.make_async_remote_copy(
            src_ref=tab_ref.at[pl.ds(pl.multiple_of(other * own_blocks, 8), own_blocks)],
            dst_ref=tab_land.at[slot], send_sem=tab_sends.at[slot], recv_sem=tab_recvs.at[slot],
            device_id=(dp, other), device_id_type=MESH,
        )
        copy.start()
        tables.append(copy)

    def keys_values(x, at):
        k_ref[pl.ds(at, width), :] = dot(x, wk_ref[...]).astype(BF16)
        v_ref[pl.ds(at, width), :] = (dot(x, wv_ref[...]) + bias_ref[1:2, :]).astype(BF16)

    def own(r, _):
        at = pl.multiple_of(r * width, width)
        x = x_ref[pl.ds(at, width), :]
        q_ref[pl.ds(at, width), :] = (
            (dot(x, wq_ref[...]) + bias_ref[0:1, :]).astype(BF16) * jnp.asarray(SCALE, BF16)
        )
        keys_values(x, pl.multiple_of(me * rows + at, width))
        return 0

    lax.fori_loop(0, rows // width, own, 0)

    def block(slot, owner, start, count):
        def step(r, _):
            at = pl.multiple_of(start + r * width, width)
            keys_values(land[slot, pl.ds(at, width), :], pl.multiple_of(owner * rows + at, width))
            return 0

        lax.fori_loop(0, count // width, step, 0)

    near.wait()
    block(1, mate, 0, rows)
    relayed = []
    for r in range(parts):
        far[r].wait()
        piece = pl.ds(r * part, part)
        relayed.append(send(land.at[0, piece], land.at[2, piece], parts + 1 + r, mate))
        block(0, across, r * part, part)
        if r:
            relayed[r - 1].wait()
            block(2, diagonal, (r - 1) * part, part)
    far_ref[...] = land[0]
    for copy in tables:
        copy.wait()
    relayed[-1].wait()
    block(2, diagonal, (parts - 1) * part, part)
    tab_out[pl.ds(me, 1)] = tab_ref[pl.ds(pl.multiple_of(me * own_blocks, 8), own_blocks)][None]
    for slot, other in enumerate((mate, across, diagonal)):
        tab_out[pl.ds(other, 1)] = tab_land[slot][None]


def gather_project(tokens, table, query_weight, key_weight, value_weight, biases):
    rows, features = tokens.shape
    own_blocks = rows // BLK
    copies = 4 + 1 + 4
    return pl.pallas_call(
        functools.partial(gather_kernel, rows, 128),
        out_shape=(
            jax.ShapeDtypeStruct((rows, features), BF16),
            jax.ShapeDtypeStruct((4 * rows, features), BF16),
            jax.ShapeDtypeStruct((4 * rows, features), BF16),
            jax.ShapeDtypeStruct((rows, features), BF16),
            jax.ShapeDtypeStruct((4, own_blocks, 128), jnp.int32),
        ),
        in_specs=[whole_vmem()] * 6,
        out_specs=(whole_vmem(),) * 5,
        scratch_shapes=[
            VMEM((3, rows, features), BF16),
            VMEM((3, own_blocks, 128), jnp.int32),
            pltpu.SemaphoreType.DMA((copies,)),
            pltpu.SemaphoreType.DMA((copies,)),
            pltpu.SemaphoreType.DMA((3,)),
            pltpu.SemaphoreType.DMA((3,)),
        ],
        compiler_params=pltpu.CompilerParams(
            collective_id=0, has_side_effects=True, vmem_limit_bytes=LIMIT
        ),
        name="gather_project",
    )(tokens, table, query_weight, key_weight, value_weight, biases)


def key_blocks(tab_ref, end, pair, i, at, own_blocks, last_row):
    def chosen(head, t):
        group, inner = lax.div(head, 3), lax.rem(head, 3)
        return tab_ref[(group * own_blocks + i) * 128 + inner * 3 + t]

    head = 2 * pair
    both = [(chosen(head, t), chosen(head + 1, t)) for t in range(3)]
    shared = [
        jnp.maximum(at - 1, 0), at, jnp.minimum(at + 1, last_row), jnp.int32(0), end,
    ]
    return shared, both


def rows_of(block):
    return pl.ds(pl.multiple_of(block * BLK, BLK), BLK)


def lanes_low(rows):
    return lax.broadcasted_iota(jnp.int32, (rows, PAIR), 1) < HEAD_DIM


def split_pair(x, low):
    zero = jnp.zeros_like(x)
    return jnp.concatenate([jnp.where(low, x, zero), jnp.where(low, zero, x)], axis=0)


def gathered(ref, shared, both, low, lanes=slice(None)):
    tiles = [ref[b, :, lanes] for b in shared]
    for first, second in both:
        tiles.append(jnp.where(low, ref[first, :, lanes], ref[second, :, lanes]))
    return jnp.concatenate(tiles, axis=0)


def masked_scores(scores, mask_ref, i):
    parts = [scores[n * BLK:(n + 1) * BLK] + mask_ref[i * 8 + n] for n in range(5)]
    return jnp.concatenate(parts + [scores[5 * BLK:]], axis=0)


def forward_kernel(own_blocks, tab_ref, filled_ref, mask_ref, q_ref, k_ref, v_ref, out_ref, lse_ref):
    pair = pl.program_id(0)
    filled = filled_ref[0]
    first_block = lax.axis_index("seq") * own_blocks
    last_row = k_ref.shape[0] - 1
    low = lanes_low(BLK)

    def step(i, _):
        at = first_block + i
        shared, both = key_blocks(tab_ref, filled - 1, pair, i, at, own_blocks, last_row)
        keys = gathered(k_ref, shared, both, low)
        values = gathered(v_ref, shared, both, low)
        query = split_pair(q_ref[rows_of(i), :], low)
        scores = masked_scores(dot_nt(keys, query), mask_ref, i)
        highest = jnp.max(scores, axis=0, keepdims=True)
        weights = jnp.exp(scores - highest)
        total = jnp.sum(weights, axis=0, keepdims=True)
        share = (weights * (1.0 / total)).astype(BF16)
        output = dot_tn(share, values)
        merged = jnp.where(low, output[:BLK], output[BLK:])
        merged = jnp.where(at < filled, merged, 0.0)
        out_ref[rows_of(i), :] = merged.astype(BF16)
        lse_ref[0, pl.ds(i, 1), :] = highest + jnp.log(total)
        return 0

    lax.fori_loop(0, own_blocks, step, 0, unroll=own_blocks)


def attention_forward(table, filled, mask, query, keys, values):
    rows, features = query.shape
    own_blocks = rows // BLK
    slot_blocks = keys.shape[0]
    pairs = features // PAIR
    column = lambda n: pl.BlockSpec((n, PAIR), lambda p, *_: (0, p))
    blocks = lambda n: pl.BlockSpec((n, BLK, PAIR), lambda p, *_: (0, 0, p))
    return pl.pallas_call(
        functools.partial(forward_kernel, own_blocks),
        out_shape=(
            jax.ShapeDtypeStruct((rows, features), BF16),
            jax.ShapeDtypeStruct((pairs, own_blocks, PAIR), F32),
        ),
        grid_spec=pltpu.PrefetchScalarGridSpec(
            num_scalar_prefetch=3,
            grid=(pairs,),
            in_specs=[column(rows), blocks(slot_blocks), blocks(slot_blocks)],
            out_specs=(column(rows), pl.BlockSpec((1, own_blocks, PAIR), lambda p, *_: (p, 0, 0))),
        ),
        compiler_params=pltpu.CompilerParams(vmem_limit_bytes=LIMIT),
        name="attention_forward",
    )(table, filled, mask, query, keys, values)


def backward_kernel(
    own_blocks, tab_ref, filled_ref, mask_ref, q_ref, k_ref, v_ref, g_ref, lse_ref,
    dq_ref, dk_ref, dv_ref, dk_sum, dv_sum,
):
    pair = pl.program_id(0)
    filled = filled_ref[0]
    first_block = lax.axis_index("seq") * own_blocks
    last_row = k_ref.shape[0] - 1
    low = lanes_low(BLK)
    dk_sum[...] = jnp.zeros_like(dk_sum)
    dv_sum[...] = jnp.zeros_like(dv_sum)

    def step(i, _):
        at = first_block + i
        shared, both = key_blocks(tab_ref, filled - 1, pair, i, at, own_blocks, last_row)
        keys = gathered(k_ref, shared, both, low)
        values = gathered(v_ref, shared, both, low)
        query = split_pair(q_ref[rows_of(i), :], low)
        grad = split_pair(jnp.where(at < filled, g_ref[rows_of(i), :], jnp.zeros((), BF16)), low)
        scores = masked_scores(dot_nt(keys, query), mask_ref, i)
        share = jnp.exp(scores - lse_ref[0, pl.ds(i, 1), :])
        d_share = dot_nt(values, grad)
        centre = jnp.sum(share * d_share, axis=0, keepdims=True)
        d_scores = (share * (d_share - centre)).astype(BF16)
        d_query = dot_tn(d_scores, keys) * SCALE
        dq_ref[rows_of(i), :] = jnp.where(low, d_query[:BLK], d_query[BLK:]).astype(BF16)
        for total, part in ((dk_sum, dot(d_scores, query)), (dv_sum, dot(share.astype(BF16), grad))):
            for slot, block in enumerate(shared):
                total[rows_of(block), :] += part[slot * BLK:(slot + 1) * BLK]
            for t, (one, two) in enumerate(both):
                tile = part[(5 + t) * BLK:(6 + t) * BLK]
                total[rows_of(one), :] += jnp.where(low, tile, 0.0)
                total[rows_of(two), :] += jnp.where(low, 0.0, tile)
        return 0

    lax.fori_loop(0, own_blocks, step, 0, unroll=own_blocks)
    dk_ref[...] = dk_sum[...].astype(BF16)
    dv_ref[...] = dv_sum[...].astype(BF16)


def attention_backward(table, filled, mask, query, keys, values, grad, lse):
    rows, features = query.shape
    slot_blocks = keys.shape[0]
    slot_rows = slot_blocks * BLK
    own_blocks = rows // BLK
    pairs = features // PAIR
    blocks = lambda n: pl.BlockSpec((n, BLK, PAIR), lambda p, *_: (0, 0, p))
    column = lambda n: pl.BlockSpec((n, PAIR), lambda p, *_: (0, p))
    return pl.pallas_call(
        functools.partial(backward_kernel, own_blocks),
        out_shape=(
            jax.ShapeDtypeStruct((rows, features), BF16),
            jax.ShapeDtypeStruct((slot_rows, features), BF16),
            jax.ShapeDtypeStruct((slot_rows, features), BF16),
        ),
        grid_spec=pltpu.PrefetchScalarGridSpec(
            num_scalar_prefetch=3,
            grid=(pairs,),
            in_specs=[
                column(rows), blocks(slot_blocks), blocks(slot_blocks), column(rows),
                pl.BlockSpec((1, own_blocks, PAIR), lambda p, *_: (p, 0, 0)),
            ],
            out_specs=(column(rows), column(slot_rows), column(slot_rows)),
            scratch_shapes=[VMEM((slot_rows, PAIR), F32), VMEM((slot_rows, PAIR), F32)],
        ),
        compiler_params=pltpu.CompilerParams(vmem_limit_bytes=LIMIT),
        name="attention_backward",
    )(table, filled, mask, query, keys, values, grad, lse)


def exchange_kernel(
    rows, width, dk_ref, dv_ref, dq_ref, base_ref, wq_ref, wk_ref, wv_ref,
    dx_ref, dko_ref, dvo_ref, dkr_ref, dvr_ref,
    land, out_far, in_far, sends, recvs,
):
    dp, me = lax.axis_index("dp"), lax.axis_index("seq")
    mate, across, diagonal = (lax.bitwise_xor(me, bit) for bit in (1, 2, 3))
    barrier = pltpu.get_barrier_semaphore()
    for other in (mate, across):
        pl.semaphore_signal(barrier, inc=1, device_id=(dp, other), device_id_type=MESH)
    pl.semaphore_wait(barrier, 2)

    def send(src, dst, slot, target):
        copy = pltpu.make_async_remote_copy(
            src_ref=src, dst_ref=dst, send_sem=sends.at[slot], recv_sem=recvs.at[slot],
            device_id=(dp, target), device_id_type=MESH,
        )
        copy.start()
        return copy

    def owned(index):
        return pl.ds(pl.multiple_of(index * rows, rows), rows)

    copies = [
        send(ref.at[owned(owner)], land.at[slot], slot, mate)
        for slot, (ref, owner) in enumerate(
            ((dk_ref, diagonal), (dv_ref, diagonal), (dk_ref, mate), (dv_ref, mate))
        )
    ]

    def summed(ref, owner, slot, to_ref):
        to_ref[...] = (ref[owned(owner), :].astype(F32) + land[slot].astype(F32)).astype(BF16)

    copies[0].wait()
    summed(dk_ref, across, 0, dkr_ref)
    copies[1].wait()
    summed(dv_ref, across, 1, dvr_ref)

    steps = rows // width
    for r in range(steps):
        at = pl.ds(r * width, width)
        out_far[at, :] = (
            dot_nt(dkr_ref[at, :], wk_ref[...]) + dot_nt(dvr_ref[at, :], wv_ref[...])
        ).astype(BF16)
    far = send(out_far, in_far, 4, across)
    copies[2].wait()
    summed(dk_ref, me, 2, dko_ref)
    copies[3].wait()
    summed(dv_ref, me, 3, dvo_ref)

    def one(r, _):
        at = pl.ds(pl.multiple_of(r * width, width), width)
        dx_ref[at, :] = (
            base_ref[at, :]
            + dot_nt(dq_ref[at, :], wq_ref[...])
            + dot_nt(dko_ref[at, :], wk_ref[...])
            + dot_nt(dvo_ref[at, :], wv_ref[...])
        )
        return 0

    lax.fori_loop(0, steps, one, 0)
    far.wait()
    dx_ref[...] += in_far[...].astype(F32)


def exchange(d_keys, d_values, d_query, base, query_weight, key_weight, value_weight):
    rows, features = d_query.shape
    small = jax.ShapeDtypeStruct((rows, features), BF16)
    return pl.pallas_call(
        functools.partial(exchange_kernel, rows, 128),
        out_shape=(jax.ShapeDtypeStruct((rows, features), F32), small, small, small, small),
        in_specs=[whole_vmem()] * 7,
        out_specs=(whole_vmem(),) * 5,
        scratch_shapes=[
            VMEM((4, rows, features), BF16),
            VMEM((rows, features), BF16),
            VMEM((rows, features), BF16),
            pltpu.SemaphoreType.DMA((5,)),
            pltpu.SemaphoreType.DMA((5,)),
        ],
        compiler_params=pltpu.CompilerParams(
            collective_id=1, has_side_effects=True, vmem_limit_bytes=LIMIT
        ),
        name="exchange",
    )(d_keys, d_values, d_query, base, query_weight, key_weight, value_weight)


def summed_anywhere(square, up, down, vectors, up_bias):
    def one(g):
        return lax.psum_scatter(g, ("dp", "seq"), scatter_dimension=0, tiled=True)

    return [one(g) for g in square], one(up), one(down), [one(v) for v in vectors], one(up_bias)


GELU_A = 0.044715
GELU_C = 0.7978845608028654
UNIT = (48, 384)
KINDS = "ABACABBCBABB"
AXES = {"A": "yxz", "B": "xyz", "C": "zxy"}
DOWN, UP, SQUARE = 0, 4, 8
BETWEEN = (
    (),
    ((0, 0), (2, 0)),
    ((3, 0), (1, 1)),
    ((5, 0), (6, 0), (4, 0)),
    ((7, 0), (11, 0), (0, 1), (2, 1)),
    ((3, 1), (1, 2)),
)
AFTER = ((5, 1), (6, 1), (4, 1), (7, 1), (11, 1), (0, 2), (2, 2), (3, 2))
LAST = (
    (5, 2), (6, 2), (4, 2), (7, 2), (11, 2), (9, 0), (10, 0), (8, 0), (9, 1), (10, 1), (8, 1),
    (9, 2), (10, 2), (8, 2),
)


def normed_rows(values):
    center = jnp.mean(values, axis=-1, keepdims=True)
    centered = values - center
    variance = jnp.mean(centered * centered, axis=-1, keepdims=True)
    inv_root = lax.rsqrt(variance + NORM_EPS)
    return centered * inv_root, inv_root


def norm_pull(grad_out, normed, inv_root, gain):
    d_normed = grad_out * gain
    return inv_root * (
        d_normed
        - jnp.mean(d_normed, axis=-1, keepdims=True)
        - normed * jnp.mean(d_normed * normed, axis=-1, keepdims=True)
    )


def column_sum(values):
    return jnp.sum(values, axis=0, keepdims=True)


def masks(filled, seq, own_blocks):
    at = seq * own_blocks + jnp.arange(own_blocks, dtype=jnp.int32)[:, None]
    kind = jnp.arange(8, dtype=jnp.int32)[None, :]
    window = at + kind - 1
    ok = jnp.where(
        kind < 3, (window >= 0) & (window < filled),
        jnp.where(kind == 3, at >= 2, jnp.abs(at - (filled - 1)) > 1))
    last = jnp.arange(4 * own_blocks, dtype=jnp.int32) == filled - 1
    return jnp.concatenate([jnp.where(ok, 0.0, MASKED).astype(F32).reshape(-1), last.astype(F32)])


def links(table, filled, own_blocks):
    mine = table.reshape(4, own_blocks, 128)[:, :, :9].reshape(4, own_blocks, 3, 3)
    blocks = mine.transpose(0, 2, 1, 3).reshape(12, own_blocks * 3)
    count = blocks.shape[1]
    at = jnp.arange(count, dtype=jnp.int32)
    same = (blocks[:, :, None] == blocks[:, None, :]) & (at[None, None, :] < at[None, :, None])
    before = jnp.max(jnp.where(same, at[None, None, :], -1), axis=2)
    where = jnp.arange(32, dtype=jnp.int32)[None, :, None] == blocks[:, None, :]
    tail = jnp.max(jnp.where(where, at[None, None, :], -1), axis=2)
    both = jnp.concatenate([before.reshape(-1), tail.reshape(-1)])
    return jnp.concatenate([jnp.where(both < 0, count, both), (filled - 1)[None]])


def layer_kernel(
    rows, tile, own_blocks, groups, tab_ref, link_ref, mask_ref, bias_ref, bu_ref, lse_ref,
    x_any, merged_any, cot_any, wo_any, wu_any, wd_any, q_any, k_any, v_any, wk_any, wv_any, wq_any,
    far_any,
    result_ref, dx_ref, gq_ref, gk_ref, gv_ref, go_ref, up_ref, down_ref, vec_ref,
    work, land, core_down, core_up, core_out, pair_in, in_far, small, small_in, small_z,
    x_ref, merged_ref, d_attn_ref, d_merged_ref,
    loads, sends, recvs, c_sends, c_recvs, p_sends, p_recvs, s_sends, s_recvs, far_sems,
):
    features = x_ref.shape[1]
    hidden = bu_ref.shape[1]
    wide = hidden // features
    pairs = features // PAIR
    picks_count = own_blocks * 3
    share = features // (8 * groups)
    shards = 4 * groups
    half = features // 2
    dp, seq = lax.axis_index("dp"), lax.axis_index("seq")
    x, z = lax.rem(dp, 2), dp // 2
    core, y = lax.rem(seq, 2), seq // 2
    mate, across, diagonal = (lax.bitwise_xor(seq, bit) for bit in (1, 2, 3))
    end = link_ref[2 * pairs * (picks_count + 4 * own_blocks)]
    first_block = seq * own_blocks
    low = lanes_low(BLK)
    to_mate, to_y = (dp, mate), (dp, across)
    place_of = {"x": (x, 2), "y": (y, 2), "z": (z, groups)}

    def device(axis, index):
        if axis == "x":
            return (2 * z + index, seq)
        if axis == "y":
            return (dp, 2 * index + core)
        return (2 * index + x, seq)

    neighbours = [to_mate, to_y, device("x", 1 - x)] + [
        device("z", lax.rem(z + step, groups)) for step in range(1, groups)]

    loading = {}

    def load(name, src, dst):
        copy = pltpu.make_async_copy(src, dst, loads.at[len(loading)])
        copy.start()
        loading[name] = copy

    def remote(src, dst, one, two, target):
        return pltpu.make_async_remote_copy(
            src_ref=src, dst_ref=dst, send_sem=one, recv_sem=two, device_id=target,
            device_id_type=MESH,
        )

    def lanes_of(p):
        return pl.ds(pl.multiple_of(p * PAIR, PAIR), PAIR)

    def columns(j):
        return pl.ds(pl.multiple_of(j * features, features), features)

    def tiles(body):
        def step(r, _):
            body(pl.ds(pl.multiple_of(r * tile, tile), tile), r)
            return 0

        lax.fori_loop(0, rows // tile, step, 0)


    def index_of(u, at_x, at_y, at_z):
        at = {"x": at_x, "y": at_y, "z": at_z}
        flat = 0
        for axis in AXES[KINDS[u]]:
            flat = flat * place_of[axis][1] + at[axis]
        return flat

    def shard_of(s):
        return s // 4, lax.rem(s // 2, 2), lax.rem(s, 2)

    def stage_of(u, stage):
        sizes = [place_of[axis][1] for axis in AXES[KINDS[u]]] + [1]
        base, offset, sem, block = 0, 0, 0, shards
        for n, axis in enumerate(AXES[KINDS[u]]):
            block = block // sizes[n]
            if n == stage:
                return axis, place_of[axis][0], sizes[n], block, base, offset, sem
            base = base + place_of[axis][0] * block
            offset += (sizes[n] - 1) * block
            sem += sizes[n] - 1
        return None

    def stage_copies(u, stage):
        axis, mine, size, block, base, offset, sem = stage_of(u, stage)
        copies = []
        for step in range(1, size):
            index = lax.rem(mine + step, size)
            copies.append(remote(
                work.at[u, pl.ds(base + index * block, block)],
                land.at[u, pl.ds(offset + (step - 1) * block, block)],
                sends.at[u, sem + step - 1], recvs.at[u, sem + step - 1], device(axis, index)))
        return copies

    def begin(u, stage):
        for copy in stage_copies(u, stage):
            copy.start()

    def finish(u, stage):
        _, mine, size, block, base, offset, _ = stage_of(u, stage)
        for copy in stage_copies(u, stage):
            copy.wait()

        def total(r):
            value = work[u, base + mine * block + r].astype(F32)
            for step in range(size - 1):
                value = value + land[u, offset + step * block + r].astype(F32)
            return value

        if stage < 2:
            def body(r, _):
                work[u, base + mine * block + r] = total(r).astype(BF16)
                return 0

            lax.fori_loop(0, block, body, 0)
            begin(u, stage + 1)
            return
        value = total(0)
        if u < UP:
            down_ref[(u // 2) * UNIT[0]:(u // 2 + 1) * UNIT[0], (u % 2) * half:(u % 2 + 1) * half] = value
        else:
            to = up_ref if u < SQUARE else (gq_ref, gk_ref, gv_ref, go_ref)[u - SQUARE]
            at = (u - UP) * features if u < SQUARE else 0
            to[:, at:at + half] = value[:share]
            to[:, at + half:at + features] = value[share:]

    def folded(source, at, count):
        return jnp.concatenate(
            [source[pl.ds(at, count), 0:half], source[pl.ds(at, count), half:features]], axis=0)

    def square_pieces(u, source, other):
        def body(s, _):
            at_z, at_x, at_y = shard_of(s)
            index = index_of(u, at_x, at_y, at_z)
            for own in (True, False):
                row = 2 * s + (core if own else 1 - core)
                value = folded(source, pl.multiple_of(row * share, 8), share).astype(BF16)
                if own:
                    work[u, index] = value
                else:
                    other[index // 4, lax.rem(index, 4)] = value
            return 0

        lax.fori_loop(0, shards, body, 0)

    def add_core(u, landed):
        def body(n, _):
            work[u, n] = (
                work[u, n].astype(F32) + landed[n // 4, lax.rem(n, 4)].astype(F32)
            ).astype(BF16)
            return 0

        lax.fori_loop(0, shards, body, 0)

    def core_copy(src, dst, slot):
        return remote(src, dst, c_sends.at[slot], c_recvs.at[slot], to_mate)

    load("x", x_any, x_ref)
    load("merged", merged_any, merged_ref)


    def dense(
        wo, wu, wd, cot_ref, normed_one, root_one, first_low, act, slope, ffn, d_ffn, tmp,
        other_down, other_up,
    ):
        load("wo", wo_any, wo)
        load("wu", wu_any, wu)
        load("wd", wd_any, wd)
        load("cot", cot_any, cot_ref)
        barrier = pltpu.get_barrier_semaphore()
        for target in neighbours:
            pl.semaphore_signal(barrier, inc=1, device_id=target, device_id_type=MESH)
        pl.semaphore_wait(barrier, len(neighbours))
        bo, g1, s1, bd, g2, s2 = (bias_ref.at[n:n + 1, :] for n in range(2, 8))

        for name in ("x", "merged", "wo"):
            loading[name].wait()
        ffn[...] = dot(merged_ref[...], wo[...])

        def norm_one(at, r):
            normed, inv_root = normed_rows(x_ref[at, :].astype(F32) + (ffn[at, :] + bo[...]))
            normed_one[at, :] = normed
            root_one[at, :] = inv_root
            first_low[at, :] = (normed * g1[...] + s1[...]).astype(BF16)

        tiles(norm_one)

        loading["wu"].wait()
        loading["wd"].wait()
        ffn[...] = jnp.zeros_like(ffn)

        def forward(j, _):
            at = columns(j)
            u = dot(first_low[...], wu[:, at]) + bu_ref[:, at]
            square = u * u
            t = jnp.tanh(GELU_C * (u + GELU_A * (square * u)))
            upper = 0.5 * (1.0 + t)
            act[j] = (u * upper).astype(BF16)
            slope[j] = (
                upper + (0.5 * GELU_C) * u * (1.0 - t * t) * (1.0 + (3.0 * GELU_A) * square)
            ).astype(slope.dtype)
            ffn[...] += dot(act[j], wd[at, :])
            return 0

        lax.fori_loop(0, wide, forward, 0)

        small[...] = jnp.zeros_like(small)
        limit = (end + 1) * BLK - seq * rows
        loading["cot"].wait()

        def norm_two(at, r):
            first = normed_one[at, :] * g1[...] + s1[...]
            normed, inv_root = normed_rows(first + (ffn[at, :] + bd[...]))
            result_ref[at, :] = (normed * g2[...] + s2[...]).astype(BF16)
            place = lax.broadcasted_iota(jnp.int32, (tile, 1), 0) + r * tile
            grad = cot_ref[at, :].astype(F32) * (place < limit).astype(F32)
            pulled = norm_pull(grad, normed, inv_root, g2[...])
            rounded = pulled.astype(BF16)
            ffn[at, :] = pulled
            d_ffn[at, :] = rounded
            small[0:1, :] += column_sum(grad * normed)
            small[1:2, :] += column_sum(grad)
            small[2:3, :] += column_sum(rounded.astype(F32))

        tiles(norm_two)

        down_copies = []
        for j in range(wide):
            tmp[...] = dot_tn(act[j], d_ffn[...])

            def pieces(n, _):
                at_x, at_y = n // 2, lax.rem(n, 2)
                for own in (True, False):
                    row = 2 * n + (core if own else 1 - core)
                    at = pl.multiple_of(row * (wide * share), 8)
                    for u in range(4):
                        value = tmp[
                            pl.ds(pl.multiple_of(at + (u // 2) * UNIT[0], 8), UNIT[0]),
                            (u % 2) * half:(u % 2 + 1) * half].astype(BF16)
                        if own:
                            work[u, index_of(u, at_x, at_y, j)] = value
                        else:
                            other_down[j, u, n] = value
                return 0

            lax.fori_loop(0, 4, pieces, 0)
            down_copies.append(core_copy(other_down.at[j], core_down.at[j], j))
            down_copies[-1].start()

        def backward(j, _):
            d_hidden = (dot_nt(d_ffn[...], wd[columns(j), :]) * slope[j].astype(F32)).astype(BF16)
            act[j] = d_hidden
            for n in range(wide):
                @pl.when(j == n)
                def _():
                    small[8 + n:9 + n, :] = column_sum(d_hidden.astype(F32))
            return 0

        lax.fori_loop(0, wide, backward, 0)

        for copy in down_copies:
            copy.wait()

        def sum_down(s, _):
            at_z, at_x, at_y = shard_of(s)
            for u in range(4):
                index = index_of(u, at_x, at_y, at_z)
                work[u, index] = (
                    work[u, index].astype(F32) + core_down[at_z, u, at_x * 2 + at_y].astype(F32)
                ).astype(BF16)
            return 0

        lax.fori_loop(0, shards, sum_down, 0)
        for u in range(4):
            begin(u, 0)

        up_copies = []
        for j in range(wide):
            tmp[...] = dot_tn(first_low[...], act[j])
            square_pieces(UP + j, tmp, other_up.at[j])
            up_copies.append(core_copy(other_up.at[j], core_up.at[j], wide + j))
            up_copies[-1].start()

        for j in range(wide):
            ffn[...] += dot_nt(act[j], wu[:, j * features:(j + 1) * features])
        for j in range(wide):
            up_copies[j].wait()
            add_core(UP + j, core_up.at[j])
            begin(UP + j, 0)
        finish(1, 0)

        def pull_one(at, r):
            grad = ffn[at, :]
            normed = normed_one[at, :]
            pulled = norm_pull(grad, normed, root_one[at, :], g1[...])
            rounded = pulled.astype(BF16)
            dx_ref[at, :] = pulled
            d_attn_ref[at, :] = rounded
            small[3:4, :] += column_sum(grad * normed)
            small[4:5, :] += column_sum(grad)
            small[5:6, :] += column_sum(rounded.astype(F32))

        tiles(pull_one)
        live = lax.broadcasted_iota(jnp.int32, (rows, 1), 0) < limit
        d_merged_ref[...] = jnp.where(live, dot_nt(d_attn_ref[...], wo[...]), 0.0).astype(BF16)

    low_rows = VMEM((rows, features), BF16)
    full_rows = VMEM((rows, features), F32)
    square_low = VMEM((features, features), BF16)
    pl.run_scoped(
        dense, square_low, VMEM((features, hidden), BF16), VMEM((hidden, features), BF16),
        low_rows, full_rows, VMEM((rows, 1), F32), low_rows, VMEM((wide, rows, features), BF16),
        VMEM((wide, rows, features), SLOPE), full_rows, low_rows, VMEM((features, features), F32),
        VMEM((4, 4, 4) + UNIT, BF16), VMEM((4, 4, 4) + UNIT, BF16),
    )


    def attention(
        k_ref, v_ref, q_ref, dq_ref, far_ref, wk, wv, wq, acc, last, picked, buf, dko, dvo, dkr,
        dvr, out_far, other, tmp,
    ):
        for name, src, dst in (
            ("q", q_any, q_ref), ("k", k_any, k_ref), ("v", v_any, v_ref), ("wk", wk_any, wk),
            ("wv", wv_any, wv), ("wq", wq_any, wq), ("far", far_any, far_ref),
        ):
            load(name, src, dst)
        square_copies = {
            u: core_copy(other.at[u - SQUARE],
                         core_out if u == SQUARE + 3 else core_down.at[u - SQUARE], u)
            for u in range(SQUARE, SQUARE + 4)
        }

        def square(u, source):
            square_pieces(u, source, other.at[u - SQUARE])
            square_copies[u].start()

        def end_square(u):
            square_copies[u].wait()
            add_core(u, core_out if u == SQUARE + 3 else core_down.at[u - SQUARE])
            begin(u, 0)

        def copy_pair(p, slot, owner):
            return remote(buf.at[p, owner], pair_in.at[p, slot], p_sends.at[p, slot],
                          p_recvs.at[p, slot], to_mate)

        def sum_pair(p):
            lanes = lanes_of(p)
            for slot, owner, keys_to, values_to in ((0, across, dkr, dvr), (1, seq, dko, dvo)):
                copy_pair(p, slot, diagonal if slot == 0 else mate).wait()
                for n, to in ((0, keys_to), (1, values_to)):
                    to[:, lanes] = (
                        buf[p, owner, n].astype(F32) + pair_in[p, slot, n].astype(F32)
                    ).astype(BF16)

        def heads():
            for n in range(2):
                picked[n, picks_count] = jnp.zeros((BLK, PAIR), F32)
            last_row = k_ref.shape[0] - 1
            for name in ("q", "k", "v"):
                loading[name].wait()

            def one_pair(p, _):
                lanes = lanes_of(p)
                acc[...] = jnp.zeros_like(acc)
                last[...] = jnp.zeros_like(last)

                def step(i, _):
                    at = first_block + i
                    shared, both = key_blocks(tab_ref, end, p, i, at, own_blocks, last_row)
                    keys = gathered(k_ref, shared, both, low, lanes)
                    values = gathered(v_ref, shared, both, low, lanes)
                    query = split_pair(q_ref[rows_of(i), lanes], low)
                    grad = split_pair(d_merged_ref[rows_of(i), lanes], low)
                    scores = masked_scores(dot_nt(keys, query), mask_ref, i)
                    share_of = jnp.exp(scores - lse_ref[p, pl.ds(i, 1), :])
                    d_share = dot_nt(values, grad)
                    centre = jnp.sum(share_of * d_share, axis=0, keepdims=True)
                    d_scores = (share_of * (d_share - centre)).astype(BF16)
                    d_query = dot_tn(d_scores, keys) * SCALE
                    dq_ref[rows_of(i), lanes] = jnp.where(
                        low, d_query[:BLK], d_query[BLK:]).astype(BF16)
                    parts = (dot(d_scores, query), dot(share_of.astype(BF16), grad))
                    for n, part in enumerate(parts):
                        for slot in range(3):
                            acc[n, rows_of(at + slot), :] += part[slot * BLK:(slot + 1) * BLK]
                        acc[n, BLK:2 * BLK, :] += part[3 * BLK:4 * BLK]
                        last[n] += part[4 * BLK:5 * BLK]
                    for t in range(3):
                        one = link_ref[2 * p * picks_count + i * 3 + t]
                        two = link_ref[(2 * p + 1) * picks_count + i * 3 + t]
                        for n, part in enumerate(parts):
                            picked[n, i * 3 + t] = part[(5 + t) * BLK:(6 + t) * BLK] + jnp.where(
                                low, picked[n, one], picked[n, two])
                    return 0

                lax.fori_loop(0, own_blocks, step, 0, unroll=own_blocks)
                tails = 2 * pairs * picks_count

                def gather(owner, _):
                    for inner in range(own_blocks):
                        block = owner * own_blocks + inner
                        one = link_ref[tails + 2 * p * (last_row + 1) + block]
                        two = link_ref[tails + (2 * p + 1) * (last_row + 1) + block]
                        for n in range(2):
                            total = acc[n, rows_of(block + 1), :]
                            total = total + jnp.where(low, picked[n, one], picked[n, two])
                            total = total + last[n] * mask_ref[own_blocks * 8 + block]
                            buf[p, owner, n, inner * BLK:(inner + 1) * BLK] = total.astype(BF16)
                    return 0

                lax.fori_loop(0, 4, gather, 0)
                copy_pair(p, 0, diagonal).start()
                copy_pair(p, 1, mate).start()

                @pl.when(p > 0)
                def _():
                    sum_pair(p - 1)

                for n, events in enumerate(BETWEEN):
                    @pl.when(p == n)
                    def _():
                        if n == 0:
                            end_square(SQUARE + 3)
                        for u, stage in events:
                            finish(u, stage)

                return 0

            lax.fori_loop(0, pairs, one_pair, 0)

        tmp[...] = dot_tn(merged_ref[...], d_attn_ref[...])
        square(SQUARE + 3, tmp)
        heads()
        sum_pair(pairs - 1)

        loading["wk"].wait()
        loading["wv"].wait()
        out_far[...] = (dot_nt(dkr[...], wk[...]) + dot_nt(dvr[...], wv[...])).astype(BF16)
        far = remote(out_far, in_far, far_sems.at[0], far_sems.at[1], to_y)
        far.start()
        loading["wq"].wait()
        loading["far"].wait()

        tmp[...] = dot_tn(x_ref[...], dko[...]) + dot_tn(far_ref[...], dkr[...])
        square(SQUARE + 1, tmp)
        for u, stage in AFTER[:4]:
            finish(u, stage)
        tmp[...] = dot_tn(x_ref[...], dvo[...]) + dot_tn(far_ref[...], dvr[...])
        square(SQUARE + 2, tmp)
        end_square(SQUARE + 1)
        tmp[...] = dot_tn(x_ref[...], dq_ref[...])
        square(SQUARE, tmp)
        end_square(SQUARE + 2)
        for u, stage in AFTER[4:]:
            finish(u, stage)
        end_square(SQUARE)

        small[6:7, :] = column_sum(dq_ref[...].astype(F32))
        small[7:8, :] = column_sum(dvo[...].astype(F32)) + column_sum(dvr[...].astype(F32))

        def small_copies(stage):
            axis = ("core", "y", "x", "z")[stage]
            if axis == "z":
                return [
                    remote(small, small_z.at[step - 1], s_sends.at[2 + step], s_recvs.at[2 + step],
                           device("z", lax.rem(z + step, groups)))
                    for step in range(1, groups)
                ]
            target = {"core": to_mate, "y": to_y, "x": device("x", 1 - x)}[axis]
            return [remote(small, small_in.at[stage], s_sends.at[stage], s_recvs.at[stage], target)]

        def small_begin(stage):
            for copy in small_copies(stage):
                copy.start()

        def small_end(stage):
            for copy in small_copies(stage):
                copy.wait()
            if stage < 3:
                small[...] += small_in[stage]
                small_begin(stage + 1)
            else:
                total = small[...]
                for step in range(1, groups):
                    total = total + small_z[step - 1]
                vec_ref[...] = total

        small_begin(0)
        dx_ref[...] += (
            dot_nt(dq_ref[...], wq[...]) + dot_nt(dko[...], wk[...]) + dot_nt(dvo[...], wv[...])
        )
        for n, (u, stage) in enumerate(LAST):
            if n in (2, 5, 6, 8):
                small_end((2, 5, 6, 8).index(n))
            if n == 6:
                far.wait()
                dx_ref[...] += in_far[...].astype(F32)
            finish(u, stage)

    pl.run_scoped(
        attention, VMEM((4 * own_blocks, BLK, features), BF16),
        VMEM((4 * own_blocks, BLK, features), BF16), low_rows, low_rows, low_rows, square_low, square_low, square_low,
        VMEM((2, (4 * own_blocks + 2) * BLK, PAIR), F32), VMEM((2, BLK, PAIR), F32),
        VMEM((2, picks_count + 1, BLK, PAIR), F32), VMEM((pairs, 4, 2, rows, PAIR), BF16),
        low_rows, low_rows, low_rows, low_rows, low_rows, VMEM((4, 4, 4) + UNIT, BF16),
        VMEM((features, features), F32),
    )


SLOPE = F32


def layer_tail(
    groups, table, link, mask, biases, up_bias, lse, tokens, merged, cotangent, out_weight,
    up_weight, down_weight, query, keys, values, key_weight, value_weight, query_weight, far_tokens,
):
    rows, features = tokens.shape
    hidden = up_weight.shape[1]
    own_blocks = rows // BLK
    pairs = features // PAIR
    share = features // (8 * groups)
    wide = hidden // features
    low = VMEM((rows, features), BF16)
    line = jax.ShapeDtypeStruct((share, features), F32)
    any_space = pl.BlockSpec(memory_space=pl.ANY)
    in_smem = pl.BlockSpec(memory_space=pltpu.SMEM)
    dma = pltpu.SemaphoreType.DMA
    return pl.pallas_call(
        functools.partial(layer_kernel, rows, 128, own_blocks, groups),
        out_shape=(
            jax.ShapeDtypeStruct((rows, features), BF16),
            jax.ShapeDtypeStruct((rows, features), F32), line, line, line, line,
            jax.ShapeDtypeStruct((share, hidden), F32),
            jax.ShapeDtypeStruct((wide * share, features), F32),
            jax.ShapeDtypeStruct((16, features), F32),
        ),
        in_specs=[in_smem] * 3 + [whole_vmem()] * 3 + [any_space] * 13,
        out_specs=(whole_vmem(),) * 9,
        scratch_shapes=[
            VMEM((12, 4 * groups) + UNIT, BF16),
            VMEM((12, 4 * groups - 1) + UNIT, BF16),
            VMEM((4, 4, 4) + UNIT, BF16),
            VMEM((4, 4, 4) + UNIT, BF16),
            VMEM((4, 4) + UNIT, BF16),
            VMEM((pairs, 2, 2, rows, PAIR), BF16),
            low,
            VMEM((16, features), F32),
            VMEM((3, 16, features), F32),
            VMEM((groups - 1, 16, features), F32),
            low, low, low, low,
            dma((13,)), dma((12, groups + 1)), dma((12, groups + 1)), dma((12,)), dma((12,)),
            dma((pairs, 2)), dma((pairs, 2)), dma((groups + 2,)), dma((groups + 2,)), dma((2,)),
        ],
        compiler_params=pltpu.CompilerParams(
            collective_id=3, has_side_effects=True, vmem_limit_bytes=LIMIT
        ),
        name="layer_tail",
    )(
        table, link, mask, biases, up_bias, lse, tokens, merged, cotangent, out_weight, up_weight,
        down_weight, query, keys, values, key_weight, value_weight, query_weight, far_tokens,
    )


def layer_norm(values, gain, shift):
    center = jnp.mean(values, axis=-1, keepdims=True)
    centered = values - center
    variance = jnp.mean(centered * centered, axis=-1, keepdims=True)
    inv_root = lax.rsqrt(variance + NORM_EPS)
    normed = centered * inv_root
    return (normed * gain + shift, normed, inv_root)


def norm_back(grad_out, normed, inv_root, gain):
    d_normed = grad_out * gain
    grad_in = inv_root * (
        d_normed
        - jnp.mean(d_normed, axis=-1, keepdims=True)
        - normed * jnp.mean(d_normed * normed, axis=-1, keepdims=True)
    )
    return (grad_in, jnp.sum(grad_out * normed, axis=0), jnp.sum(grad_out, axis=0))


def on_device(
    groups,
    tokens, filled_blocks, random_blocks, query_weight, query_bias, key_weight, value_weight,
    value_bias, out_weight, out_bias, attn_gain, attn_shift, up_weight, up_bias, down_weight,
    down_bias, ffn_gain, ffn_shift, cotangent,
):
    row_count, feature_count = tokens.shape
    filled = filled_blocks[0]
    place = lax.axis_index("seq") * row_count + jnp.arange(row_count, dtype=jnp.int32)
    live_tokens = (place < filled * BLK).astype(F32)[:, None]

    table = random_blocks[0].reshape(random_blocks.shape[1], -1)
    table = jnp.pad(table, ((0, 0), (0, 128 - table.shape[1])))
    biases = jnp.stack([
        query_bias, value_bias, out_bias, attn_gain, attn_shift, down_bias, ffn_gain, ffn_shift])
    query, keys, values, far_tokens, table = gather_project(
        tokens, table, query_weight, key_weight, value_weight, biases
    )
    table = table.reshape(-1)
    mask = masks(filled, lax.axis_index("seq"), row_count // BLK)
    keys, values = (t.reshape(-1, BLK, feature_count) for t in (keys, values))
    merged, lse = attention_forward(table, filled_blocks, mask, query, keys, values)

    if groups:
        seq = lax.axis_index("seq")
        result, grad_tokens, gq, gk, gv, go, up, down, vectors = layer_tail(
            groups, table, links(table, filled, row_count // BLK), mask, biases, up_bias[None], lse,
            tokens, merged, cotangent, out_weight, up_weight, down_weight, query, keys, values,
            key_weight, value_weight, query_weight, far_tokens)
        shard = lax.axis_index("dp") * 4 + seq
        share = gq.shape[0]
        mine = lax.dynamic_slice(vectors, (0, shard * share), (8, share))
        wide = up.shape[1] // feature_count
        up_sum = lax.dynamic_slice(
            vectors[8:8 + wide].reshape(-1), (shard * wide * share,), (wide * share,))
        return (
            result, grad_tokens, gq, mine[6], gk, gv, mine[7], go, mine[5], mine[3], mine[4], up,
            up_sum, down, mine[2], mine[0], mine[1],
        )

    attn = dot(merged, out_weight) + out_bias
    first, normed_one, root_one = layer_norm(tokens.astype(F32) + attn, attn_gain, attn_shift)
    first_low = first.astype(BF16)
    hidden = dot(first_low, up_weight) + up_bias
    act, gelu_pull = jax.vjp(jax.nn.gelu, hidden)
    act_low = act.astype(BF16)
    ffn = dot(act_low, down_weight) + down_bias
    result, normed_two, root_two = layer_norm(first + ffn, ffn_gain, ffn_shift)
    grad_result = cotangent.astype(F32) * live_tokens
    d_sum_two, grad_ffn_gain, grad_ffn_shift = norm_back(
        grad_result, normed_two, root_two, ffn_gain
    )
    d_ffn = d_sum_two.astype(BF16)
    grad_down_bias = jnp.sum(d_ffn, axis=0, dtype=F32)
    grad_down_weight = dot_tn(act_low, d_ffn)
    d_act = dot_nt(d_ffn, down_weight)
    d_hidden = gelu_pull(d_act)[0].astype(BF16)
    grad_up_bias = jnp.sum(d_hidden, axis=0, dtype=F32)
    grad_up_weight = dot_tn(first_low, d_hidden)
    d_first = d_sum_two + dot_nt(d_hidden, up_weight)
    d_sum_one, grad_attn_gain, grad_attn_shift = norm_back(d_first, normed_one, root_one, attn_gain)
    d_attn = d_sum_one.astype(BF16)
    grad_out_bias = jnp.sum(d_attn, axis=0, dtype=F32)
    grad_out_weight = dot_tn(merged, d_attn)
    d_merged = dot_nt(d_attn, out_weight).astype(BF16)

    d_query, d_keys, d_values = attention_backward(
        table, filled_blocks, mask, query, keys, values, d_merged, lse
    )
    grad_tokens, dk_own, dv_own, dk_far, dv_far = exchange(
        d_keys, d_values, d_query, d_sum_one, query_weight, key_weight, value_weight
    )
    grad_query_weight = dot_tn(tokens, d_query)
    grad_query_bias = jnp.sum(d_query, axis=0, dtype=F32)
    grad_key_weight = dot_tn(tokens, dk_own) + dot_tn(far_tokens, dk_far)
    grad_value_weight = dot_tn(tokens, dv_own) + dot_tn(far_tokens, dv_far)
    grad_value_bias = jnp.sum(dv_own, axis=0, dtype=F32) + jnp.sum(dv_far, axis=0, dtype=F32)

    square = (grad_query_weight, grad_key_weight, grad_value_weight, grad_out_weight)
    vectors = (
        grad_query_bias, grad_value_bias, grad_out_bias, grad_attn_gain, grad_attn_shift,
        grad_down_bias, grad_ffn_gain, grad_ffn_shift,
    )
    square, up, down, vectors, up_sum = summed_anywhere(
        square, grad_up_weight, grad_down_weight, vectors, grad_up_bias)
    return (
        result.astype(BF16), grad_tokens, square[0], vectors[0], square[1], square[2], vectors[1],
        square[3], vectors[2], vectors[3], vectors[4], up, up_sum, down, vectors[5], vectors[6],
        vectors[7],
    )


def solution(mesh):
    both = P(("dp", "seq"), None)
    line = P(("dp", "seq"))
    placed = (both, P("dp"), P("dp", None, "seq", None)) + (P(),) * 15 + (both,)
    groups = 4 if mesh.shape["dp"] == 8 and mesh.shape["seq"] == 4 else 0
    return jax.shard_map(
        functools.partial(on_device, groups),
        mesh=mesh,
        in_specs=placed,
        out_specs=(
            both, both, both, line, both, both, line, both, line, line, line, both, line, both,
            line, line, line,
        ),
        check_vma=False,
    )
```

```python
import functools

import jax
import jax.numpy as jnp
from jax import lax
from jax.experimental import pallas as pl
from jax.experimental.pallas import tpu as pltpu
from jax.sharding import PartitionSpec as P

HEAD_DIM = 64
BLK = 64
PAIR = 2 * HEAD_DIM
TABLE = 8
NORM_EPS = 1e-05
MASKED = -1e30
SCALE = HEAD_DIM ** (-0.5)
MESH = pl.DeviceIdType.MESH
BF16 = jnp.bfloat16
F32 = jnp.float32
VMEM = pltpu.VMEM
LIMIT = 63 << 20


def whole_vmem():
    return pl.BlockSpec(memory_space=pltpu.VMEM)


def dot(left, right):
    return jnp.dot(left, right, preferred_element_type=F32)


def dot_nt(left, right):
    return lax.dot_general(left, right, (((1,), (1,)), ((), ())), preferred_element_type=F32)


def dot_tn(left, right):
    return lax.dot_general(left, right, (((0,), (0,)), ((), ())), preferred_element_type=F32)


def tables_of(tab_out, filled, first_block, each, prev_out, tail_out, mask_out):
    groups, blocks, width = tab_out.shape
    slot_blocks = tail_out.shape[1]
    none = blocks * each
    lane = lax.broadcasted_iota(jnp.int32, (blocks, width), 1)
    row = lax.broadcasted_iota(jnp.int32, (blocks, width), 0)
    pick = lax.rem(lane, each)
    key_row = lax.broadcasted_iota(jnp.int32, (slot_blocks, width), 0)
    key_pick = lax.rem(lax.broadcasted_iota(jnp.int32, (slot_blocks, width), 1), each)
    for g in range(groups):
        table = tab_out[g]
        prev = jnp.full((blocks, width), -1, jnp.int32)
        for shift in range(1 - each, each):
            moved = pltpu.roll(table, (-shift) % width, axis=1)
            inside = (pick + shift >= 0) & (pick + shift < each)
            for i in range(blocks - 1):
                same = (moved[i:i + 1] == table) & (row > i) & inside
                prev = jnp.maximum(prev, jnp.where(same, i * each + pick + shift, -1))
        prev = jnp.where(prev < 0, none, prev)
        prev_out[g] = jnp.where(lane == width - 1, filled - 1, prev)
        tail = jnp.full((slot_blocks, width), -1, jnp.int32)
        for i in range(blocks):
            tail = jnp.maximum(tail, jnp.where(table[i:i + 1] == key_row, i * each + key_pick, -1))
        best = tail
        for shift in range(1, each):
            best = jnp.maximum(best, pltpu.roll(tail, width - shift, axis=1))
        tail_out[g] = jnp.where(best < 0, none, best)
    at = first_block + row
    window = at + lane - 1
    ok = jnp.where(
        lane < 3, ((window >= 0) & (window < filled)).astype(jnp.int32),
        jnp.where(lane == 3, (at >= 2).astype(jnp.int32),
                  (jnp.abs(at - (filled - 1)) > 1).astype(jnp.int32)))
    mask_out[0:blocks, :] = jnp.where(ok == 1, 0.0, MASKED)
    mask_out[blocks:2 * blocks, :] = (lane == filled - 1).astype(F32)


def gather_kernel(
    rows, width, filled_ref, x_ref, picks_ref, wq_ref, wk_ref, wv_ref, qb_ref, vb_ref,
    q_ref, k_ref, v_ref, far_ref, tab_out, prev_out, tail_out, mask_out,
    tab_ref, land, tab_land, sends, recvs, tab_sends, tab_recvs,
):
    parts = 4
    part = rows // parts
    dp, me = lax.axis_index("dp"), lax.axis_index("seq")
    mate, across, diagonal = (lax.bitwise_xor(me, bit) for bit in (1, 2, 3))
    barrier = pltpu.get_barrier_semaphore()
    for other in (mate, across, diagonal):
        pl.semaphore_signal(barrier, inc=1, device_id=(dp, other), device_id_type=MESH)
    chosen = picks_ref[...]
    heads_here, each = chosen.shape[1:]
    tab_ref[...] = jnp.concatenate(
        [chosen[:, h, :] for h in range(heads_here)]
        + [jnp.zeros((chosen.shape[0], 128 - heads_here * each), jnp.int32)], axis=1)
    pl.semaphore_wait(barrier, 3)

    def send(src, dst, slot, target):
        copy = pltpu.make_async_remote_copy(
            src_ref=src, dst_ref=dst, send_sem=sends.at[slot], recv_sem=recvs.at[slot],
            device_id=(dp, target), device_id_type=MESH,
        )
        copy.start()
        return copy

    tables = []
    own_blocks = tab_ref.shape[0] // 4
    for slot, other in enumerate((mate, across, diagonal)):
        copy = pltpu.make_async_remote_copy(
            src_ref=tab_ref.at[pl.ds(pl.multiple_of(other * own_blocks, 8), own_blocks)],
            dst_ref=tab_land.at[slot], send_sem=tab_sends.at[slot], recv_sem=tab_recvs.at[slot],
            device_id=(dp, other), device_id_type=MESH,
        )
        copy.start()
        tables.append(copy)
    far = [
        send(x_ref.at[pl.ds(r * part, part)], land.at[0, pl.ds(r * part, part)], r, across)
        for r in range(parts)
    ]
    near = send(x_ref, land.at[1], parts, mate)

    def keys_values(x, at):
        k_ref[pl.ds(at, width), :] = dot(x, wk_ref[...]).astype(BF16)
        v_ref[pl.ds(at, width), :] = (dot(x, wv_ref[...]) + vb_ref[...][None]).astype(BF16)

    def own(r, _):
        at = pl.multiple_of(r * width, width)
        x = x_ref[pl.ds(at, width), :]
        q_ref[pl.ds(at, width), :] = (
            (dot(x, wq_ref[...]) + qb_ref[...][None]).astype(BF16) * jnp.asarray(SCALE, BF16)
        )
        keys_values(x, pl.multiple_of(me * rows + at, width))
        return 0

    lax.fori_loop(0, rows // width, own, 0)

    def block(slot, owner, start, count):
        def step(r, _):
            at = pl.multiple_of(start + r * width, width)
            keys_values(land[slot, pl.ds(at, width), :], pl.multiple_of(owner * rows + at, width))
            return 0

        lax.fori_loop(0, count // width, step, 0)

    near.wait()
    block(1, mate, 0, rows)
    for copy in tables:
        copy.wait()
    tab_out[pl.ds(me, 1)] = tab_ref[pl.ds(pl.multiple_of(me * own_blocks, 8), own_blocks)][None]
    for slot, other in enumerate((mate, across, diagonal)):
        tab_out[pl.ds(other, 1)] = tab_land[slot][None]
    tables_of(tab_out, filled_ref[0], me * own_blocks, each, prev_out, tail_out, mask_out)
    relayed = []
    for r in range(parts):
        far[r].wait()
        piece = pl.ds(r * part, part)
        relayed.append(send(land.at[0, piece], land.at[2, piece], parts + 1 + r, mate))
        block(0, across, r * part, part)
        if r:
            relayed[r - 1].wait()
            block(2, diagonal, (r - 1) * part, part)
    far_ref[...] = land[0]
    relayed[-1].wait()
    block(2, diagonal, (parts - 1) * part, part)


def gather_project(
    filled, tokens, chosen, query_weight, key_weight, value_weight, query_bias, value_bias,
):
    rows, features = tokens.shape
    own_blocks = rows // BLK
    slot_blocks = chosen.shape[0]
    copies = 4 + 1 + 4
    return pl.pallas_call(
        functools.partial(gather_kernel, rows, 128),
        out_shape=(
            jax.ShapeDtypeStruct((rows, features), BF16),
            jax.ShapeDtypeStruct((4 * rows, features), BF16),
            jax.ShapeDtypeStruct((4 * rows, features), BF16),
            jax.ShapeDtypeStruct((rows, features), BF16),
            jax.ShapeDtypeStruct((4, own_blocks, 128), jnp.int32),
            jax.ShapeDtypeStruct((4, own_blocks, 128), jnp.int32),
            jax.ShapeDtypeStruct((4, slot_blocks, 128), jnp.int32),
            jax.ShapeDtypeStruct((2 * own_blocks, 128), F32),
        ),
        in_specs=[pl.BlockSpec(memory_space=pltpu.SMEM)] + [whole_vmem()] * 7,
        out_specs=(whole_vmem(),) * 8,
        scratch_shapes=[
            VMEM((slot_blocks, 128), jnp.int32),
            VMEM((3, rows, features), BF16),
            VMEM((3, own_blocks, 128), jnp.int32),
            pltpu.SemaphoreType.DMA((copies,)),
            pltpu.SemaphoreType.DMA((copies,)),
            pltpu.SemaphoreType.DMA((3,)),
            pltpu.SemaphoreType.DMA((3,)),
        ],
        compiler_params=pltpu.CompilerParams(
            collective_id=0, has_side_effects=True, vmem_limit_bytes=LIMIT
        ),
        name="gather_project",
    )(filled, tokens, chosen, query_weight, key_weight, value_weight, query_bias, value_bias)


def key_blocks(tab_ref, end, pair, i, at, last_row):
    def chosen(head, t):
        group, inner = lax.div(head, 3), lax.rem(head, 3)
        return tab_ref[group, i, inner * 3 + t]

    head = 2 * pair
    both = [(chosen(head, t), chosen(head + 1, t)) for t in range(3)]
    shared = [
        jnp.maximum(at - 1, 0), at, jnp.minimum(at + 1, last_row), jnp.int32(0), end,
    ]
    return shared, both


def rows_of(block):
    return pl.ds(pl.multiple_of(block * BLK, BLK), BLK)


def lanes_low(rows):
    return lax.broadcasted_iota(jnp.int32, (rows, PAIR), 1) < HEAD_DIM


def split_pair(x, low):
    zero = jnp.zeros_like(x)
    return jnp.concatenate([jnp.where(low, x, zero), jnp.where(low, zero, x)], axis=0)


def gathered(ref, shared, both, low, lanes=slice(None)):
    tiles = [ref[b, :, lanes] for b in shared]
    for first, second in both:
        tiles.append(jnp.where(low, ref[first, :, lanes], ref[second, :, lanes]))
    return jnp.concatenate(tiles, axis=0)


def masked_scores(scores, mask_ref, i):
    parts = [scores[n * BLK:(n + 1) * BLK] + mask_ref[i, n] for n in range(5)]
    return jnp.concatenate(parts + [scores[5 * BLK:]], axis=0)


def forward_kernel(own_blocks, tab_ref, filled_ref, mask_ref, q_ref, k_ref, v_ref, out_ref, lse_ref):
    pair = pl.program_id(0)
    filled = filled_ref[0]
    first_block = lax.axis_index("seq") * own_blocks
    last_row = k_ref.shape[0] - 1
    low = lanes_low(BLK)

    def step(i, _):
        at = first_block + i
        shared, both = key_blocks(tab_ref, filled - 1, pair, i, at, last_row)
        keys = gathered(k_ref, shared, both, low)
        values = gathered(v_ref, shared, both, low)
        query = split_pair(q_ref[rows_of(i), :], low)
        scores = masked_scores(dot_nt(keys, query), mask_ref, i)
        highest = jnp.max(scores, axis=0, keepdims=True)
        weights = jnp.exp(scores - highest)
        total = jnp.sum(weights, axis=0, keepdims=True)
        share = (weights * (1.0 / total)).astype(BF16)
        output = dot_tn(share, values)
        merged = jnp.where(low, output[:BLK], output[BLK:])
        merged = jnp.where(at < filled, merged, 0.0)
        out_ref[rows_of(i), :] = merged.astype(BF16)
        lse_ref[0, pl.ds(i, 1), :] = highest + jnp.log(total)
        return 0

    lax.fori_loop(0, own_blocks, step, 0, unroll=own_blocks)


def attention_forward(table, filled, mask, query, keys, values):
    rows, features = query.shape
    own_blocks = rows // BLK
    slot_blocks = keys.shape[0]
    pairs = features // PAIR
    column = lambda n: pl.BlockSpec((n, PAIR), lambda p, *_: (0, p))
    blocks = lambda n: pl.BlockSpec((n, BLK, PAIR), lambda p, *_: (0, 0, p))
    return pl.pallas_call(
        functools.partial(forward_kernel, own_blocks),
        out_shape=(
            jax.ShapeDtypeStruct((rows, features), BF16),
            jax.ShapeDtypeStruct((pairs, own_blocks, PAIR), F32),
        ),
        grid_spec=pltpu.PrefetchScalarGridSpec(
            num_scalar_prefetch=3,
            grid=(pairs,),
            in_specs=[column(rows), blocks(slot_blocks), blocks(slot_blocks)],
            out_specs=(column(rows), pl.BlockSpec((1, own_blocks, PAIR), lambda p, *_: (p, 0, 0))),
        ),
        compiler_params=pltpu.CompilerParams(vmem_limit_bytes=LIMIT),
        name="attention_forward",
    )(table, filled, mask, query, keys, values)


def backward_kernel(
    own_blocks, tab_ref, filled_ref, mask_ref, q_ref, k_ref, v_ref, g_ref, lse_ref,
    dq_ref, dk_ref, dv_ref, dk_sum, dv_sum,
):
    pair = pl.program_id(0)
    filled = filled_ref[0]
    first_block = lax.axis_index("seq") * own_blocks
    last_row = k_ref.shape[0] - 1
    low = lanes_low(BLK)
    dk_sum[...] = jnp.zeros_like(dk_sum)
    dv_sum[...] = jnp.zeros_like(dv_sum)

    def step(i, _):
        at = first_block + i
        shared, both = key_blocks(tab_ref, filled - 1, pair, i, at, last_row)
        keys = gathered(k_ref, shared, both, low)
        values = gathered(v_ref, shared, both, low)
        query = split_pair(q_ref[rows_of(i), :], low)
        grad = split_pair(jnp.where(at < filled, g_ref[rows_of(i), :], jnp.zeros((), BF16)), low)
        scores = masked_scores(dot_nt(keys, query), mask_ref, i)
        share = jnp.exp(scores - lse_ref[0, pl.ds(i, 1), :])
        d_share = dot_nt(values, grad)
        centre = jnp.sum(share * d_share, axis=0, keepdims=True)
        d_scores = (share * (d_share - centre)).astype(BF16)
        d_query = dot_tn(d_scores, keys) * SCALE
        dq_ref[rows_of(i), :] = jnp.where(low, d_query[:BLK], d_query[BLK:]).astype(BF16)
        for total, part in ((dk_sum, dot(d_scores, query)), (dv_sum, dot(share.astype(BF16), grad))):
            for slot, block in enumerate(shared):
                total[rows_of(block), :] += part[slot * BLK:(slot + 1) * BLK]
            for t, (one, two) in enumerate(both):
                tile = part[(5 + t) * BLK:(6 + t) * BLK]
                total[rows_of(one), :] += jnp.where(low, tile, 0.0)
                total[rows_of(two), :] += jnp.where(low, 0.0, tile)
        return 0

    lax.fori_loop(0, own_blocks, step, 0, unroll=own_blocks)
    dk_ref[...] = dk_sum[...].astype(BF16)
    dv_ref[...] = dv_sum[...].astype(BF16)


def attention_backward(table, filled, mask, query, keys, values, grad, lse):
    rows, features = query.shape
    slot_blocks = keys.shape[0]
    slot_rows = slot_blocks * BLK
    own_blocks = rows // BLK
    pairs = features // PAIR
    blocks = lambda n: pl.BlockSpec((n, BLK, PAIR), lambda p, *_: (0, 0, p))
    column = lambda n: pl.BlockSpec((n, PAIR), lambda p, *_: (0, p))
    return pl.pallas_call(
        functools.partial(backward_kernel, own_blocks),
        out_shape=(
            jax.ShapeDtypeStruct((rows, features), BF16),
            jax.ShapeDtypeStruct((slot_rows, features), BF16),
            jax.ShapeDtypeStruct((slot_rows, features), BF16),
        ),
        grid_spec=pltpu.PrefetchScalarGridSpec(
            num_scalar_prefetch=3,
            grid=(pairs,),
            in_specs=[
                column(rows), blocks(slot_blocks), blocks(slot_blocks), column(rows),
                pl.BlockSpec((1, own_blocks, PAIR), lambda p, *_: (p, 0, 0)),
            ],
            out_specs=(column(rows), column(slot_rows), column(slot_rows)),
            scratch_shapes=[VMEM((slot_rows, PAIR), F32), VMEM((slot_rows, PAIR), F32)],
        ),
        compiler_params=pltpu.CompilerParams(vmem_limit_bytes=LIMIT),
        name="attention_backward",
    )(table, filled, mask, query, keys, values, grad, lse)


def exchange_kernel(
    rows, width, dk_ref, dv_ref, dq_ref, base_ref, wq_ref, wk_ref, wv_ref,
    dx_ref, dko_ref, dvo_ref, dkr_ref, dvr_ref,
    land, out_far, in_far, sends, recvs,
):
    dp, me = lax.axis_index("dp"), lax.axis_index("seq")
    mate, across, diagonal = (lax.bitwise_xor(me, bit) for bit in (1, 2, 3))
    barrier = pltpu.get_barrier_semaphore()
    for other in (mate, across):
        pl.semaphore_signal(barrier, inc=1, device_id=(dp, other), device_id_type=MESH)
    pl.semaphore_wait(barrier, 2)

    def send(src, dst, slot, target):
        copy = pltpu.make_async_remote_copy(
            src_ref=src, dst_ref=dst, send_sem=sends.at[slot], recv_sem=recvs.at[slot],
            device_id=(dp, target), device_id_type=MESH,
        )
        copy.start()
        return copy

    def owned(index):
        return pl.ds(pl.multiple_of(index * rows, rows), rows)

    copies = [
        send(ref.at[owned(owner)], land.at[slot], slot, mate)
        for slot, (ref, owner) in enumerate(
            ((dk_ref, diagonal), (dv_ref, diagonal), (dk_ref, mate), (dv_ref, mate))
        )
    ]

    def summed(ref, owner, slot, to_ref):
        to_ref[...] = (ref[owned(owner), :].astype(F32) + land[slot].astype(F32)).astype(BF16)

    copies[0].wait()
    summed(dk_ref, across, 0, dkr_ref)
    copies[1].wait()
    summed(dv_ref, across, 1, dvr_ref)

    steps = rows // width
    for r in range(steps):
        at = pl.ds(r * width, width)
        out_far[at, :] = (
            dot_nt(dkr_ref[at, :], wk_ref[...]) + dot_nt(dvr_ref[at, :], wv_ref[...])
        ).astype(BF16)
    far = send(out_far, in_far, 4, across)
    copies[2].wait()
    summed(dk_ref, me, 2, dko_ref)
    copies[3].wait()
    summed(dv_ref, me, 3, dvo_ref)

    def one(r, _):
        at = pl.ds(pl.multiple_of(r * width, width), width)
        dx_ref[at, :] = (
            base_ref[at, :]
            + dot_nt(dq_ref[at, :], wq_ref[...])
            + dot_nt(dko_ref[at, :], wk_ref[...])
            + dot_nt(dvo_ref[at, :], wv_ref[...])
        )
        return 0

    lax.fori_loop(0, steps, one, 0)
    far.wait()
    dx_ref[...] += in_far[...].astype(F32)


def exchange(d_keys, d_values, d_query, base, query_weight, key_weight, value_weight):
    rows, features = d_query.shape
    small = jax.ShapeDtypeStruct((rows, features), BF16)
    return pl.pallas_call(
        functools.partial(exchange_kernel, rows, 128),
        out_shape=(jax.ShapeDtypeStruct((rows, features), F32), small, small, small, small),
        in_specs=[whole_vmem()] * 7,
        out_specs=(whole_vmem(),) * 5,
        scratch_shapes=[
            VMEM((4, rows, features), BF16),
            VMEM((rows, features), BF16),
            VMEM((rows, features), BF16),
            pltpu.SemaphoreType.DMA((5,)),
            pltpu.SemaphoreType.DMA((5,)),
        ],
        compiler_params=pltpu.CompilerParams(
            collective_id=1, has_side_effects=True, vmem_limit_bytes=LIMIT
        ),
        name="exchange",
    )(d_keys, d_values, d_query, base, query_weight, key_weight, value_weight)


def summed_anywhere(square, up, down, vectors, up_bias):
    def one(g):
        return lax.psum_scatter(g, ("dp", "seq"), scatter_dimension=0, tiled=True)

    return [one(g) for g in square], one(up), one(down), [one(v) for v in vectors], one(up_bias)


GELU_A = 0.044715
GELU_C = 0.7978845608028654
UNIT = (48, 384)
KINDS = "ABACABBCBABB"
AXES = {"A": "yxz", "B": "xyz", "C": "zxy"}
DOWN, UP, SQUARE = 0, 4, 8
BETWEEN = (
    (),
    ((0, 0), (2, 0)),
    ((3, 0), (1, 1)),
    ((5, 0), (6, 0), (4, 0)),
    ((7, 0), (11, 0), (0, 1), (2, 1)),
    ((3, 1), (1, 2)),
)
AFTER = ((5, 1), (6, 1), (4, 1), (7, 1), (11, 1), (0, 2), (2, 2), (3, 2))
LAST = (
    (5, 2), (6, 2), (4, 2), (7, 2), (11, 2), (9, 0), (10, 0), (8, 0), (9, 1), (10, 1), (8, 1),
    (9, 2), (10, 2), (8, 2),
)


def normed_rows(values):
    center = jnp.mean(values, axis=-1, keepdims=True)
    centered = values - center
    variance = jnp.mean(centered * centered, axis=-1, keepdims=True)
    inv_root = lax.rsqrt(variance + NORM_EPS)
    return centered * inv_root, inv_root


def norm_pull(grad_out, normed, inv_root, gain):
    d_normed = grad_out * gain
    return inv_root * (
        d_normed
        - jnp.mean(d_normed, axis=-1, keepdims=True)
        - normed * jnp.mean(d_normed * normed, axis=-1, keepdims=True)
    )


def column_sum(values):
    return jnp.sum(values, axis=0, keepdims=True)


def layer_kernel(
    rows, tile, own_blocks, groups, tab_ref, prev_ref, tail_ref, mask_ref, bo_ref, g1_ref, s1_ref,
    bd_ref, g2_ref, s2_ref, bu_ref, lse_ref,
    x_any, merged_any, cot_any, wo_any, wu_any, wd_any, q_any, k_any, v_any, wk_any, wv_any, wq_any,
    far_any,
    result_ref, dx_ref, gq_ref, gk_ref, gv_ref, go_ref, up_ref, down_ref, vec_ref,
    work, land, core_down, core_up, core_out, pair_in, in_far, small, small_in, small_z,
    x_ref, merged_ref, d_attn_ref, d_merged_ref,
    loads, sends, recvs, c_sends, c_recvs, p_sends, p_recvs, s_sends, s_recvs, far_sems,
):
    features = x_ref.shape[1]
    hidden = bu_ref.shape[1]
    wide = hidden // features
    pairs = features // PAIR
    picks_count = own_blocks * 3
    share = features // (8 * groups)
    shards = 4 * groups
    half = features // 2
    dp, seq = lax.axis_index("dp"), lax.axis_index("seq")
    x, z = lax.rem(dp, 2), dp // 2
    core, y = lax.rem(seq, 2), seq // 2
    mate, across, diagonal = (lax.bitwise_xor(seq, bit) for bit in (1, 2, 3))
    end = prev_ref[0, 0, 127]
    first_block = seq * own_blocks
    low = lanes_low(BLK)
    to_mate, to_y = (dp, mate), (dp, across)
    place_of = {"x": (x, 2), "y": (y, 2), "z": (z, groups)}

    def device(axis, index):
        if axis == "x":
            return (2 * z + index, seq)
        if axis == "y":
            return (dp, 2 * index + core)
        return (2 * index + x, seq)

    neighbours = [to_mate, to_y, device("x", 1 - x)] + [
        device("z", lax.rem(z + step, groups)) for step in range(1, groups)]

    loading = {}

    def load(name, src, dst):
        copy = pltpu.make_async_copy(src, dst, loads.at[len(loading)])
        copy.start()
        loading[name] = copy

    def remote(src, dst, one, two, target):
        return pltpu.make_async_remote_copy(
            src_ref=src, dst_ref=dst, send_sem=one, recv_sem=two, device_id=target,
            device_id_type=MESH,
        )

    def lanes_of(p):
        return pl.ds(pl.multiple_of(p * PAIR, PAIR), PAIR)

    def columns(j):
        return pl.ds(pl.multiple_of(j * features, features), features)

    def tiles(body):
        def step(r, _):
            body(pl.ds(pl.multiple_of(r * tile, tile), tile), r)
            return 0

        lax.fori_loop(0, rows // tile, step, 0)


    def index_of(u, at_x, at_y, at_z):
        at = {"x": at_x, "y": at_y, "z": at_z}
        flat = 0
        for axis in AXES[KINDS[u]]:
            flat = flat * place_of[axis][1] + at[axis]
        return flat

    def shard_of(s):
        return s // 4, lax.rem(s // 2, 2), lax.rem(s, 2)

    def stage_of(u, stage):
        sizes = [place_of[axis][1] for axis in AXES[KINDS[u]]] + [1]
        base, offset, sem, block = 0, 0, 0, shards
        for n, axis in enumerate(AXES[KINDS[u]]):
            block = block // sizes[n]
            if n == stage:
                return axis, place_of[axis][0], sizes[n], block, base, offset, sem
            base = base + place_of[axis][0] * block
            offset += (sizes[n] - 1) * block
            sem += sizes[n] - 1
        return None

    def stage_copies(u, stage):
        axis, mine, size, block, base, offset, sem = stage_of(u, stage)
        copies = []
        for step in range(1, size):
            index = lax.rem(mine + step, size)
            copies.append(remote(
                work.at[u, pl.ds(base + index * block, block)],
                land.at[u, pl.ds(offset + (step - 1) * block, block)],
                sends.at[u, sem + step - 1], recvs.at[u, sem + step - 1], device(axis, index)))
        return copies

    def begin(u, stage):
        for copy in stage_copies(u, stage):
            copy.start()

    def finish(u, stage):
        _, mine, size, block, base, offset, _ = stage_of(u, stage)
        for copy in stage_copies(u, stage):
            copy.wait()

        def total(r):
            value = work[u, base + mine * block + r].astype(F32)
            for step in range(size - 1):
                value = value + land[u, offset + step * block + r].astype(F32)
            return value

        if stage < 2:
            def body(r, _):
                work[u, base + mine * block + r] = total(r).astype(BF16)
                return 0

            lax.fori_loop(0, block, body, 0)
            begin(u, stage + 1)
            return
        value = total(0)
        if u < UP:
            down_ref[(u // 2) * UNIT[0]:(u // 2 + 1) * UNIT[0], (u % 2) * half:(u % 2 + 1) * half] = value
        else:
            to = up_ref if u < SQUARE else (gq_ref, gk_ref, gv_ref, go_ref)[u - SQUARE]
            at = (u - UP) * features if u < SQUARE else 0
            to[:, at:at + half] = value[:share]
            to[:, at + half:at + features] = value[share:]

    def folded(source, at, count):
        return jnp.concatenate(
            [source[pl.ds(at, count), 0:half], source[pl.ds(at, count), half:features]], axis=0)

    def square_pieces(u, source, other):
        def body(s, _):
            at_z, at_x, at_y = shard_of(s)
            index = index_of(u, at_x, at_y, at_z)
            for own in (True, False):
                row = 2 * s + (core if own else 1 - core)
                value = folded(source, pl.multiple_of(row * share, 8), share).astype(BF16)
                if own:
                    work[u, index] = value
                else:
                    other[index // 4, lax.rem(index, 4)] = value
            return 0

        lax.fori_loop(0, shards, body, 0)

    def add_core(u, landed):
        def body(n, _):
            work[u, n] = (
                work[u, n].astype(F32) + landed[n // 4, lax.rem(n, 4)].astype(F32)
            ).astype(BF16)
            return 0

        lax.fori_loop(0, shards, body, 0)

    def core_copy(src, dst, slot):
        return remote(src, dst, c_sends.at[slot], c_recvs.at[slot], to_mate)

    load("x", x_any, x_ref)
    load("merged", merged_any, merged_ref)


    def dense(
        wo, wu, wd, cot_ref, normed_one, root_one, first_low, act, slope, ffn, d_ffn, tmp,
        other_down, other_up,
    ):
        load("wo", wo_any, wo)
        load("wu", wu_any, wu)
        load("wd", wd_any, wd)
        load("cot", cot_any, cot_ref)
        barrier = pltpu.get_barrier_semaphore()
        for target in neighbours:
            pl.semaphore_signal(barrier, inc=1, device_id=target, device_id_type=MESH)
        pl.semaphore_wait(barrier, len(neighbours))
        bo, g1, s1, bd, g2, s2 = (
            ref[...][None] for ref in (bo_ref, g1_ref, s1_ref, bd_ref, g2_ref, s2_ref))

        for name in ("x", "merged", "wo"):
            loading[name].wait()
        ffn[...] = dot(merged_ref[...], wo[...])

        def norm_one(at, r):
            normed, inv_root = normed_rows(x_ref[at, :].astype(F32) + (ffn[at, :] + bo))
            normed_one[at, :] = normed
            root_one[at, :] = inv_root
            first_low[at, :] = (normed * g1 + s1).astype(BF16)

        tiles(norm_one)

        loading["wu"].wait()
        loading["wd"].wait()
        ffn[...] = jnp.zeros_like(ffn)

        def forward(j, _):
            at = columns(j)
            u = dot(first_low[...], wu[:, at]) + bu_ref[:, at]
            square = u * u
            t = jnp.tanh(GELU_C * (u + GELU_A * (square * u)))
            upper = 0.5 * (1.0 + t)
            act[j] = (u * upper).astype(BF16)
            slope[j] = (
                upper + (0.5 * GELU_C) * u * (1.0 - t * t) * (1.0 + (3.0 * GELU_A) * square)
            ).astype(slope.dtype)
            ffn[...] += dot(act[j], wd[at, :])
            return 0

        lax.fori_loop(0, wide, forward, 0)

        small[...] = jnp.zeros_like(small)
        limit = (end + 1) * BLK - seq * rows
        loading["cot"].wait()

        def norm_two(at, r):
            first = normed_one[at, :] * g1 + s1
            normed, inv_root = normed_rows(first + (ffn[at, :] + bd))
            result_ref[at, :] = (normed * g2 + s2).astype(BF16)
            place = lax.broadcasted_iota(jnp.int32, (tile, 1), 0) + r * tile
            grad = cot_ref[at, :].astype(F32) * (place < limit).astype(F32)
            pulled = norm_pull(grad, normed, inv_root, g2)
            rounded = pulled.astype(BF16)
            ffn[at, :] = pulled
            d_ffn[at, :] = rounded
            small[0:1, :] += column_sum(grad * normed)
            small[1:2, :] += column_sum(grad)
            small[2:3, :] += column_sum(rounded.astype(F32))

        tiles(norm_two)

        down_copies = []
        for j in range(wide):
            tmp[...] = dot_tn(act[j], d_ffn[...])

            def pieces(n, _):
                at_x, at_y = n // 2, lax.rem(n, 2)
                for own in (True, False):
                    row = 2 * n + (core if own else 1 - core)
                    at = pl.multiple_of(row * (wide * share), 8)
                    for u in range(4):
                        value = tmp[
                            pl.ds(pl.multiple_of(at + (u // 2) * UNIT[0], 8), UNIT[0]),
                            (u % 2) * half:(u % 2 + 1) * half].astype(BF16)
                        if own:
                            work[u, index_of(u, at_x, at_y, j)] = value
                        else:
                            other_down[j, u, n] = value
                return 0

            lax.fori_loop(0, 4, pieces, 0)
            down_copies.append(core_copy(other_down.at[j], core_down.at[j], j))
            down_copies[-1].start()

        def backward(j, _):
            d_hidden = (dot_nt(d_ffn[...], wd[columns(j), :]) * slope[j].astype(F32)).astype(BF16)
            act[j] = d_hidden
            for n in range(wide):
                @pl.when(j == n)
                def _():
                    small[8 + n:9 + n, :] = column_sum(d_hidden.astype(F32))
            return 0

        lax.fori_loop(0, wide, backward, 0)

        for copy in down_copies:
            copy.wait()

        def sum_down(s, _):
            at_z, at_x, at_y = shard_of(s)
            for u in range(4):
                index = index_of(u, at_x, at_y, at_z)
                work[u, index] = (
                    work[u, index].astype(F32) + core_down[at_z, u, at_x * 2 + at_y].astype(F32)
                ).astype(BF16)
            return 0

        lax.fori_loop(0, shards, sum_down, 0)
        for u in range(4):
            begin(u, 0)

        up_copies = []
        for j in range(wide):
            tmp[...] = dot_tn(first_low[...], act[j])
            square_pieces(UP + j, tmp, other_up.at[j])
            up_copies.append(core_copy(other_up.at[j], core_up.at[j], wide + j))
            up_copies[-1].start()

        for j in range(wide):
            ffn[...] += dot_nt(act[j], wu[:, j * features:(j + 1) * features])
        for j in range(wide):
            up_copies[j].wait()
            add_core(UP + j, core_up.at[j])
            begin(UP + j, 0)
        finish(1, 0)

        def pull_one(at, r):
            grad = ffn[at, :]
            normed = normed_one[at, :]
            pulled = norm_pull(grad, normed, root_one[at, :], g1)
            rounded = pulled.astype(BF16)
            dx_ref[at, :] = pulled
            d_attn_ref[at, :] = rounded
            small[3:4, :] += column_sum(grad * normed)
            small[4:5, :] += column_sum(grad)
            small[5:6, :] += column_sum(rounded.astype(F32))

        tiles(pull_one)
        live = lax.broadcasted_iota(jnp.int32, (rows, 1), 0) < limit
        d_merged_ref[...] = jnp.where(live, dot_nt(d_attn_ref[...], wo[...]), 0.0).astype(BF16)

    low_rows = VMEM((rows, features), BF16)
    full_rows = VMEM((rows, features), F32)
    square_low = VMEM((features, features), BF16)
    pl.run_scoped(
        dense, square_low, VMEM((features, hidden), BF16), VMEM((hidden, features), BF16),
        low_rows, full_rows, VMEM((rows, 1), F32), low_rows, VMEM((wide, rows, features), BF16),
        VMEM((wide, rows, features), SLOPE), full_rows, low_rows, VMEM((features, features), F32),
        VMEM((4, 4, 4) + UNIT, BF16), VMEM((4, 4, 4) + UNIT, BF16),
    )


    def attention(
        k_ref, v_ref, q_ref, dq_ref, far_ref, wk, wv, wq, acc, last, picked, buf, dko, dvo, dkr,
        dvr, out_far, other, tmp,
    ):
        for name, src, dst in (
            ("q", q_any, q_ref), ("k", k_any, k_ref), ("v", v_any, v_ref), ("wk", wk_any, wk),
            ("wv", wv_any, wv), ("wq", wq_any, wq), ("far", far_any, far_ref),
        ):
            load(name, src, dst)
        square_copies = {
            u: core_copy(other.at[u - SQUARE],
                         core_out if u == SQUARE + 3 else core_down.at[u - SQUARE], u)
            for u in range(SQUARE, SQUARE + 4)
        }

        def square(u, source):
            square_pieces(u, source, other.at[u - SQUARE])
            square_copies[u].start()

        def end_square(u):
            square_copies[u].wait()
            add_core(u, core_out if u == SQUARE + 3 else core_down.at[u - SQUARE])
            begin(u, 0)

        def copy_pair(p, slot, owner):
            return remote(buf.at[p, owner], pair_in.at[p, slot], p_sends.at[p, slot],
                          p_recvs.at[p, slot], to_mate)

        def sum_pair(p):
            lanes = lanes_of(p)
            for slot, owner, keys_to, values_to in ((0, across, dkr, dvr), (1, seq, dko, dvo)):
                copy_pair(p, slot, diagonal if slot == 0 else mate).wait()
                for n, to in ((0, keys_to), (1, values_to)):
                    to[:, lanes] = (
                        buf[p, owner, n].astype(F32) + pair_in[p, slot, n].astype(F32)
                    ).astype(BF16)

        def heads():
            for n in range(2):
                picked[n, picks_count] = jnp.zeros((BLK, PAIR), F32)
            last_row = k_ref.shape[0] - 1
            for name in ("q", "k", "v"):
                loading[name].wait()

            def one_pair(p, _):
                lanes = lanes_of(p)
                acc[...] = jnp.zeros_like(acc)
                last[...] = jnp.zeros_like(last)

                def step(i, _):
                    at = first_block + i
                    shared, both = key_blocks(tab_ref, end, p, i, at, last_row)
                    keys = gathered(k_ref, shared, both, low, lanes)
                    values = gathered(v_ref, shared, both, low, lanes)
                    query = split_pair(q_ref[rows_of(i), lanes], low)
                    grad = split_pair(d_merged_ref[rows_of(i), lanes], low)
                    scores = masked_scores(dot_nt(keys, query), mask_ref, i)
                    share_of = jnp.exp(scores - lse_ref[p, pl.ds(i, 1), :])
                    d_share = dot_nt(values, grad)
                    centre = jnp.sum(share_of * d_share, axis=0, keepdims=True)
                    d_scores = (share_of * (d_share - centre)).astype(BF16)
                    d_query = dot_tn(d_scores, keys) * SCALE
                    dq_ref[rows_of(i), lanes] = jnp.where(
                        low, d_query[:BLK], d_query[BLK:]).astype(BF16)
                    parts = (dot(d_scores, query), dot(share_of.astype(BF16), grad))
                    for n, part in enumerate(parts):
                        for slot in range(3):
                            acc[n, rows_of(at + slot), :] += part[slot * BLK:(slot + 1) * BLK]
                        acc[n, BLK:2 * BLK, :] += part[3 * BLK:4 * BLK]
                        last[n] += part[4 * BLK:5 * BLK]
                    for t in range(3):
                        one, two = (
                            prev_ref[lax.div(h, 3), i, lax.rem(h, 3) * 3 + t]
                            for h in (2 * p, 2 * p + 1))
                        for n, part in enumerate(parts):
                            picked[n, i * 3 + t] = part[(5 + t) * BLK:(6 + t) * BLK] + jnp.where(
                                low, picked[n, one], picked[n, two])
                    return 0

                lax.fori_loop(0, own_blocks, step, 0, unroll=own_blocks)

                def gather(owner, _):
                    for inner in range(own_blocks):
                        block = owner * own_blocks + inner
                        one, two = (
                            tail_ref[lax.div(h, 3), block, lax.rem(h, 3) * 3]
                            for h in (2 * p, 2 * p + 1))
                        for n in range(2):
                            total = acc[n, rows_of(block + 1), :]
                            total = total + jnp.where(low, picked[n, one], picked[n, two])
                            total = total + last[n] * mask_ref[own_blocks, block]
                            buf[p, owner, n, inner * BLK:(inner + 1) * BLK] = total.astype(BF16)
                    return 0

                lax.fori_loop(0, 4, gather, 0)
                copy_pair(p, 0, diagonal).start()
                copy_pair(p, 1, mate).start()

                @pl.when(p > 0)
                def _():
                    sum_pair(p - 1)

                for n, events in enumerate(BETWEEN):
                    @pl.when(p == n)
                    def _():
                        if n == 0:
                            end_square(SQUARE + 3)
                        for u, stage in events:
                            finish(u, stage)

                return 0

            lax.fori_loop(0, pairs, one_pair, 0)

        tmp[...] = dot_tn(merged_ref[...], d_attn_ref[...])
        square(SQUARE + 3, tmp)
        heads()
        sum_pair(pairs - 1)

        loading["wk"].wait()
        loading["wv"].wait()
        out_far[...] = (dot_nt(dkr[...], wk[...]) + dot_nt(dvr[...], wv[...])).astype(BF16)
        far = remote(out_far, in_far, far_sems.at[0], far_sems.at[1], to_y)
        far.start()
        loading["wq"].wait()
        loading["far"].wait()

        tmp[...] = dot_tn(x_ref[...], dko[...]) + dot_tn(far_ref[...], dkr[...])
        square(SQUARE + 1, tmp)
        for u, stage in AFTER[:4]:
            finish(u, stage)
        tmp[...] = dot_tn(x_ref[...], dvo[...]) + dot_tn(far_ref[...], dvr[...])
        square(SQUARE + 2, tmp)
        end_square(SQUARE + 1)
        tmp[...] = dot_tn(x_ref[...], dq_ref[...])
        square(SQUARE, tmp)
        end_square(SQUARE + 2)
        for u, stage in AFTER[4:]:
            finish(u, stage)
        end_square(SQUARE)

        small[6:7, :] = column_sum(dq_ref[...].astype(F32))
        small[7:8, :] = column_sum(dvo[...].astype(F32)) + column_sum(dvr[...].astype(F32))

        def small_copies(stage):
            axis = ("core", "y", "x", "z")[stage]
            if axis == "z":
                return [
                    remote(small, small_z.at[step - 1], s_sends.at[2 + step], s_recvs.at[2 + step],
                           device("z", lax.rem(z + step, groups)))
                    for step in range(1, groups)
                ]
            target = {"core": to_mate, "y": to_y, "x": device("x", 1 - x)}[axis]
            return [remote(small, small_in.at[stage], s_sends.at[stage], s_recvs.at[stage], target)]

        def small_begin(stage):
            for copy in small_copies(stage):
                copy.start()

        def small_end(stage):
            for copy in small_copies(stage):
                copy.wait()
            if stage < 3:
                small[...] += small_in[stage]
                small_begin(stage + 1)
            else:
                total = small[...]
                for step in range(1, groups):
                    total = total + small_z[step - 1]
                vec_ref[...] = total

        small_begin(0)
        dx_ref[...] += (
            dot_nt(dq_ref[...], wq[...]) + dot_nt(dko[...], wk[...]) + dot_nt(dvo[...], wv[...])
        )
        for n, (u, stage) in enumerate(LAST):
            if n in (2, 5, 6, 8):
                small_end((2, 5, 6, 8).index(n))
            if n == 6:
                far.wait()
                dx_ref[...] += in_far[...].astype(F32)
            finish(u, stage)

    pl.run_scoped(
        attention, VMEM((4 * own_blocks, BLK, features), BF16),
        VMEM((4 * own_blocks, BLK, features), BF16), low_rows, low_rows, low_rows, square_low, square_low, square_low,
        VMEM((2, (4 * own_blocks + 2) * BLK, PAIR), F32), VMEM((2, BLK, PAIR), F32),
        VMEM((2, picks_count + 1, BLK, PAIR), F32), VMEM((pairs, 4, 2, rows, PAIR), BF16),
        low_rows, low_rows, low_rows, low_rows, low_rows, VMEM((4, 4, 4) + UNIT, BF16),
        VMEM((features, features), F32),
    )


SLOPE = F32


def layer_tail(
    groups, table, prev, tail, mask, biases, up_bias, lse, tokens, merged, cotangent, out_weight,
    up_weight, down_weight, query, keys, values, key_weight, value_weight, query_weight, far_tokens,
):
    rows, features = tokens.shape
    hidden = up_weight.shape[1]
    own_blocks = rows // BLK
    pairs = features // PAIR
    share = features // (8 * groups)
    wide = hidden // features
    low = VMEM((rows, features), BF16)
    line = jax.ShapeDtypeStruct((share, features), F32)
    any_space = pl.BlockSpec(memory_space=pl.ANY)
    in_smem = pl.BlockSpec(memory_space=pltpu.SMEM)
    dma = pltpu.SemaphoreType.DMA
    return pl.pallas_call(
        functools.partial(layer_kernel, rows, 128, own_blocks, groups),
        out_shape=(
            jax.ShapeDtypeStruct((rows, features), BF16),
            jax.ShapeDtypeStruct((rows, features), F32), line, line, line, line,
            jax.ShapeDtypeStruct((share, hidden), F32),
            jax.ShapeDtypeStruct((wide * share, features), F32),
            jax.ShapeDtypeStruct((16, features), F32),
        ),
        in_specs=[in_smem] * 4 + [whole_vmem()] * 8 + [any_space] * 13,
        out_specs=(whole_vmem(),) * 9,
        scratch_shapes=[
            VMEM((12, 4 * groups) + UNIT, BF16),
            VMEM((12, 4 * groups - 1) + UNIT, BF16),
            VMEM((4, 4, 4) + UNIT, BF16),
            VMEM((4, 4, 4) + UNIT, BF16),
            VMEM((4, 4) + UNIT, BF16),
            VMEM((pairs, 2, 2, rows, PAIR), BF16),
            low,
            VMEM((16, features), F32),
            VMEM((3, 16, features), F32),
            VMEM((groups - 1, 16, features), F32),
            low, low, low, low,
            dma((13,)), dma((12, groups + 1)), dma((12, groups + 1)), dma((12,)), dma((12,)),
            dma((pairs, 2)), dma((pairs, 2)), dma((groups + 2,)), dma((groups + 2,)), dma((2,)),
        ],
        compiler_params=pltpu.CompilerParams(
            collective_id=3, has_side_effects=True, vmem_limit_bytes=LIMIT
        ),
        name="layer_tail",
    )(
        table, prev, tail, mask, *biases, up_bias, lse, tokens, merged, cotangent, out_weight, up_weight,
        down_weight, query, keys, values, key_weight, value_weight, query_weight, far_tokens,
    )


def finish_kernel(groups, vec_ref, *refs):
    count = len(refs) - 9
    given, out, vectors = refs[:count // 2], refs[count // 2:count], refs[count:]
    for src, dst in zip(given, out):
        dst[...] = src[...]
    features = vec_ref.shape[1]
    share = vectors[0].shape[0]
    shard = lax.axis_index("dp") * 4 + lax.axis_index("seq")
    moved = pltpu.roll(vec_ref[...], lax.rem(features - shard * share, features), axis=1)
    for n in range(8):
        vectors[n][...] = moved[n, 0:share]
    wide = vectors[8].shape[0] // share
    per_row = features // (wide * share)
    mine = vec_ref[pl.ds(8 + shard // per_row, 1), :]
    start = lax.rem(shard, per_row) * (wide * share)
    mine = pltpu.roll(mine, lax.rem(features - start, features), axis=1)
    vectors[8][...] = mine[0, 0:wide * share]


def hand_out(groups, vectors, arrays):
    features = vectors.shape[1]
    share = features // (8 * groups)
    wide = arrays[-1].shape[0] // share
    shapes = [jax.ShapeDtypeStruct(a.shape, a.dtype) for a in arrays]
    lines = [jax.ShapeDtypeStruct((share,), F32)] * 8 + [jax.ShapeDtypeStruct((wide * share,), F32)]
    return pl.pallas_call(
        functools.partial(finish_kernel, groups),
        out_shape=tuple(shapes + lines),
        in_specs=[whole_vmem()] * (1 + len(arrays)),
        out_specs=(whole_vmem(),) * (len(arrays) + 9),
        name="hand_out",
    )(vectors, *arrays)


def layer_norm(values, gain, shift):
    center = jnp.mean(values, axis=-1, keepdims=True)
    centered = values - center
    variance = jnp.mean(centered * centered, axis=-1, keepdims=True)
    inv_root = lax.rsqrt(variance + NORM_EPS)
    normed = centered * inv_root
    return (normed * gain + shift, normed, inv_root)


def norm_back(grad_out, normed, inv_root, gain):
    d_normed = grad_out * gain
    grad_in = inv_root * (
        d_normed
        - jnp.mean(d_normed, axis=-1, keepdims=True)
        - normed * jnp.mean(d_normed * normed, axis=-1, keepdims=True)
    )
    return (grad_in, jnp.sum(grad_out * normed, axis=0), jnp.sum(grad_out, axis=0))


def on_device(
    groups,
    tokens, filled_blocks, random_blocks, query_weight, query_bias, key_weight, value_weight,
    value_bias, out_weight, out_bias, attn_gain, attn_shift, up_weight, up_bias, down_weight,
    down_bias, ffn_gain, ffn_shift, cotangent,
):
    row_count, feature_count = tokens.shape
    filled = filled_blocks[0]
    place = lax.axis_index("seq") * row_count + jnp.arange(row_count, dtype=jnp.int32)
    live_tokens = (place < filled * BLK).astype(F32)[:, None]

    query, keys, values, far_tokens, table, prev, tail, mask = gather_project(
        filled_blocks, tokens, random_blocks[0], query_weight, key_weight, value_weight, query_bias,
        value_bias)
    keys, values = (t.reshape(-1, BLK, feature_count) for t in (keys, values))
    merged, lse = attention_forward(table, filled_blocks, mask, query, keys, values)

    if groups:
        *arrays, vectors = layer_tail(
            groups, table, prev, tail, mask,
            (out_bias, attn_gain, attn_shift, down_bias, ffn_gain, ffn_shift), up_bias[None], lse,
            tokens, merged, cotangent, out_weight, up_weight, down_weight, query, keys, values,
            key_weight, value_weight, query_weight, far_tokens)
        (result, grad_tokens, gq, gk, gv, go, up, down, g2, s2, bd, g1, s1, bo, bq, bv,
         bu) = hand_out(groups, vectors, arrays)
        return (
            result, grad_tokens, gq, bq, gk, gv, bv, go, bo, g1, s1, up, bu, down, bd, g2, s2)

    attn = dot(merged, out_weight) + out_bias
    first, normed_one, root_one = layer_norm(tokens.astype(F32) + attn, attn_gain, attn_shift)
    first_low = first.astype(BF16)
    hidden = dot(first_low, up_weight) + up_bias
    act, gelu_pull = jax.vjp(jax.nn.gelu, hidden)
    act_low = act.astype(BF16)
    ffn = dot(act_low, down_weight) + down_bias
    result, normed_two, root_two = layer_norm(first + ffn, ffn_gain, ffn_shift)
    grad_result = cotangent.astype(F32) * live_tokens
    d_sum_two, grad_ffn_gain, grad_ffn_shift = norm_back(
        grad_result, normed_two, root_two, ffn_gain
    )
    d_ffn = d_sum_two.astype(BF16)
    grad_down_bias = jnp.sum(d_ffn, axis=0, dtype=F32)
    grad_down_weight = dot_tn(act_low, d_ffn)
    d_act = dot_nt(d_ffn, down_weight)
    d_hidden = gelu_pull(d_act)[0].astype(BF16)
    grad_up_bias = jnp.sum(d_hidden, axis=0, dtype=F32)
    grad_up_weight = dot_tn(first_low, d_hidden)
    d_first = d_sum_two + dot_nt(d_hidden, up_weight)
    d_sum_one, grad_attn_gain, grad_attn_shift = norm_back(d_first, normed_one, root_one, attn_gain)
    d_attn = d_sum_one.astype(BF16)
    grad_out_bias = jnp.sum(d_attn, axis=0, dtype=F32)
    grad_out_weight = dot_tn(merged, d_attn)
    d_merged = dot_nt(d_attn, out_weight).astype(BF16)

    d_query, d_keys, d_values = attention_backward(
        table, filled_blocks, mask, query, keys, values, d_merged, lse
    )
    grad_tokens, dk_own, dv_own, dk_far, dv_far = exchange(
        d_keys, d_values, d_query, d_sum_one, query_weight, key_weight, value_weight
    )
    grad_query_weight = dot_tn(tokens, d_query)
    grad_query_bias = jnp.sum(d_query, axis=0, dtype=F32)
    grad_key_weight = dot_tn(tokens, dk_own) + dot_tn(far_tokens, dk_far)
    grad_value_weight = dot_tn(tokens, dv_own) + dot_tn(far_tokens, dv_far)
    grad_value_bias = jnp.sum(dv_own, axis=0, dtype=F32) + jnp.sum(dv_far, axis=0, dtype=F32)

    square = (grad_query_weight, grad_key_weight, grad_value_weight, grad_out_weight)
    vectors = (
        grad_query_bias, grad_value_bias, grad_out_bias, grad_attn_gain, grad_attn_shift,
        grad_down_bias, grad_ffn_gain, grad_ffn_shift,
    )
    square, up, down, vectors, up_sum = summed_anywhere(
        square, grad_up_weight, grad_down_weight, vectors, grad_up_bias)
    return (
        result.astype(BF16), grad_tokens, square[0], vectors[0], square[1], square[2], vectors[1],
        square[3], vectors[2], vectors[3], vectors[4], up, up_sum, down, vectors[5], vectors[6],
        vectors[7],
    )


def solution(mesh):
    both = P(("dp", "seq"), None)
    line = P(("dp", "seq"))
    placed = (both, P("dp"), P("dp", None, "seq", None)) + (P(),) * 15 + (both,)
    groups = 4 if mesh.shape["dp"] == 8 and mesh.shape["seq"] == 4 else 0
    return jax.shard_map(
        functools.partial(on_device, groups),
        mesh=mesh,
        in_specs=placed,
        out_specs=(
            both, both, both, line, both, both, line, both, line, line, line, both, line, both,
            line, line, line,
        ),
        check_vma=False,
    )
```

```python
import functools

import jax
import jax.numpy as jnp
from jax import lax
from jax.experimental import pallas as pl
from jax.experimental.pallas import tpu as pltpu
from jax.sharding import PartitionSpec as P

HEAD_DIM = 64
BLK = 64
PAIR = 2 * HEAD_DIM
TABLE = 8
NORM_EPS = 1e-05
MASKED = -1e30
SCALE = HEAD_DIM ** (-0.5)
MESH = pl.DeviceIdType.MESH
BF16 = jnp.bfloat16
F32 = jnp.float32
VMEM = pltpu.VMEM
LIMIT = 63 << 20


def whole_vmem():
    return pl.BlockSpec(memory_space=pltpu.VMEM)


def dot(left, right):
    return jnp.dot(left, right, preferred_element_type=F32)


def dot_nt(left, right):
    return lax.dot_general(left, right, (((1,), (1,)), ((), ())), preferred_element_type=F32)


def dot_tn(left, right):
    return lax.dot_general(left, right, (((0,), (0,)), ((), ())), preferred_element_type=F32)


def tables_of(tab_out, filled, first_block, each, prev_out, tail_out, mask_out):
    groups, blocks, width = tab_out.shape
    slot_blocks = width
    none = blocks * each
    lane = lax.broadcasted_iota(jnp.int32, (blocks, width), 1)
    row = lax.broadcasted_iota(jnp.int32, (blocks, width), 0)
    pick = lax.rem(lane, each)
    key_row = lax.broadcasted_iota(jnp.int32, (slot_blocks, width), 0)
    key_pick = lax.rem(lax.broadcasted_iota(jnp.int32, (slot_blocks, width), 1), each)
    for g in range(groups):
        table = tab_out[g]
        prev = jnp.full((blocks, width), -1, jnp.int32)
        for shift in range(1 - each, each):
            moved = pltpu.roll(table, (-shift) % width, axis=1)
            inside = (pick + shift >= 0) & (pick + shift < each)
            for i in range(blocks - 1):
                same = (moved[i:i + 1] == table) & (row > i) & inside
                prev = jnp.maximum(prev, jnp.where(same, i * each + pick + shift, -1))
        prev = jnp.where(prev < 0, none, prev)
        prev_out[g] = jnp.where(lane == width - 1, filled - 1, prev)
        tail = jnp.full((slot_blocks, width), -1, jnp.int32)
        for i in range(blocks):
            tail = jnp.maximum(tail, jnp.where(table[i:i + 1] == key_row, i * each + key_pick, -1))
        best = tail
        for shift in range(1, each):
            best = jnp.maximum(best, pltpu.roll(tail, width - shift, axis=1))
        turned = jnp.where(best < 0, none, best).astype(F32).T.astype(jnp.int32)
        for h in range(3):
            tail_out[g, h:h + 1, :] = turned[h * each:h * each + 1, :]
        tail_out[g, 3:blocks, :] = jnp.full((blocks - 3, width), none, jnp.int32)
    at = first_block + row
    window = at + lane - 1
    ok = jnp.where(
        lane < 3, ((window >= 0) & (window < filled)).astype(jnp.int32),
        jnp.where(lane == 3, (at >= 2).astype(jnp.int32),
                  (jnp.abs(at - (filled - 1)) > 1).astype(jnp.int32)))
    mask_out[0:blocks, :] = jnp.where(ok == 1, 0.0, MASKED)
    mask_out[blocks:2 * blocks, :] = (lane == filled - 1).astype(F32)


def gather_kernel(
    rows, width, filled_ref, x_ref, picks_ref, wq_any, wk_any, wv_any, qb_ref, vb_ref,
    q_any, k_any, v_any, far_any, tab_out, prev_out, tail_out, mask_out,
    wq_ref, wk_ref, wv_ref, q_ref, k_ref, v_ref,
    tab_ref, land, tab_land, loads, stores, sends, recvs, tab_sends, tab_recvs,
):
    parts = 4
    part = rows // parts
    dp, me = lax.axis_index("dp"), lax.axis_index("seq")
    mate, across, diagonal = (lax.bitwise_xor(me, bit) for bit in (1, 2, 3))
    weights = [
        pltpu.make_async_copy(src, dst, loads.at[n])
        for n, (src, dst) in enumerate(((wq_any, wq_ref), (wk_any, wk_ref), (wv_any, wv_ref)))
    ]
    for copy in weights:
        copy.start()
    barrier = pltpu.get_barrier_semaphore()
    for other in (mate, across, diagonal):
        pl.semaphore_signal(barrier, inc=1, device_id=(dp, other), device_id_type=MESH)
    heads_here, each = 3, picks_ref.shape[0] // 3
    blocks = picks_ref.shape[2]
    chosen = picks_ref[...].reshape(heads_here * each, blocks).astype(F32)
    chosen = jnp.concatenate(
        [chosen, jnp.zeros((heads_here * each, 128 - blocks), F32)], axis=1)
    chosen = jnp.concatenate([chosen, jnp.zeros((128 - heads_here * each, 128), F32)], axis=0)
    tab_ref[...] = chosen.T[0:blocks].astype(jnp.int32)
    pl.semaphore_wait(barrier, 3)

    def send(src, dst, slot, target):
        copy = pltpu.make_async_remote_copy(
            src_ref=src, dst_ref=dst, send_sem=sends.at[slot], recv_sem=recvs.at[slot],
            device_id=(dp, target), device_id_type=MESH,
        )
        copy.start()
        return copy

    tables = []
    own_blocks = tab_ref.shape[0] // 4
    for slot, other in enumerate((mate, across, diagonal)):
        copy = pltpu.make_async_remote_copy(
            src_ref=tab_ref.at[pl.ds(pl.multiple_of(other * own_blocks, 8), own_blocks)],
            dst_ref=tab_land.at[slot], send_sem=tab_sends.at[slot], recv_sem=tab_recvs.at[slot],
            device_id=(dp, other), device_id_type=MESH,
        )
        copy.start()
        tables.append(copy)
    far = [
        send(x_ref.at[pl.ds(r * part, part)], land.at[0, pl.ds(r * part, part)], r, across)
        for r in range(parts)
    ]
    near = send(x_ref, land.at[1], parts, mate)
    stored = []

    def store(src, dst, start, count):
        at = pl.ds(pl.multiple_of(start, part), count)
        copy = pltpu.make_async_copy(src.at[at], dst.at[at], stores.at[len(stored)])
        copy.start()
        stored.append(copy)

    def keys_values(x, at):
        k_ref[pl.ds(at, width), :] = dot(x, wk_ref[...]).astype(BF16)
        v_ref[pl.ds(at, width), :] = (dot(x, wv_ref[...]) + vb_ref[...][None]).astype(BF16)

    for copy in weights:
        copy.wait()

    def own(r, _):
        at = pl.multiple_of(r * width, width)
        x = x_ref[pl.ds(at, width), :]
        q_ref[pl.ds(at, width), :] = (
            (dot(x, wq_ref[...]) + qb_ref[...][None]).astype(BF16) * jnp.asarray(SCALE, BF16)
        )
        keys_values(x, pl.multiple_of(me * rows + at, width))
        return 0

    lax.fori_loop(0, rows // width, own, 0)
    store(q_ref, q_any, 0, rows)
    store(k_ref, k_any, me * rows, rows)
    store(v_ref, v_any, me * rows, rows)

    def block(slot, owner, start, count):
        def step(r, _):
            at = pl.multiple_of(start + r * width, width)
            keys_values(land[slot, pl.ds(at, width), :], pl.multiple_of(owner * rows + at, width))
            return 0

        lax.fori_loop(0, count // width, step, 0)
        store(k_ref, k_any, owner * rows + start, count)
        store(v_ref, v_any, owner * rows + start, count)

    near.wait()
    block(1, mate, 0, rows)
    for copy in tables:
        copy.wait()
    tab_out[pl.ds(me, 1)] = tab_ref[pl.ds(pl.multiple_of(me * own_blocks, 8), own_blocks)][None]
    for slot, other in enumerate((mate, across, diagonal)):
        tab_out[pl.ds(other, 1)] = tab_land[slot][None]
    tables_of(tab_out, filled_ref[0], me * own_blocks, each, prev_out, tail_out, mask_out)
    relayed = []
    for r in range(parts):
        far[r].wait()
        piece = pl.ds(r * part, part)
        relayed.append(send(land.at[0, piece], land.at[2, piece], parts + 1 + r, mate))
        store(land.at[0], far_any, r * part, part)
        block(0, across, r * part, part)
        if r:
            relayed[r - 1].wait()
            block(2, diagonal, (r - 1) * part, part)
    relayed[-1].wait()
    block(2, diagonal, (parts - 1) * part, part)
    for copy in stored:
        copy.wait()


def gather_project(
    filled, tokens, chosen, query_weight, key_weight, value_weight, query_bias, value_bias,
):
    rows, features = tokens.shape
    own_blocks = rows // BLK
    slot_blocks = chosen.shape[2]
    copies = 4 + 1 + 4
    any_space = pl.BlockSpec(memory_space=pl.ANY)
    low = jax.ShapeDtypeStruct((rows, features), BF16)
    slot = jax.ShapeDtypeStruct((4 * rows, features), BF16)
    table = jax.ShapeDtypeStruct((4, own_blocks, 128), jnp.int32)
    dma = pltpu.SemaphoreType.DMA
    return pl.pallas_call(
        functools.partial(gather_kernel, rows, 128),
        out_shape=(
            low, slot, slot, low, table, table, table,
            jax.ShapeDtypeStruct((2 * own_blocks, 128), F32),
        ),
        in_specs=[pl.BlockSpec(memory_space=pltpu.SMEM)] + [whole_vmem()] * 2 + [any_space] * 3
        + [whole_vmem()] * 2,
        out_specs=(any_space,) * 4 + (whole_vmem(),) * 4,
        scratch_shapes=[
            VMEM((features, features), BF16),
            VMEM((features, features), BF16),
            VMEM((features, features), BF16),
            VMEM((rows, features), BF16),
            VMEM((4 * rows, features), BF16),
            VMEM((4 * rows, features), BF16),
            VMEM((slot_blocks, 128), jnp.int32),
            VMEM((3, rows, features), BF16),
            VMEM((3, own_blocks, 128), jnp.int32),
            dma((3,)), dma((25,)), dma((copies,)), dma((copies,)), dma((3,)), dma((3,)),
        ],
        compiler_params=pltpu.CompilerParams(
            collective_id=0, has_side_effects=True, vmem_limit_bytes=LIMIT
        ),
        name="gather_project",
    )(filled, tokens, chosen, query_weight, key_weight, value_weight, query_bias, value_bias)


def key_blocks(tab_ref, end, pair, i, at, last_row):
    def chosen(head, t):
        group, inner = lax.div(head, 3), lax.rem(head, 3)
        return tab_ref[group, i, inner * 3 + t]

    head = 2 * pair
    both = [(chosen(head, t), chosen(head + 1, t)) for t in range(3)]
    shared = [
        jnp.maximum(at - 1, 0), at, jnp.minimum(at + 1, last_row), jnp.int32(0), end,
    ]
    return shared, both


def rows_of(block):
    return pl.ds(pl.multiple_of(block * BLK, BLK), BLK)


def lanes_low(rows):
    return lax.broadcasted_iota(jnp.int32, (rows, PAIR), 1) < HEAD_DIM


def split_pair(x, low):
    zero = jnp.zeros_like(x)
    return jnp.concatenate([jnp.where(low, x, zero), jnp.where(low, zero, x)], axis=0)


def gathered(ref, shared, both, low, lanes=slice(None)):
    tiles = [ref[b, :, lanes] for b in shared]
    for first, second in both:
        tiles.append(jnp.where(low, ref[first, :, lanes], ref[second, :, lanes]))
    return jnp.concatenate(tiles, axis=0)


def masked_scores(scores, mask_ref, i):
    parts = [scores[n * BLK:(n + 1) * BLK] + mask_ref[i, n] for n in range(5)]
    return jnp.concatenate(parts + [scores[5 * BLK:]], axis=0)


def attend(keys, values, query, mask_ref, i, low):
    scores = masked_scores(dot_nt(keys, query), mask_ref, i)
    highest = jnp.max(scores, axis=0, keepdims=True)
    weights = jnp.exp(scores - highest)
    total = jnp.sum(weights, axis=0, keepdims=True)
    share = (weights * (1.0 / total)).astype(BF16)
    output = dot_tn(share, values)
    return jnp.where(low, output[:BLK], output[BLK:]), highest + jnp.log(total)


def forward_kernel(own_blocks, tab_ref, filled_ref, mask_ref, q_ref, k_ref, v_ref, out_ref, lse_ref):
    pair = pl.program_id(0)
    filled = filled_ref[0]
    first_block = lax.axis_index("seq") * own_blocks
    last_row = k_ref.shape[0] - 1
    low = lanes_low(BLK)

    def step(i, _):
        at = first_block + i
        shared, both = key_blocks(tab_ref, filled - 1, pair, i, at, last_row)
        keys = gathered(k_ref, shared, both, low)
        values = gathered(v_ref, shared, both, low)
        query = split_pair(q_ref[rows_of(i), :], low)
        merged, lse = attend(keys, values, query, mask_ref, i, low)
        out_ref[rows_of(i), :] = jnp.where(at < filled, merged, 0.0).astype(BF16)
        lse_ref[0, pl.ds(i, 1), :] = lse
        return 0

    lax.fori_loop(0, own_blocks, step, 0, unroll=own_blocks)


def attention_forward(table, filled, mask, query, keys, values):
    rows, features = query.shape
    own_blocks = rows // BLK
    slot_blocks = keys.shape[0]
    pairs = features // PAIR
    column = lambda n: pl.BlockSpec((n, PAIR), lambda p, *_: (0, p))
    blocks = lambda n: pl.BlockSpec((n, BLK, PAIR), lambda p, *_: (0, 0, p))
    return pl.pallas_call(
        functools.partial(forward_kernel, own_blocks),
        out_shape=(
            jax.ShapeDtypeStruct((rows, features), BF16),
            jax.ShapeDtypeStruct((pairs, own_blocks, PAIR), F32),
        ),
        grid_spec=pltpu.PrefetchScalarGridSpec(
            num_scalar_prefetch=3,
            grid=(pairs,),
            in_specs=[column(rows), blocks(slot_blocks), blocks(slot_blocks)],
            out_specs=(column(rows), pl.BlockSpec((1, own_blocks, PAIR), lambda p, *_: (p, 0, 0))),
        ),
        compiler_params=pltpu.CompilerParams(vmem_limit_bytes=LIMIT),
        name="attention_forward",
    )(table, filled, mask, query, keys, values)


def backward_kernel(
    own_blocks, tab_ref, filled_ref, mask_ref, q_ref, k_ref, v_ref, g_ref, lse_ref,
    dq_ref, dk_ref, dv_ref, dk_sum, dv_sum,
):
    pair = pl.program_id(0)
    filled = filled_ref[0]
    first_block = lax.axis_index("seq") * own_blocks
    last_row = k_ref.shape[0] - 1
    low = lanes_low(BLK)
    dk_sum[...] = jnp.zeros_like(dk_sum)
    dv_sum[...] = jnp.zeros_like(dv_sum)

    def step(i, _):
        at = first_block + i
        shared, both = key_blocks(tab_ref, filled - 1, pair, i, at, last_row)
        keys = gathered(k_ref, shared, both, low)
        values = gathered(v_ref, shared, both, low)
        query = split_pair(q_ref[rows_of(i), :], low)
        grad = split_pair(jnp.where(at < filled, g_ref[rows_of(i), :], jnp.zeros((), BF16)), low)
        scores = masked_scores(dot_nt(keys, query), mask_ref, i)
        share = jnp.exp(scores - lse_ref[0, pl.ds(i, 1), :])
        d_share = dot_nt(values, grad)
        centre = jnp.sum(share * d_share, axis=0, keepdims=True)
        d_scores = (share * (d_share - centre)).astype(BF16)
        d_query = dot_tn(d_scores, keys) * SCALE
        dq_ref[rows_of(i), :] = jnp.where(low, d_query[:BLK], d_query[BLK:]).astype(BF16)
        for total, part in ((dk_sum, dot(d_scores, query)), (dv_sum, dot(share.astype(BF16), grad))):
            for slot, block in enumerate(shared):
                total[rows_of(block), :] += part[slot * BLK:(slot + 1) * BLK]
            for t, (one, two) in enumerate(both):
                tile = part[(5 + t) * BLK:(6 + t) * BLK]
                total[rows_of(one), :] += jnp.where(low, tile, 0.0)
                total[rows_of(two), :] += jnp.where(low, 0.0, tile)
        return 0

    lax.fori_loop(0, own_blocks, step, 0, unroll=own_blocks)
    dk_ref[...] = dk_sum[...].astype(BF16)
    dv_ref[...] = dv_sum[...].astype(BF16)


def attention_backward(table, filled, mask, query, keys, values, grad, lse):
    rows, features = query.shape
    slot_blocks = keys.shape[0]
    slot_rows = slot_blocks * BLK
    own_blocks = rows // BLK
    pairs = features // PAIR
    blocks = lambda n: pl.BlockSpec((n, BLK, PAIR), lambda p, *_: (0, 0, p))
    column = lambda n: pl.BlockSpec((n, PAIR), lambda p, *_: (0, p))
    return pl.pallas_call(
        functools.partial(backward_kernel, own_blocks),
        out_shape=(
            jax.ShapeDtypeStruct((rows, features), BF16),
            jax.ShapeDtypeStruct((slot_rows, features), BF16),
            jax.ShapeDtypeStruct((slot_rows, features), BF16),
        ),
        grid_spec=pltpu.PrefetchScalarGridSpec(
            num_scalar_prefetch=3,
            grid=(pairs,),
            in_specs=[
                column(rows), blocks(slot_blocks), blocks(slot_blocks), column(rows),
                pl.BlockSpec((1, own_blocks, PAIR), lambda p, *_: (p, 0, 0)),
            ],
            out_specs=(column(rows), column(slot_rows), column(slot_rows)),
            scratch_shapes=[VMEM((slot_rows, PAIR), F32), VMEM((slot_rows, PAIR), F32)],
        ),
        compiler_params=pltpu.CompilerParams(vmem_limit_bytes=LIMIT),
        name="attention_backward",
    )(table, filled, mask, query, keys, values, grad, lse)


def exchange_kernel(
    rows, width, dk_ref, dv_ref, dq_ref, base_ref, wq_ref, wk_ref, wv_ref,
    dx_ref, dko_ref, dvo_ref, dkr_ref, dvr_ref,
    land, out_far, in_far, sends, recvs,
):
    dp, me = lax.axis_index("dp"), lax.axis_index("seq")
    mate, across, diagonal = (lax.bitwise_xor(me, bit) for bit in (1, 2, 3))
    barrier = pltpu.get_barrier_semaphore()
    for other in (mate, across):
        pl.semaphore_signal(barrier, inc=1, device_id=(dp, other), device_id_type=MESH)
    pl.semaphore_wait(barrier, 2)

    def send(src, dst, slot, target):
        copy = pltpu.make_async_remote_copy(
            src_ref=src, dst_ref=dst, send_sem=sends.at[slot], recv_sem=recvs.at[slot],
            device_id=(dp, target), device_id_type=MESH,
        )
        copy.start()
        return copy

    def owned(index):
        return pl.ds(pl.multiple_of(index * rows, rows), rows)

    copies = [
        send(ref.at[owned(owner)], land.at[slot], slot, mate)
        for slot, (ref, owner) in enumerate(
            ((dk_ref, diagonal), (dv_ref, diagonal), (dk_ref, mate), (dv_ref, mate))
        )
    ]

    def summed(ref, owner, slot, to_ref):
        to_ref[...] = (ref[owned(owner), :].astype(F32) + land[slot].astype(F32)).astype(BF16)

    copies[0].wait()
    summed(dk_ref, across, 0, dkr_ref)
    copies[1].wait()
    summed(dv_ref, across, 1, dvr_ref)

    steps = rows // width
    for r in range(steps):
        at = pl.ds(r * width, width)
        out_far[at, :] = (
            dot_nt(dkr_ref[at, :], wk_ref[...]) + dot_nt(dvr_ref[at, :], wv_ref[...])
        ).astype(BF16)
    far = send(out_far, in_far, 4, across)
    copies[2].wait()
    summed(dk_ref, me, 2, dko_ref)
    copies[3].wait()
    summed(dv_ref, me, 3, dvo_ref)

    def one(r, _):
        at = pl.ds(pl.multiple_of(r * width, width), width)
        dx_ref[at, :] = (
            base_ref[at, :]
            + dot_nt(dq_ref[at, :], wq_ref[...])
            + dot_nt(dko_ref[at, :], wk_ref[...])
            + dot_nt(dvo_ref[at, :], wv_ref[...])
        )
        return 0

    lax.fori_loop(0, steps, one, 0)
    far.wait()
    dx_ref[...] += in_far[...].astype(F32)


def exchange(d_keys, d_values, d_query, base, query_weight, key_weight, value_weight):
    rows, features = d_query.shape
    small = jax.ShapeDtypeStruct((rows, features), BF16)
    return pl.pallas_call(
        functools.partial(exchange_kernel, rows, 128),
        out_shape=(jax.ShapeDtypeStruct((rows, features), F32), small, small, small, small),
        in_specs=[whole_vmem()] * 7,
        out_specs=(whole_vmem(),) * 5,
        scratch_shapes=[
            VMEM((4, rows, features), BF16),
            VMEM((rows, features), BF16),
            VMEM((rows, features), BF16),
            pltpu.SemaphoreType.DMA((5,)),
            pltpu.SemaphoreType.DMA((5,)),
        ],
        compiler_params=pltpu.CompilerParams(
            collective_id=1, has_side_effects=True, vmem_limit_bytes=LIMIT
        ),
        name="exchange",
    )(d_keys, d_values, d_query, base, query_weight, key_weight, value_weight)


def summed_anywhere(square, up, down, vectors, up_bias):
    def one(g):
        return lax.psum_scatter(g, ("dp", "seq"), scatter_dimension=0, tiled=True)

    return [one(g) for g in square], one(up), one(down), [one(v) for v in vectors], one(up_bias)


GELU_A = 0.044715
GELU_C = 0.7978845608028654
UNIT = (48, 384)
ORDERS = (
    "yzx", "zxy", "yxz", "xzy", "xzy", "yxz", "xyz", "yxz", "yzx", "xyz", "zxy", "xzy",
)
UP, SQUARE = 4, 8
OUT, KEY, VALUE, QUERY = 8, 9, 10, 11
RIDERS = (OUT, QUERY)
EVENTS = {
    "up": ((0, 0), (3, 0)),
    "dense": (),
    0: ((2, 0), (4, 0), (1, 0)),
    1: ((5, 0), (6, 0), (0, 1)),
    2: ((2, 1), (1, 1), (7, 0), (3, 1)),
    3: ((5, 1), (0, 2)),
    4: ((8, 0), (4, 1), (7, 1), (6, 1), (1, 2), (2, 2)),
    5: ((3, 2), (5, 2), (4, 2)),
    "sum": (),
    "far": (),
    "v": ((8, 1),),
    "x": ((7, 2), (6, 2)),
    "end": ((9, 0), (8, 2), (11, 0), (10, 0), ("far", 0), (9, 1), (10, 1), (11, 1), (10, 2), (9, 2), (11, 2)),
}


def normed_rows(values):
    center = jnp.mean(values, axis=-1, keepdims=True)
    centered = values - center
    variance = jnp.mean(centered * centered, axis=-1, keepdims=True)
    inv_root = lax.rsqrt(variance + NORM_EPS)
    return centered * inv_root, inv_root


def norm_pull(grad_out, normed, inv_root, gain):
    d_normed = grad_out * gain
    return inv_root * (
        d_normed
        - jnp.mean(d_normed, axis=-1, keepdims=True)
        - normed * jnp.mean(d_normed * normed, axis=-1, keepdims=True)
    )


def column_sum(values):
    return jnp.sum(values, axis=0, keepdims=True)


def layer_kernel(
    rows, tile, own_blocks, groups, tab_ref, prev_ref, tail_ref, mask_ref, bo_ref, g1_ref, s1_ref,
    bd_ref, g2_ref, s2_ref, bu_ref,
    x_any, cot_any, wo_any, wu_any, wd_any, q_any, k_any, v_any, wk_any, wv_any, wq_any,
    far_any,
    result_ref, dx_ref, gq_ref, gk_ref, gv_ref, go_ref, up_ref, down_ref, vec_ref,
    work, land, core_down, core_up, pair_in, in_far, small, late,
    ride, ride_land, ride_core_in,
    x_ref, merged_ref, d_attn_ref, d_merged_ref, q_ref, k_ref, v_ref, lse_ref,
    loads, sends, recvs, c_sends, c_recvs, p_sends, p_recvs, r_sends, r_recvs, far_sems,
):
    features = x_ref.shape[1]
    hidden = bu_ref.shape[1]
    wide = hidden // features
    pairs = features // PAIR
    picks_count = own_blocks * 3
    share = features // (8 * groups)
    shards = 4 * groups
    half = features // 2
    dp, seq = lax.axis_index("dp"), lax.axis_index("seq")
    x, z = lax.rem(dp, 2), dp // 2
    core, y = lax.rem(seq, 2), seq // 2
    mate, across, diagonal = (lax.bitwise_xor(seq, bit) for bit in (1, 2, 3))
    end = prev_ref[0, 0, 127]
    first_block = seq * own_blocks
    low = lanes_low(BLK)
    to_mate, to_y = (dp, mate), (dp, across)
    place_of = {"x": (x, 2), "y": (y, 2), "z": (z, groups)}

    def device(axis, index):
        if axis == "x":
            return (2 * z + index, seq)
        if axis == "y":
            return (dp, 2 * index + core)
        return (2 * index + x, seq)

    neighbours = [to_mate, to_y, device("x", 1 - x)] + [
        device("z", lax.rem(z + step, groups)) for step in range(1, groups)]

    loading = {}

    def load(name, src, dst):
        copy = pltpu.make_async_copy(src, dst, loads.at[len(loading)])
        copy.start()
        loading[name] = copy

    def remote(src, dst, one, two, target):
        return pltpu.make_async_remote_copy(
            src_ref=src, dst_ref=dst, send_sem=one, recv_sem=two, device_id=target,
            device_id_type=MESH,
        )

    def lanes_of(p):
        return pl.ds(pl.multiple_of(p * PAIR, PAIR), PAIR)

    def columns(j):
        return pl.ds(pl.multiple_of(j * features, features), features)

    def tiles(body):
        def step(r, _):
            body(pl.ds(pl.multiple_of(r * tile, tile), tile), r)
            return 0

        lax.fori_loop(0, rows // tile, step, 0)


    def index_of(u, at_x, at_y, at_z):
        at = {"x": at_x, "y": at_y, "z": at_z}
        flat = 0
        for axis in ORDERS[u]:
            flat = flat * place_of[axis][1] + at[axis]
        return flat

    def shard_of(s):
        return s // 4, lax.rem(s // 2, 2), lax.rem(s, 2)

    def stage_of(u, stage):
        sizes = [place_of[axis][1] for axis in ORDERS[u]] + [1]
        base, offset, sem, block = 0, 0, 0, shards
        for n, axis in enumerate(ORDERS[u]):
            block = block // sizes[n]
            if n == stage:
                return axis, place_of[axis][0], sizes[n], block, base, offset, sem
            base = base + place_of[axis][0] * block
            offset += (sizes[n] - 1) * block
            sem += sizes[n] - 1
        return None

    def stage_copies(u, stage):
        axis, mine, size, block, base, offset, sem = stage_of(u, stage)
        copies = []
        for step in range(1, size):
            index = lax.rem(mine + step, size)
            copies.append(remote(
                work.at[u, pl.ds(base + index * block, block)],
                land.at[u, pl.ds(offset + (step - 1) * block, block)],
                sends.at[u, sem + step - 1], recvs.at[u, sem + step - 1], device(axis, index)))
            if u in RIDERS:
                n = RIDERS.index(u)
                copies.append(remote(
                    ride.at[n, core, pl.ds(base + index * block, block)],
                    ride_land.at[n, pl.ds(offset + (step - 1) * block, block)],
                    r_sends.at[n, sem + step - 1], r_recvs.at[n, sem + step - 1],
                    device(axis, index)))
        return copies

    def begin(u, stage):
        for copy in stage_copies(u, stage):
            copy.start()

    def finish(u, stage):
        _, mine, size, block, base, offset, _ = stage_of(u, stage)
        for copy in stage_copies(u, stage):
            copy.wait()

        def total(r):
            value = work[u, base + mine * block + r].astype(F32)
            for step in range(size - 1):
                value = value + land[u, offset + step * block + r].astype(F32)
            return value

        if u in RIDERS:
            n = RIDERS.index(u)

            def ridden(r):
                value = ride[n, core, base + mine * block + r]
                for step in range(size - 1):
                    value = value + ride_land[n, offset + step * block + r]
                return value

        if stage < 2:
            def body(r, _):
                work[u, base + mine * block + r] = total(r).astype(BF16)
                if u in RIDERS:
                    ride[n, core, base + mine * block + r] = ridden(r)
                return 0

            lax.fori_loop(0, block, body, 0)
            begin(u, stage + 1)
            return
        value = total(0)
        if u in RIDERS:
            vec_ref[n * 16:(n + 1) * 16, :] = ridden(0)
        if u < UP:
            down_ref[(u // 2) * UNIT[0]:(u // 2 + 1) * UNIT[0], (u % 2) * half:(u % 2 + 1) * half] = value
        else:
            to = up_ref if u < SQUARE else (go_ref, gk_ref, gv_ref, gq_ref)[u - SQUARE]
            at = (u - UP) * features if u < SQUARE else 0
            to[:, at:at + half] = value[:share]
            to[:, at + half:at + features] = value[share:]

    def folded(source, at, count):
        return jnp.concatenate(
            [source[pl.ds(at, count), 0:half], source[pl.ds(at, count), half:features]], axis=0)

    def split_pieces(u, read, other):
        def body(s, _):
            at_z, at_x, at_y = shard_of(s)
            index = index_of(u, at_x, at_y, at_z)
            for own in (True, False):
                row = 2 * s + (core if own else 1 - core)
                value = read(pl.multiple_of(row * share, 8), share).astype(BF16)
                if own:
                    work[u, index] = value
                else:
                    other[index // 4, lax.rem(index, 4)] = value
            return 0

        lax.fori_loop(0, shards, body, 0)

    def add_core(u, landed):
        def body(n, _):
            work[u, n] = (
                work[u, n].astype(F32) + landed[n // 4, lax.rem(n, 4)].astype(F32)
            ).astype(BF16)
            return 0

        lax.fori_loop(0, shards, body, 0)

    def at_point(name):
        for u, stage in EVENTS[name]:
            finish(u, stage)

    def vector_pieces(rider):
        count = 6 if rider == 0 else 2
        padded = jnp.zeros((16 - 8, 128 - share), F32)
        for s in range(shards):
            index = index_of(RIDERS[rider], (s // 2) % 2, s % 2, s // 4)
            for n in range(2):
                row = 2 * s + n
                at = row * share
                source = small if rider == 0 else late
                value = source[0:8, at:at + share]
                ride[rider, n, index, 0:8, :] = jnp.concatenate([value, padded], axis=1)
                if rider == 0:
                    start = (row % (2 * groups)) * (wide * share)
                    ride[rider, n, index, 8:16, :] = jnp.concatenate(
                        [small[8:16, start:start + wide * share],
                         jnp.zeros((8, 128 - wide * share), F32)], axis=1)
                else:
                    ride[rider, n, index, 8:16, :] = jnp.zeros((8, 128), F32)

    def ride_core(rider):
        return remote(ride.at[rider, 1 - core], ride_core_in.at[rider], r_sends.at[rider, groups + 1],
                      r_recvs.at[rider, groups + 1], to_mate)

    def core_copy(src, dst, slot):
        return remote(src, dst, c_sends.at[slot], c_recvs.at[slot], to_mate)

    load("q", q_any, q_ref)
    load("k", k_any, k_ref)
    load("v", v_any, v_ref)
    barrier = pltpu.get_barrier_semaphore()
    for target in neighbours:
        pl.semaphore_signal(barrier, inc=1, device_id=target, device_id_type=MESH)
    last_row = k_ref.shape[0] - 1

    def forward_pair(p):
        lanes = lanes_of(p)

        def step(i, _):
            at = first_block + i
            shared, both = key_blocks(tab_ref, end, p, i, at, last_row)
            keys = gathered(k_ref, shared, both, low, lanes)
            values = gathered(v_ref, shared, both, low, lanes)
            query = split_pair(q_ref[rows_of(i), lanes], low)
            merged, lse = attend(keys, values, query, mask_ref, i, low)
            live = lax.broadcasted_iota(jnp.int32, (BLK, 1), 0) < (end + 1 - at) * BLK
            merged_ref[rows_of(i), lanes] = jnp.where(live, merged, 0.0).astype(BF16)
            lse_ref[p, pl.ds(i, 1), :] = lse
            return 0

        lax.fori_loop(0, own_blocks, step, 0, unroll=own_blocks)


    def dense(
        wo, wu, wd, cot_ref, normed_one, root_one, first_low, act, slope, ffn, tmp, other,
    ):
        d_ffn = cot_ref
        for name in ("q", "k", "v"):
            loading[name].wait()
        for name, src, dst in (
            ("x", x_any, x_ref), ("wo", wo_any, wo), ("wu", wu_any, wu), ("wd", wd_any, wd),
            ("cot", cot_any, cot_ref),
        ):
            load(name, src, dst)

        def forward_two(n, _):
            for inner in range(2):
                forward_pair(2 * n + inner)
            return 0

        lax.fori_loop(0, pairs // 2, forward_two, 0)
        bo, g1, s1, bd, g2, s2 = (
            ref[...][None] for ref in (bo_ref, g1_ref, s1_ref, bd_ref, g2_ref, s2_ref))

        for name in ("x", "wo"):
            loading[name].wait()
        ffn[...] = dot(merged_ref[...], wo[...])

        def norm_one(at, r):
            normed, inv_root = normed_rows(x_ref[at, :].astype(F32) + (ffn[at, :] + bo))
            normed_one[at, :] = normed
            root_one[at, :] = inv_root
            first_low[at, :] = (normed * g1 + s1).astype(BF16)

        tiles(norm_one)

        loading["wu"].wait()
        loading["wd"].wait()
        ffn[...] = jnp.zeros_like(ffn)

        def forward(j, _):
            at = columns(j)
            u = dot(first_low[...], wu[:, at]) + bu_ref[:, at]
            square = u * u
            t = jnp.tanh(GELU_C * (u + GELU_A * (square * u)))
            upper = 0.5 * (1.0 + t)
            act[j] = (u * upper).astype(BF16)
            slope[j] = (
                upper + (0.5 * GELU_C) * u * (1.0 - t * t) * (1.0 + (3.0 * GELU_A) * square)
            ).astype(slope.dtype)
            ffn[...] += dot(act[j], wd[at, :])
            return 0

        lax.fori_loop(0, wide, forward, 0)

        small[...] = jnp.zeros_like(small)
        limit = (end + 1) * BLK - seq * rows
        loading["cot"].wait()

        def norm_two(at, r):
            first = normed_one[at, :] * g1 + s1
            normed, inv_root = normed_rows(first + (ffn[at, :] + bd))
            result_ref[at, :] = (normed * g2 + s2).astype(BF16)
            place = lax.broadcasted_iota(jnp.int32, (tile, 1), 0) + r * tile
            grad = cot_ref[at, :].astype(F32) * (place < limit).astype(F32)
            pulled = norm_pull(grad, normed, inv_root, g2)
            rounded = pulled.astype(BF16)
            ffn[at, :] = pulled
            d_ffn[at, :] = rounded
            small[0:1, :] += column_sum(grad * normed)
            small[1:2, :] += column_sum(grad)
            small[2:3, :] += column_sum(rounded.astype(F32))

        tiles(norm_two)

        pl.semaphore_wait(barrier, len(neighbours))
        down_copies = []
        for j in range(wide):
            tmp[...] = dot_tn(act[j], d_ffn[...])

            def pieces(n, _):
                at_x, at_y = n // 2, lax.rem(n, 2)
                for own in (True, False):
                    row = 2 * n + (core if own else 1 - core)
                    at = pl.multiple_of(row * (wide * share), 8)
                    for u in range(4):
                        value = tmp[
                            pl.ds(pl.multiple_of(at + (u // 2) * UNIT[0], 8), UNIT[0]),
                            (u % 2) * half:(u % 2 + 1) * half].astype(BF16)
                        if own:
                            work[u, index_of(u, at_x, at_y, j)] = value
                        else:
                            other[j, u, n] = value
                return 0

            lax.fori_loop(0, 4, pieces, 0)
            down_copies.append(core_copy(other.at[j], core_down.at[j], j))
            down_copies[-1].start()

        def backward(j, _):
            d_hidden = (dot_nt(d_ffn[...], wd[columns(j), :]) * slope[j].astype(F32)).astype(BF16)
            act[j] = d_hidden
            for n in range(wide):
                @pl.when(j == n)
                def _():
                    small[8 + n:9 + n, :] = column_sum(d_hidden.astype(F32))
            return 0

        lax.fori_loop(0, wide, backward, 0)

        for copy in down_copies:
            copy.wait()

        def sum_down(s, _):
            at_z, at_x, at_y = shard_of(s)
            for u in range(4):
                index = index_of(u, at_x, at_y, at_z)
                work[u, index] = (
                    work[u, index].astype(F32) + core_down[at_z, u, at_x * 2 + at_y].astype(F32)
                ).astype(BF16)
            return 0

        lax.fori_loop(0, shards, sum_down, 0)
        for u in range(4):
            begin(u, 0)

        up_copies = []

        def end_up(j):
            up_copies[j].wait()
            add_core(UP + j, core_up.at[j])
            begin(UP + j, 0)

        for j in range(wide):
            tmp[...] = dot_tn(first_low[...], act[j])
            split_pieces(UP + j, functools.partial(folded, tmp), other.at[j])
            up_copies.append(core_copy(other.at[j], core_up.at[j], wide + j))
            up_copies[-1].start()
            if j:
                end_up(j - 1)

        for j in range(wide):
            ffn[...] += dot_nt(act[j], wu[:, j * features:(j + 1) * features])
            if j == 1:
                end_up(wide - 1)
        at_point("up")

        def pull_one(at, r):
            grad = ffn[at, :]
            normed = normed_one[at, :]
            pulled = norm_pull(grad, normed, root_one[at, :], g1)
            rounded = pulled.astype(BF16)
            dx_ref[at, :] = pulled
            d_attn_ref[at, :] = rounded
            small[3:4, :] += column_sum(grad * normed)
            small[4:5, :] += column_sum(grad)
            small[5:6, :] += column_sum(rounded.astype(F32))

        tiles(pull_one)
        live = lax.broadcasted_iota(jnp.int32, (rows, 1), 0) < limit
        d_merged_ref[...] = jnp.where(live, dot_nt(d_attn_ref[...], wo[...]), 0.0).astype(BF16)
        at_point("dense")

    low_rows = VMEM((rows, features), BF16)
    full_rows = VMEM((rows, features), F32)
    square_low = VMEM((features, features), BF16)
    pl.run_scoped(
        dense, square_low, VMEM((features, hidden), BF16), VMEM((hidden, features), BF16),
        low_rows, full_rows, VMEM((rows, 1), F32), low_rows, VMEM((wide, rows, features), BF16),
        VMEM((wide, rows, features), SLOPE), full_rows, VMEM((features, features), F32),
        VMEM((4, 4, 4) + UNIT, BF16),
    )


    def attention(
        dq_ref, far_ref, wk, wv, wq, acc, last, picked, buf, dko, dvo, dkr, dvr, out_far, other,
        tmp,
    ):
        for name, src, dst in (
            ("far", far_any, far_ref), ("wk", wk_any, wk), ("wv", wv_any, wv), ("wq", wq_any, wq),
        ):
            load(name, src, dst)
        square_copies = [
            core_copy(other.at[n], core_down.at[n], SQUARE + n) for n in range(4)
        ]

        def square(u):
            split_pieces(u, functools.partial(folded, tmp), other.at[u - SQUARE])
            square_copies[u - SQUARE].start()

        def end_square(u):
            square_copies[u - SQUARE].wait()
            if u in RIDERS:
                n = RIDERS.index(u)
                ride_core(n).wait()
                ride[n, core] = ride[n, core] + ride_core_in[n]
            add_core(u, core_down.at[u - SQUARE])
            begin(u, 0)

        def copy_pair(p, slot, owner):
            return remote(buf.at[p, owner], pair_in.at[p, slot], p_sends.at[p, slot],
                          p_recvs.at[p, slot], to_mate)

        def sum_pair(p):
            lanes = lanes_of(p)
            for slot, owner, keys_to, values_to in ((0, across, dkr, dvr), (1, seq, dko, dvo)):
                copy_pair(p, slot, diagonal if slot == 0 else mate).wait()
                for n, to in ((0, keys_to), (1, values_to)):
                    to[:, lanes] = (
                        buf[p, owner, n].astype(F32) + pair_in[p, slot, n].astype(F32)
                    ).astype(BF16)

        def heads():
            for n in range(2):
                picked[n, picks_count] = jnp.zeros((BLK, PAIR), F32)
                for edge in (0, own_blocks + 3):
                    acc[n, edge] = jnp.zeros((BLK, PAIR), F32)
            def one_pair(p, _):
                lanes = lanes_of(p)
                acc[:, 1:own_blocks + 3] = jnp.zeros((2, own_blocks + 2, BLK, PAIR), F32)
                last[...] = jnp.zeros_like(last)

                def step(i, _):
                    at = first_block + i
                    shared, both = key_blocks(tab_ref, end, p, i, at, last_row)
                    keys = gathered(k_ref, shared, both, low, lanes)
                    values = gathered(v_ref, shared, both, low, lanes)
                    query = split_pair(q_ref[rows_of(i), lanes], low)
                    grad = split_pair(d_merged_ref[rows_of(i), lanes], low)
                    scores = masked_scores(dot_nt(keys, query), mask_ref, i)
                    share_of = jnp.exp(scores - lse_ref[p, pl.ds(i, 1), :])
                    d_share = dot_nt(values, grad)
                    centre = jnp.sum(share_of * d_share, axis=0, keepdims=True)
                    d_scores = (share_of * (d_share - centre)).astype(BF16)
                    d_query = dot_tn(d_scores, keys) * SCALE
                    dq_ref[rows_of(i), lanes] = jnp.where(
                        low, d_query[:BLK], d_query[BLK:]).astype(BF16)
                    parts = (dot(d_scores, query), dot(share_of.astype(BF16), grad))
                    for n, part in enumerate(parts):
                        for slot in range(3):
                            acc[n, i + slot + 1] += part[slot * BLK:(slot + 1) * BLK]
                        for slot in range(2):
                            last[n, slot] += part[(3 + slot) * BLK:(4 + slot) * BLK]
                    for t in range(3):
                        one, two = (
                            prev_ref[lax.div(h, 3), i, lax.rem(h, 3) * 3 + t]
                            for h in (2 * p, 2 * p + 1))
                        for n, part in enumerate(parts):
                            picked[n, i * 3 + t] = part[(5 + t) * BLK:(6 + t) * BLK] + jnp.where(
                                low, picked[n, one], picked[n, two])
                    return 0

                lax.fori_loop(0, own_blocks, step, 0, unroll=own_blocks)

                def gather(owner, _):
                    first_owner = (owner == 0).astype(F32)
                    for inner in range(own_blocks):
                        block = owner * own_blocks + inner
                        window = jnp.minimum(
                            jnp.maximum(block - first_block + 2, 0), own_blocks + 3)
                        one, two = (
                            tail_ref[lax.div(h, 3), lax.rem(h, 3), block]
                            for h in (2 * p, 2 * p + 1))
                        for n in range(2):
                            total = acc[n, window] + jnp.where(low, picked[n, one], picked[n, two])
                            total = total + last[n, 1] * mask_ref[own_blocks, block]
                            if inner == 0:
                                total = total + last[n, 0] * first_owner
                            buf[p, owner, n, inner * BLK:(inner + 1) * BLK] = total.astype(BF16)
                    return 0

                lax.fori_loop(0, 4, gather, 0)
                copy_pair(p, 0, diagonal).start()
                copy_pair(p, 1, mate).start()

                @pl.when(p > 0)
                def _():
                    sum_pair(p - 1)

                for n in range(pairs):
                    @pl.when(p == n)
                    def _():
                        if n == 0:
                            end_square(OUT)
                        at_point(n)

                return 0

            lax.fori_loop(0, pairs, one_pair, 0)

        vector_pieces(0)
        ride_core(0).start()
        tmp[...] = dot_tn(merged_ref[...], d_attn_ref[...])
        square(OUT)
        heads()
        for name in ("far", "wk", "wv", "wq"):
            loading[name].wait()
        sum_pair(pairs - 1)
        at_point("sum")

        tmp[...] = dot_tn(x_ref[...], dko[...]) + dot_tn(far_ref[...], dkr[...])
        square(KEY)
        out_far[...] = (dot_nt(dkr[...], wk[...]) + dot_nt(dvr[...], wv[...])).astype(BF16)
        far = remote(out_far, in_far, far_sems.at[0], far_sems.at[1], to_y)
        far.start()
        end_square(KEY)
        at_point("far")
        tmp[...] = dot_tn(x_ref[...], dvo[...]) + dot_tn(far_ref[...], dvr[...])
        square(VALUE)
        at_point("v")
        tmp[...] = dot_tn(x_ref[...], dq_ref[...])
        square(QUERY)
        end_square(VALUE)
        late[...] = jnp.zeros_like(late)
        late[0:1, :] = column_sum(dq_ref[...].astype(F32))
        late[1:2, :] = column_sum(dvo[...].astype(F32)) + column_sum(dvr[...].astype(F32))
        vector_pieces(1)
        ride_core(1).start()
        end_square(QUERY)
        dx_ref[...] += (
            dot_nt(dko[...], wk[...]) + dot_nt(dvo[...], wv[...]) + dot_nt(dq_ref[...], wq[...])
        )
        at_point("x")
        for u, stage in EVENTS["end"]:
            if u == "far":
                far.wait()
                dx_ref[...] += in_far[...].astype(F32)
            else:
                finish(u, stage)

    pl.run_scoped(
        attention, low_rows, low_rows, square_low, square_low, square_low,
        VMEM((2, own_blocks + 4, BLK, PAIR), F32), VMEM((2, 2, BLK, PAIR), F32),
        VMEM((2, picks_count + 1, BLK, PAIR), F32), VMEM((pairs, 4, 2, rows, PAIR), BF16),
        low_rows, low_rows, low_rows, low_rows, low_rows, VMEM((4, 4, 4) + UNIT, BF16),
        VMEM((features, features), F32),
    )


SLOPE = BF16


def layer_tail(
    groups, table, prev, tail, mask, biases, up_bias, tokens, cotangent, out_weight,
    up_weight, down_weight, query, keys, values, key_weight, value_weight, query_weight, far_tokens,
):
    rows, features = tokens.shape
    hidden = up_weight.shape[1]
    own_blocks = rows // BLK
    pairs = features // PAIR
    share = features // (8 * groups)
    wide = hidden // features
    low = VMEM((rows, features), BF16)
    kv = VMEM((4 * own_blocks, BLK, features), BF16)
    line = jax.ShapeDtypeStruct((share, features), F32)
    any_space = pl.BlockSpec(memory_space=pl.ANY)
    in_smem = pl.BlockSpec(memory_space=pltpu.SMEM)
    dma = pltpu.SemaphoreType.DMA
    return pl.pallas_call(
        functools.partial(layer_kernel, rows, 128, own_blocks, groups),
        out_shape=(
            jax.ShapeDtypeStruct((rows, features), BF16),
            jax.ShapeDtypeStruct((rows, features), F32), line, line, line, line,
            jax.ShapeDtypeStruct((share, hidden), F32),
            jax.ShapeDtypeStruct((wide * share, features), F32),
            jax.ShapeDtypeStruct((32, 128), F32),
        ),
        in_specs=[in_smem] * 4 + [whole_vmem()] * 7 + [any_space] * 12,
        out_specs=(whole_vmem(),) * 9,
        scratch_shapes=[
            VMEM((12, 4 * groups) + UNIT, BF16),
            VMEM((12, 4 * groups - 1) + UNIT, BF16),
            VMEM((4, 4, 4) + UNIT, BF16),
            VMEM((4, 4, 4) + UNIT, BF16),
            VMEM((pairs, 2, 2, rows, PAIR), BF16),
            low,
            VMEM((16, features), F32),
            VMEM((8, features), F32),
            VMEM((2, 2, 4 * groups, 16, 128), F32),
            VMEM((2, 4 * groups - 1, 16, 128), F32),
            VMEM((2, 4 * groups, 16, 128), F32),
            low, low, low, low, low, kv, kv, VMEM((pairs, own_blocks, PAIR), F32),
            dma((13,)), dma((12, groups + 1)), dma((12, groups + 1)), dma((12,)), dma((12,)),
            dma((pairs, 2)), dma((pairs, 2)), dma((2, groups + 2)), dma((2, groups + 2)),
            dma((2,)),
        ],
        compiler_params=pltpu.CompilerParams(
            collective_id=3, has_side_effects=True, vmem_limit_bytes=LIMIT
        ),
        name="layer_tail",
    )(
        table, prev, tail, mask, *biases, up_bias, tokens, cotangent, out_weight, up_weight,
        down_weight, query, keys, values, key_weight, value_weight, query_weight, far_tokens,
    )


def finish_kernel(groups, vec_ref, *refs):
    count = len(refs) - 9
    given, out, vectors = refs[:count // 2], refs[count // 2:count], refs[count:]
    for src, dst in zip(given, out):
        dst[...] = src[...]
    share = vectors[0].shape[0]
    for n in range(8):
        vectors[n][...] = vec_ref[n if n < 6 else n + 10, 0:share]
    shard = lax.axis_index("dp") * 4 + lax.axis_index("seq")
    mine = vec_ref[pl.ds(8 + shard // (2 * groups), 1), :]
    vectors[8][...] = mine[0, 0:vectors[8].shape[0]]


STEPS = 2


def whole(shape):
    return pl.BlockSpec(shape, lambda i: (0,) * len(shape))


def hand_out(groups, vectors, arrays):
    features = arrays[0].shape[1]
    share = features // (8 * groups)
    wide = arrays[-1].shape[0] // share
    shapes = [jax.ShapeDtypeStruct(a.shape, a.dtype) for a in arrays]
    specs = [
        pl.BlockSpec((a.shape[0] // STEPS, a.shape[1]), lambda i: (i, 0))
        if a.shape[0] % (16 * STEPS) == 0 else whole(a.shape) for a in arrays
    ]
    lines = [jax.ShapeDtypeStruct((share,), F32)] * 8 + [jax.ShapeDtypeStruct((wide * share,), F32)]
    return pl.pallas_call(
        functools.partial(finish_kernel, groups),
        out_shape=tuple(shapes + lines),
        grid=(STEPS,),
        in_specs=[whole((32, 128))] + specs,
        out_specs=tuple(specs) + (whole((share,)),) * 8 + (whole((wide * share,)),),
        name="hand_out",
    )(vectors, *arrays)


def layer_norm(values, gain, shift):
    center = jnp.mean(values, axis=-1, keepdims=True)
    centered = values - center
    variance = jnp.mean(centered * centered, axis=-1, keepdims=True)
    inv_root = lax.rsqrt(variance + NORM_EPS)
    normed = centered * inv_root
    return (normed * gain + shift, normed, inv_root)


def norm_back(grad_out, normed, inv_root, gain):
    d_normed = grad_out * gain
    grad_in = inv_root * (
        d_normed
        - jnp.mean(d_normed, axis=-1, keepdims=True)
        - normed * jnp.mean(d_normed * normed, axis=-1, keepdims=True)
    )
    return (grad_in, jnp.sum(grad_out * normed, axis=0), jnp.sum(grad_out, axis=0))


def on_device(
    groups,
    tokens, filled_blocks, random_blocks, query_weight, query_bias, key_weight, value_weight,
    value_bias, out_weight, out_bias, attn_gain, attn_shift, up_weight, up_bias, down_weight,
    down_bias, ffn_gain, ffn_shift, cotangent,
):
    row_count, feature_count = tokens.shape
    filled = filled_blocks[0]
    place = lax.axis_index("seq") * row_count + jnp.arange(row_count, dtype=jnp.int32)
    live_tokens = (place < filled * BLK).astype(F32)[:, None]

    query, keys, values, far_tokens, table, prev, tail, mask = gather_project(
        filled_blocks, tokens,
        random_blocks[0].transpose(1, 2, 0).reshape(-1, 1, random_blocks.shape[1]), query_weight, key_weight, value_weight, query_bias,
        value_bias)
    keys, values = (t.reshape(-1, BLK, feature_count) for t in (keys, values))
    if groups:
        *arrays, vectors = layer_tail(
            groups, table, prev, tail, mask,
            (out_bias, attn_gain, attn_shift, down_bias, ffn_gain, ffn_shift), up_bias[None],
            tokens, cotangent, out_weight, up_weight, down_weight, query, keys, values,
            key_weight, value_weight, query_weight, far_tokens)
        (result, grad_tokens, gq, gk, gv, go, up, down, g2, s2, bd, g1, s1, bo, bq, bv,
         bu) = hand_out(groups, vectors, arrays)
        return (
            result, grad_tokens, gq, bq, gk, gv, bv, go, bo, g1, s1, up, bu, down, bd, g2, s2)

    merged, lse = attention_forward(table, filled_blocks, mask, query, keys, values)
    attn = dot(merged, out_weight) + out_bias
    first, normed_one, root_one = layer_norm(tokens.astype(F32) + attn, attn_gain, attn_shift)
    first_low = first.astype(BF16)
    hidden = dot(first_low, up_weight) + up_bias
    act, gelu_pull = jax.vjp(jax.nn.gelu, hidden)
    act_low = act.astype(BF16)
    ffn = dot(act_low, down_weight) + down_bias
    result, normed_two, root_two = layer_norm(first + ffn, ffn_gain, ffn_shift)
    grad_result = cotangent.astype(F32) * live_tokens
    d_sum_two, grad_ffn_gain, grad_ffn_shift = norm_back(
        grad_result, normed_two, root_two, ffn_gain
    )
    d_ffn = d_sum_two.astype(BF16)
    grad_down_bias = jnp.sum(d_ffn, axis=0, dtype=F32)
    grad_down_weight = dot_tn(act_low, d_ffn)
    d_act = dot_nt(d_ffn, down_weight)
    d_hidden = gelu_pull(d_act)[0].astype(BF16)
    grad_up_bias = jnp.sum(d_hidden, axis=0, dtype=F32)
    grad_up_weight = dot_tn(first_low, d_hidden)
    d_first = d_sum_two + dot_nt(d_hidden, up_weight)
    d_sum_one, grad_attn_gain, grad_attn_shift = norm_back(d_first, normed_one, root_one, attn_gain)
    d_attn = d_sum_one.astype(BF16)
    grad_out_bias = jnp.sum(d_attn, axis=0, dtype=F32)
    grad_out_weight = dot_tn(merged, d_attn)
    d_merged = dot_nt(d_attn, out_weight).astype(BF16)

    d_query, d_keys, d_values = attention_backward(
        table, filled_blocks, mask, query, keys, values, d_merged, lse
    )
    grad_tokens, dk_own, dv_own, dk_far, dv_far = exchange(
        d_keys, d_values, d_query, d_sum_one, query_weight, key_weight, value_weight
    )
    grad_query_weight = dot_tn(tokens, d_query)
    grad_query_bias = jnp.sum(d_query, axis=0, dtype=F32)
    grad_key_weight = dot_tn(tokens, dk_own) + dot_tn(far_tokens, dk_far)
    grad_value_weight = dot_tn(tokens, dv_own) + dot_tn(far_tokens, dv_far)
    grad_value_bias = jnp.sum(dv_own, axis=0, dtype=F32) + jnp.sum(dv_far, axis=0, dtype=F32)

    square = (grad_query_weight, grad_key_weight, grad_value_weight, grad_out_weight)
    vectors = (
        grad_query_bias, grad_value_bias, grad_out_bias, grad_attn_gain, grad_attn_shift,
        grad_down_bias, grad_ffn_gain, grad_ffn_shift,
    )
    square, up, down, vectors, up_sum = summed_anywhere(
        square, grad_up_weight, grad_down_weight, vectors, grad_up_bias)
    return (
        result.astype(BF16), grad_tokens, square[0], vectors[0], square[1], square[2], vectors[1],
        square[3], vectors[2], vectors[3], vectors[4], up, up_sum, down, vectors[5], vectors[6],
        vectors[7],
    )


def solution(mesh):
    both = P(("dp", "seq"), None)
    line = P(("dp", "seq"))
    placed = (both, P("dp"), P("dp", None, "seq", None)) + (P(),) * 15 + (both,)
    groups = 4 if mesh.shape["dp"] == 8 and mesh.shape["seq"] == 4 else 0
    return jax.shard_map(
        functools.partial(on_device, groups),
        mesh=mesh,
        in_specs=placed,
        out_specs=(
            both, both, both, line, both, both, line, both, line, line, line, both, line, both,
            line, line, line,
        ),
        check_vma=False,
    )
```

```python
import functools

import jax
import jax.numpy as jnp
from jax import lax
from jax.experimental import pallas as pl
from jax.experimental.pallas import tpu as pltpu
from jax.sharding import PartitionSpec as P

HEAD_DIM = 64
BLK = 64
PAIR = 2 * HEAD_DIM
TABLE = 8
NORM_EPS = 1e-05
MASKED = -1e30
SCALE = HEAD_DIM ** (-0.5)
MESH = pl.DeviceIdType.MESH
BF16 = jnp.bfloat16
F32 = jnp.float32
VMEM = pltpu.VMEM
LIMIT = 63 << 20


def whole_vmem():
    return pl.BlockSpec(memory_space=pltpu.VMEM)


def dot(left, right):
    return jnp.dot(left, right, preferred_element_type=F32)


def dot_nt(left, right):
    return lax.dot_general(left, right, (((1,), (1,)), ((), ())), preferred_element_type=F32)


def dot_tn(left, right):
    return lax.dot_general(left, right, (((0,), (0,)), ((), ())), preferred_element_type=F32)


def tables_of(tab_out, filled, first_block, each, prev_out, tail_out, mask_out):
    groups, blocks, width = tab_out.shape
    slot_blocks = width
    none = blocks * each
    lane = lax.broadcasted_iota(jnp.int32, (blocks, width), 1)
    row = lax.broadcasted_iota(jnp.int32, (blocks, width), 0)
    pick = lax.rem(lane, each)
    key_row = lax.broadcasted_iota(jnp.int32, (slot_blocks, width), 0)
    key_pick = lax.rem(lax.broadcasted_iota(jnp.int32, (slot_blocks, width), 1), each)
    for g in range(groups):
        table = tab_out[g]
        prev = jnp.full((blocks, width), -1, jnp.int32)
        for shift in range(1 - each, each):
            moved = pltpu.roll(table, (-shift) % width, axis=1)
            inside = (pick + shift >= 0) & (pick + shift < each)
            for i in range(blocks - 1):
                same = (moved[i:i + 1] == table) & (row > i) & inside
                prev = jnp.maximum(prev, jnp.where(same, i * each + pick + shift, -1))
        prev = jnp.where(prev < 0, none, prev)
        prev_out[g] = jnp.where(lane == width - 1, filled - 1, prev)
        tail = jnp.full((slot_blocks, width), -1, jnp.int32)
        for i in range(blocks):
            tail = jnp.maximum(tail, jnp.where(table[i:i + 1] == key_row, i * each + key_pick, -1))
        best = tail
        for shift in range(1, each):
            best = jnp.maximum(best, pltpu.roll(tail, width - shift, axis=1))
        turned = jnp.where(best < 0, none, best).astype(F32).T.astype(jnp.int32)
        for h in range(3):
            tail_out[g, h:h + 1, :] = turned[h * each:h * each + 1, :]
        tail_out[g, 3:blocks, :] = jnp.full((blocks - 3, width), none, jnp.int32)
    at = first_block + row
    window = at + lane - 1
    ok = jnp.where(
        lane < 3, ((window >= 0) & (window < filled)).astype(jnp.int32),
        jnp.where(lane == 3, (at >= 2).astype(jnp.int32),
                  (jnp.abs(at - (filled - 1)) > 1).astype(jnp.int32)))
    mask_out[0:blocks, :] = jnp.where(ok == 1, 0.0, MASKED)
    mask_out[blocks:2 * blocks, :] = (lane == filled - 1).astype(F32)


def gather_kernel(
    rows, width, filled_ref, x_ref, picks_ref, wq_any, wk_any, wv_any, qb_ref, vb_ref,
    q_any, k_any, v_any, far_any, tab_out, prev_out, tail_out, mask_out,
    wq_ref, wk_ref, wv_ref, q_ref, k_ref, v_ref,
    tab_ref, land, tab_land, loads, stores, sends, recvs, tab_sends, tab_recvs,
):
    parts = 4
    part = rows // parts
    dp, me = lax.axis_index("dp"), lax.axis_index("seq")
    mate, across, diagonal = (lax.bitwise_xor(me, bit) for bit in (1, 2, 3))
    weights = [
        pltpu.make_async_copy(src, dst, loads.at[n])
        for n, (src, dst) in enumerate(((wq_any, wq_ref), (wk_any, wk_ref), (wv_any, wv_ref)))
    ]
    for copy in weights:
        copy.start()
    barrier = pltpu.get_barrier_semaphore()
    for other in (mate, across, diagonal):
        pl.semaphore_signal(barrier, inc=1, device_id=(dp, other), device_id_type=MESH)
    heads_here, each, _, blocks = picks_ref.shape
    chosen = picks_ref[...].reshape(heads_here * each, blocks).astype(F32)
    chosen = jnp.concatenate(
        [chosen, jnp.zeros((heads_here * each, 128 - blocks), F32)], axis=1)
    chosen = jnp.concatenate([chosen, jnp.zeros((128 - heads_here * each, 128), F32)], axis=0)
    tab_ref[...] = chosen.T[0:blocks].astype(jnp.int32)
    pl.semaphore_wait(barrier, 3)

    def send(src, dst, slot, target):
        copy = pltpu.make_async_remote_copy(
            src_ref=src, dst_ref=dst, send_sem=sends.at[slot], recv_sem=recvs.at[slot],
            device_id=(dp, target), device_id_type=MESH,
        )
        copy.start()
        return copy

    tables = []
    own_blocks = tab_ref.shape[0] // 4
    for slot, other in enumerate((mate, across, diagonal)):
        copy = pltpu.make_async_remote_copy(
            src_ref=tab_ref.at[pl.ds(pl.multiple_of(other * own_blocks, 8), own_blocks)],
            dst_ref=tab_land.at[slot], send_sem=tab_sends.at[slot], recv_sem=tab_recvs.at[slot],
            device_id=(dp, other), device_id_type=MESH,
        )
        copy.start()
        tables.append(copy)
    far = [
        send(x_ref.at[pl.ds(r * part, part)], land.at[0, pl.ds(r * part, part)], r, across)
        for r in range(parts)
    ]
    near = send(x_ref, land.at[1], parts, mate)
    stored = []

    def store(src, dst, start, count):
        at = pl.ds(pl.multiple_of(start, part), count)
        copy = pltpu.make_async_copy(src.at[at], dst.at[at], stores.at[len(stored)])
        copy.start()
        stored.append(copy)

    def keys_values(x, at):
        k_ref[pl.ds(at, width), :] = dot(x, wk_ref[...]).astype(BF16)
        v_ref[pl.ds(at, width), :] = (dot(x, wv_ref[...]) + vb_ref[...][None]).astype(BF16)

    for copy in weights:
        copy.wait()

    def own(r, _):
        at = pl.multiple_of(r * width, width)
        x = x_ref[pl.ds(at, width), :]
        q_ref[pl.ds(at, width), :] = (
            (dot(x, wq_ref[...]) + qb_ref[...][None]).astype(BF16) * jnp.asarray(SCALE, BF16)
        )
        keys_values(x, pl.multiple_of(me * rows + at, width))
        return 0

    lax.fori_loop(0, rows // width, own, 0)
    store(q_ref, q_any, 0, rows)
    store(k_ref, k_any, me * rows, rows)
    store(v_ref, v_any, me * rows, rows)

    def block(slot, owner, start, count):
        def step(r, _):
            at = pl.multiple_of(start + r * width, width)
            keys_values(land[slot, pl.ds(at, width), :], pl.multiple_of(owner * rows + at, width))
            return 0

        lax.fori_loop(0, count // width, step, 0)
        store(k_ref, k_any, owner * rows + start, count)
        store(v_ref, v_any, owner * rows + start, count)

    near.wait()
    block(1, mate, 0, rows)
    for copy in tables:
        copy.wait()
    tab_out[pl.ds(me, 1)] = tab_ref[pl.ds(pl.multiple_of(me * own_blocks, 8), own_blocks)][None]
    for slot, other in enumerate((mate, across, diagonal)):
        tab_out[pl.ds(other, 1)] = tab_land[slot][None]
    tables_of(tab_out, filled_ref[0], me * own_blocks, each, prev_out, tail_out, mask_out)
    relayed = []
    for r in range(parts):
        far[r].wait()
        piece = pl.ds(r * part, part)
        relayed.append(send(land.at[0, piece], land.at[2, piece], parts + 1 + r, mate))
        store(land.at[0], far_any, r * part, part)
        block(0, across, r * part, part)
        if r:
            relayed[r - 1].wait()
            block(2, diagonal, (r - 1) * part, part)
    relayed[-1].wait()
    block(2, diagonal, (parts - 1) * part, part)
    for copy in stored:
        copy.wait()


def gather_project(
    filled, tokens, chosen, query_weight, key_weight, value_weight, query_bias, value_bias,
):
    rows, features = tokens.shape
    own_blocks = rows // BLK
    slot_blocks = chosen.shape[3]
    copies = 4 + 1 + 4
    any_space = pl.BlockSpec(memory_space=pl.ANY)
    low = jax.ShapeDtypeStruct((rows, features), BF16)
    slot = jax.ShapeDtypeStruct((4 * rows, features), BF16)
    table = jax.ShapeDtypeStruct((4, own_blocks, 128), jnp.int32)
    dma = pltpu.SemaphoreType.DMA
    return pl.pallas_call(
        functools.partial(gather_kernel, rows, 128),
        out_shape=(
            low, slot, slot, low, table, table, table,
            jax.ShapeDtypeStruct((2 * own_blocks, 128), F32),
        ),
        in_specs=[pl.BlockSpec(memory_space=pltpu.SMEM)] + [whole_vmem()] * 2 + [any_space] * 3
        + [whole_vmem()] * 2,
        out_specs=(any_space,) * 4 + (whole_vmem(),) * 4,
        scratch_shapes=[
            VMEM((features, features), BF16),
            VMEM((features, features), BF16),
            VMEM((features, features), BF16),
            VMEM((rows, features), BF16),
            VMEM((4 * rows, features), BF16),
            VMEM((4 * rows, features), BF16),
            VMEM((slot_blocks, 128), jnp.int32),
            VMEM((3, rows, features), BF16),
            VMEM((3, own_blocks, 128), jnp.int32),
            dma((3,)), dma((25,)), dma((copies,)), dma((copies,)), dma((3,)), dma((3,)),
        ],
        compiler_params=pltpu.CompilerParams(
            collective_id=0, has_side_effects=True, vmem_limit_bytes=LIMIT
        ),
        name="gather_project",
    )(filled, tokens, chosen, query_weight, key_weight, value_weight, query_bias, value_bias)


def key_blocks(tab_ref, end, pair, i, at, last_row):
    def chosen(head, t):
        group, inner = lax.div(head, 3), lax.rem(head, 3)
        return tab_ref[group, i, inner * 3 + t]

    head = 2 * pair
    both = [(chosen(head, t), chosen(head + 1, t)) for t in range(3)]
    shared = [
        jnp.maximum(at - 1, 0), at, jnp.minimum(at + 1, last_row), jnp.int32(0), end,
    ]
    return shared, both


def rows_of(block):
    return pl.ds(pl.multiple_of(block * BLK, BLK), BLK)


def lanes_low(rows):
    return lax.broadcasted_iota(jnp.int32, (rows, PAIR), 1) < HEAD_DIM


def split_pair(x, low):
    zero = jnp.zeros_like(x)
    return jnp.concatenate([jnp.where(low, x, zero), jnp.where(low, zero, x)], axis=0)


def gathered(ref, shared, both, low, lanes=slice(None)):
    tiles = [ref[b, :, lanes] for b in shared]
    for first, second in both:
        tiles.append(jnp.where(low, ref[first, :, lanes], ref[second, :, lanes]))
    return jnp.concatenate(tiles, axis=0)


def masked_scores(scores, mask_ref, i):
    parts = [scores[n * BLK:(n + 1) * BLK] + mask_ref[i, n] for n in range(5)]
    return jnp.concatenate(parts + [scores[5 * BLK:]], axis=0)


def attend(keys, values, query, mask_ref, i, low):
    scores = masked_scores(dot_nt(keys, query), mask_ref, i)
    highest = jnp.max(scores, axis=0, keepdims=True)
    weights = jnp.exp(scores - highest)
    total = jnp.sum(weights, axis=0, keepdims=True)
    share = (weights * (1.0 / total)).astype(BF16)
    output = dot_tn(share, values)
    return jnp.where(low, output[:BLK], output[BLK:]), highest + jnp.log(total)


def forward_kernel(own_blocks, tab_ref, filled_ref, mask_ref, q_ref, k_ref, v_ref, out_ref, lse_ref):
    pair = pl.program_id(0)
    filled = filled_ref[0]
    first_block = lax.axis_index("seq") * own_blocks
    last_row = k_ref.shape[0] - 1
    low = lanes_low(BLK)

    def step(i, _):
        at = first_block + i
        shared, both = key_blocks(tab_ref, filled - 1, pair, i, at, last_row)
        keys = gathered(k_ref, shared, both, low)
        values = gathered(v_ref, shared, both, low)
        query = split_pair(q_ref[rows_of(i), :], low)
        merged, lse = attend(keys, values, query, mask_ref, i, low)
        out_ref[rows_of(i), :] = jnp.where(at < filled, merged, 0.0).astype(BF16)
        lse_ref[0, pl.ds(i, 1), :] = lse
        return 0

    lax.fori_loop(0, own_blocks, step, 0, unroll=own_blocks)


def attention_forward(table, filled, mask, query, keys, values):
    rows, features = query.shape
    own_blocks = rows // BLK
    slot_blocks = keys.shape[0]
    pairs = features // PAIR
    column = lambda n: pl.BlockSpec((n, PAIR), lambda p, *_: (0, p))
    blocks = lambda n: pl.BlockSpec((n, BLK, PAIR), lambda p, *_: (0, 0, p))
    return pl.pallas_call(
        functools.partial(forward_kernel, own_blocks),
        out_shape=(
            jax.ShapeDtypeStruct((rows, features), BF16),
            jax.ShapeDtypeStruct((pairs, own_blocks, PAIR), F32),
        ),
        grid_spec=pltpu.PrefetchScalarGridSpec(
            num_scalar_prefetch=3,
            grid=(pairs,),
            in_specs=[column(rows), blocks(slot_blocks), blocks(slot_blocks)],
            out_specs=(column(rows), pl.BlockSpec((1, own_blocks, PAIR), lambda p, *_: (p, 0, 0))),
        ),
        compiler_params=pltpu.CompilerParams(vmem_limit_bytes=LIMIT),
        name="attention_forward",
    )(table, filled, mask, query, keys, values)


def backward_kernel(
    own_blocks, tab_ref, filled_ref, mask_ref, q_ref, k_ref, v_ref, g_ref, lse_ref,
    dq_ref, dk_ref, dv_ref, dk_sum, dv_sum,
):
    pair = pl.program_id(0)
    filled = filled_ref[0]
    first_block = lax.axis_index("seq") * own_blocks
    last_row = k_ref.shape[0] - 1
    low = lanes_low(BLK)
    dk_sum[...] = jnp.zeros_like(dk_sum)
    dv_sum[...] = jnp.zeros_like(dv_sum)

    def step(i, _):
        at = first_block + i
        shared, both = key_blocks(tab_ref, filled - 1, pair, i, at, last_row)
        keys = gathered(k_ref, shared, both, low)
        values = gathered(v_ref, shared, both, low)
        query = split_pair(q_ref[rows_of(i), :], low)
        grad = split_pair(jnp.where(at < filled, g_ref[rows_of(i), :], jnp.zeros((), BF16)), low)
        scores = masked_scores(dot_nt(keys, query), mask_ref, i)
        share = jnp.exp(scores - lse_ref[0, pl.ds(i, 1), :])
        d_share = dot_nt(values, grad)
        centre = jnp.sum(share * d_share, axis=0, keepdims=True)
        d_scores = (share * (d_share - centre)).astype(BF16)
        d_query = dot_tn(d_scores, keys) * SCALE
        dq_ref[rows_of(i), :] = jnp.where(low, d_query[:BLK], d_query[BLK:]).astype(BF16)
        for total, part in ((dk_sum, dot(d_scores, query)), (dv_sum, dot(share.astype(BF16), grad))):
            for slot, block in enumerate(shared):
                total[rows_of(block), :] += part[slot * BLK:(slot + 1) * BLK]
            for t, (one, two) in enumerate(both):
                tile = part[(5 + t) * BLK:(6 + t) * BLK]
                total[rows_of(one), :] += jnp.where(low, tile, 0.0)
                total[rows_of(two), :] += jnp.where(low, 0.0, tile)
        return 0

    lax.fori_loop(0, own_blocks, step, 0, unroll=own_blocks)
    dk_ref[...] = dk_sum[...].astype(BF16)
    dv_ref[...] = dv_sum[...].astype(BF16)


def attention_backward(table, filled, mask, query, keys, values, grad, lse):
    rows, features = query.shape
    slot_blocks = keys.shape[0]
    slot_rows = slot_blocks * BLK
    own_blocks = rows // BLK
    pairs = features // PAIR
    blocks = lambda n: pl.BlockSpec((n, BLK, PAIR), lambda p, *_: (0, 0, p))
    column = lambda n: pl.BlockSpec((n, PAIR), lambda p, *_: (0, p))
    return pl.pallas_call(
        functools.partial(backward_kernel, own_blocks),
        out_shape=(
            jax.ShapeDtypeStruct((rows, features), BF16),
            jax.ShapeDtypeStruct((slot_rows, features), BF16),
            jax.ShapeDtypeStruct((slot_rows, features), BF16),
        ),
        grid_spec=pltpu.PrefetchScalarGridSpec(
            num_scalar_prefetch=3,
            grid=(pairs,),
            in_specs=[
                column(rows), blocks(slot_blocks), blocks(slot_blocks), column(rows),
                pl.BlockSpec((1, own_blocks, PAIR), lambda p, *_: (p, 0, 0)),
            ],
            out_specs=(column(rows), column(slot_rows), column(slot_rows)),
            scratch_shapes=[VMEM((slot_rows, PAIR), F32), VMEM((slot_rows, PAIR), F32)],
        ),
        compiler_params=pltpu.CompilerParams(vmem_limit_bytes=LIMIT),
        name="attention_backward",
    )(table, filled, mask, query, keys, values, grad, lse)


def exchange_kernel(
    rows, width, dk_ref, dv_ref, dq_ref, base_ref, wq_ref, wk_ref, wv_ref,
    dx_ref, dko_ref, dvo_ref, dkr_ref, dvr_ref,
    land, out_far, in_far, sends, recvs,
):
    dp, me = lax.axis_index("dp"), lax.axis_index("seq")
    mate, across, diagonal = (lax.bitwise_xor(me, bit) for bit in (1, 2, 3))
    barrier = pltpu.get_barrier_semaphore()
    for other in (mate, across):
        pl.semaphore_signal(barrier, inc=1, device_id=(dp, other), device_id_type=MESH)
    pl.semaphore_wait(barrier, 2)

    def send(src, dst, slot, target):
        copy = pltpu.make_async_remote_copy(
            src_ref=src, dst_ref=dst, send_sem=sends.at[slot], recv_sem=recvs.at[slot],
            device_id=(dp, target), device_id_type=MESH,
        )
        copy.start()
        return copy

    def owned(index):
        return pl.ds(pl.multiple_of(index * rows, rows), rows)

    copies = [
        send(ref.at[owned(owner)], land.at[slot], slot, mate)
        for slot, (ref, owner) in enumerate(
            ((dk_ref, diagonal), (dv_ref, diagonal), (dk_ref, mate), (dv_ref, mate))
        )
    ]

    def summed(ref, owner, slot, to_ref):
        to_ref[...] = (ref[owned(owner), :].astype(F32) + land[slot].astype(F32)).astype(BF16)

    copies[0].wait()
    summed(dk_ref, across, 0, dkr_ref)
    copies[1].wait()
    summed(dv_ref, across, 1, dvr_ref)

    steps = rows // width
    for r in range(steps):
        at = pl.ds(r * width, width)
        out_far[at, :] = (
            dot_nt(dkr_ref[at, :], wk_ref[...]) + dot_nt(dvr_ref[at, :], wv_ref[...])
        ).astype(BF16)
    far = send(out_far, in_far, 4, across)
    copies[2].wait()
    summed(dk_ref, me, 2, dko_ref)
    copies[3].wait()
    summed(dv_ref, me, 3, dvo_ref)

    def one(r, _):
        at = pl.ds(pl.multiple_of(r * width, width), width)
        dx_ref[at, :] = (
            base_ref[at, :]
            + dot_nt(dq_ref[at, :], wq_ref[...])
            + dot_nt(dko_ref[at, :], wk_ref[...])
            + dot_nt(dvo_ref[at, :], wv_ref[...])
        )
        return 0

    lax.fori_loop(0, steps, one, 0)
    far.wait()
    dx_ref[...] += in_far[...].astype(F32)


def exchange(d_keys, d_values, d_query, base, query_weight, key_weight, value_weight):
    rows, features = d_query.shape
    small = jax.ShapeDtypeStruct((rows, features), BF16)
    return pl.pallas_call(
        functools.partial(exchange_kernel, rows, 128),
        out_shape=(jax.ShapeDtypeStruct((rows, features), F32), small, small, small, small),
        in_specs=[whole_vmem()] * 7,
        out_specs=(whole_vmem(),) * 5,
        scratch_shapes=[
            VMEM((4, rows, features), BF16),
            VMEM((rows, features), BF16),
            VMEM((rows, features), BF16),
            pltpu.SemaphoreType.DMA((5,)),
            pltpu.SemaphoreType.DMA((5,)),
        ],
        compiler_params=pltpu.CompilerParams(
            collective_id=1, has_side_effects=True, vmem_limit_bytes=LIMIT
        ),
        name="exchange",
    )(d_keys, d_values, d_query, base, query_weight, key_weight, value_weight)


def summed_anywhere(square, up, down, vectors, up_bias):
    def one(g):
        return lax.psum_scatter(g, ("dp", "seq"), scatter_dimension=0, tiled=True)

    return [one(g) for g in square], one(up), one(down), [one(v) for v in vectors], one(up_bias)


GELU_A = 0.044715
GELU_C = 0.7978845608028654
UNIT = (48, 384)
ORDERS = (
    "yxz", "yxz", "zxy", "zxy", "yxz", "xzy", "xyz", "xzy", "xyz", "xzy", "xzy", "yxz",
)
UP, SQUARE = 4, 8
OUT, KEY, VALUE, QUERY = 8, 9, 10, 11
RIDERS = (OUT, QUERY)
EVENTS = {
    "up": ((0, 0),),
    "dense": (),
    0: ((5, 0), (1, 0), (2, 0)),
    1: ((6, 0), (4, 0)),
    2: (),
    3: ((7, 0), (3, 0), (0, 1), (6, 1)),
    4: (),
    5: ((5, 1), (8, 0)),
    "sum": ((1, 1),),
    "far": ((2, 1), (7, 1), (4, 1), (5, 2), (0, 2), (3, 1)),
    "v": ((8, 1), (6, 2)),
    "x": (),
    "y": ((1, 2),),
    "end": ((11, 0), (9, 0), (4, 2), (8, 2), (10, 0), (11, 1), (9, 1), (10, 1), ("far", 0), (2, 2), (7, 2), (3, 2), (9, 2), (11, 2), (10, 2)),
}


def normed_rows(values):
    center = jnp.mean(values, axis=-1, keepdims=True)
    centered = values - center
    variance = jnp.mean(centered * centered, axis=-1, keepdims=True)
    inv_root = lax.rsqrt(variance + NORM_EPS)
    return centered * inv_root, inv_root


def norm_pull(grad_out, normed, inv_root, gain):
    d_normed = grad_out * gain
    return inv_root * (
        d_normed
        - jnp.mean(d_normed, axis=-1, keepdims=True)
        - normed * jnp.mean(d_normed * normed, axis=-1, keepdims=True)
    )


def column_sum(values):
    return jnp.sum(values, axis=0, keepdims=True)


def layer_kernel(
    rows, tile, own_blocks, groups, tab_ref, prev_ref, tail_ref, mask_ref, bo_ref, g1_ref, s1_ref,
    bd_ref, g2_ref, s2_ref, bu_ref,
    x_any, cot_any, wo_any, wu_any, wd_any, q_any, k_any, v_any, wk_any, wv_any, wq_any,
    far_any,
    result_ref, dx_ref, gq_ref, gk_ref, gv_ref, go_ref, up_ref, down_ref, vec_ref,
    work, land, core_down, core_up, pair_in, in_far, small, late,
    ride, ride_land, ride_core_in,
    x_ref, merged_ref, d_attn_ref, d_merged_ref, q_ref, k_ref, v_ref, lse_ref,
    loads, sends, recvs, c_sends, c_recvs, p_sends, p_recvs, r_sends, r_recvs, far_sems,
):
    features = x_ref.shape[1]
    hidden = bu_ref.shape[1]
    wide = hidden // features
    pairs = features // PAIR
    picks_count = own_blocks * 3
    share = features // (8 * groups)
    shards = 4 * groups
    half = features // 2
    dp, seq = lax.axis_index("dp"), lax.axis_index("seq")
    x, z = lax.rem(dp, 2), dp // 2
    core, y = lax.rem(seq, 2), seq // 2
    mate, across, diagonal = (lax.bitwise_xor(seq, bit) for bit in (1, 2, 3))
    end = prev_ref[0, 0, 127]
    first_block = seq * own_blocks
    low = lanes_low(BLK)
    to_mate, to_y = (dp, mate), (dp, across)
    place_of = {"x": (x, 2), "y": (y, 2), "z": (z, groups)}

    def device(axis, index):
        if axis == "x":
            return (2 * z + index, seq)
        if axis == "y":
            return (dp, 2 * index + core)
        return (2 * index + x, seq)

    neighbours = [to_mate, to_y, device("x", 1 - x)] + [
        device("z", lax.rem(z + step, groups)) for step in range(1, groups)]

    loading = {}

    def load(name, src, dst):
        copy = pltpu.make_async_copy(src, dst, loads.at[len(loading)])
        copy.start()
        loading[name] = copy

    def remote(src, dst, one, two, target):
        return pltpu.make_async_remote_copy(
            src_ref=src, dst_ref=dst, send_sem=one, recv_sem=two, device_id=target,
            device_id_type=MESH,
        )

    def lanes_of(p):
        return pl.ds(pl.multiple_of(p * PAIR, PAIR), PAIR)

    def columns(j):
        return pl.ds(pl.multiple_of(j * features, features), features)

    def tiles(body):
        def step(r, _):
            body(pl.ds(pl.multiple_of(r * tile, tile), tile), r)
            return 0

        lax.fori_loop(0, rows // tile, step, 0)


    def index_of(u, at_x, at_y, at_z):
        at = {"x": at_x, "y": at_y, "z": at_z}
        flat = 0
        for axis in ORDERS[u]:
            flat = flat * place_of[axis][1] + at[axis]
        return flat

    def shard_of(s):
        return s // 4, lax.rem(s // 2, 2), lax.rem(s, 2)

    def stage_of(u, stage):
        sizes = [place_of[axis][1] for axis in ORDERS[u]] + [1]
        base, offset, sem, block = 0, 0, 0, shards
        for n, axis in enumerate(ORDERS[u]):
            block = block // sizes[n]
            if n == stage:
                return axis, place_of[axis][0], sizes[n], block, base, offset, sem
            base = base + place_of[axis][0] * block
            offset += (sizes[n] - 1) * block
            sem += sizes[n] - 1
        return None

    def stage_copies(u, stage):
        axis, mine, size, block, base, offset, sem = stage_of(u, stage)
        copies = []
        for step in range(1, size):
            index = lax.rem(mine + step, size)
            copies.append(remote(
                work.at[u, pl.ds(base + index * block, block)],
                land.at[u, pl.ds(offset + (step - 1) * block, block)],
                sends.at[u, sem + step - 1], recvs.at[u, sem + step - 1], device(axis, index)))
            if u in RIDERS:
                n = RIDERS.index(u)
                copies.append(remote(
                    ride.at[n, core, pl.ds(base + index * block, block)],
                    ride_land.at[n, pl.ds(offset + (step - 1) * block, block)],
                    r_sends.at[n, sem + step - 1], r_recvs.at[n, sem + step - 1],
                    device(axis, index)))
        return copies

    def begin(u, stage):
        for copy in stage_copies(u, stage):
            copy.start()

    def finish(u, stage):
        _, mine, size, block, base, offset, _ = stage_of(u, stage)
        for copy in stage_copies(u, stage):
            copy.wait()

        def total(r):
            value = work[u, base + mine * block + r].astype(F32)
            for step in range(size - 1):
                value = value + land[u, offset + step * block + r].astype(F32)
            return value

        if u in RIDERS:
            n = RIDERS.index(u)

            def ridden(r):
                value = ride[n, core, base + mine * block + r]
                for step in range(size - 1):
                    value = value + ride_land[n, offset + step * block + r]
                return value

        if stage < 2:
            def body(r, _):
                work[u, base + mine * block + r] = total(r).astype(BF16)
                if u in RIDERS:
                    ride[n, core, base + mine * block + r] = ridden(r)
                return 0

            lax.fori_loop(0, block, body, 0)
            begin(u, stage + 1)
            return
        value = total(0)
        if u in RIDERS:
            vec_ref[n * 16:(n + 1) * 16, :] = ridden(0)
        if u < UP:
            down_ref[(u // 2) * UNIT[0]:(u // 2 + 1) * UNIT[0], (u % 2) * half:(u % 2 + 1) * half] = value
        else:
            to = up_ref if u < SQUARE else (go_ref, gk_ref, gv_ref, gq_ref)[u - SQUARE]
            at = (u - UP) * features if u < SQUARE else 0
            to[:, at:at + half] = value[:share]
            to[:, at + half:at + features] = value[share:]

    def folded(source, at, count):
        return jnp.concatenate(
            [source[pl.ds(at, count), 0:half], source[pl.ds(at, count), half:features]], axis=0)

    def split_pieces(u, read, other):
        def body(s, _):
            at_z, at_x, at_y = shard_of(s)
            index = index_of(u, at_x, at_y, at_z)
            for own in (True, False):
                row = 2 * s + (core if own else 1 - core)
                value = read(pl.multiple_of(row * share, 8), share).astype(BF16)
                if own:
                    work[u, index] = value
                else:
                    other[index // 4, lax.rem(index, 4)] = value
            return 0

        lax.fori_loop(0, shards, body, 0)

    def add_core(u, landed):
        def body(n, _):
            work[u, n] = (
                work[u, n].astype(F32) + landed[n // 4, lax.rem(n, 4)].astype(F32)
            ).astype(BF16)
            return 0

        lax.fori_loop(0, shards, body, 0)

    def at_point(name):
        for u, stage in EVENTS[name]:
            finish(u, stage)

    def vector_pieces(rider):
        count = 6 if rider == 0 else 2
        padded = jnp.zeros((16 - 8, 128 - share), F32)
        for s in range(shards):
            index = index_of(RIDERS[rider], (s // 2) % 2, s % 2, s // 4)
            for n in range(2):
                row = 2 * s + n
                at = row * share
                source = small if rider == 0 else late
                value = source[0:8, at:at + share]
                ride[rider, n, index, 0:8, :] = jnp.concatenate([value, padded], axis=1)
                if rider == 0:
                    start = (row % (2 * groups)) * (wide * share)
                    ride[rider, n, index, 8:16, :] = jnp.concatenate(
                        [small[8:16, start:start + wide * share],
                         jnp.zeros((8, 128 - wide * share), F32)], axis=1)
                else:
                    ride[rider, n, index, 8:16, :] = jnp.zeros((8, 128), F32)

    def ride_core(rider):
        return remote(ride.at[rider, 1 - core], ride_core_in.at[rider], r_sends.at[rider, groups + 1],
                      r_recvs.at[rider, groups + 1], to_mate)

    def core_copy(src, dst, slot):
        return remote(src, dst, c_sends.at[slot], c_recvs.at[slot], to_mate)

    load("q", q_any, q_ref)
    load("k", k_any, k_ref)
    load("v", v_any, v_ref)
    barrier = pltpu.get_barrier_semaphore()
    for target in neighbours:
        pl.semaphore_signal(barrier, inc=1, device_id=target, device_id_type=MESH)
    last_row = k_ref.shape[0] - 1

    def forward_pair(p):
        lanes = lanes_of(p)

        def step(i, _):
            at = first_block + i
            shared, both = key_blocks(tab_ref, end, p, i, at, last_row)
            keys = gathered(k_ref, shared, both, low, lanes)
            values = gathered(v_ref, shared, both, low, lanes)
            query = split_pair(q_ref[rows_of(i), lanes], low)
            merged, lse = attend(keys, values, query, mask_ref, i, low)
            live = lax.broadcasted_iota(jnp.int32, (BLK, 1), 0) < (end + 1 - at) * BLK
            merged_ref[rows_of(i), lanes] = jnp.where(live, merged, 0.0).astype(BF16)
            lse_ref[p, pl.ds(i, 1), :] = lse
            return 0

        lax.fori_loop(0, own_blocks, step, 0, unroll=own_blocks)


    def dense(
        wo, wu, wd, cot_ref, normed_one, root_one, first_low, act, slope, ffn, tmp, other,
    ):
        d_ffn = cot_ref
        for name in ("q", "k", "v"):
            loading[name].wait()
        for name, src, dst in (
            ("x", x_any, x_ref), ("wo", wo_any, wo), ("wu", wu_any, wu), ("wd", wd_any, wd),
            ("cot", cot_any, cot_ref),
        ):
            load(name, src, dst)

        def forward_two(n, _):
            for inner in range(2):
                forward_pair(2 * n + inner)
            return 0

        lax.fori_loop(0, pairs // 2, forward_two, 0)
        bo, g1, s1, bd, g2, s2 = (
            ref[...][None] for ref in (bo_ref, g1_ref, s1_ref, bd_ref, g2_ref, s2_ref))

        for name in ("x", "wo"):
            loading[name].wait()
        ffn[...] = dot(merged_ref[...], wo[...])

        def norm_one(at, r):
            normed, inv_root = normed_rows(x_ref[at, :].astype(F32) + (ffn[at, :] + bo))
            normed_one[at, :] = normed
            root_one[at, :] = inv_root
            first_low[at, :] = (normed * g1 + s1).astype(BF16)

        tiles(norm_one)

        loading["wu"].wait()
        loading["wd"].wait()
        ffn[...] = jnp.zeros_like(ffn)

        def forward(j, _):
            at = columns(j)
            u = dot(first_low[...], wu[:, at]) + bu_ref[:, at]
            square = u * u
            t = jnp.tanh(GELU_C * (u + GELU_A * (square * u)))
            upper = 0.5 * (1.0 + t)
            act[j] = (u * upper).astype(BF16)
            slope[j] = (
                upper + (0.5 * GELU_C) * u * (1.0 - t * t) * (1.0 + (3.0 * GELU_A) * square)
            ).astype(slope.dtype)
            ffn[...] += dot(act[j], wd[at, :])
            return 0

        lax.fori_loop(0, wide, forward, 0)

        small[...] = jnp.zeros_like(small)
        limit = (end + 1) * BLK - seq * rows
        loading["cot"].wait()

        def norm_two(at, r):
            first = normed_one[at, :] * g1 + s1
            normed, inv_root = normed_rows(first + (ffn[at, :] + bd))
            result_ref[at, :] = (normed * g2 + s2).astype(BF16)
            place = lax.broadcasted_iota(jnp.int32, (tile, 1), 0) + r * tile
            grad = cot_ref[at, :].astype(F32) * (place < limit).astype(F32)
            pulled = norm_pull(grad, normed, inv_root, g2)
            rounded = pulled.astype(BF16)
            ffn[at, :] = pulled
            d_ffn[at, :] = rounded
            small[0:1, :] += column_sum(grad * normed)
            small[1:2, :] += column_sum(grad)
            small[2:3, :] += column_sum(rounded.astype(F32))

        tiles(norm_two)

        pl.semaphore_wait(barrier, len(neighbours))
        down_copies = []
        for j in range(wide):
            tmp[...] = dot_tn(act[j], d_ffn[...])

            def pieces(n, _):
                at_x, at_y = n // 2, lax.rem(n, 2)
                for own in (True, False):
                    row = 2 * n + (core if own else 1 - core)
                    at = pl.multiple_of(row * (wide * share), 8)
                    for u in range(4):
                        value = tmp[
                            pl.ds(pl.multiple_of(at + (u // 2) * UNIT[0], 8), UNIT[0]),
                            (u % 2) * half:(u % 2 + 1) * half].astype(BF16)
                        if own:
                            work[u, index_of(u, at_x, at_y, j)] = value
                        else:
                            other[j, u, n] = value
                return 0

            lax.fori_loop(0, 4, pieces, 0)
            down_copies.append(core_copy(other.at[j], core_down.at[j], j))
            down_copies[-1].start()

        def backward(j, _):
            d_hidden = (dot_nt(d_ffn[...], wd[columns(j), :]) * slope[j].astype(F32)).astype(BF16)
            act[j] = d_hidden
            for n in range(wide):
                @pl.when(j == n)
                def _():
                    small[8 + n:9 + n, :] = column_sum(d_hidden.astype(F32))
            return 0

        lax.fori_loop(0, wide, backward, 0)

        for copy in down_copies:
            copy.wait()

        def sum_down(s, _):
            at_z, at_x, at_y = shard_of(s)
            for u in range(4):
                index = index_of(u, at_x, at_y, at_z)
                work[u, index] = (
                    work[u, index].astype(F32) + core_down[at_z, u, at_x * 2 + at_y].astype(F32)
                ).astype(BF16)
            return 0

        lax.fori_loop(0, shards, sum_down, 0)
        for u in range(4):
            begin(u, 0)

        up_copies = []

        def end_up(j):
            up_copies[j].wait()
            add_core(UP + j, core_up.at[j])
            begin(UP + j, 0)

        for j in range(wide):
            tmp[...] = dot_tn(first_low[...], act[j])
            split_pieces(UP + j, functools.partial(folded, tmp), other.at[j])
            up_copies.append(core_copy(other.at[j], core_up.at[j], wide + j))
            up_copies[-1].start()
            if j:
                end_up(j - 1)

        for j in range(wide):
            ffn[...] += dot_nt(act[j], wu[:, j * features:(j + 1) * features])
            if j == 1:
                end_up(wide - 1)
        at_point("up")

        def pull_one(at, r):
            grad = ffn[at, :]
            normed = normed_one[at, :]
            pulled = norm_pull(grad, normed, root_one[at, :], g1)
            rounded = pulled.astype(BF16)
            dx_ref[at, :] = pulled
            d_attn_ref[at, :] = rounded
            small[3:4, :] += column_sum(grad * normed)
            small[4:5, :] += column_sum(grad)
            small[5:6, :] += column_sum(rounded.astype(F32))

        tiles(pull_one)
        live = lax.broadcasted_iota(jnp.int32, (rows, 1), 0) < limit
        d_merged_ref[...] = jnp.where(live, dot_nt(d_attn_ref[...], wo[...]), 0.0).astype(BF16)
        at_point("dense")

    low_rows = VMEM((rows, features), BF16)
    full_rows = VMEM((rows, features), F32)
    square_low = VMEM((features, features), BF16)
    pl.run_scoped(
        dense, square_low, VMEM((features, hidden), BF16), VMEM((hidden, features), BF16),
        low_rows, full_rows, VMEM((rows, 1), F32), low_rows, VMEM((wide, rows, features), BF16),
        VMEM((wide, rows, features), SLOPE), full_rows, VMEM((features, features), F32),
        VMEM((4, 4, 4) + UNIT, BF16),
    )


    def attention(
        dq_ref, far_ref, wk, wv, wq, acc, last, picked, buf, dko, dvo, dkr, dvr, out_far, other,
        tmp,
    ):
        for name, src, dst in (
            ("far", far_any, far_ref), ("wk", wk_any, wk), ("wv", wv_any, wv), ("wq", wq_any, wq),
        ):
            load(name, src, dst)
        square_copies = [
            core_copy(other.at[n], core_down.at[n], SQUARE + n) for n in range(4)
        ]

        def square(u):
            split_pieces(u, functools.partial(folded, tmp), other.at[u - SQUARE])
            square_copies[u - SQUARE].start()

        def end_square(u):
            square_copies[u - SQUARE].wait()
            if u in RIDERS:
                n = RIDERS.index(u)
                ride_core(n).wait()
                ride[n, core] = ride[n, core] + ride_core_in[n]
            add_core(u, core_down.at[u - SQUARE])
            begin(u, 0)

        def copy_pair(p, slot, owner):
            return remote(buf.at[p, owner], pair_in.at[p, slot], p_sends.at[p, slot],
                          p_recvs.at[p, slot], to_mate)

        def sum_pair(p):
            lanes = lanes_of(p)
            for slot, owner, keys_to, values_to in ((0, across, dkr, dvr), (1, seq, dko, dvo)):
                copy_pair(p, slot, diagonal if slot == 0 else mate).wait()
                for n, to in ((0, keys_to), (1, values_to)):
                    to[:, lanes] = (
                        buf[p, owner, n].astype(F32) + pair_in[p, slot, n].astype(F32)
                    ).astype(BF16)

        def heads():
            for n in range(2):
                picked[n, picks_count] = jnp.zeros((BLK, PAIR), F32)
                for edge in (0, own_blocks + 3):
                    acc[n, edge] = jnp.zeros((BLK, PAIR), F32)
            def one_pair(p, _):
                lanes = lanes_of(p)
                acc[:, 1:own_blocks + 3] = jnp.zeros((2, own_blocks + 2, BLK, PAIR), F32)
                last[...] = jnp.zeros_like(last)

                def step(i, _):
                    at = first_block + i
                    shared, both = key_blocks(tab_ref, end, p, i, at, last_row)
                    keys = gathered(k_ref, shared, both, low, lanes)
                    values = gathered(v_ref, shared, both, low, lanes)
                    query = split_pair(q_ref[rows_of(i), lanes], low)
                    grad = split_pair(d_merged_ref[rows_of(i), lanes], low)
                    blank = jnp.zeros_like(query)
                    both_in = jnp.concatenate(
                        [jnp.concatenate([query, blank], axis=1),
                         jnp.concatenate([blank, grad], axis=1)], axis=0)
                    products = dot_nt(jnp.concatenate([keys, values], axis=1), both_in)
                    scores = masked_scores(products[:, :PAIR], mask_ref, i)
                    share_of = jnp.exp(scores - lse_ref[p, pl.ds(i, 1), :])
                    d_share = products[:, PAIR:]
                    centre = jnp.sum(share_of * d_share, axis=0, keepdims=True)
                    d_scores = (share_of * (d_share - centre)).astype(BF16)
                    d_query = dot_tn(d_scores, keys) * SCALE
                    dq_ref[rows_of(i), lanes] = jnp.where(
                        low, d_query[:BLK], d_query[BLK:]).astype(BF16)
                    products = dot(
                        jnp.concatenate([d_scores, share_of.astype(BF16)], axis=1), both_in)
                    parts = (products[:, :PAIR], products[:, PAIR:])
                    for n, part in enumerate(parts):
                        for slot in range(3):
                            acc[n, i + slot + 1] += part[slot * BLK:(slot + 1) * BLK]
                        for slot in range(2):
                            last[n, slot] += part[(3 + slot) * BLK:(4 + slot) * BLK]
                    for t in range(3):
                        one, two = (
                            prev_ref[lax.div(h, 3), i, lax.rem(h, 3) * 3 + t]
                            for h in (2 * p, 2 * p + 1))
                        for n, part in enumerate(parts):
                            picked[n, i * 3 + t] = part[(5 + t) * BLK:(6 + t) * BLK] + jnp.where(
                                low, picked[n, one], picked[n, two])
                    return 0

                lax.fori_loop(0, own_blocks, step, 0, unroll=own_blocks)

                def gather(owner, _):
                    first_owner = (owner == 0).astype(F32)
                    for inner in range(own_blocks):
                        block = owner * own_blocks + inner
                        window = jnp.minimum(
                            jnp.maximum(block - first_block + 2, 0), own_blocks + 3)
                        one, two = (
                            tail_ref[lax.div(h, 3), lax.rem(h, 3), block]
                            for h in (2 * p, 2 * p + 1))
                        for n in range(2):
                            total = acc[n, window] + jnp.where(low, picked[n, one], picked[n, two])
                            total = total + last[n, 1] * mask_ref[own_blocks, block]
                            if inner == 0:
                                total = total + last[n, 0] * first_owner
                            buf[p, owner, n, inner * BLK:(inner + 1) * BLK] = total.astype(BF16)
                    return 0

                lax.fori_loop(0, 4, gather, 0)
                copy_pair(p, 0, diagonal).start()
                copy_pair(p, 1, mate).start()

                @pl.when(p > 0)
                def _():
                    sum_pair(p - 1)

                for n in range(pairs):
                    @pl.when(p == n)
                    def _():
                        if n == 0:
                            end_square(OUT)
                        at_point(n)

                return 0

            lax.fori_loop(0, pairs, one_pair, 0)

        vector_pieces(0)
        ride_core(0).start()
        tmp[...] = dot_tn(merged_ref[...], d_attn_ref[...])
        square(OUT)
        heads()
        tmp[...] = dot_tn(x_ref[...], dq_ref[...])
        square(QUERY)
        for name in ("far", "wk", "wv", "wq"):
            loading[name].wait()
        sum_pair(pairs - 1)
        at_point("sum")
        tmp[...] = dot_tn(x_ref[...], dko[...]) + dot_tn(far_ref[...], dkr[...])
        square(KEY)
        late[...] = jnp.zeros_like(late)
        late[0:1, :] = column_sum(dq_ref[...].astype(F32))
        late[1:2, :] = column_sum(dvo[...].astype(F32)) + column_sum(dvr[...].astype(F32))
        vector_pieces(1)
        ride_core(1).start()
        end_square(QUERY)
        out_far[...] = (dot_nt(dkr[...], wk[...]) + dot_nt(dvr[...], wv[...])).astype(BF16)
        far = remote(out_far, in_far, far_sems.at[0], far_sems.at[1], to_y)
        far.start()
        end_square(KEY)
        at_point("far")
        tmp[...] = dot_tn(x_ref[...], dvo[...]) + dot_tn(far_ref[...], dvr[...])
        square(VALUE)
        at_point("v")
        dx_ref[...] += dot_nt(dko[...], wk[...]) + dot_nt(dvo[...], wv[...])
        end_square(VALUE)
        at_point("x")
        dx_ref[...] += dot_nt(dq_ref[...], wq[...])
        at_point("y")
        for u, stage in EVENTS["end"]:
            if u == "far":
                far.wait()
                dx_ref[...] += in_far[...].astype(F32)
            else:
                finish(u, stage)

    pl.run_scoped(
        attention, low_rows, low_rows, square_low, square_low, square_low,
        VMEM((2, own_blocks + 4, BLK, PAIR), F32), VMEM((2, 2, BLK, PAIR), F32),
        VMEM((2, picks_count + 1, BLK, PAIR), F32), VMEM((pairs, 4, 2, rows, PAIR), BF16),
        low_rows, low_rows, low_rows, low_rows, low_rows, VMEM((4, 4, 4) + UNIT, BF16),
        VMEM((features, features), F32),
    )


SLOPE = BF16


def layer_tail(
    groups, table, prev, tail, mask, biases, up_bias, tokens, cotangent, out_weight,
    up_weight, down_weight, query, keys, values, key_weight, value_weight, query_weight, far_tokens,
):
    rows, features = tokens.shape
    hidden = up_weight.shape[1]
    own_blocks = rows // BLK
    pairs = features // PAIR
    share = features // (8 * groups)
    wide = hidden // features
    low = VMEM((rows, features), BF16)
    kv = VMEM((4 * own_blocks, BLK, features), BF16)
    line = jax.ShapeDtypeStruct((share, features), F32)
    any_space = pl.BlockSpec(memory_space=pl.ANY)
    in_smem = pl.BlockSpec(memory_space=pltpu.SMEM)
    dma = pltpu.SemaphoreType.DMA
    return pl.pallas_call(
        functools.partial(layer_kernel, rows, 128, own_blocks, groups),
        out_shape=(
            jax.ShapeDtypeStruct((rows, features), BF16),
            jax.ShapeDtypeStruct((rows, features), F32), line, line, line, line,
            jax.ShapeDtypeStruct((share, hidden), F32),
            jax.ShapeDtypeStruct((wide * share, features), F32),
            jax.ShapeDtypeStruct((32, 128), F32),
        ),
        in_specs=[in_smem] * 4 + [whole_vmem()] * 7 + [any_space] * 12,
        out_specs=(whole_vmem(),) * 9,
        scratch_shapes=[
            VMEM((12, 4 * groups) + UNIT, BF16),
            VMEM((12, 4 * groups - 1) + UNIT, BF16),
            VMEM((4, 4, 4) + UNIT, BF16),
            VMEM((4, 4, 4) + UNIT, BF16),
            VMEM((pairs, 2, 2, rows, PAIR), BF16),
            low,
            VMEM((16, features), F32),
            VMEM((8, features), F32),
            VMEM((2, 2, 4 * groups, 16, 128), F32),
            VMEM((2, 4 * groups - 1, 16, 128), F32),
            VMEM((2, 4 * groups, 16, 128), F32),
            low, low, low, low, low, kv, kv, VMEM((pairs, own_blocks, PAIR), F32),
            dma((13,)), dma((12, groups + 1)), dma((12, groups + 1)), dma((12,)), dma((12,)),
            dma((pairs, 2)), dma((pairs, 2)), dma((2, groups + 2)), dma((2, groups + 2)),
            dma((2,)),
        ],
        compiler_params=pltpu.CompilerParams(
            collective_id=3, has_side_effects=True, vmem_limit_bytes=LIMIT
        ),
        name="layer_tail",
    )(
        table, prev, tail, mask, *biases, up_bias, tokens, cotangent, out_weight, up_weight,
        down_weight, query, keys, values, key_weight, value_weight, query_weight, far_tokens,
    )


def finish_kernel(groups, vec_ref, *refs):
    count = len(refs) - 9
    given, out, vectors = refs[:count // 2], refs[count // 2:count], refs[count:]
    for src, dst in zip(given, out):
        dst[...] = src[...]
    share = vectors[0].shape[0]
    for n in range(8):
        vectors[n][...] = vec_ref[n if n < 6 else n + 10, 0:share]
    shard = lax.axis_index("dp") * 4 + lax.axis_index("seq")
    mine = vec_ref[pl.ds(8 + shard // (2 * groups), 1), :]
    vectors[8][...] = mine[0, 0:vectors[8].shape[0]]


STEPS = 2


def whole(shape):
    return pl.BlockSpec(shape, lambda i: (0,) * len(shape))


def hand_out(groups, vectors, arrays):
    features = arrays[0].shape[1]
    share = features // (8 * groups)
    wide = arrays[-1].shape[0] // share
    shapes = [jax.ShapeDtypeStruct(a.shape, a.dtype) for a in arrays]
    specs = [
        pl.BlockSpec((a.shape[0] // STEPS, a.shape[1]), lambda i: (i, 0))
        if a.shape[0] % (16 * STEPS) == 0 else whole(a.shape) for a in arrays
    ]
    lines = [jax.ShapeDtypeStruct((share,), F32)] * 8 + [jax.ShapeDtypeStruct((wide * share,), F32)]
    return pl.pallas_call(
        functools.partial(finish_kernel, groups),
        out_shape=tuple(shapes + lines),
        grid=(STEPS,),
        in_specs=[whole((32, 128))] + specs,
        out_specs=tuple(specs) + (whole((share,)),) * 8 + (whole((wide * share,)),),
        name="hand_out",
    )(vectors, *arrays)


def layer_norm(values, gain, shift):
    center = jnp.mean(values, axis=-1, keepdims=True)
    centered = values - center
    variance = jnp.mean(centered * centered, axis=-1, keepdims=True)
    inv_root = lax.rsqrt(variance + NORM_EPS)
    normed = centered * inv_root
    return (normed * gain + shift, normed, inv_root)


def norm_back(grad_out, normed, inv_root, gain):
    d_normed = grad_out * gain
    grad_in = inv_root * (
        d_normed
        - jnp.mean(d_normed, axis=-1, keepdims=True)
        - normed * jnp.mean(d_normed * normed, axis=-1, keepdims=True)
    )
    return (grad_in, jnp.sum(grad_out * normed, axis=0), jnp.sum(grad_out, axis=0))


def on_device(
    groups,
    tokens, filled_blocks, random_blocks, query_weight, query_bias, key_weight, value_weight,
    value_bias, out_weight, out_bias, attn_gain, attn_shift, up_weight, up_bias, down_weight,
    down_bias, ffn_gain, ffn_shift, cotangent,
):
    row_count, feature_count = tokens.shape
    filled = filled_blocks[0]
    place = lax.axis_index("seq") * row_count + jnp.arange(row_count, dtype=jnp.int32)
    live_tokens = (place < filled * BLK).astype(F32)[:, None]

    query, keys, values, far_tokens, table, prev, tail, mask = gather_project(
        filled_blocks, tokens,
        random_blocks.transpose(2, 3, 0, 1), query_weight, key_weight, value_weight, query_bias,
        value_bias)
    keys, values = (t.reshape(-1, BLK, feature_count) for t in (keys, values))
    if groups:
        *arrays, vectors = layer_tail(
            groups, table, prev, tail, mask,
            (out_bias, attn_gain, attn_shift, down_bias, ffn_gain, ffn_shift), up_bias[None],
            tokens, cotangent, out_weight, up_weight, down_weight, query, keys, values,
            key_weight, value_weight, query_weight, far_tokens)
        (result, grad_tokens, gq, gk, gv, go, up, down, g2, s2, bd, g1, s1, bo, bq, bv,
         bu) = hand_out(groups, vectors, arrays)
        return (
            result, grad_tokens, gq, bq, gk, gv, bv, go, bo, g1, s1, up, bu, down, bd, g2, s2)

    merged, lse = attention_forward(table, filled_blocks, mask, query, keys, values)
    attn = dot(merged, out_weight) + out_bias
    first, normed_one, root_one = layer_norm(tokens.astype(F32) + attn, attn_gain, attn_shift)
    first_low = first.astype(BF16)
    hidden = dot(first_low, up_weight) + up_bias
    act, gelu_pull = jax.vjp(jax.nn.gelu, hidden)
    act_low = act.astype(BF16)
    ffn = dot(act_low, down_weight) + down_bias
    result, normed_two, root_two = layer_norm(first + ffn, ffn_gain, ffn_shift)
    grad_result = cotangent.astype(F32) * live_tokens
    d_sum_two, grad_ffn_gain, grad_ffn_shift = norm_back(
        grad_result, normed_two, root_two, ffn_gain
    )
    d_ffn = d_sum_two.astype(BF16)
    grad_down_bias = jnp.sum(d_ffn, axis=0, dtype=F32)
    grad_down_weight = dot_tn(act_low, d_ffn)
    d_act = dot_nt(d_ffn, down_weight)
    d_hidden = gelu_pull(d_act)[0].astype(BF16)
    grad_up_bias = jnp.sum(d_hidden, axis=0, dtype=F32)
    grad_up_weight = dot_tn(first_low, d_hidden)
    d_first = d_sum_two + dot_nt(d_hidden, up_weight)
    d_sum_one, grad_attn_gain, grad_attn_shift = norm_back(d_first, normed_one, root_one, attn_gain)
    d_attn = d_sum_one.astype(BF16)
    grad_out_bias = jnp.sum(d_attn, axis=0, dtype=F32)
    grad_out_weight = dot_tn(merged, d_attn)
    d_merged = dot_nt(d_attn, out_weight).astype(BF16)

    d_query, d_keys, d_values = attention_backward(
        table, filled_blocks, mask, query, keys, values, d_merged, lse
    )
    grad_tokens, dk_own, dv_own, dk_far, dv_far = exchange(
        d_keys, d_values, d_query, d_sum_one, query_weight, key_weight, value_weight
    )
    grad_query_weight = dot_tn(tokens, d_query)
    grad_query_bias = jnp.sum(d_query, axis=0, dtype=F32)
    grad_key_weight = dot_tn(tokens, dk_own) + dot_tn(far_tokens, dk_far)
    grad_value_weight = dot_tn(tokens, dv_own) + dot_tn(far_tokens, dv_far)
    grad_value_bias = jnp.sum(dv_own, axis=0, dtype=F32) + jnp.sum(dv_far, axis=0, dtype=F32)

    square = (grad_query_weight, grad_key_weight, grad_value_weight, grad_out_weight)
    vectors = (
        grad_query_bias, grad_value_bias, grad_out_bias, grad_attn_gain, grad_attn_shift,
        grad_down_bias, grad_ffn_gain, grad_ffn_shift,
    )
    square, up, down, vectors, up_sum = summed_anywhere(
        square, grad_up_weight, grad_down_weight, vectors, grad_up_bias)
    return (
        result.astype(BF16), grad_tokens, square[0], vectors[0], square[1], square[2], vectors[1],
        square[3], vectors[2], vectors[3], vectors[4], up, up_sum, down, vectors[5], vectors[6],
        vectors[7],
    )


def solution(mesh):
    both = P(("dp", "seq"), None)
    line = P(("dp", "seq"))
    placed = (both, P("dp"), P("dp", None, "seq", None)) + (P(),) * 15 + (both,)
    groups = 4 if mesh.shape["dp"] == 8 and mesh.shape["seq"] == 4 else 0
    return jax.shard_map(
        functools.partial(on_device, groups),
        mesh=mesh,
        in_specs=placed,
        out_specs=(
            both, both, both, line, both, both, line, both, line, line, line, both, line, both,
            line, line, line,
        ),
        check_vma=False,
    )
```

```python
import functools

import jax
import jax.numpy as jnp
from jax import lax
from jax.experimental import pallas as pl
from jax.experimental.pallas import tpu as pltpu
from jax.sharding import PartitionSpec as P

HEAD_DIM = 64
BLK = 64
PAIR = 2 * HEAD_DIM
TABLE = 8
NORM_EPS = 1e-05
MASKED = -1e30
SCALE = HEAD_DIM ** (-0.5)
MESH = pl.DeviceIdType.MESH
BF16 = jnp.bfloat16
F32 = jnp.float32
VMEM = pltpu.VMEM
LIMIT = 63 << 20


def whole_vmem():
    return pl.BlockSpec(memory_space=pltpu.VMEM)


def dot(left, right):
    return jnp.dot(left, right, preferred_element_type=F32)


def dot_nt(left, right):
    return lax.dot_general(left, right, (((1,), (1,)), ((), ())), preferred_element_type=F32)


def dot_tn(left, right):
    return lax.dot_general(left, right, (((0,), (0,)), ((), ())), preferred_element_type=F32)


def tables_of(tab_out, filled, first_block, each, prev_out, tail_out, mask_out):
    groups, blocks, width = tab_out.shape
    slot_blocks = width
    none = blocks * each
    lane = lax.broadcasted_iota(jnp.int32, (blocks, width), 1)
    row = lax.broadcasted_iota(jnp.int32, (blocks, width), 0)
    pick = lax.rem(lane, each)
    key_row = lax.broadcasted_iota(jnp.int32, (slot_blocks, width), 0)
    key_pick = lax.rem(lax.broadcasted_iota(jnp.int32, (slot_blocks, width), 1), each)
    for g in range(groups):
        table = tab_out[g]
        prev = jnp.full((blocks, width), -1, jnp.int32)
        for shift in range(1 - each, each):
            moved = pltpu.roll(table, (-shift) % width, axis=1)
            inside = (pick + shift >= 0) & (pick + shift < each)
            for i in range(blocks - 1):
                same = (moved[i:i + 1] == table) & (row > i) & inside
                prev = jnp.maximum(prev, jnp.where(same, i * each + pick + shift, -1))
        prev = jnp.where(prev < 0, none, prev)
        prev_out[g] = jnp.where(lane == width - 1, filled - 1, prev)
        tail = jnp.full((slot_blocks, width), -1, jnp.int32)
        for i in range(blocks):
            tail = jnp.maximum(tail, jnp.where(table[i:i + 1] == key_row, i * each + key_pick, -1))
        best = tail
        for shift in range(1, each):
            best = jnp.maximum(best, pltpu.roll(tail, width - shift, axis=1))
        turned = jnp.where(best < 0, none, best).astype(F32).T.astype(jnp.int32)
        for h in range(3):
            tail_out[g, h:h + 1, :] = turned[h * each:h * each + 1, :]
        tail_out[g, 3:blocks, :] = jnp.full((blocks - 3, width), none, jnp.int32)
    at = first_block + row
    window = at + lane - 1
    ok = jnp.where(
        lane < 3, ((window >= 0) & (window < filled)).astype(jnp.int32),
        jnp.where(lane == 3, (at >= 2).astype(jnp.int32),
                  (jnp.abs(at - (filled - 1)) > 1).astype(jnp.int32)))
    mask_out[0:blocks, :] = jnp.where(ok == 1, 0.0, MASKED)
    mask_out[blocks:2 * blocks, :] = (lane == filled - 1).astype(F32)


def gather_kernel(
    rows, width, filled_ref, x_ref, picks_ref, wq_any, wk_any, wv_any, qb_ref, vb_ref,
    q_any, k_any, v_any, far_any, tab_out, prev_out, tail_out, mask_out,
    wq_ref, wk_ref, wv_ref, q_ref, k_ref, v_ref,
    tab_ref, land, tab_land, loads, stores, sends, recvs, tab_sends, tab_recvs,
):
    parts = 4
    part = rows // parts
    dp, me = lax.axis_index("dp"), lax.axis_index("seq")
    mate, across, diagonal = (lax.bitwise_xor(me, bit) for bit in (1, 2, 3))
    weights = [
        pltpu.make_async_copy(src, dst, loads.at[n])
        for n, (src, dst) in enumerate(((wq_any, wq_ref), (wk_any, wk_ref), (wv_any, wv_ref)))
    ]
    for copy in weights:
        copy.start()
    barrier = pltpu.get_barrier_semaphore()
    for other in (mate, across, diagonal):
        pl.semaphore_signal(barrier, inc=1, device_id=(dp, other), device_id_type=MESH)
    heads_here, each, _, blocks = picks_ref.shape
    chosen = picks_ref[...].reshape(heads_here * each, blocks).astype(F32)
    chosen = jnp.concatenate(
        [chosen, jnp.zeros((heads_here * each, 128 - blocks), F32)], axis=1)
    chosen = jnp.concatenate([chosen, jnp.zeros((128 - heads_here * each, 128), F32)], axis=0)
    tab_ref[...] = chosen.T[0:blocks].astype(jnp.int32)
    pl.semaphore_wait(barrier, 3)

    def send(src, dst, slot, target):
        copy = pltpu.make_async_remote_copy(
            src_ref=src, dst_ref=dst, send_sem=sends.at[slot], recv_sem=recvs.at[slot],
            device_id=(dp, target), device_id_type=MESH,
        )
        copy.start()
        return copy

    tables = []
    own_blocks = tab_ref.shape[0] // 4
    for slot, other in enumerate((mate, across, diagonal)):
        copy = pltpu.make_async_remote_copy(
            src_ref=tab_ref.at[pl.ds(pl.multiple_of(other * own_blocks, 8), own_blocks)],
            dst_ref=tab_land.at[slot], send_sem=tab_sends.at[slot], recv_sem=tab_recvs.at[slot],
            device_id=(dp, other), device_id_type=MESH,
        )
        copy.start()
        tables.append(copy)
    far = [
        send(x_ref.at[pl.ds(r * part, part)], land.at[0, pl.ds(r * part, part)], r, across)
        for r in range(parts)
    ]
    near = send(x_ref, land.at[1], parts, mate)
    stored = []

    def store(src, dst, start, count):
        at = pl.ds(pl.multiple_of(start, part), count)
        copy = pltpu.make_async_copy(src.at[at], dst.at[at], stores.at[len(stored)])
        copy.start()
        stored.append(copy)

    def keys_values(x, at):
        k_ref[pl.ds(at, width), :] = dot(x, wk_ref[...]).astype(BF16)
        v_ref[pl.ds(at, width), :] = (dot(x, wv_ref[...]) + vb_ref[...][None]).astype(BF16)

    for copy in weights:
        copy.wait()

    def own(r, _):
        at = pl.multiple_of(r * width, width)
        x = x_ref[pl.ds(at, width), :]
        q_ref[pl.ds(at, width), :] = (
            (dot(x, wq_ref[...]) + qb_ref[...][None]).astype(BF16) * jnp.asarray(SCALE, BF16)
        )
        keys_values(x, pl.multiple_of(me * rows + at, width))
        return 0

    lax.fori_loop(0, rows // width, own, 0)
    store(q_ref, q_any, 0, rows)
    store(k_ref, k_any, me * rows, rows)
    store(v_ref, v_any, me * rows, rows)

    def block(slot, owner, start, count):
        def step(r, _):
            at = pl.multiple_of(start + r * width, width)
            keys_values(land[slot, pl.ds(at, width), :], pl.multiple_of(owner * rows + at, width))
            return 0

        lax.fori_loop(0, count // width, step, 0)
        store(k_ref, k_any, owner * rows + start, count)
        store(v_ref, v_any, owner * rows + start, count)

    near.wait()
    block(1, mate, 0, rows)
    for copy in tables:
        copy.wait()
    tab_out[pl.ds(me, 1)] = tab_ref[pl.ds(pl.multiple_of(me * own_blocks, 8), own_blocks)][None]
    for slot, other in enumerate((mate, across, diagonal)):
        tab_out[pl.ds(other, 1)] = tab_land[slot][None]
    tables_of(tab_out, filled_ref[0], me * own_blocks, each, prev_out, tail_out, mask_out)
    relayed = []
    for r in range(parts):
        far[r].wait()
        piece = pl.ds(r * part, part)
        relayed.append(send(land.at[0, piece], land.at[2, piece], parts + 1 + r, mate))
        store(land.at[0], far_any, r * part, part)
        block(0, across, r * part, part)
        if r:
            relayed[r - 1].wait()
            block(2, diagonal, (r - 1) * part, part)
    relayed[-1].wait()
    block(2, diagonal, (parts - 1) * part, part)
    for copy in stored:
        copy.wait()


def gather_project(
    filled, tokens, chosen, query_weight, key_weight, value_weight, query_bias, value_bias,
):
    rows, features = tokens.shape
    own_blocks = rows // BLK
    slot_blocks = chosen.shape[3]
    copies = 4 + 1 + 4
    any_space = pl.BlockSpec(memory_space=pl.ANY)
    low = jax.ShapeDtypeStruct((rows, features), BF16)
    slot = jax.ShapeDtypeStruct((4 * rows, features), BF16)
    table = jax.ShapeDtypeStruct((4, own_blocks, 128), jnp.int32)
    dma = pltpu.SemaphoreType.DMA
    return pl.pallas_call(
        functools.partial(gather_kernel, rows, 128),
        out_shape=(
            low, slot, slot, low, table, table, table,
            jax.ShapeDtypeStruct((2 * own_blocks, 128), F32),
        ),
        in_specs=[pl.BlockSpec(memory_space=pltpu.SMEM)] + [whole_vmem()] * 2 + [any_space] * 3
        + [whole_vmem()] * 2,
        out_specs=(any_space,) * 4 + (whole_vmem(),) * 4,
        scratch_shapes=[
            VMEM((features, features), BF16),
            VMEM((features, features), BF16),
            VMEM((features, features), BF16),
            VMEM((rows, features), BF16),
            VMEM((4 * rows, features), BF16),
            VMEM((4 * rows, features), BF16),
            VMEM((slot_blocks, 128), jnp.int32),
            VMEM((3, rows, features), BF16),
            VMEM((3, own_blocks, 128), jnp.int32),
            dma((3,)), dma((25,)), dma((copies,)), dma((copies,)), dma((3,)), dma((3,)),
        ],
        compiler_params=pltpu.CompilerParams(
            collective_id=0, has_side_effects=True, vmem_limit_bytes=LIMIT
        ),
        name="gather_project",
    )(filled, tokens, chosen, query_weight, key_weight, value_weight, query_bias, value_bias)


def key_blocks(tab_ref, end, pair, i, at, last_row):
    def chosen(head, t):
        group, inner = lax.div(head, 3), lax.rem(head, 3)
        return tab_ref[group, i, inner * 3 + t]

    head = 2 * pair
    both = [(chosen(head, t), chosen(head + 1, t)) for t in range(3)]
    shared = [
        jnp.maximum(at - 1, 0), at, jnp.minimum(at + 1, last_row), jnp.int32(0), end,
    ]
    return shared, both


def rows_of(block):
    return pl.ds(pl.multiple_of(block * BLK, BLK), BLK)


def lanes_low(rows):
    return lax.broadcasted_iota(jnp.int32, (rows, PAIR), 1) < HEAD_DIM


def split_pair(x, low):
    zero = jnp.zeros_like(x)
    return jnp.concatenate([jnp.where(low, x, zero), jnp.where(low, zero, x)], axis=0)


def gathered(ref, shared, both, low, lanes=slice(None)):
    tiles = [ref[b, :, lanes] for b in shared]
    for first, second in both:
        tiles.append(jnp.where(low, ref[first, :, lanes], ref[second, :, lanes]))
    return jnp.concatenate(tiles, axis=0)


def masked_scores(scores, mask_ref, i):
    parts = [scores[n * BLK:(n + 1) * BLK] + mask_ref[i, n] for n in range(5)]
    return jnp.concatenate(parts + [scores[5 * BLK:]], axis=0)


def attend(keys, values, query, mask_ref, i, low):
    scores = masked_scores(dot_nt(keys, query), mask_ref, i)
    highest = jnp.max(scores, axis=0, keepdims=True)
    weights = jnp.exp(scores - highest)
    total = jnp.sum(weights, axis=0, keepdims=True)
    share = (weights * (1.0 / total)).astype(BF16)
    output = dot_tn(share, values)
    return jnp.where(low, output[:BLK], output[BLK:]), highest + jnp.log(total)


def forward_kernel(own_blocks, tab_ref, filled_ref, mask_ref, q_ref, k_ref, v_ref, out_ref, lse_ref):
    pair = pl.program_id(0)
    filled = filled_ref[0]
    first_block = lax.axis_index("seq") * own_blocks
    last_row = k_ref.shape[0] - 1
    low = lanes_low(BLK)

    def step(i, _):
        at = first_block + i
        shared, both = key_blocks(tab_ref, filled - 1, pair, i, at, last_row)
        keys = gathered(k_ref, shared, both, low)
        values = gathered(v_ref, shared, both, low)
        query = split_pair(q_ref[rows_of(i), :], low)
        merged, lse = attend(keys, values, query, mask_ref, i, low)
        out_ref[rows_of(i), :] = jnp.where(at < filled, merged, 0.0).astype(BF16)
        lse_ref[0, pl.ds(i, 1), :] = lse
        return 0

    lax.fori_loop(0, own_blocks, step, 0, unroll=own_blocks)


def attention_forward(table, filled, mask, query, keys, values):
    rows, features = query.shape
    own_blocks = rows // BLK
    slot_blocks = keys.shape[0]
    pairs = features // PAIR
    column = lambda n: pl.BlockSpec((n, PAIR), lambda p, *_: (0, p))
    blocks = lambda n: pl.BlockSpec((n, BLK, PAIR), lambda p, *_: (0, 0, p))
    return pl.pallas_call(
        functools.partial(forward_kernel, own_blocks),
        out_shape=(
            jax.ShapeDtypeStruct((rows, features), BF16),
            jax.ShapeDtypeStruct((pairs, own_blocks, PAIR), F32),
        ),
        grid_spec=pltpu.PrefetchScalarGridSpec(
            num_scalar_prefetch=3,
            grid=(pairs,),
            in_specs=[column(rows), blocks(slot_blocks), blocks(slot_blocks)],
            out_specs=(column(rows), pl.BlockSpec((1, own_blocks, PAIR), lambda p, *_: (p, 0, 0))),
        ),
        compiler_params=pltpu.CompilerParams(vmem_limit_bytes=LIMIT),
        name="attention_forward",
    )(table, filled, mask, query, keys, values)


def backward_kernel(
    own_blocks, tab_ref, filled_ref, mask_ref, q_ref, k_ref, v_ref, g_ref, lse_ref,
    dq_ref, dk_ref, dv_ref, dk_sum, dv_sum,
):
    pair = pl.program_id(0)
    filled = filled_ref[0]
    first_block = lax.axis_index("seq") * own_blocks
    last_row = k_ref.shape[0] - 1
    low = lanes_low(BLK)
    dk_sum[...] = jnp.zeros_like(dk_sum)
    dv_sum[...] = jnp.zeros_like(dv_sum)

    def step(i, _):
        at = first_block + i
        shared, both = key_blocks(tab_ref, filled - 1, pair, i, at, last_row)
        keys = gathered(k_ref, shared, both, low)
        values = gathered(v_ref, shared, both, low)
        query = split_pair(q_ref[rows_of(i), :], low)
        grad = split_pair(jnp.where(at < filled, g_ref[rows_of(i), :], jnp.zeros((), BF16)), low)
        scores = masked_scores(dot_nt(keys, query), mask_ref, i)
        share = jnp.exp(scores - lse_ref[0, pl.ds(i, 1), :])
        d_share = dot_nt(values, grad)
        centre = jnp.sum(share * d_share, axis=0, keepdims=True)
        d_scores = (share * (d_share - centre)).astype(BF16)
        d_query = dot_tn(d_scores, keys) * SCALE
        dq_ref[rows_of(i), :] = jnp.where(low, d_query[:BLK], d_query[BLK:]).astype(BF16)
        for total, part in ((dk_sum, dot(d_scores, query)), (dv_sum, dot(share.astype(BF16), grad))):
            for slot, block in enumerate(shared):
                total[rows_of(block), :] += part[slot * BLK:(slot + 1) * BLK]
            for t, (one, two) in enumerate(both):
                tile = part[(5 + t) * BLK:(6 + t) * BLK]
                total[rows_of(one), :] += jnp.where(low, tile, 0.0)
                total[rows_of(two), :] += jnp.where(low, 0.0, tile)
        return 0

    lax.fori_loop(0, own_blocks, step, 0, unroll=own_blocks)
    dk_ref[...] = dk_sum[...].astype(BF16)
    dv_ref[...] = dv_sum[...].astype(BF16)


def attention_backward(table, filled, mask, query, keys, values, grad, lse):
    rows, features = query.shape
    slot_blocks = keys.shape[0]
    slot_rows = slot_blocks * BLK
    own_blocks = rows // BLK
    pairs = features // PAIR
    blocks = lambda n: pl.BlockSpec((n, BLK, PAIR), lambda p, *_: (0, 0, p))
    column = lambda n: pl.BlockSpec((n, PAIR), lambda p, *_: (0, p))
    return pl.pallas_call(
        functools.partial(backward_kernel, own_blocks),
        out_shape=(
            jax.ShapeDtypeStruct((rows, features), BF16),
            jax.ShapeDtypeStruct((slot_rows, features), BF16),
            jax.ShapeDtypeStruct((slot_rows, features), BF16),
        ),
        grid_spec=pltpu.PrefetchScalarGridSpec(
            num_scalar_prefetch=3,
            grid=(pairs,),
            in_specs=[
                column(rows), blocks(slot_blocks), blocks(slot_blocks), column(rows),
                pl.BlockSpec((1, own_blocks, PAIR), lambda p, *_: (p, 0, 0)),
            ],
            out_specs=(column(rows), column(slot_rows), column(slot_rows)),
            scratch_shapes=[VMEM((slot_rows, PAIR), F32), VMEM((slot_rows, PAIR), F32)],
        ),
        compiler_params=pltpu.CompilerParams(vmem_limit_bytes=LIMIT),
        name="attention_backward",
    )(table, filled, mask, query, keys, values, grad, lse)


def exchange_kernel(
    rows, width, dk_ref, dv_ref, dq_ref, base_ref, wq_ref, wk_ref, wv_ref,
    dx_ref, dko_ref, dvo_ref, dkr_ref, dvr_ref,
    land, out_far, in_far, sends, recvs,
):
    dp, me = lax.axis_index("dp"), lax.axis_index("seq")
    mate, across, diagonal = (lax.bitwise_xor(me, bit) for bit in (1, 2, 3))
    barrier = pltpu.get_barrier_semaphore()
    for other in (mate, across):
        pl.semaphore_signal(barrier, inc=1, device_id=(dp, other), device_id_type=MESH)
    pl.semaphore_wait(barrier, 2)

    def send(src, dst, slot, target):
        copy = pltpu.make_async_remote_copy(
            src_ref=src, dst_ref=dst, send_sem=sends.at[slot], recv_sem=recvs.at[slot],
            device_id=(dp, target), device_id_type=MESH,
        )
        copy.start()
        return copy

    def owned(index):
        return pl.ds(pl.multiple_of(index * rows, rows), rows)

    copies = [
        send(ref.at[owned(owner)], land.at[slot], slot, mate)
        for slot, (ref, owner) in enumerate(
            ((dk_ref, diagonal), (dv_ref, diagonal), (dk_ref, mate), (dv_ref, mate))
        )
    ]

    def summed(ref, owner, slot, to_ref):
        to_ref[...] = (ref[owned(owner), :].astype(F32) + land[slot].astype(F32)).astype(BF16)

    copies[0].wait()
    summed(dk_ref, across, 0, dkr_ref)
    copies[1].wait()
    summed(dv_ref, across, 1, dvr_ref)

    steps = rows // width
    for r in range(steps):
        at = pl.ds(r * width, width)
        out_far[at, :] = (
            dot_nt(dkr_ref[at, :], wk_ref[...]) + dot_nt(dvr_ref[at, :], wv_ref[...])
        ).astype(BF16)
    far = send(out_far, in_far, 4, across)
    copies[2].wait()
    summed(dk_ref, me, 2, dko_ref)
    copies[3].wait()
    summed(dv_ref, me, 3, dvo_ref)

    def one(r, _):
        at = pl.ds(pl.multiple_of(r * width, width), width)
        dx_ref[at, :] = (
            base_ref[at, :]
            + dot_nt(dq_ref[at, :], wq_ref[...])
            + dot_nt(dko_ref[at, :], wk_ref[...])
            + dot_nt(dvo_ref[at, :], wv_ref[...])
        )
        return 0

    lax.fori_loop(0, steps, one, 0)
    far.wait()
    dx_ref[...] += in_far[...].astype(F32)


def exchange(d_keys, d_values, d_query, base, query_weight, key_weight, value_weight):
    rows, features = d_query.shape
    small = jax.ShapeDtypeStruct((rows, features), BF16)
    return pl.pallas_call(
        functools.partial(exchange_kernel, rows, 128),
        out_shape=(jax.ShapeDtypeStruct((rows, features), F32), small, small, small, small),
        in_specs=[whole_vmem()] * 7,
        out_specs=(whole_vmem(),) * 5,
        scratch_shapes=[
            VMEM((4, rows, features), BF16),
            VMEM((rows, features), BF16),
            VMEM((rows, features), BF16),
            pltpu.SemaphoreType.DMA((5,)),
            pltpu.SemaphoreType.DMA((5,)),
        ],
        compiler_params=pltpu.CompilerParams(
            collective_id=1, has_side_effects=True, vmem_limit_bytes=LIMIT
        ),
        name="exchange",
    )(d_keys, d_values, d_query, base, query_weight, key_weight, value_weight)


def summed_anywhere(square, up, down, vectors, up_bias):
    def one(g):
        return lax.psum_scatter(g, ("dp", "seq"), scatter_dimension=0, tiled=True)

    return [one(g) for g in square], one(up), one(down), [one(v) for v in vectors], one(up_bias)


GELU_A = 0.044715
GELU_C = 0.7978845608028654
UNIT = (48, 384)
ORDERS = (
    "xyz", "zyx", "yxz", "zxy", "yxz", "xyz", "yzx", "yxz", "yzx", "yxz", "xzy", "xzy",
)
UP, SQUARE = 4, 8
OUT, KEY, VALUE, QUERY = 8, 9, 10, 11
RIDERS = (OUT, VALUE)
EVENTS = {
    "up": ((0, 0), (2, 0)),
    "dense": (),
    0: ((4, 0), (5, 0), (1, 0), (2, 1)),
    1: ((6, 0),),
    2: ((4, 1),),
    3: ((7, 0), (3, 0)),
    4: ((0, 1), (2, 2)),
    5: ((7, 1),),
    "sum": ((8, 0), (6, 1), (3, 1)),
    "far": ((5, 1), (1, 1), (4, 2), (6, 2), (3, 2), (0, 2), (7, 2)),
    "x": (),
    "y": (),
    "end": ((11, 0), (8, 1), (9, 0), (10, 0), (5, 2), (1, 2), (8, 2), (9, 1), (11, 1), (10, 1), ("far", 0), (11, 2), (9, 2), (10, 2)),
}


def normed_rows(values):
    center = jnp.mean(values, axis=-1, keepdims=True)
    centered = values - center
    variance = jnp.mean(centered * centered, axis=-1, keepdims=True)
    inv_root = lax.rsqrt(variance + NORM_EPS)
    return centered * inv_root, inv_root


def norm_pull(grad_out, normed, inv_root, gain):
    d_normed = grad_out * gain
    return inv_root * (
        d_normed
        - jnp.mean(d_normed, axis=-1, keepdims=True)
        - normed * jnp.mean(d_normed * normed, axis=-1, keepdims=True)
    )


def column_sum(values):
    return jnp.sum(values, axis=0, keepdims=True)


def layer_kernel(
    rows, tile, own_blocks, groups, tab_ref, prev_ref, tail_ref, mask_ref, bo_ref, g1_ref, s1_ref,
    bd_ref, g2_ref, s2_ref, bu_ref,
    x_any, cot_any, wo_any, wu_any, wd_any, q_any, k_any, v_any, wk_any, wv_any, wq_any,
    far_any,
    result_ref, dx_ref, gq_ref, gk_ref, gv_ref, go_ref, up_ref, down_ref, vec_ref,
    work, land, core_down, core_up, pair_in, in_far, small, late,
    ride, ride_land, ride_core_in,
    x_ref, merged_ref, d_attn_ref, d_merged_ref, q_ref, k_ref, v_ref, lse_ref,
    loads, sends, recvs, c_sends, c_recvs, p_sends, p_recvs, r_sends, r_recvs, far_sems,
):
    features = x_ref.shape[1]
    hidden = bu_ref.shape[1]
    wide = hidden // features
    pairs = features // PAIR
    picks_count = own_blocks * 3
    share = features // (8 * groups)
    shards = 4 * groups
    half = features // 2
    dp, seq = lax.axis_index("dp"), lax.axis_index("seq")
    x, z = lax.rem(dp, 2), dp // 2
    core, y = lax.rem(seq, 2), seq // 2
    mate, across, diagonal = (lax.bitwise_xor(seq, bit) for bit in (1, 2, 3))
    end = prev_ref[0, 0, 127]
    first_block = seq * own_blocks
    low = lanes_low(BLK)
    to_mate, to_y = (dp, mate), (dp, across)
    place_of = {"x": (x, 2), "y": (y, 2), "z": (z, groups)}

    def device(axis, index):
        if axis == "x":
            return (2 * z + index, seq)
        if axis == "y":
            return (dp, 2 * index + core)
        return (2 * index + x, seq)

    neighbours = [to_mate, to_y, device("x", 1 - x)] + [
        device("z", lax.rem(z + step, groups)) for step in range(1, groups)]

    loading = {}

    def load(name, src, dst):
        copy = pltpu.make_async_copy(src, dst, loads.at[len(loading)])
        copy.start()
        loading[name] = copy

    def remote(src, dst, one, two, target):
        return pltpu.make_async_remote_copy(
            src_ref=src, dst_ref=dst, send_sem=one, recv_sem=two, device_id=target,
            device_id_type=MESH,
        )

    def lanes_of(p):
        return pl.ds(pl.multiple_of(p * PAIR, PAIR), PAIR)

    def columns(j):
        return pl.ds(pl.multiple_of(j * features, features), features)

    def tiles(body):
        def step(r, _):
            body(pl.ds(pl.multiple_of(r * tile, tile), tile), r)
            return 0

        lax.fori_loop(0, rows // tile, step, 0)


    def index_of(u, at_x, at_y, at_z):
        at = {"x": at_x, "y": at_y, "z": at_z}
        flat = 0
        for axis in ORDERS[u]:
            flat = flat * place_of[axis][1] + at[axis]
        return flat

    def shard_of(s):
        return s // 4, lax.rem(s // 2, 2), lax.rem(s, 2)

    def stage_of(u, stage):
        sizes = [place_of[axis][1] for axis in ORDERS[u]] + [1]
        base, offset, sem, block = 0, 0, 0, shards
        for n, axis in enumerate(ORDERS[u]):
            block = block // sizes[n]
            if n == stage:
                return axis, place_of[axis][0], sizes[n], block, base, offset, sem
            base = base + place_of[axis][0] * block
            offset += (sizes[n] - 1) * block
            sem += sizes[n] - 1
        return None

    def stage_copies(u, stage):
        axis, mine, size, block, base, offset, sem = stage_of(u, stage)
        copies = []
        for step in range(1, size):
            index = lax.rem(mine + step, size)
            copies.append(remote(
                work.at[u, pl.ds(base + index * block, block)],
                land.at[u, pl.ds(offset + (step - 1) * block, block)],
                sends.at[u, sem + step - 1], recvs.at[u, sem + step - 1], device(axis, index)))
            if u in RIDERS:
                n = RIDERS.index(u)
                copies.append(remote(
                    ride.at[n, core, pl.ds(base + index * block, block)],
                    ride_land.at[n, pl.ds(offset + (step - 1) * block, block)],
                    r_sends.at[n, sem + step - 1], r_recvs.at[n, sem + step - 1],
                    device(axis, index)))
        return copies

    def begin(u, stage):
        for copy in stage_copies(u, stage):
            copy.start()

    def finish(u, stage):
        _, mine, size, block, base, offset, _ = stage_of(u, stage)
        for copy in stage_copies(u, stage):
            copy.wait()

        def total(r):
            value = work[u, base + mine * block + r].astype(F32)
            for step in range(size - 1):
                value = value + land[u, offset + step * block + r].astype(F32)
            return value

        if u in RIDERS:
            n = RIDERS.index(u)

            def ridden(r):
                value = ride[n, core, base + mine * block + r]
                for step in range(size - 1):
                    value = value + ride_land[n, offset + step * block + r]
                return value

        if stage < 2:
            def body(r, _):
                work[u, base + mine * block + r] = total(r).astype(BF16)
                if u in RIDERS:
                    ride[n, core, base + mine * block + r] = ridden(r)
                return 0

            lax.fori_loop(0, block, body, 0)
            begin(u, stage + 1)
            return
        value = total(0)
        if u in RIDERS:
            vec_ref[n * 16:(n + 1) * 16, :] = ridden(0)
        if u < UP:
            down_ref[(u // 2) * UNIT[0]:(u // 2 + 1) * UNIT[0], (u % 2) * half:(u % 2 + 1) * half] = value
        else:
            to = up_ref if u < SQUARE else (go_ref, gk_ref, gv_ref, gq_ref)[u - SQUARE]
            at = (u - UP) * features if u < SQUARE else 0
            to[:, at:at + half] = value[:share]
            to[:, at + half:at + features] = value[share:]

    def folded(source, at, count):
        return jnp.concatenate(
            [source[pl.ds(at, count), 0:half], source[pl.ds(at, count), half:features]], axis=0)

    def split_pieces(u, read, other):
        def body(s, _):
            at_z, at_x, at_y = shard_of(s)
            index = index_of(u, at_x, at_y, at_z)
            for own in (True, False):
                row = 2 * s + (core if own else 1 - core)
                value = read(pl.multiple_of(row * share, 8), share).astype(BF16)
                if own:
                    work[u, index] = value
                else:
                    other[index // 4, lax.rem(index, 4)] = value
            return 0

        lax.fori_loop(0, shards, body, 0)

    def add_core(u, landed):
        def body(n, _):
            work[u, n] = (
                work[u, n].astype(F32) + landed[n // 4, lax.rem(n, 4)].astype(F32)
            ).astype(BF16)
            return 0

        lax.fori_loop(0, shards, body, 0)

    def at_point(name):
        for u, stage in EVENTS[name]:
            finish(u, stage)

    def vector_pieces(rider):
        count = 6 if rider == 0 else 2
        padded = jnp.zeros((16 - 8, 128 - share), F32)
        for s in range(shards):
            index = index_of(RIDERS[rider], (s // 2) % 2, s % 2, s // 4)
            for n in range(2):
                row = 2 * s + n
                at = row * share
                source = small if rider == 0 else late
                value = source[0:8, at:at + share]
                ride[rider, n, index, 0:8, :] = jnp.concatenate([value, padded], axis=1)
                if rider == 0:
                    start = (row % (2 * groups)) * (wide * share)
                    ride[rider, n, index, 8:16, :] = jnp.concatenate(
                        [small[8:16, start:start + wide * share],
                         jnp.zeros((8, 128 - wide * share), F32)], axis=1)
                else:
                    ride[rider, n, index, 8:16, :] = jnp.zeros((8, 128), F32)

    def ride_core(rider):
        return remote(ride.at[rider, 1 - core], ride_core_in.at[rider], r_sends.at[rider, groups + 1],
                      r_recvs.at[rider, groups + 1], to_mate)

    def core_copy(src, dst, slot):
        return remote(src, dst, c_sends.at[slot], c_recvs.at[slot], to_mate)

    load("q", q_any, q_ref)
    load("k", k_any, k_ref)
    load("v", v_any, v_ref)
    barrier = pltpu.get_barrier_semaphore()
    for target in neighbours:
        pl.semaphore_signal(barrier, inc=1, device_id=target, device_id_type=MESH)
    last_row = k_ref.shape[0] - 1

    def forward_pair(p):
        lanes = lanes_of(p)

        def step(i, _):
            at = first_block + i
            shared, both = key_blocks(tab_ref, end, p, i, at, last_row)
            keys = gathered(k_ref, shared, both, low, lanes)
            values = gathered(v_ref, shared, both, low, lanes)
            query = split_pair(q_ref[rows_of(i), lanes], low)
            merged, lse = attend(keys, values, query, mask_ref, i, low)
            live = lax.broadcasted_iota(jnp.int32, (BLK, 1), 0) < (end + 1 - at) * BLK
            merged_ref[rows_of(i), lanes] = jnp.where(live, merged, 0.0).astype(BF16)
            lse_ref[p, pl.ds(i, 1), :] = lse
            return 0

        lax.fori_loop(0, own_blocks, step, 0, unroll=own_blocks)


    def dense(
        wo, wu, wd, cot_ref, normed_one, root_one, first_low, act, slope, ffn, tmp, other,
    ):
        d_ffn = cot_ref
        for name in ("q", "k", "v"):
            loading[name].wait()
        for name, src, dst in (
            ("x", x_any, x_ref), ("wo", wo_any, wo), ("wu", wu_any, wu), ("wd", wd_any, wd),
            ("cot", cot_any, cot_ref),
        ):
            load(name, src, dst)

        def forward_two(n, _):
            for inner in range(2):
                forward_pair(2 * n + inner)
            return 0

        lax.fori_loop(0, pairs // 2, forward_two, 0)
        bo, g1, s1, bd, g2, s2 = (
            ref[...][None] for ref in (bo_ref, g1_ref, s1_ref, bd_ref, g2_ref, s2_ref))

        for name in ("x", "wo"):
            loading[name].wait()
        ffn[...] = dot(merged_ref[...], wo[...])

        def norm_one(at, r):
            normed, inv_root = normed_rows(x_ref[at, :].astype(F32) + (ffn[at, :] + bo))
            normed_one[at, :] = normed
            root_one[at, :] = inv_root
            first_low[at, :] = (normed * g1 + s1).astype(BF16)

        tiles(norm_one)

        loading["wu"].wait()
        loading["wd"].wait()
        ffn[...] = jnp.zeros_like(ffn)

        def forward(j, _):
            at = columns(j)
            u = dot(first_low[...], wu[:, at]) + bu_ref[:, at]
            square = u * u
            t = jnp.tanh(GELU_C * (u + GELU_A * (square * u)))
            upper = 0.5 * (1.0 + t)
            act[j] = (u * upper).astype(BF16)
            slope[j] = (
                upper + (0.5 * GELU_C) * u * (1.0 - t * t) * (1.0 + (3.0 * GELU_A) * square)
            ).astype(slope.dtype)
            ffn[...] += dot(act[j], wd[at, :])
            return 0

        lax.fori_loop(0, wide, forward, 0)

        small[...] = jnp.zeros_like(small)
        limit = (end + 1) * BLK - seq * rows
        loading["cot"].wait()

        def norm_two(at, r):
            first = normed_one[at, :] * g1 + s1
            normed, inv_root = normed_rows(first + (ffn[at, :] + bd))
            result_ref[at, :] = (normed * g2 + s2).astype(BF16)
            place = lax.broadcasted_iota(jnp.int32, (tile, 1), 0) + r * tile
            grad = cot_ref[at, :].astype(F32) * (place < limit).astype(F32)
            pulled = norm_pull(grad, normed, inv_root, g2)
            rounded = pulled.astype(BF16)
            ffn[at, :] = pulled
            d_ffn[at, :] = rounded
            small[0:1, :] += column_sum(grad * normed)
            small[1:2, :] += column_sum(grad)
            small[2:3, :] += column_sum(rounded.astype(F32))

        tiles(norm_two)

        pl.semaphore_wait(barrier, len(neighbours))
        down_copies = []
        for j in range(wide):
            tmp[...] = dot_tn(act[j], d_ffn[...])

            def pieces(n, _):
                at_x, at_y = n // 2, lax.rem(n, 2)
                for own in (True, False):
                    row = 2 * n + (core if own else 1 - core)
                    at = pl.multiple_of(row * (wide * share), 8)
                    for u in range(4):
                        value = tmp[
                            pl.ds(pl.multiple_of(at + (u // 2) * UNIT[0], 8), UNIT[0]),
                            (u % 2) * half:(u % 2 + 1) * half].astype(BF16)
                        if own:
                            work[u, index_of(u, at_x, at_y, j)] = value
                        else:
                            other[j, u, n] = value
                return 0

            lax.fori_loop(0, 4, pieces, 0)
            down_copies.append(core_copy(other.at[j], core_down.at[j], j))
            down_copies[-1].start()

        def backward(j, _):
            d_hidden = (dot_nt(d_ffn[...], wd[columns(j), :]) * slope[j].astype(F32)).astype(BF16)
            act[j] = d_hidden
            for n in range(wide):
                @pl.when(j == n)
                def _():
                    small[8 + n:9 + n, :] = column_sum(d_hidden.astype(F32))
            return 0

        lax.fori_loop(0, wide, backward, 0)

        for copy in down_copies:
            copy.wait()

        def sum_down(s, _):
            at_z, at_x, at_y = shard_of(s)
            for u in range(4):
                index = index_of(u, at_x, at_y, at_z)
                work[u, index] = (
                    work[u, index].astype(F32) + core_down[at_z, u, at_x * 2 + at_y].astype(F32)
                ).astype(BF16)
            return 0

        lax.fori_loop(0, shards, sum_down, 0)
        for u in range(4):
            begin(u, 0)

        up_copies = []

        def end_up(j):
            up_copies[j].wait()
            add_core(UP + j, core_up.at[j])
            begin(UP + j, 0)

        for j in range(wide):
            tmp[...] = dot_tn(first_low[...], act[j])
            split_pieces(UP + j, functools.partial(folded, tmp), other.at[j])
            up_copies.append(core_copy(other.at[j], core_up.at[j], wide + j))
            up_copies[-1].start()
            if j:
                end_up(j - 1)

        for j in range(wide):
            ffn[...] += dot_nt(act[j], wu[:, j * features:(j + 1) * features])
            if j == 1:
                end_up(wide - 1)
        at_point("up")

        def pull_one(at, r):
            grad = ffn[at, :]
            normed = normed_one[at, :]
            pulled = norm_pull(grad, normed, root_one[at, :], g1)
            rounded = pulled.astype(BF16)
            dx_ref[at, :] = pulled
            d_attn_ref[at, :] = rounded
            small[3:4, :] += column_sum(grad * normed)
            small[4:5, :] += column_sum(grad)
            small[5:6, :] += column_sum(rounded.astype(F32))

        tiles(pull_one)
        live = lax.broadcasted_iota(jnp.int32, (rows, 1), 0) < limit
        d_merged_ref[...] = jnp.where(live, dot_nt(d_attn_ref[...], wo[...]), 0.0).astype(BF16)
        at_point("dense")

    low_rows = VMEM((rows, features), BF16)
    full_rows = VMEM((rows, features), F32)
    square_low = VMEM((features, features), BF16)
    pl.run_scoped(
        dense, square_low, VMEM((features, hidden), BF16), VMEM((hidden, features), BF16),
        low_rows, full_rows, VMEM((rows, 1), F32), low_rows, VMEM((wide, rows, features), BF16),
        VMEM((wide, rows, features), SLOPE), full_rows, VMEM((features, features), F32),
        VMEM((4, 4, 4) + UNIT, BF16),
    )


    def attention(
        dq_ref, far_ref, wk, wv, wq, acc, last, picked, buf, dko, dvo, dkr, dvr, out_far, other,
        tmp,
    ):
        for name, src, dst in (
            ("far", far_any, far_ref), ("wk", wk_any, wk), ("wv", wv_any, wv), ("wq", wq_any, wq),
        ):
            load(name, src, dst)
        square_copies = [
            core_copy(other.at[n], core_down.at[n], SQUARE + n) for n in range(4)
        ]

        def square(u):
            split_pieces(u, functools.partial(folded, tmp), other.at[u - SQUARE])
            square_copies[u - SQUARE].start()

        def end_square(u):
            square_copies[u - SQUARE].wait()
            if u in RIDERS:
                n = RIDERS.index(u)
                ride_core(n).wait()
                ride[n, core] = ride[n, core] + ride_core_in[n]
            add_core(u, core_down.at[u - SQUARE])
            begin(u, 0)

        def copy_pair(p, slot, owner):
            return remote(buf.at[p, owner], pair_in.at[p, slot], p_sends.at[p, slot],
                          p_recvs.at[p, slot], to_mate)

        def sum_pair(p):
            lanes = lanes_of(p)
            for slot, owner, keys_to, values_to in ((0, across, dkr, dvr), (1, seq, dko, dvo)):
                copy_pair(p, slot, diagonal if slot == 0 else mate).wait()
                for n, to in ((0, keys_to), (1, values_to)):
                    to[:, lanes] = (
                        buf[p, owner, n].astype(F32) + pair_in[p, slot, n].astype(F32)
                    ).astype(BF16)

        def heads():
            for n in range(2):
                picked[n, picks_count] = jnp.zeros((BLK, PAIR), F32)
                for edge in (0, own_blocks + 3):
                    acc[n, edge] = jnp.zeros((BLK, PAIR), F32)
            def one_pair(p, _):
                lanes = lanes_of(p)
                acc[:, 1:own_blocks + 3] = jnp.zeros((2, own_blocks + 2, BLK, PAIR), F32)
                last[...] = jnp.zeros_like(last)

                def step(i, _):
                    at = first_block + i
                    shared, both = key_blocks(tab_ref, end, p, i, at, last_row)
                    keys = gathered(k_ref, shared, both, low, lanes)
                    values = gathered(v_ref, shared, both, low, lanes)
                    query = split_pair(q_ref[rows_of(i), lanes], low)
                    grad = split_pair(d_merged_ref[rows_of(i), lanes], low)
                    blank = jnp.zeros_like(query)
                    both_in = jnp.concatenate(
                        [jnp.concatenate([query, blank], axis=1),
                         jnp.concatenate([blank, grad], axis=1)], axis=0)
                    products = dot_nt(jnp.concatenate([keys, values], axis=1), both_in)
                    scores = masked_scores(products[:, :PAIR], mask_ref, i)
                    share_of = jnp.exp(scores - lse_ref[p, pl.ds(i, 1), :])
                    d_share = products[:, PAIR:]
                    centre = jnp.sum(share_of * d_share, axis=0, keepdims=True)
                    d_scores = (share_of * (d_share - centre)).astype(BF16)
                    d_query = dot_tn(d_scores, keys) * SCALE
                    dq_ref[rows_of(i), lanes] = jnp.where(
                        low, d_query[:BLK], d_query[BLK:]).astype(BF16)
                    products = dot(
                        jnp.concatenate([d_scores, share_of.astype(BF16)], axis=1), both_in)
                    parts = (products[:, :PAIR], products[:, PAIR:])
                    for n, part in enumerate(parts):
                        for slot in range(3):
                            acc[n, i + slot + 1] += part[slot * BLK:(slot + 1) * BLK]
                        for slot in range(2):
                            last[n, slot] += part[(3 + slot) * BLK:(4 + slot) * BLK]
                    for t in range(3):
                        one, two = (
                            prev_ref[lax.div(h, 3), i, lax.rem(h, 3) * 3 + t]
                            for h in (2 * p, 2 * p + 1))
                        for n, part in enumerate(parts):
                            picked[n, i * 3 + t] = part[(5 + t) * BLK:(6 + t) * BLK] + jnp.where(
                                low, picked[n, one], picked[n, two])
                    return 0

                lax.fori_loop(0, own_blocks, step, 0, unroll=own_blocks)

                def gather(owner, _):
                    first_owner = (owner == 0).astype(F32)
                    for inner in range(own_blocks):
                        block = owner * own_blocks + inner
                        window = jnp.minimum(
                            jnp.maximum(block - first_block + 2, 0), own_blocks + 3)
                        one, two = (
                            tail_ref[lax.div(h, 3), lax.rem(h, 3), block]
                            for h in (2 * p, 2 * p + 1))
                        for n in range(2):
                            total = acc[n, window] + jnp.where(low, picked[n, one], picked[n, two])
                            total = total + last[n, 1] * mask_ref[own_blocks, block]
                            if inner == 0:
                                total = total + last[n, 0] * first_owner
                            buf[p, owner, n, inner * BLK:(inner + 1) * BLK] = total.astype(BF16)
                    return 0

                lax.fori_loop(0, 4, gather, 0)
                copy_pair(p, 0, diagonal).start()
                copy_pair(p, 1, mate).start()

                @pl.when(p > 0)
                def _():
                    sum_pair(p - 1)

                for n in range(pairs):
                    @pl.when(p == n)
                    def _():
                        if n == 0:
                            end_square(OUT)
                        at_point(n)

                return 0

            lax.fori_loop(0, pairs, one_pair, 0)

        vector_pieces(0)
        ride_core(0).start()
        tmp[...] = dot_tn(merged_ref[...], d_attn_ref[...])
        square(OUT)
        heads()
        tmp[...] = dot_tn(x_ref[...], dq_ref[...])
        square(QUERY)
        for name in ("far", "wk", "wv", "wq"):
            loading[name].wait()
        sum_pair(pairs - 1)
        at_point("sum")
        tmp[...] = dot_tn(x_ref[...], dko[...]) + dot_tn(far_ref[...], dkr[...])
        square(KEY)
        end_square(QUERY)
        tmp[...] = dot_tn(x_ref[...], dvo[...]) + dot_tn(far_ref[...], dvr[...])
        square(VALUE)
        end_square(KEY)
        late[...] = jnp.zeros_like(late)
        late[0:1, :] = column_sum(dq_ref[...].astype(F32))
        late[1:2, :] = column_sum(dvo[...].astype(F32)) + column_sum(dvr[...].astype(F32))
        vector_pieces(1)
        ride_core(1).start()
        out_far[...] = (dot_nt(dkr[...], wk[...]) + dot_nt(dvr[...], wv[...])).astype(BF16)
        far = remote(out_far, in_far, far_sems.at[0], far_sems.at[1], to_y)
        far.start()
        end_square(VALUE)
        at_point("far")
        dx_ref[...] += dot_nt(dko[...], wk[...]) + dot_nt(dvo[...], wv[...])
        at_point("x")
        dx_ref[...] += dot_nt(dq_ref[...], wq[...])
        at_point("y")
        for u, stage in EVENTS["end"]:
            if u == "far":
                far.wait()
                dx_ref[...] += in_far[...].astype(F32)
            else:
                finish(u, stage)

    pl.run_scoped(
        attention, low_rows, low_rows, square_low, square_low, square_low,
        VMEM((2, own_blocks + 4, BLK, PAIR), F32), VMEM((2, 2, BLK, PAIR), F32),
        VMEM((2, picks_count + 1, BLK, PAIR), F32), VMEM((pairs, 4, 2, rows, PAIR), BF16),
        low_rows, low_rows, low_rows, low_rows, low_rows, VMEM((4, 4, 4) + UNIT, BF16),
        VMEM((features, features), F32),
    )


SLOPE = BF16


def layer_tail(
    groups, table, prev, tail, mask, biases, up_bias, tokens, cotangent, out_weight,
    up_weight, down_weight, query, keys, values, key_weight, value_weight, query_weight, far_tokens,
):
    rows, features = tokens.shape
    hidden = up_weight.shape[1]
    own_blocks = rows // BLK
    pairs = features // PAIR
    share = features // (8 * groups)
    wide = hidden // features
    low = VMEM((rows, features), BF16)
    kv = VMEM((4 * own_blocks, BLK, features), BF16)
    line = jax.ShapeDtypeStruct((share, features), F32)
    any_space = pl.BlockSpec(memory_space=pl.ANY)
    in_smem = pl.BlockSpec(memory_space=pltpu.SMEM)
    dma = pltpu.SemaphoreType.DMA
    return pl.pallas_call(
        functools.partial(layer_kernel, rows, 128, own_blocks, groups),
        out_shape=(
            jax.ShapeDtypeStruct((rows, features), BF16),
            jax.ShapeDtypeStruct((rows, features), F32), line, line, line, line,
            jax.ShapeDtypeStruct((share, hidden), F32),
            jax.ShapeDtypeStruct((wide * share, features), F32),
            jax.ShapeDtypeStruct((32, 128), F32),
        ),
        in_specs=[in_smem] * 4 + [whole_vmem()] * 7 + [any_space] * 12,
        out_specs=(whole_vmem(),) * 9,
        scratch_shapes=[
            VMEM((12, 4 * groups) + UNIT, BF16),
            VMEM((12, 4 * groups - 1) + UNIT, BF16),
            VMEM((4, 4, 4) + UNIT, BF16),
            VMEM((4, 4, 4) + UNIT, BF16),
            VMEM((pairs, 2, 2, rows, PAIR), BF16),
            low,
            VMEM((16, features), F32),
            VMEM((8, features), F32),
            VMEM((2, 2, 4 * groups, 16, 128), F32),
            VMEM((2, 4 * groups - 1, 16, 128), F32),
            VMEM((2, 4 * groups, 16, 128), F32),
            low, low, low, low, low, kv, kv, VMEM((pairs, own_blocks, PAIR), F32),
            dma((13,)), dma((12, groups + 1)), dma((12, groups + 1)), dma((12,)), dma((12,)),
            dma((pairs, 2)), dma((pairs, 2)), dma((2, groups + 2)), dma((2, groups + 2)),
            dma((2,)),
        ],
        compiler_params=pltpu.CompilerParams(
            collective_id=3, has_side_effects=True, vmem_limit_bytes=LIMIT
        ),
        name="layer_tail",
    )(
        table, prev, tail, mask, *biases, up_bias, tokens, cotangent, out_weight, up_weight,
        down_weight, query, keys, values, key_weight, value_weight, query_weight, far_tokens,
    )


def finish_kernel(groups, vec_ref, *refs):
    count = len(refs) - 9
    given, out, vectors = refs[:count // 2], refs[count // 2:count], refs[count:]
    for src, dst in zip(given, out):
        dst[...] = src[...]
    share = vectors[0].shape[0]
    for n in range(8):
        vectors[n][...] = vec_ref[n if n < 6 else n + 10, 0:share]
    shard = lax.axis_index("dp") * 4 + lax.axis_index("seq")
    mine = vec_ref[pl.ds(8 + shard // (2 * groups), 1), :]
    vectors[8][...] = mine[0, 0:vectors[8].shape[0]]


STEPS = 2


def whole(shape):
    return pl.BlockSpec(shape, lambda i: (0,) * len(shape))


def hand_out(groups, vectors, arrays):
    features = arrays[0].shape[1]
    share = features // (8 * groups)
    wide = arrays[-1].shape[0] // share
    shapes = [jax.ShapeDtypeStruct(a.shape, a.dtype) for a in arrays]
    specs = [
        pl.BlockSpec((a.shape[0] // STEPS, a.shape[1]), lambda i: (i, 0))
        if a.shape[0] % (16 * STEPS) == 0 else whole(a.shape) for a in arrays
    ]
    lines = [jax.ShapeDtypeStruct((share,), F32)] * 8 + [jax.ShapeDtypeStruct((wide * share,), F32)]
    return pl.pallas_call(
        functools.partial(finish_kernel, groups),
        out_shape=tuple(shapes + lines),
        grid=(STEPS,),
        in_specs=[whole((32, 128))] + specs,
        out_specs=tuple(specs) + (whole((share,)),) * 8 + (whole((wide * share,)),),
        name="hand_out",
    )(vectors, *arrays)


def layer_norm(values, gain, shift):
    center = jnp.mean(values, axis=-1, keepdims=True)
    centered = values - center
    variance = jnp.mean(centered * centered, axis=-1, keepdims=True)
    inv_root = lax.rsqrt(variance + NORM_EPS)
    normed = centered * inv_root
    return (normed * gain + shift, normed, inv_root)


def norm_back(grad_out, normed, inv_root, gain):
    d_normed = grad_out * gain
    grad_in = inv_root * (
        d_normed
        - jnp.mean(d_normed, axis=-1, keepdims=True)
        - normed * jnp.mean(d_normed * normed, axis=-1, keepdims=True)
    )
    return (grad_in, jnp.sum(grad_out * normed, axis=0), jnp.sum(grad_out, axis=0))


def on_device(
    groups,
    tokens, filled_blocks, random_blocks, query_weight, query_bias, key_weight, value_weight,
    value_bias, out_weight, out_bias, attn_gain, attn_shift, up_weight, up_bias, down_weight,
    down_bias, ffn_gain, ffn_shift, cotangent,
):
    row_count, feature_count = tokens.shape
    filled = filled_blocks[0]
    place = lax.axis_index("seq") * row_count + jnp.arange(row_count, dtype=jnp.int32)
    live_tokens = (place < filled * BLK).astype(F32)[:, None]

    query, keys, values, far_tokens, table, prev, tail, mask = gather_project(
        filled_blocks, tokens,
        random_blocks.transpose(2, 3, 0, 1), query_weight, key_weight, value_weight, query_bias,
        value_bias)
    keys, values = (t.reshape(-1, BLK, feature_count) for t in (keys, values))
    if groups:
        *arrays, vectors = layer_tail(
            groups, table, prev, tail, mask,
            (out_bias, attn_gain, attn_shift, down_bias, ffn_gain, ffn_shift), up_bias[None],
            tokens, cotangent, out_weight, up_weight, down_weight, query, keys, values,
            key_weight, value_weight, query_weight, far_tokens)
        (result, grad_tokens, gq, gk, gv, go, up, down, g2, s2, bd, g1, s1, bo, bq, bv,
         bu) = hand_out(groups, vectors, arrays)
        return (
            result, grad_tokens, gq, bq, gk, gv, bv, go, bo, g1, s1, up, bu, down, bd, g2, s2)

    merged, lse = attention_forward(table, filled_blocks, mask, query, keys, values)
    attn = dot(merged, out_weight) + out_bias
    first, normed_one, root_one = layer_norm(tokens.astype(F32) + attn, attn_gain, attn_shift)
    first_low = first.astype(BF16)
    hidden = dot(first_low, up_weight) + up_bias
    act, gelu_pull = jax.vjp(jax.nn.gelu, hidden)
    act_low = act.astype(BF16)
    ffn = dot(act_low, down_weight) + down_bias
    result, normed_two, root_two = layer_norm(first + ffn, ffn_gain, ffn_shift)
    grad_result = cotangent.astype(F32) * live_tokens
    d_sum_two, grad_ffn_gain, grad_ffn_shift = norm_back(
        grad_result, normed_two, root_two, ffn_gain
    )
    d_ffn = d_sum_two.astype(BF16)
    grad_down_bias = jnp.sum(d_ffn, axis=0, dtype=F32)
    grad_down_weight = dot_tn(act_low, d_ffn)
    d_act = dot_nt(d_ffn, down_weight)
    d_hidden = gelu_pull(d_act)[0].astype(BF16)
    grad_up_bias = jnp.sum(d_hidden, axis=0, dtype=F32)
    grad_up_weight = dot_tn(first_low, d_hidden)
    d_first = d_sum_two + dot_nt(d_hidden, up_weight)
    d_sum_one, grad_attn_gain, grad_attn_shift = norm_back(d_first, normed_one, root_one, attn_gain)
    d_attn = d_sum_one.astype(BF16)
    grad_out_bias = jnp.sum(d_attn, axis=0, dtype=F32)
    grad_out_weight = dot_tn(merged, d_attn)
    d_merged = dot_nt(d_attn, out_weight).astype(BF16)

    d_query, d_keys, d_values = attention_backward(
        table, filled_blocks, mask, query, keys, values, d_merged, lse
    )
    grad_tokens, dk_own, dv_own, dk_far, dv_far = exchange(
        d_keys, d_values, d_query, d_sum_one, query_weight, key_weight, value_weight
    )
    grad_query_weight = dot_tn(tokens, d_query)
    grad_query_bias = jnp.sum(d_query, axis=0, dtype=F32)
    grad_key_weight = dot_tn(tokens, dk_own) + dot_tn(far_tokens, dk_far)
    grad_value_weight = dot_tn(tokens, dv_own) + dot_tn(far_tokens, dv_far)
    grad_value_bias = jnp.sum(dv_own, axis=0, dtype=F32) + jnp.sum(dv_far, axis=0, dtype=F32)

    square = (grad_query_weight, grad_key_weight, grad_value_weight, grad_out_weight)
    vectors = (
        grad_query_bias, grad_value_bias, grad_out_bias, grad_attn_gain, grad_attn_shift,
        grad_down_bias, grad_ffn_gain, grad_ffn_shift,
    )
    square, up, down, vectors, up_sum = summed_anywhere(
        square, grad_up_weight, grad_down_weight, vectors, grad_up_bias)
    return (
        result.astype(BF16), grad_tokens, square[0], vectors[0], square[1], square[2], vectors[1],
        square[3], vectors[2], vectors[3], vectors[4], up, up_sum, down, vectors[5], vectors[6],
        vectors[7],
    )


def solution(mesh):
    both = P(("dp", "seq"), None)
    line = P(("dp", "seq"))
    placed = (both, P("dp"), P("dp", None, "seq", None)) + (P(),) * 15 + (both,)
    groups = 4 if mesh.shape["dp"] == 8 and mesh.shape["seq"] == 4 else 0
    return jax.shard_map(
        functools.partial(on_device, groups),
        mesh=mesh,
        in_specs=placed,
        out_specs=(
            both, both, both, line, both, both, line, both, line, line, line, both, line, both,
            line, line, line,
        ),
        check_vma=False,
    )
```

```python
import functools

import jax
import jax.numpy as jnp
from jax import lax
from jax.experimental import pallas as pl
from jax.experimental.pallas import tpu as pltpu
from jax.sharding import PartitionSpec as P

HEAD_DIM = 64
BLK = 64
PAIR = 2 * HEAD_DIM
TABLE = 8
NORM_EPS = 1e-05
MASKED = -1e30
SCALE = HEAD_DIM ** (-0.5)
MESH = pl.DeviceIdType.MESH
BF16 = jnp.bfloat16
F32 = jnp.float32
VMEM = pltpu.VMEM
LIMIT = 63 << 20


def whole_vmem():
    return pl.BlockSpec(memory_space=pltpu.VMEM)


def dot(left, right):
    return jnp.dot(left, right, preferred_element_type=F32)


def dot_nt(left, right):
    return lax.dot_general(left, right, (((1,), (1,)), ((), ())), preferred_element_type=F32)


def dot_tn(left, right):
    return lax.dot_general(left, right, (((0,), (0,)), ((), ())), preferred_element_type=F32)


def tables_of(tab_out, filled, first_block, each, prev_out, tail_out, mask_out):
    groups, blocks, width = tab_out.shape
    slot_blocks = width
    none = blocks * each
    lane = lax.broadcasted_iota(jnp.int32, (blocks, width), 1)
    row = lax.broadcasted_iota(jnp.int32, (blocks, width), 0)
    pick = lax.rem(lane, each)
    key_row = lax.broadcasted_iota(jnp.int32, (slot_blocks, width), 0)
    key_pick = lax.rem(lax.broadcasted_iota(jnp.int32, (slot_blocks, width), 1), each)
    for g in range(groups):
        table = tab_out[g]
        prev = jnp.full((blocks, width), -1, jnp.int32)
        for shift in range(1 - each, each):
            moved = pltpu.roll(table, (-shift) % width, axis=1)
            inside = (pick + shift >= 0) & (pick + shift < each)
            for i in range(blocks - 1):
                same = (moved[i:i + 1] == table) & (row > i) & inside
                prev = jnp.maximum(prev, jnp.where(same, i * each + pick + shift, -1))
        prev = jnp.where(prev < 0, none, prev)
        prev_out[g] = jnp.where(lane == width - 1, filled - 1, prev)
        tail = jnp.full((slot_blocks, width), -1, jnp.int32)
        for i in range(blocks):
            tail = jnp.maximum(tail, jnp.where(table[i:i + 1] == key_row, i * each + key_pick, -1))
        best = tail
        for shift in range(1, each):
            best = jnp.maximum(best, pltpu.roll(tail, width - shift, axis=1))
        turned = jnp.where(best < 0, none, best).astype(F32).T.astype(jnp.int32)
        for h in range(3):
            tail_out[g, h:h + 1, :] = turned[h * each:h * each + 1, :]
        tail_out[g, 3:blocks, :] = jnp.full((blocks - 3, width), none, jnp.int32)
    at = first_block + row
    window = at + lane - 1
    ok = jnp.where(
        lane < 3, ((window >= 0) & (window < filled)).astype(jnp.int32),
        jnp.where(lane == 3, (at >= 2).astype(jnp.int32),
                  (jnp.abs(at - (filled - 1)) > 1).astype(jnp.int32)))
    mask_out[0:blocks, :] = jnp.where(ok == 1, 0.0, MASKED)
    mask_out[blocks:2 * blocks, :] = (lane == filled - 1).astype(F32)


def gather_kernel(
    rows, width, filled_ref, x_ref, picks_ref, wq_any, wk_any, wv_any, qb_ref, vb_ref,
    q_any, k_any, v_any, far_any, tab_out, prev_out, tail_out, mask_out,
    wq_ref, wk_ref, wv_ref, q_ref, k_ref, v_ref,
    tab_ref, land, tab_land, loads, stores, sends, recvs, tab_sends, tab_recvs,
):
    parts = 4
    part = rows // parts
    dp, me = lax.axis_index("dp"), lax.axis_index("seq")
    mate, across, diagonal = (lax.bitwise_xor(me, bit) for bit in (1, 2, 3))
    weights = [
        pltpu.make_async_copy(src, dst, loads.at[n])
        for n, (src, dst) in enumerate(((wq_any, wq_ref), (wk_any, wk_ref), (wv_any, wv_ref)))
    ]
    for copy in weights:
        copy.start()
    barrier = pltpu.get_barrier_semaphore()
    for other in (mate, across, diagonal):
        pl.semaphore_signal(barrier, inc=1, device_id=(dp, other), device_id_type=MESH)
    heads_here, each, _, blocks = picks_ref.shape
    chosen = picks_ref[...].reshape(heads_here * each, blocks).astype(F32)
    chosen = jnp.concatenate(
        [chosen, jnp.zeros((heads_here * each, 128 - blocks), F32)], axis=1)
    chosen = jnp.concatenate([chosen, jnp.zeros((128 - heads_here * each, 128), F32)], axis=0)
    tab_ref[...] = chosen.T[0:blocks].astype(jnp.int32)
    pl.semaphore_wait(barrier, 3)

    def send(src, dst, slot, target):
        copy = pltpu.make_async_remote_copy(
            src_ref=src, dst_ref=dst, send_sem=sends.at[slot], recv_sem=recvs.at[slot],
            device_id=(dp, target), device_id_type=MESH,
        )
        copy.start()
        return copy

    tables = []
    own_blocks = tab_ref.shape[0] // 4
    for slot, other in enumerate((mate, across, diagonal)):
        copy = pltpu.make_async_remote_copy(
            src_ref=tab_ref.at[pl.ds(pl.multiple_of(other * own_blocks, 8), own_blocks)],
            dst_ref=tab_land.at[slot], send_sem=tab_sends.at[slot], recv_sem=tab_recvs.at[slot],
            device_id=(dp, other), device_id_type=MESH,
        )
        copy.start()
        tables.append(copy)
    far = [
        send(x_ref.at[pl.ds(r * part, part)], land.at[0, pl.ds(r * part, part)], r, across)
        for r in range(parts)
    ]
    near = send(x_ref, land.at[1], parts, mate)
    stored = []

    def store(src, dst, start, count):
        at = pl.ds(pl.multiple_of(start, part), count)
        copy = pltpu.make_async_copy(src.at[at], dst.at[at], stores.at[len(stored)])
        copy.start()
        stored.append(copy)

    def keys_values(x, at):
        k_ref[pl.ds(at, width), :] = dot(x, wk_ref[...]).astype(BF16)
        v_ref[pl.ds(at, width), :] = (dot(x, wv_ref[...]) + vb_ref[...][None]).astype(BF16)

    for copy in weights:
        copy.wait()

    def own(r, _):
        at = pl.multiple_of(r * width, width)
        x = x_ref[pl.ds(at, width), :]
        q_ref[pl.ds(at, width), :] = (
            (dot(x, wq_ref[...]) + qb_ref[...][None]).astype(BF16) * jnp.asarray(SCALE, BF16)
        )
        keys_values(x, pl.multiple_of(me * rows + at, width))
        return 0

    lax.fori_loop(0, rows // width, own, 0)
    store(q_ref, q_any, 0, rows)
    store(k_ref, k_any, me * rows, rows)
    store(v_ref, v_any, me * rows, rows)

    def block(slot, owner, start, count):
        def step(r, _):
            at = pl.multiple_of(start + r * width, width)
            keys_values(land[slot, pl.ds(at, width), :], pl.multiple_of(owner * rows + at, width))
            return 0

        lax.fori_loop(0, count // width, step, 0)
        store(k_ref, k_any, owner * rows + start, count)
        store(v_ref, v_any, owner * rows + start, count)

    near.wait()
    block(1, mate, 0, rows)
    for copy in tables:
        copy.wait()
    tab_out[pl.ds(me, 1)] = tab_ref[pl.ds(pl.multiple_of(me * own_blocks, 8), own_blocks)][None]
    for slot, other in enumerate((mate, across, diagonal)):
        tab_out[pl.ds(other, 1)] = tab_land[slot][None]
    tables_of(tab_out, filled_ref[0], me * own_blocks, each, prev_out, tail_out, mask_out)
    relayed = []
    for r in range(parts):
        far[r].wait()
        piece = pl.ds(r * part, part)
        relayed.append(send(land.at[0, piece], land.at[2, piece], parts + 1 + r, mate))
        store(land.at[0], far_any, r * part, part)
        block(0, across, r * part, part)
        if r:
            relayed[r - 1].wait()
            block(2, diagonal, (r - 1) * part, part)
    relayed[-1].wait()
    block(2, diagonal, (parts - 1) * part, part)
    for copy in stored:
        copy.wait()


def gather_project(
    filled, tokens, chosen, query_weight, key_weight, value_weight, query_bias, value_bias,
):
    rows, features = tokens.shape
    own_blocks = rows // BLK
    slot_blocks = chosen.shape[3]
    copies = 4 + 1 + 4
    any_space = pl.BlockSpec(memory_space=pl.ANY)
    low = jax.ShapeDtypeStruct((rows, features), BF16)
    slot = jax.ShapeDtypeStruct((4 * rows, features), BF16)
    table = jax.ShapeDtypeStruct((4, own_blocks, 128), jnp.int32)
    dma = pltpu.SemaphoreType.DMA
    return pl.pallas_call(
        functools.partial(gather_kernel, rows, 128),
        out_shape=(
            low, slot, slot, low, table, table, table,
            jax.ShapeDtypeStruct((2 * own_blocks, 128), F32),
        ),
        in_specs=[pl.BlockSpec(memory_space=pltpu.SMEM)] + [whole_vmem()] * 2 + [any_space] * 3
        + [whole_vmem()] * 2,
        out_specs=(any_space,) * 4 + (whole_vmem(),) * 4,
        scratch_shapes=[
            VMEM((features, features), BF16),
            VMEM((features, features), BF16),
            VMEM((features, features), BF16),
            VMEM((rows, features), BF16),
            VMEM((4 * rows, features), BF16),
            VMEM((4 * rows, features), BF16),
            VMEM((slot_blocks, 128), jnp.int32),
            VMEM((3, rows, features), BF16),
            VMEM((3, own_blocks, 128), jnp.int32),
            dma((3,)), dma((25,)), dma((copies,)), dma((copies,)), dma((3,)), dma((3,)),
        ],
        compiler_params=pltpu.CompilerParams(
            collective_id=0, has_side_effects=True, vmem_limit_bytes=LIMIT
        ),
        name="gather_project",
    )(filled, tokens, chosen, query_weight, key_weight, value_weight, query_bias, value_bias)


def key_blocks(tab_ref, end, pair, i, at, last_row):
    def chosen(head, t):
        group, inner = lax.div(head, 3), lax.rem(head, 3)
        return tab_ref[group, i, inner * 3 + t]

    head = 2 * pair
    both = [(chosen(head, t), chosen(head + 1, t)) for t in range(3)]
    shared = [
        jnp.maximum(at - 1, 0), at, jnp.minimum(at + 1, last_row), jnp.int32(0), end,
    ]
    return shared, both


def rows_of(block):
    return pl.ds(pl.multiple_of(block * BLK, BLK), BLK)


def lanes_low(rows):
    return lax.broadcasted_iota(jnp.int32, (rows, PAIR), 1) < HEAD_DIM


def split_pair(x, low):
    zero = jnp.zeros_like(x)
    return jnp.concatenate([jnp.where(low, x, zero), jnp.where(low, zero, x)], axis=0)


def gathered(ref, shared, both, low, lanes=slice(None)):
    tiles = [ref[b, :, lanes] for b in shared]
    for first, second in both:
        tiles.append(jnp.where(low, ref[first, :, lanes], ref[second, :, lanes]))
    return jnp.concatenate(tiles, axis=0)


def masked_scores(scores, mask_ref, i):
    parts = [scores[n * BLK:(n + 1) * BLK] + mask_ref[i, n] for n in range(5)]
    return jnp.concatenate(parts + [scores[5 * BLK:]], axis=0)


def attend(keys, values, query, mask_ref, i, low):
    scores = masked_scores(dot_nt(keys, query), mask_ref, i)
    highest = jnp.max(scores, axis=0, keepdims=True)
    weights = jnp.exp(scores - highest)
    total = jnp.sum(weights, axis=0, keepdims=True)
    share = (weights * (1.0 / total)).astype(BF16)
    output = dot_tn(share, values)
    return jnp.where(low, output[:BLK], output[BLK:]), highest + jnp.log(total)


def forward_kernel(own_blocks, tab_ref, filled_ref, mask_ref, q_ref, k_ref, v_ref, out_ref, lse_ref):
    pair = pl.program_id(0)
    filled = filled_ref[0]
    first_block = lax.axis_index("seq") * own_blocks
    last_row = k_ref.shape[0] - 1
    low = lanes_low(BLK)

    def step(i, _):
        at = first_block + i
        shared, both = key_blocks(tab_ref, filled - 1, pair, i, at, last_row)
        keys = gathered(k_ref, shared, both, low)
        values = gathered(v_ref, shared, both, low)
        query = split_pair(q_ref[rows_of(i), :], low)
        merged, lse = attend(keys, values, query, mask_ref, i, low)
        out_ref[rows_of(i), :] = jnp.where(at < filled, merged, 0.0).astype(BF16)
        lse_ref[0, pl.ds(i, 1), :] = lse
        return 0

    lax.fori_loop(0, own_blocks, step, 0, unroll=own_blocks)


def attention_forward(table, filled, mask, query, keys, values):
    rows, features = query.shape
    own_blocks = rows // BLK
    slot_blocks = keys.shape[0]
    pairs = features // PAIR
    column = lambda n: pl.BlockSpec((n, PAIR), lambda p, *_: (0, p))
    blocks = lambda n: pl.BlockSpec((n, BLK, PAIR), lambda p, *_: (0, 0, p))
    return pl.pallas_call(
        functools.partial(forward_kernel, own_blocks),
        out_shape=(
            jax.ShapeDtypeStruct((rows, features), BF16),
            jax.ShapeDtypeStruct((pairs, own_blocks, PAIR), F32),
        ),
        grid_spec=pltpu.PrefetchScalarGridSpec(
            num_scalar_prefetch=3,
            grid=(pairs,),
            in_specs=[column(rows), blocks(slot_blocks), blocks(slot_blocks)],
            out_specs=(column(rows), pl.BlockSpec((1, own_blocks, PAIR), lambda p, *_: (p, 0, 0))),
        ),
        compiler_params=pltpu.CompilerParams(vmem_limit_bytes=LIMIT),
        name="attention_forward",
    )(table, filled, mask, query, keys, values)


def backward_kernel(
    own_blocks, tab_ref, filled_ref, mask_ref, q_ref, k_ref, v_ref, g_ref, lse_ref,
    dq_ref, dk_ref, dv_ref, dk_sum, dv_sum,
):
    pair = pl.program_id(0)
    filled = filled_ref[0]
    first_block = lax.axis_index("seq") * own_blocks
    last_row = k_ref.shape[0] - 1
    low = lanes_low(BLK)
    dk_sum[...] = jnp.zeros_like(dk_sum)
    dv_sum[...] = jnp.zeros_like(dv_sum)

    def step(i, _):
        at = first_block + i
        shared, both = key_blocks(tab_ref, filled - 1, pair, i, at, last_row)
        keys = gathered(k_ref, shared, both, low)
        values = gathered(v_ref, shared, both, low)
        query = split_pair(q_ref[rows_of(i), :], low)
        grad = split_pair(jnp.where(at < filled, g_ref[rows_of(i), :], jnp.zeros((), BF16)), low)
        scores = masked_scores(dot_nt(keys, query), mask_ref, i)
        share = jnp.exp(scores - lse_ref[0, pl.ds(i, 1), :])
        d_share = dot_nt(values, grad)
        centre = jnp.sum(share * d_share, axis=0, keepdims=True)
        d_scores = (share * (d_share - centre)).astype(BF16)
        d_query = dot_tn(d_scores, keys) * SCALE
        dq_ref[rows_of(i), :] = jnp.where(low, d_query[:BLK], d_query[BLK:]).astype(BF16)
        for total, part in ((dk_sum, dot(d_scores, query)), (dv_sum, dot(share.astype(BF16), grad))):
            for slot, block in enumerate(shared):
                total[rows_of(block), :] += part[slot * BLK:(slot + 1) * BLK]
            for t, (one, two) in enumerate(both):
                tile = part[(5 + t) * BLK:(6 + t) * BLK]
                total[rows_of(one), :] += jnp.where(low, tile, 0.0)
                total[rows_of(two), :] += jnp.where(low, 0.0, tile)
        return 0

    lax.fori_loop(0, own_blocks, step, 0, unroll=own_blocks)
    dk_ref[...] = dk_sum[...].astype(BF16)
    dv_ref[...] = dv_sum[...].astype(BF16)


def attention_backward(table, filled, mask, query, keys, values, grad, lse):
    rows, features = query.shape
    slot_blocks = keys.shape[0]
    slot_rows = slot_blocks * BLK
    own_blocks = rows // BLK
    pairs = features // PAIR
    blocks = lambda n: pl.BlockSpec((n, BLK, PAIR), lambda p, *_: (0, 0, p))
    column = lambda n: pl.BlockSpec((n, PAIR), lambda p, *_: (0, p))
    return pl.pallas_call(
        functools.partial(backward_kernel, own_blocks),
        out_shape=(
            jax.ShapeDtypeStruct((rows, features), BF16),
            jax.ShapeDtypeStruct((slot_rows, features), BF16),
            jax.ShapeDtypeStruct((slot_rows, features), BF16),
        ),
        grid_spec=pltpu.PrefetchScalarGridSpec(
            num_scalar_prefetch=3,
            grid=(pairs,),
            in_specs=[
                column(rows), blocks(slot_blocks), blocks(slot_blocks), column(rows),
                pl.BlockSpec((1, own_blocks, PAIR), lambda p, *_: (p, 0, 0)),
            ],
            out_specs=(column(rows), column(slot_rows), column(slot_rows)),
            scratch_shapes=[VMEM((slot_rows, PAIR), F32), VMEM((slot_rows, PAIR), F32)],
        ),
        compiler_params=pltpu.CompilerParams(vmem_limit_bytes=LIMIT),
        name="attention_backward",
    )(table, filled, mask, query, keys, values, grad, lse)


def exchange_kernel(
    rows, width, dk_ref, dv_ref, dq_ref, base_ref, wq_ref, wk_ref, wv_ref,
    dx_ref, dko_ref, dvo_ref, dkr_ref, dvr_ref,
    land, out_far, in_far, sends, recvs,
):
    dp, me = lax.axis_index("dp"), lax.axis_index("seq")
    mate, across, diagonal = (lax.bitwise_xor(me, bit) for bit in (1, 2, 3))
    barrier = pltpu.get_barrier_semaphore()
    for other in (mate, across):
        pl.semaphore_signal(barrier, inc=1, device_id=(dp, other), device_id_type=MESH)
    pl.semaphore_wait(barrier, 2)

    def send(src, dst, slot, target):
        copy = pltpu.make_async_remote_copy(
            src_ref=src, dst_ref=dst, send_sem=sends.at[slot], recv_sem=recvs.at[slot],
            device_id=(dp, target), device_id_type=MESH,
        )
        copy.start()
        return copy

    def owned(index):
        return pl.ds(pl.multiple_of(index * rows, rows), rows)

    copies = [
        send(ref.at[owned(owner)], land.at[slot], slot, mate)
        for slot, (ref, owner) in enumerate(
            ((dk_ref, diagonal), (dv_ref, diagonal), (dk_ref, mate), (dv_ref, mate))
        )
    ]

    def summed(ref, owner, slot, to_ref):
        to_ref[...] = (ref[owned(owner), :].astype(F32) + land[slot].astype(F32)).astype(BF16)

    copies[0].wait()
    summed(dk_ref, across, 0, dkr_ref)
    copies[1].wait()
    summed(dv_ref, across, 1, dvr_ref)

    steps = rows // width
    for r in range(steps):
        at = pl.ds(r * width, width)
        out_far[at, :] = (
            dot_nt(dkr_ref[at, :], wk_ref[...]) + dot_nt(dvr_ref[at, :], wv_ref[...])
        ).astype(BF16)
    far = send(out_far, in_far, 4, across)
    copies[2].wait()
    summed(dk_ref, me, 2, dko_ref)
    copies[3].wait()
    summed(dv_ref, me, 3, dvo_ref)

    def one(r, _):
        at = pl.ds(pl.multiple_of(r * width, width), width)
        dx_ref[at, :] = (
            base_ref[at, :]
            + dot_nt(dq_ref[at, :], wq_ref[...])
            + dot_nt(dko_ref[at, :], wk_ref[...])
            + dot_nt(dvo_ref[at, :], wv_ref[...])
        )
        return 0

    lax.fori_loop(0, steps, one, 0)
    far.wait()
    dx_ref[...] += in_far[...].astype(F32)


def exchange(d_keys, d_values, d_query, base, query_weight, key_weight, value_weight):
    rows, features = d_query.shape
    small = jax.ShapeDtypeStruct((rows, features), BF16)
    return pl.pallas_call(
        functools.partial(exchange_kernel, rows, 128),
        out_shape=(jax.ShapeDtypeStruct((rows, features), F32), small, small, small, small),
        in_specs=[whole_vmem()] * 7,
        out_specs=(whole_vmem(),) * 5,
        scratch_shapes=[
            VMEM((4, rows, features), BF16),
            VMEM((rows, features), BF16),
            VMEM((rows, features), BF16),
            pltpu.SemaphoreType.DMA((5,)),
            pltpu.SemaphoreType.DMA((5,)),
        ],
        compiler_params=pltpu.CompilerParams(
            collective_id=1, has_side_effects=True, vmem_limit_bytes=LIMIT
        ),
        name="exchange",
    )(d_keys, d_values, d_query, base, query_weight, key_weight, value_weight)


def summed_anywhere(square, up, down, vectors, up_bias):
    def one(g):
        return lax.psum_scatter(g, ("dp", "seq"), scatter_dimension=0, tiled=True)

    return [one(g) for g in square], one(up), one(down), [one(v) for v in vectors], one(up_bias)


GELU_A = 0.044715
GELU_C = 0.7978845608028654
UNIT = (48, 384)
ORDERS = (
    "xyz", "zyx", "yxz", "zxy", "yxz", "xyz", "yzx", "yxz", "yzx", "yxz", "xzy", "xzy",
)
UP, SQUARE = 4, 8
OUT, KEY, VALUE, QUERY = 8, 9, 10, 11
RIDERS = (OUT, VALUE)
EVENTS = {
    "up": ((0, 0), (2, 0)),
    "dense": (),
    0: ((4, 0), (5, 0), (1, 0), (2, 1)),
    1: ((6, 0),),
    2: ((4, 1),),
    3: ((7, 0), (3, 0)),
    4: ((0, 1),),
    5: ((7, 1),),
    "sum": ((8, 0), (6, 1), (3, 1)),
    "far": ((5, 1), (1, 1)),
    "x": (),
    "y": ((2, 2), (4, 2), (6, 2), (3, 2), (0, 2)),
    "end": ((11, 0), (8, 1), (9, 0), (10, 0), (9, 1), (11, 1), (7, 2), (5, 2), (1, 2), (8, 2), (10, 1), ("far", 0), (11, 2), (9, 2), (10, 2)),
}


def normed_rows(values):
    center = jnp.mean(values, axis=-1, keepdims=True)
    centered = values - center
    variance = jnp.mean(centered * centered, axis=-1, keepdims=True)
    inv_root = lax.rsqrt(variance + NORM_EPS)
    return centered * inv_root, inv_root


def norm_pull(grad_out, normed, inv_root, gain):
    d_normed = grad_out * gain
    return inv_root * (
        d_normed
        - jnp.mean(d_normed, axis=-1, keepdims=True)
        - normed * jnp.mean(d_normed * normed, axis=-1, keepdims=True)
    )


def column_sum(values):
    return jnp.sum(values, axis=0, keepdims=True)


def layer_kernel(
    rows, tile, own_blocks, groups, tab_ref, prev_ref, tail_ref, mask_ref, bo_ref, g1_ref, s1_ref,
    bd_ref, g2_ref, s2_ref, bu_ref,
    x_any, cot_any, wo_any, wu_any, wd_any, q_any, k_any, v_any, wk_any, wv_any, wq_any,
    far_any,
    result_ref, dx_ref, gq_ref, gk_ref, gv_ref, go_ref, up_ref, down_ref, vec_ref,
    work, land, core_down, core_up, pair_in, in_far, small, late,
    ride, ride_land, ride_core_in,
    x_ref, merged_ref, d_attn_ref, d_merged_ref, q_ref, k_ref, v_ref, lse_ref,
    loads, sends, recvs, c_sends, c_recvs, p_sends, p_recvs, r_sends, r_recvs, far_sems,
):
    features = x_ref.shape[1]
    hidden = bu_ref.shape[1]
    wide = hidden // features
    pairs = features // PAIR
    picks_count = own_blocks * 3
    share = features // (8 * groups)
    shards = 4 * groups
    half = features // 2
    dp, seq = lax.axis_index("dp"), lax.axis_index("seq")
    x, z = lax.rem(dp, 2), dp // 2
    core, y = lax.rem(seq, 2), seq // 2
    mate, across, diagonal = (lax.bitwise_xor(seq, bit) for bit in (1, 2, 3))
    end = prev_ref[0, 0, 127]
    first_block = seq * own_blocks
    low = lanes_low(BLK)
    to_mate, to_y = (dp, mate), (dp, across)
    place_of = {"x": (x, 2), "y": (y, 2), "z": (z, groups)}

    def device(axis, index):
        if axis == "x":
            return (2 * z + index, seq)
        if axis == "y":
            return (dp, 2 * index + core)
        return (2 * index + x, seq)

    neighbours = [to_mate, to_y, device("x", 1 - x)] + [
        device("z", lax.rem(z + step, groups)) for step in range(1, groups)]

    loading = {}

    def load(name, src, dst):
        copy = pltpu.make_async_copy(src, dst, loads.at[len(loading)])
        copy.start()
        loading[name] = copy

    def remote(src, dst, one, two, target):
        return pltpu.make_async_remote_copy(
            src_ref=src, dst_ref=dst, send_sem=one, recv_sem=two, device_id=target,
            device_id_type=MESH,
        )

    def lanes_of(p):
        return pl.ds(pl.multiple_of(p * PAIR, PAIR), PAIR)

    def columns(j):
        return pl.ds(pl.multiple_of(j * features, features), features)

    def tiles(body):
        def step(r, _):
            body(pl.ds(pl.multiple_of(r * tile, tile), tile), r)
            return 0

        lax.fori_loop(0, rows // tile, step, 0)


    def index_of(u, at_x, at_y, at_z):
        at = {"x": at_x, "y": at_y, "z": at_z}
        flat = 0
        for axis in ORDERS[u]:
            flat = flat * place_of[axis][1] + at[axis]
        return flat

    def shard_of(s):
        return s // 4, lax.rem(s // 2, 2), lax.rem(s, 2)

    def stage_of(u, stage):
        sizes = [place_of[axis][1] for axis in ORDERS[u]] + [1]
        base, offset, sem, block = 0, 0, 0, shards
        for n, axis in enumerate(ORDERS[u]):
            block = block // sizes[n]
            if n == stage:
                return axis, place_of[axis][0], sizes[n], block, base, offset, sem
            base = base + place_of[axis][0] * block
            offset += (sizes[n] - 1) * block
            sem += sizes[n] - 1
        return None

    def stage_copies(u, stage):
        axis, mine, size, block, base, offset, sem = stage_of(u, stage)
        copies = []
        for step in range(1, size):
            index = lax.rem(mine + step, size)
            copies.append(remote(
                work.at[u, pl.ds(base + index * block, block)],
                land.at[u, pl.ds(offset + (step - 1) * block, block)],
                sends.at[u, sem + step - 1], recvs.at[u, sem + step - 1], device(axis, index)))
            if u in RIDERS:
                n = RIDERS.index(u)
                copies.append(remote(
                    ride.at[n, core, pl.ds(base + index * block, block)],
                    ride_land.at[n, pl.ds(offset + (step - 1) * block, block)],
                    r_sends.at[n, sem + step - 1], r_recvs.at[n, sem + step - 1],
                    device(axis, index)))
        return copies

    def begin(u, stage):
        for copy in stage_copies(u, stage):
            copy.start()

    def finish(u, stage):
        _, mine, size, block, base, offset, _ = stage_of(u, stage)
        for copy in stage_copies(u, stage):
            copy.wait()

        def total(r):
            value = work[u, base + mine * block + r].astype(F32)
            for step in range(size - 1):
                value = value + land[u, offset + step * block + r].astype(F32)
            return value

        if u in RIDERS:
            n = RIDERS.index(u)

            def ridden(r):
                value = ride[n, core, base + mine * block + r]
                for step in range(size - 1):
                    value = value + ride_land[n, offset + step * block + r]
                return value

        if stage < 2:
            def body(r, _):
                work[u, base + mine * block + r] = total(r).astype(BF16)
                if u in RIDERS:
                    ride[n, core, base + mine * block + r] = ridden(r)
                return 0

            lax.fori_loop(0, block, body, 0)
            begin(u, stage + 1)
            return
        value = total(0)
        if u in RIDERS:
            vec_ref[n * 16:(n + 1) * 16, :] = ridden(0)
        if u < UP:
            down_ref[(u // 2) * UNIT[0]:(u // 2 + 1) * UNIT[0], (u % 2) * half:(u % 2 + 1) * half] = value
        else:
            to = up_ref if u < SQUARE else (go_ref, gk_ref, gv_ref, gq_ref)[u - SQUARE]
            at = (u - UP) * features if u < SQUARE else 0
            to[:, at:at + half] = value[:share]
            to[:, at + half:at + features] = value[share:]

    def folded(source, at, count):
        return jnp.concatenate(
            [source[pl.ds(at, count), 0:half], source[pl.ds(at, count), half:features]], axis=0)

    def split_pieces(u, read, other):
        def body(s, _):
            at_z, at_x, at_y = shard_of(s)
            index = index_of(u, at_x, at_y, at_z)
            for own in (True, False):
                row = 2 * s + (core if own else 1 - core)
                value = read(pl.multiple_of(row * share, 8), share).astype(BF16)
                if own:
                    work[u, index] = value
                else:
                    other[index // 4, lax.rem(index, 4)] = value
            return 0

        lax.fori_loop(0, shards, body, 0)

    def add_core(u, landed):
        def body(n, _):
            work[u, n] = (
                work[u, n].astype(F32) + landed[n // 4, lax.rem(n, 4)].astype(F32)
            ).astype(BF16)
            return 0

        lax.fori_loop(0, shards, body, 0)

    def at_point(name):
        for u, stage in EVENTS[name]:
            finish(u, stage)

    def vector_pieces(rider):
        count = 6 if rider == 0 else 2
        padded = jnp.zeros((16 - 8, 128 - share), F32)
        for s in range(shards):
            index = index_of(RIDERS[rider], (s // 2) % 2, s % 2, s // 4)
            for n in range(2):
                row = 2 * s + n
                at = row * share
                source = small if rider == 0 else late
                value = source[0:8, at:at + share]
                ride[rider, n, index, 0:8, :] = jnp.concatenate([value, padded], axis=1)
                if rider == 0:
                    start = (row % (2 * groups)) * (wide * share)
                    ride[rider, n, index, 8:16, :] = jnp.concatenate(
                        [small[8:16, start:start + wide * share],
                         jnp.zeros((8, 128 - wide * share), F32)], axis=1)
                else:
                    ride[rider, n, index, 8:16, :] = jnp.zeros((8, 128), F32)

    def ride_core(rider):
        return remote(ride.at[rider, 1 - core], ride_core_in.at[rider], r_sends.at[rider, groups + 1],
                      r_recvs.at[rider, groups + 1], to_mate)

    def core_copy(src, dst, slot):
        return remote(src, dst, c_sends.at[slot], c_recvs.at[slot], to_mate)

    load("q", q_any, q_ref)
    load("k", k_any, k_ref)
    load("v", v_any, v_ref)
    barrier = pltpu.get_barrier_semaphore()
    for target in neighbours:
        pl.semaphore_signal(barrier, inc=1, device_id=target, device_id_type=MESH)
    last_row = k_ref.shape[0] - 1

    def forward_pair(p):
        lanes = lanes_of(p)

        def step(i, _):
            at = first_block + i
            shared, both = key_blocks(tab_ref, end, p, i, at, last_row)
            keys = gathered(k_ref, shared, both, low, lanes)
            values = gathered(v_ref, shared, both, low, lanes)
            query = split_pair(q_ref[rows_of(i), lanes], low)
            merged, lse = attend(keys, values, query, mask_ref, i, low)
            live = lax.broadcasted_iota(jnp.int32, (BLK, 1), 0) < (end + 1 - at) * BLK
            merged_ref[rows_of(i), lanes] = jnp.where(live, merged, 0.0).astype(BF16)
            lse_ref[p, pl.ds(i, 1), :] = lse
            return 0

        lax.fori_loop(0, own_blocks, step, 0, unroll=own_blocks)


    def dense(
        wo, wu, wd, cot_ref, normed_one, root_one, first_low, act, slope, ffn, tmp, other,
    ):
        d_ffn = cot_ref
        for name in ("q", "k", "v"):
            loading[name].wait()
        for name, src, dst in (
            ("x", x_any, x_ref), ("wo", wo_any, wo), ("wu", wu_any, wu), ("wd", wd_any, wd),
            ("cot", cot_any, cot_ref),
        ):
            load(name, src, dst)

        def forward_two(n, _):
            for inner in range(2):
                forward_pair(2 * n + inner)
            return 0

        lax.fori_loop(0, pairs // 2, forward_two, 0)
        bo, g1, s1, bd, g2, s2 = (
            ref[...][None] for ref in (bo_ref, g1_ref, s1_ref, bd_ref, g2_ref, s2_ref))

        for name in ("x", "wo"):
            loading[name].wait()
        ffn[...] = dot(merged_ref[...], wo[...])

        def norm_one(at, r):
            normed, inv_root = normed_rows(x_ref[at, :].astype(F32) + (ffn[at, :] + bo))
            normed_one[at, :] = normed
            root_one[at, :] = inv_root
            first_low[at, :] = (normed * g1 + s1).astype(BF16)

        tiles(norm_one)

        loading["wu"].wait()
        loading["wd"].wait()
        ffn[...] = jnp.zeros_like(ffn)

        def forward(j, _):
            at = columns(j)
            u = dot(first_low[...], wu[:, at]) + bu_ref[:, at]
            square = u * u
            t = jnp.tanh(GELU_C * (u + GELU_A * (square * u)))
            upper = 0.5 * (1.0 + t)
            act[j] = (u * upper).astype(BF16)
            slope[j] = (
                upper + (0.5 * GELU_C) * u * (1.0 - t * t) * (1.0 + (3.0 * GELU_A) * square)
            ).astype(slope.dtype)
            ffn[...] += dot(act[j], wd[at, :])
            return 0

        lax.fori_loop(0, wide, forward, 0)

        small[...] = jnp.zeros_like(small)
        limit = (end + 1) * BLK - seq * rows
        loading["cot"].wait()

        def norm_two(at, r):
            first = normed_one[at, :] * g1 + s1
            normed, inv_root = normed_rows(first + (ffn[at, :] + bd))
            result_ref[at, :] = (normed * g2 + s2).astype(BF16)
            place = lax.broadcasted_iota(jnp.int32, (tile, 1), 0) + r * tile
            grad = cot_ref[at, :].astype(F32) * (place < limit).astype(F32)
            pulled = norm_pull(grad, normed, inv_root, g2)
            rounded = pulled.astype(BF16)
            ffn[at, :] = pulled
            d_ffn[at, :] = rounded
            small[0:1, :] += column_sum(grad * normed)
            small[1:2, :] += column_sum(grad)
            small[2:3, :] += column_sum(rounded.astype(F32))

        tiles(norm_two)

        pl.semaphore_wait(barrier, len(neighbours))
        down_copies = []
        for j in range(wide):
            tmp[...] = dot_tn(act[j], d_ffn[...])

            def pieces(n, _):
                at_x, at_y = n // 2, lax.rem(n, 2)
                for own in (True, False):
                    row = 2 * n + (core if own else 1 - core)
                    at = pl.multiple_of(row * (wide * share), 8)
                    for u in range(4):
                        value = tmp[
                            pl.ds(pl.multiple_of(at + (u // 2) * UNIT[0], 8), UNIT[0]),
                            (u % 2) * half:(u % 2 + 1) * half].astype(BF16)
                        if own:
                            work[u, index_of(u, at_x, at_y, j)] = value
                        else:
                            other[j, u, n] = value
                return 0

            lax.fori_loop(0, 4, pieces, 0)
            down_copies.append(core_copy(other.at[j], core_down.at[j], j))
            down_copies[-1].start()

        def backward(j, _):
            d_hidden = (dot_nt(d_ffn[...], wd[columns(j), :]) * slope[j].astype(F32)).astype(BF16)
            act[j] = d_hidden
            for n in range(wide):
                @pl.when(j == n)
                def _():
                    small[8 + n:9 + n, :] = column_sum(d_hidden.astype(F32))
            return 0

        lax.fori_loop(0, wide, backward, 0)

        for copy in down_copies:
            copy.wait()

        def sum_down(s, _):
            at_z, at_x, at_y = shard_of(s)
            for u in range(4):
                index = index_of(u, at_x, at_y, at_z)
                work[u, index] = (
                    work[u, index].astype(F32) + core_down[at_z, u, at_x * 2 + at_y].astype(F32)
                ).astype(BF16)
            return 0

        lax.fori_loop(0, shards, sum_down, 0)
        for u in range(4):
            begin(u, 0)

        up_copies = []

        def end_up(j):
            up_copies[j].wait()
            add_core(UP + j, core_up.at[j])
            begin(UP + j, 0)

        for j in range(wide):
            tmp[...] = dot_tn(first_low[...], act[j])
            split_pieces(UP + j, functools.partial(folded, tmp), other.at[j])
            up_copies.append(core_copy(other.at[j], core_up.at[j], wide + j))
            up_copies[-1].start()
            if j:
                end_up(j - 1)

        for j in range(wide):
            ffn[...] += dot_nt(act[j], wu[:, j * features:(j + 1) * features])
            if j == 1:
                end_up(wide - 1)
        at_point("up")

        def pull_one(at, r):
            grad = ffn[at, :]
            normed = normed_one[at, :]
            pulled = norm_pull(grad, normed, root_one[at, :], g1)
            rounded = pulled.astype(BF16)
            dx_ref[at, :] = pulled
            d_attn_ref[at, :] = rounded
            small[3:4, :] += column_sum(grad * normed)
            small[4:5, :] += column_sum(grad)
            small[5:6, :] += column_sum(rounded.astype(F32))

        tiles(pull_one)
        live = lax.broadcasted_iota(jnp.int32, (rows, 1), 0) < limit
        d_merged_ref[...] = jnp.where(live, dot_nt(d_attn_ref[...], wo[...]), 0.0).astype(BF16)
        at_point("dense")

    low_rows = VMEM((rows, features), BF16)
    full_rows = VMEM((rows, features), F32)
    square_low = VMEM((features, features), BF16)
    pl.run_scoped(
        dense, square_low, VMEM((features, hidden), BF16), VMEM((hidden, features), BF16),
        low_rows, full_rows, VMEM((rows, 1), F32), low_rows, VMEM((wide, rows, features), BF16),
        VMEM((wide, rows, features), SLOPE), full_rows, VMEM((features, features), F32),
        VMEM((4, 4, 4) + UNIT, BF16),
    )


    def attention(
        dq_ref, far_ref, wk, wv, wq, acc, last, picked, buf, dko, dvo, dkr, dvr, out_far, other,
        tmp,
    ):
        for name, src, dst in (
            ("far", far_any, far_ref), ("wk", wk_any, wk), ("wv", wv_any, wv), ("wq", wq_any, wq),
        ):
            load(name, src, dst)
        square_copies = [
            core_copy(other.at[n], core_down.at[n], SQUARE + n) for n in range(4)
        ]

        def square(u):
            split_pieces(u, functools.partial(folded, tmp), other.at[u - SQUARE])
            square_copies[u - SQUARE].start()

        def end_square(u):
            square_copies[u - SQUARE].wait()
            if u in RIDERS:
                n = RIDERS.index(u)
                ride_core(n).wait()
                ride[n, core] = ride[n, core] + ride_core_in[n]
            add_core(u, core_down.at[u - SQUARE])
            begin(u, 0)

        def copy_pair(p, slot, owner):
            return remote(buf.at[p, owner], pair_in.at[p, slot], p_sends.at[p, slot],
                          p_recvs.at[p, slot], to_mate)

        def sum_pair(p):
            lanes = lanes_of(p)
            for slot, owner, keys_to, values_to in ((0, across, dkr, dvr), (1, seq, dko, dvo)):
                copy_pair(p, slot, diagonal if slot == 0 else mate).wait()
                for n, to in ((0, keys_to), (1, values_to)):
                    to[:, lanes] = (
                        buf[p, owner, n].astype(F32) + pair_in[p, slot, n].astype(F32)
                    ).astype(BF16)

        def heads():
            for n in range(2):
                picked[n, picks_count] = jnp.zeros((BLK, PAIR), F32)
                for edge in (0, own_blocks + 3):
                    acc[n, edge] = jnp.zeros((BLK, PAIR), F32)
            def one_pair(p, _):
                lanes = lanes_of(p)
                acc[:, 1:own_blocks + 3] = jnp.zeros((2, own_blocks + 2, BLK, PAIR), F32)
                last[...] = jnp.zeros_like(last)

                def step(i, _):
                    at = first_block + i
                    shared, both = key_blocks(tab_ref, end, p, i, at, last_row)
                    keys = gathered(k_ref, shared, both, low, lanes)
                    values = gathered(v_ref, shared, both, low, lanes)
                    query = split_pair(q_ref[rows_of(i), lanes], low)
                    grad = split_pair(d_merged_ref[rows_of(i), lanes], low)
                    blank = jnp.zeros_like(query)
                    both_in = jnp.concatenate(
                        [jnp.concatenate([query, blank], axis=1),
                         jnp.concatenate([blank, grad], axis=1)], axis=0)
                    products = dot_nt(jnp.concatenate([keys, values], axis=1), both_in)
                    scores = masked_scores(products[:, :PAIR], mask_ref, i)
                    share_of = jnp.exp(scores - lse_ref[p, pl.ds(i, 1), :])
                    d_share = products[:, PAIR:]
                    centre = jnp.sum(share_of * d_share, axis=0, keepdims=True)
                    d_scores = (share_of * (d_share - centre)).astype(BF16)
                    d_query = dot_tn(d_scores, keys) * SCALE
                    dq_ref[rows_of(i), lanes] = jnp.where(
                        low, d_query[:BLK], d_query[BLK:]).astype(BF16)
                    products = dot(
                        jnp.concatenate([d_scores, share_of.astype(BF16)], axis=1), both_in)
                    parts = (products[:, :PAIR], products[:, PAIR:])
                    for n, part in enumerate(parts):
                        for slot in range(3):
                            acc[n, i + slot + 1] += part[slot * BLK:(slot + 1) * BLK]
                        for slot in range(2):
                            last[n, slot] += part[(3 + slot) * BLK:(4 + slot) * BLK]
                    for t in range(3):
                        one, two = (
                            prev_ref[lax.div(h, 3), i, lax.rem(h, 3) * 3 + t]
                            for h in (2 * p, 2 * p + 1))
                        for n, part in enumerate(parts):
                            picked[n, i * 3 + t] = part[(5 + t) * BLK:(6 + t) * BLK] + jnp.where(
                                low, picked[n, one], picked[n, two])
                    return 0

                lax.fori_loop(0, own_blocks, step, 0, unroll=own_blocks)

                def gather(owner, _):
                    first_owner = (owner == 0).astype(F32)
                    for inner in range(own_blocks):
                        block = owner * own_blocks + inner
                        window = jnp.minimum(
                            jnp.maximum(block - first_block + 2, 0), own_blocks + 3)
                        one, two = (
                            tail_ref[lax.div(h, 3), lax.rem(h, 3), block]
                            for h in (2 * p, 2 * p + 1))
                        for n in range(2):
                            total = acc[n, window] + jnp.where(low, picked[n, one], picked[n, two])
                            total = total + last[n, 1] * mask_ref[own_blocks, block]
                            if inner == 0:
                                total = total + last[n, 0] * first_owner
                            buf[p, owner, n, inner * BLK:(inner + 1) * BLK] = total.astype(BF16)
                    return 0

                lax.fori_loop(0, 4, gather, 0)
                copy_pair(p, 0, diagonal).start()
                copy_pair(p, 1, mate).start()

                @pl.when(p > 0)
                def _():
                    sum_pair(p - 1)

                for n in range(pairs):
                    @pl.when(p == n)
                    def _():
                        if n == 0:
                            end_square(OUT)
                        at_point(n)

                return 0

            lax.fori_loop(0, pairs, one_pair, 0)

        vector_pieces(0)
        ride_core(0).start()
        tmp[...] = dot_tn(merged_ref[...], d_attn_ref[...])
        square(OUT)
        heads()
        tmp[...] = dot_tn(x_ref[...], dq_ref[...])
        square(QUERY)
        for name in ("far", "wk", "wv", "wq"):
            loading[name].wait()
        sum_pair(pairs - 1)
        at_point("sum")
        tmp[...] = dot_tn(x_ref[...], dko[...]) + dot_tn(far_ref[...], dkr[...])
        square(KEY)
        end_square(QUERY)
        tmp[...] = dot_tn(x_ref[...], dvo[...]) + dot_tn(far_ref[...], dvr[...])
        square(VALUE)
        end_square(KEY)
        late[...] = jnp.zeros_like(late)
        late[0:1, :] = column_sum(dq_ref[...].astype(F32))
        late[1:2, :] = column_sum(dvo[...].astype(F32)) + column_sum(dvr[...].astype(F32))
        vector_pieces(1)
        ride_core(1).start()
        out_far[...] = (dot_nt(dkr[...], wk[...]) + dot_nt(dvr[...], wv[...])).astype(BF16)
        far = remote(out_far, in_far, far_sems.at[0], far_sems.at[1], to_y)
        far.start()
        end_square(VALUE)
        at_point("far")
        dx_ref[...] += dot_nt(dko[...], wk[...]) + dot_nt(dvo[...], wv[...])
        at_point("x")
        dx_ref[...] += dot_nt(dq_ref[...], wq[...])
        at_point("y")
        for u, stage in EVENTS["end"]:
            if u == "far":
                far.wait()
                dx_ref[...] += in_far[...].astype(F32)
            else:
                finish(u, stage)

    pl.run_scoped(
        attention, low_rows, low_rows, square_low, square_low, square_low,
        VMEM((2, own_blocks + 4, BLK, PAIR), F32), VMEM((2, 2, BLK, PAIR), F32),
        VMEM((2, picks_count + 1, BLK, PAIR), F32), VMEM((pairs, 4, 2, rows, PAIR), BF16),
        low_rows, low_rows, low_rows, low_rows, low_rows, VMEM((4, 4, 4) + UNIT, BF16),
        VMEM((features, features), F32),
    )


SLOPE = BF16


def layer_tail(
    groups, table, prev, tail, mask, biases, up_bias, tokens, cotangent, out_weight,
    up_weight, down_weight, query, keys, values, key_weight, value_weight, query_weight, far_tokens,
):
    rows, features = tokens.shape
    hidden = up_weight.shape[1]
    own_blocks = rows // BLK
    pairs = features // PAIR
    share = features // (8 * groups)
    wide = hidden // features
    low = VMEM((rows, features), BF16)
    kv = VMEM((4 * own_blocks, BLK, features), BF16)
    line = jax.ShapeDtypeStruct((share, features), F32)
    any_space = pl.BlockSpec(memory_space=pl.ANY)
    in_smem = pl.BlockSpec(memory_space=pltpu.SMEM)
    dma = pltpu.SemaphoreType.DMA
    return pl.pallas_call(
        functools.partial(layer_kernel, rows, 128, own_blocks, groups),
        out_shape=(
            jax.ShapeDtypeStruct((rows, features), BF16),
            jax.ShapeDtypeStruct((rows, features), F32), line, line, line, line,
            jax.ShapeDtypeStruct((share, hidden), F32),
            jax.ShapeDtypeStruct((wide * share, features), F32),
            jax.ShapeDtypeStruct((32, 128), F32),
        ),
        in_specs=[in_smem] * 4 + [whole_vmem()] * 7 + [any_space] * 12,
        out_specs=(whole_vmem(),) * 9,
        scratch_shapes=[
            VMEM((12, 4 * groups) + UNIT, BF16),
            VMEM((12, 4 * groups - 1) + UNIT, BF16),
            VMEM((4, 4, 4) + UNIT, BF16),
            VMEM((4, 4, 4) + UNIT, BF16),
            VMEM((pairs, 2, 2, rows, PAIR), BF16),
            low,
            VMEM((16, features), F32),
            VMEM((8, features), F32),
            VMEM((2, 2, 4 * groups, 16, 128), F32),
            VMEM((2, 4 * groups - 1, 16, 128), F32),
            VMEM((2, 4 * groups, 16, 128), F32),
            low, low, low, low, low, kv, kv, VMEM((pairs, own_blocks, PAIR), F32),
            dma((13,)), dma((12, groups + 1)), dma((12, groups + 1)), dma((12,)), dma((12,)),
            dma((pairs, 2)), dma((pairs, 2)), dma((2, groups + 2)), dma((2, groups + 2)),
            dma((2,)),
        ],
        compiler_params=pltpu.CompilerParams(
            collective_id=3, has_side_effects=True, vmem_limit_bytes=LIMIT
        ),
        name="layer_tail",
    )(
        table, prev, tail, mask, *biases, up_bias, tokens, cotangent, out_weight, up_weight,
        down_weight, query, keys, values, key_weight, value_weight, query_weight, far_tokens,
    )


def finish_kernel(groups, vec_ref, *refs):
    count = len(refs) - 9
    given, out, vectors = refs[:count // 2], refs[count // 2:count], refs[count:]
    for src, dst in zip(given, out):
        dst[...] = src[...]
    share = vectors[0].shape[0]
    for n in range(8):
        vectors[n][...] = vec_ref[n if n < 6 else n + 10, 0:share]
    shard = lax.axis_index("dp") * 4 + lax.axis_index("seq")
    mine = vec_ref[pl.ds(8 + shard // (2 * groups), 1), :]
    vectors[8][...] = mine[0, 0:vectors[8].shape[0]]


STEPS = 2


def whole(shape):
    return pl.BlockSpec(shape, lambda i: (0,) * len(shape))


def hand_out(groups, vectors, arrays):
    features = arrays[0].shape[1]
    share = features // (8 * groups)
    wide = arrays[-1].shape[0] // share
    shapes = [jax.ShapeDtypeStruct(a.shape, a.dtype) for a in arrays]
    specs = [
        pl.BlockSpec((a.shape[0] // STEPS, a.shape[1]), lambda i: (i, 0))
        if a.shape[0] % (16 * STEPS) == 0 else whole(a.shape) for a in arrays
    ]
    lines = [jax.ShapeDtypeStruct((share,), F32)] * 8 + [jax.ShapeDtypeStruct((wide * share,), F32)]
    return pl.pallas_call(
        functools.partial(finish_kernel, groups),
        out_shape=tuple(shapes + lines),
        grid=(STEPS,),
        in_specs=[whole((32, 128))] + specs,
        out_specs=tuple(specs) + (whole((share,)),) * 8 + (whole((wide * share,)),),
        name="hand_out",
    )(vectors, *arrays)


def layer_norm(values, gain, shift):
    center = jnp.mean(values, axis=-1, keepdims=True)
    centered = values - center
    variance = jnp.mean(centered * centered, axis=-1, keepdims=True)
    inv_root = lax.rsqrt(variance + NORM_EPS)
    normed = centered * inv_root
    return (normed * gain + shift, normed, inv_root)


def norm_back(grad_out, normed, inv_root, gain):
    d_normed = grad_out * gain
    grad_in = inv_root * (
        d_normed
        - jnp.mean(d_normed, axis=-1, keepdims=True)
        - normed * jnp.mean(d_normed * normed, axis=-1, keepdims=True)
    )
    return (grad_in, jnp.sum(grad_out * normed, axis=0), jnp.sum(grad_out, axis=0))


def on_device(
    groups,
    tokens, filled_blocks, random_blocks, query_weight, query_bias, key_weight, value_weight,
    value_bias, out_weight, out_bias, attn_gain, attn_shift, up_weight, up_bias, down_weight,
    down_bias, ffn_gain, ffn_shift, cotangent,
):
    row_count, feature_count = tokens.shape
    filled = filled_blocks[0]
    place = lax.axis_index("seq") * row_count + jnp.arange(row_count, dtype=jnp.int32)
    live_tokens = (place < filled * BLK).astype(F32)[:, None]

    query, keys, values, far_tokens, table, prev, tail, mask = gather_project(
        filled_blocks, tokens,
        random_blocks.transpose(2, 3, 0, 1), query_weight, key_weight, value_weight, query_bias,
        value_bias)
    keys, values = (t.reshape(-1, BLK, feature_count) for t in (keys, values))
    if groups:
        *arrays, vectors = layer_tail(
            groups, table, prev, tail, mask,
            (out_bias, attn_gain, attn_shift, down_bias, ffn_gain, ffn_shift), up_bias[None],
            tokens, cotangent, out_weight, up_weight, down_weight, query, keys, values,
            key_weight, value_weight, query_weight, far_tokens)
        (result, grad_tokens, gq, gk, gv, go, up, down, g2, s2, bd, g1, s1, bo, bq, bv,
         bu) = hand_out(groups, vectors, arrays)
        return (
            result, grad_tokens, gq, bq, gk, gv, bv, go, bo, g1, s1, up, bu, down, bd, g2, s2)

    merged, lse = attention_forward(table, filled_blocks, mask, query, keys, values)
    attn = dot(merged, out_weight) + out_bias
    first, normed_one, root_one = layer_norm(tokens.astype(F32) + attn, attn_gain, attn_shift)
    first_low = first.astype(BF16)
    hidden = dot(first_low, up_weight) + up_bias
    act, gelu_pull = jax.vjp(jax.nn.gelu, hidden)
    act_low = act.astype(BF16)
    ffn = dot(act_low, down_weight) + down_bias
    result, normed_two, root_two = layer_norm(first + ffn, ffn_gain, ffn_shift)
    grad_result = cotangent.astype(F32) * live_tokens
    d_sum_two, grad_ffn_gain, grad_ffn_shift = norm_back(
        grad_result, normed_two, root_two, ffn_gain
    )
    d_ffn = d_sum_two.astype(BF16)
    grad_down_bias = jnp.sum(d_ffn, axis=0, dtype=F32)
    grad_down_weight = dot_tn(act_low, d_ffn)
    d_act = dot_nt(d_ffn, down_weight)
    d_hidden = gelu_pull(d_act)[0].astype(BF16)
    grad_up_bias = jnp.sum(d_hidden, axis=0, dtype=F32)
    grad_up_weight = dot_tn(first_low, d_hidden)
    d_first = d_sum_two + dot_nt(d_hidden, up_weight)
    d_sum_one, grad_attn_gain, grad_attn_shift = norm_back(d_first, normed_one, root_one, attn_gain)
    d_attn = d_sum_one.astype(BF16)
    grad_out_bias = jnp.sum(d_attn, axis=0, dtype=F32)
    grad_out_weight = dot_tn(merged, d_attn)
    d_merged = dot_nt(d_attn, out_weight).astype(BF16)

    d_query, d_keys, d_values = attention_backward(
        table, filled_blocks, mask, query, keys, values, d_merged, lse
    )
    grad_tokens, dk_own, dv_own, dk_far, dv_far = exchange(
        d_keys, d_values, d_query, d_sum_one, query_weight, key_weight, value_weight
    )
    grad_query_weight = dot_tn(tokens, d_query)
    grad_query_bias = jnp.sum(d_query, axis=0, dtype=F32)
    grad_key_weight = dot_tn(tokens, dk_own) + dot_tn(far_tokens, dk_far)
    grad_value_weight = dot_tn(tokens, dv_own) + dot_tn(far_tokens, dv_far)
    grad_value_bias = jnp.sum(dv_own, axis=0, dtype=F32) + jnp.sum(dv_far, axis=0, dtype=F32)

    square = (grad_query_weight, grad_key_weight, grad_value_weight, grad_out_weight)
    vectors = (
        grad_query_bias, grad_value_bias, grad_out_bias, grad_attn_gain, grad_attn_shift,
        grad_down_bias, grad_ffn_gain, grad_ffn_shift,
    )
    square, up, down, vectors, up_sum = summed_anywhere(
        square, grad_up_weight, grad_down_weight, vectors, grad_up_bias)
    return (
        result.astype(BF16), grad_tokens, square[0], vectors[0], square[1], square[2], vectors[1],
        square[3], vectors[2], vectors[3], vectors[4], up, up_sum, down, vectors[5], vectors[6],
        vectors[7],
    )


def solution(mesh):
    both = P(("dp", "seq"), None)
    line = P(("dp", "seq"))
    placed = (both, P("dp"), P("dp", None, "seq", None)) + (P(),) * 15 + (both,)
    groups = 4 if mesh.shape["dp"] == 8 and mesh.shape["seq"] == 4 else 0
    return jax.shard_map(
        functools.partial(on_device, groups),
        mesh=mesh,
        in_specs=placed,
        out_specs=(
            both, both, both, line, both, both, line, both, line, line, line, both, line, both,
            line, line, line,
        ),
        check_vma=False,
    )
```
